32 devices in a mesh: ctx: 32 (over z, y, x, core).
Axes of the slice: x: 2, y: 2, z: 4, core: 2. Of those that a mesh axis runs over, the one named last changes fastest.
Arguments:
- hidden_in: bfloat16 [4096, 576], P('ctx'), may hold values from -6 to 6
- attention_gain: float32 [576], replicated, may hold values from 0.5 to 1.5
- query_weight: bfloat16 [32, 10368], P('ctx'), may hold values from -0.25 to 0.25
- key_weight: bfloat16 [32, 3456], P('ctx'), may hold values from -0.25 to 0.25
- value_weight: bfloat16 [32, 3456], P('ctx'), may hold values from -0.25 to 0.25
- output_weight: bfloat16 [32, 10368], P('ctx'), may hold values from -2 to 2
- feedforward_gain: float32 [576], replicated, may hold values from 0.5 to 1.5
- gate_weight: bfloat16 [32, 27648], P('ctx'), may hold values from -0.25 to 0.25
- up_weight: bfloat16 [32, 27648], P('ctx'), may hold values from -0.25 to 0.25
- down_weight: bfloat16 [32, 27648], P('ctx'), may hold values from -0.15625 to 0.15625
- doc_of_block: int32 [64], replicated, may hold values from 0 to 1, as said below
- pair_table: int32 [32], replicated, may hold values from 0 to 31, each once
- out_grad: bfloat16 [4096, 576], P('ctx'), may hold values from -6 to 6
Outputs:
- block_out: bfloat16 [4096, 576], P('ctx')
- input_grad: bfloat16 [4096, 576], P('ctx')
- attention_gain_grad: float32 [576], replicated
- query_weight_grad: float32 [32, 10368], P('ctx')
- key_weight_grad: float32 [32, 3456], P('ctx')
- value_weight_grad: float32 [32, 3456], P('ctx')
- output_weight_grad: float32 [32, 10368], P('ctx')
- feedforward_gain_grad: float32 [576], replicated
- gate_weight_grad: float32 [32, 27648], P('ctx')
- up_weight_grad: float32 [32, 27648], P('ctx')
- down_weight_grad: float32 [32, 27648], P('ctx')
The draws below stay inside these ranges and needn't reach their ends.
Inputs may be any that keep to these rules, and one draw needn't show every extreme that they name: `doc_of_block`: never falling along the stream, rising by at most one from block to block; document 0 starts at block 0 and holds 32 to 40 blocks; every document holds max(1, 16) blocks or more. `pair_table`: each value once.
All inputs are finite; a program needn't handle non-finite values.
Results may differ from the reference program's by a relative error of at most 0.025.
Values may be sent and summed in bfloat16 or wider, within the bound.
No kernel may reach another device: no remote copies, remote signals or barrier semaphores. Data moves between devices by JAX's collectives and lax.ppermute only.
A program may use at most 192 MiB of HBM per device.

```python
import math
import jax
import jax.numpy as jnp
from jax import lax

D = 576
HEADS = 9
KV_HEADS = 3
HEAD_SIZE = 64
FF = 1536
TOK_DEV = 128
DOC_MIN = 1024
TOKENS = 4096
KV_WIDTH = 192
N_CTX = 32


def draw_doc_of_block(key, part):
    key = jax.random.fold_in(key, 11)
    first_key = jax.random.fold_in(key, 1)
    split_key = jax.random.fold_in(key, 2)
    block_total = 2 * N_CTX
    least_blocks = max(1, DOC_MIN // (TOK_DEV // 2))
    later_docs = max(1, (N_CTX - N_CTX // 4) // least_blocks)
    first_length = N_CTX + jax.random.randint(first_key, (), 0, N_CTX // 4 + 1)
    leftover = block_total - first_length - later_docs * least_blocks
    shifts = jnp.sort(jax.random.randint(split_key, (later_docs - 1,), 0, 1 << 20) % (leftover + 1))
    bounds = first_length + least_blocks * jnp.arange(1, later_docs, dtype=jnp.int32) + shifts
    blocks = jnp.arange(block_total, dtype=jnp.int32)
    later = jnp.sum((blocks[:, None] >= bounds[None, :]).astype(jnp.int32), axis=1)
    doc_ids = jnp.where(blocks < first_length, 0, 1 + later)
    return doc_ids.astype(jnp.int32)


def steps_of(rng, dims, pieces, smallest, high):
    factor_of = 1.0
    for axis_at, blocks in pieces:
        draws = jax.random.uniform(jax.random.fold_in(jax.random.fold_in(rng, 6), axis_at), (blocks,), jnp.float32, smallest / len(pieces), high / len(pieces))
        factor_of = factor_of * jnp.repeat(jnp.exp(draws), dims[axis_at] // blocks).reshape((-1,) + (1,) * (len(dims) - 1 - axis_at))
    return factor_of


def noise(rng, dims, deviation, reach, pieces=(), held_as=jnp.bfloat16):
    entries = deviation * jax.random.normal(rng, dims, jnp.float32)
    if pieces:
        entries = entries * steps_of(rng, dims, pieces, -0.22, 0.18)
    return jnp.clip(entries, -reach, reach).astype(held_as)


def setup_inputs(seed: int = 0) -> dict:
    key_of = jax.random.split(jax.random.key(seed), 14)
    return {
        "hidden_in": noise(key_of[0], (TOKENS, D), 1.0, 6.0, ((0, 32),)),
        "attention_gain": jnp.clip(1.0 + 0.1 * jax.random.normal(key_of[1], (D,), jnp.float32), 0.5, 1.5),
        "query_weight": noise(key_of[2], (N_CTX, D * D // N_CTX), D ** -0.5, 0.25, ((0, 32),)),
        "key_weight": noise(key_of[3], (N_CTX, D * KV_WIDTH // N_CTX), D ** -0.5, 0.25, ((0, 32),)),
        "value_weight": noise(key_of[4], (N_CTX, D * KV_WIDTH // N_CTX), D ** -0.5, 0.25, ((0, 32),)),
        "output_weight": noise(key_of[5], (N_CTX, D * D // N_CTX), (D // 64) ** -0.5, 2.0, ((0, 32),)),
        "feedforward_gain": jnp.clip(1.0 + 0.1 * jax.random.normal(key_of[6], (D,), jnp.float32), 0.5, 1.5),
        "gate_weight": noise(key_of[7], (N_CTX, D * FF // N_CTX), D ** -0.5, 0.25, ((0, 32),)),
        "up_weight": noise(key_of[8], (N_CTX, D * FF // N_CTX), D ** -0.5, 0.25, ((0, 32),)),
        "down_weight": noise(key_of[9], (N_CTX, FF * D // N_CTX), FF ** -0.5, 0.15625, ((0, 32),)),
        "doc_of_block": draw_doc_of_block(jax.random.fold_in(key_of[13], 71), 0),
        "pair_table": jax.random.permutation(key_of[11], N_CTX).astype(jnp.int32),
        "out_grad": noise(key_of[12], (TOKENS, D), 1.0, 6.0, ((0, 32),)),
    }


epsilon = 1e-05
rope_base = 100000.0
masked_score = -1e+30
highest_score = lax.Precision.HIGHEST

@jax.custom_vjp
def lower_bound(v):
    return lax.optimization_barrier(v.astype(jnp.bfloat16)).astype(jnp.float32)

@jax.custom_vjp
def backward_lower_bound(v):
    return v

def low_keep(v):
    return (lower_bound(v), None)

def low_pass(kept, grad):
    return (grad,)

def back_keep(v):
    return (v, None)

def back_low(kept, grad):
    return (lower_bound(grad),)
lower_bound.defvjp(low_keep, low_pass)
backward_lower_bound.defvjp(back_keep, back_low)

def token_layout(doc_of_block, pair_table, half_rows):
    pair_count = pair_table.shape[0]
    block_total = 2 * pair_count
    stored = jnp.arange(block_total, dtype=jnp.int32)
    owner = stored // 2
    pair_iota = jnp.arange(pair_count, dtype=jnp.int32)
    pair_of = lax.optimization_barrier(jnp.sum(jnp.where(owner[:, None] == pair_iota[None, :], pair_table[None, :], 0), axis=1)).astype(jnp.int32)
    stream_block = jnp.where(stored % 2 == 0, pair_of, block_total - 1 - pair_of).astype(jnp.int32)
    block_iota = jnp.arange(block_total, dtype=jnp.int32)
    doc_stored = lax.optimization_barrier(jnp.sum(jnp.where(stream_block[:, None] == block_iota[None, :], doc_of_block[None, :], 0), axis=1)).astype(jnp.int32)
    same_doc = doc_stored[:, None] == doc_of_block[None, :]
    doc_start = lax.optimization_barrier(jnp.min(jnp.where(same_doc, block_iota[None, :], block_total), axis=1)).astype(jnp.int32)
    offsets = jnp.arange(half_rows, dtype=jnp.int32)
    stream_index = (stream_block[:, None] * half_rows + offsets[None, :]).reshape(-1).astype(jnp.int32)
    position = ((stream_block - doc_start)[:, None] * half_rows + offsets[None, :]).reshape(-1).astype(jnp.int32)
    document = jnp.broadcast_to(doc_stored[:, None], (block_total, half_rows)).reshape(-1).astype(jnp.int32)
    return (document, stream_index, position)

def rotary(values, positions, direction):
    row_count = values.shape[0]
    head_count = values.shape[1] // HEAD_SIZE
    half_dim = HEAD_SIZE // 2
    shaped = values.reshape(row_count, head_count, HEAD_SIZE)
    frequency = rope_base ** (-jnp.arange(half_dim, dtype=jnp.float32) * (2.0 / HEAD_SIZE))
    angles = positions.astype(jnp.float32)[:, None] * frequency[None, :]
    cosine = jnp.cos(angles)[:, None, :]
    sine = direction * jnp.sin(angles)[:, None, :]
    leading = shaped[..., :half_dim]
    trailing = shaped[..., half_dim:]
    turned = jnp.concatenate([leading * cosine - trailing * sine, trailing * cosine + leading * sine], axis=-1)
    return turned.reshape(row_count, head_count * HEAD_SIZE)

def norm_rows(values, gain):
    inverse = lax.rsqrt(lax.optimization_barrier(jnp.mean(values * values, axis=-1, keepdims=True)) + epsilon)
    return values * inverse * gain

def attend_block(query_rot, key_rot, value_rows, query_doc, query_index, key_doc, key_index):
    query_count = query_rot.shape[0]
    group_count = HEADS // KV_HEADS
    grouped_heads = query_rot.reshape(query_count, KV_HEADS, group_count, HEAD_SIZE)
    head_keys = key_rot.reshape(-1, KV_HEADS, HEAD_SIZE)
    head_values = value_rows.reshape(-1, KV_HEADS, HEAD_SIZE)
    attention_scores = backward_lower_bound(jnp.einsum('fiam,pim->iafp', grouped_heads, head_keys, precision=highest_score) * HEAD_SIZE ** (-0.5))
    allowed = (query_doc[:, None] == key_doc[None, :]) & (key_index[None, :] <= query_index[:, None])
    masked = jnp.where(allowed, attention_scores, masked_score)
    row_peak = lax.optimization_barrier(jnp.max(masked, axis=-1, keepdims=True))
    weights = jnp.where(allowed, jnp.exp(masked - row_peak), 0.0)
    attention_probability = weights / lax.optimization_barrier(jnp.sum(weights, axis=-1, keepdims=True))
    layer_result = jnp.einsum('coum,mcw->ucow', lower_bound(attention_probability), head_values, precision=highest_score)
    return layer_result.reshape(query_count, HEADS * HEAD_SIZE)

def reference(hidden_in, attention_gain, query_weight, key_weight, value_weight, output_weight, feedforward_gain, gate_weight, up_weight, down_weight, doc_of_block, pair_table, out_grad):
    document, stream_index, position = token_layout(doc_of_block, pair_table, TOK_DEV // 2)
    block_rows = math.gcd(TOKENS, 512)
    block_count = TOKENS // block_rows

    def forward(hidden, gain_one, query_w, key_w, value_w, output_w, gain_two, gate_w, up_w, down_w):
        normed = lower_bound(norm_rows(hidden, gain_one))
        queries = backward_lower_bound(jnp.dot(normed, query_w, precision=highest_score))
        key_rows = backward_lower_bound(jnp.dot(normed, key_w, precision=highest_score))
        values = backward_lower_bound(lower_bound(jnp.dot(normed, value_w, precision=highest_score)))
        queries = lower_bound(rotary(queries, position, 1.0))
        key_rows = lower_bound(rotary(key_rows, position, 1.0))

        def attend(inputs):
            return attend_block(inputs[0], key_rows, values, inputs[1], inputs[2], document, stream_index)
        mixture = lax.map(jax.checkpoint(attend), (queries.reshape(block_count, block_rows, D), document.reshape(block_count, block_rows), stream_index.reshape(block_count, block_rows)))
        mixture = backward_lower_bound(lower_bound(mixture.reshape(TOKENS, D)))
        branch = backward_lower_bound(jnp.dot(mixture, output_w, precision=highest_score))
        middle = hidden + branch
        normed_two = lower_bound(norm_rows(middle, gain_two))
        gate_act = backward_lower_bound(jnp.dot(normed_two, gate_w, precision=highest_score))
        up_act = backward_lower_bound(jnp.dot(normed_two, up_w, precision=highest_score))
        hidden_ff = lower_bound(jax.nn.silu(gate_act) * up_act)
        return middle + backward_lower_bound(jnp.dot(hidden_ff, down_w, precision=highest_score))
    layer_result, pullback = jax.vjp(forward, hidden_in.astype(jnp.float32), attention_gain.astype(jnp.float32), query_weight.astype(jnp.float32).reshape(D, D), key_weight.astype(jnp.float32).reshape(D, KV_WIDTH), value_weight.astype(jnp.float32).reshape(D, KV_WIDTH), output_weight.astype(jnp.float32).reshape(D, D), feedforward_gain.astype(jnp.float32), gate_weight.astype(jnp.float32).reshape(D, FF), up_weight.astype(jnp.float32).reshape(D, FF), down_weight.astype(jnp.float32).reshape(FF, D))
    grads = pullback(out_grad.astype(jnp.float32))
    return (layer_result.astype(jnp.bfloat16), grads[0].astype(jnp.bfloat16), grads[1], grads[2].reshape(N_CTX, -1), grads[3].reshape(N_CTX, -1), grads[4].reshape(N_CTX, -1), grads[5].reshape(N_CTX, -1), grads[6], grads[7].reshape(N_CTX, -1), grads[8].reshape(N_CTX, -1), grads[9].reshape(N_CTX, -1))
```

```python
import functools

import jax
import jax.numpy as jnp
import numpy as np
from jax import lax
from jax.experimental import pallas as pl
from jax.experimental.pallas import tpu as pltpu
from jax.sharding import PartitionSpec as P

HEADS = 9
KV_HEADS = 3
GROUP = HEADS // KV_HEADS
HEAD_SIZE = 64
KV_WIDTH = KV_HEADS * HEAD_SIZE
TILE = 16

epsilon = 1e-05
rope_base = 100000.0
masked_score = -1e30

low = jnp.bfloat16
full = jnp.float32


def exchange_steps(device_count, low_bits):
    top = device_count.bit_length() - 1
    steps = []
    if low_bits == 0 and top >= 4:
        for bit in range(top - 1, 2, -1):
            steps.append([i ^ (1 << bit) for i in range(device_count)])
        steps.append([i ^ (4 if i & 1 else 2) for i in range(device_count)])
        steps.append([i ^ (2 if i & 1 else 4) for i in range(device_count)])
        steps.append([i ^ 1 for i in range(device_count)])
    else:
        for bit in range(top - 1, low_bits - 1, -1):
            steps.append([i ^ (1 << bit) for i in range(device_count)])
    return steps


def source_table(device_count, low_bits):
    held = [[d >> low_bits] for d in range(device_count)]
    for partner in exchange_steps(device_count, low_bits):
        held = [held[d] + held[partner[d]] for d in range(device_count)]
    return np.array(held, np.int32)


def send(values, partner):
    return lax.ppermute(values, "ctx", [(i, p) for i, p in enumerate(partner)])


def gather_halves(values, steps):
    for partner in steps[:-1]:
        values = jnp.concatenate([values, send(values, partner)], axis=0)
    return values, send(values, steps[-1])


def whole_rows(flat, device, low_bits, columns):
    for bit in range(low_bits):
        partner = [i ^ (1 << bit) for i in range(lax.axis_size("ctx"))]
        other = send(flat, partner)
        is_high = (device >> bit) & 1
        flat = jnp.concatenate(
            [jnp.where(is_high, other, flat), jnp.where(is_high, flat, other)], axis=1
        )
    return flat.reshape(-1, columns)


def own_piece(rows, device, low_bits):
    flat = rows.reshape(1, -1)
    for bit in range(low_bits - 1, -1, -1):
        partner = [i ^ (1 << bit) for i in range(lax.axis_size("ctx"))]
        half = flat.shape[1] // 2
        is_high = (device >> bit) & 1
        leaving = jnp.where(is_high, flat[:, :half], flat[:, half:]).astype(low)
        staying = jnp.where(is_high, flat[:, half:], flat[:, :half])
        flat = staying + send(leaving, partner).astype(full)
    return flat


def low_bits_of(piece, columns):
    low_bits = 0
    while (piece << low_bits) < TILE * columns:
        low_bits += 1
    return low_bits


def fold_rows(rows):
    return jnp.concatenate([rows[:TILE], rows[TILE:].reshape(TILE, -1)], axis=1)


def unfold_rows(packed, columns, folded):
    return jnp.concatenate(
        [packed[:, :columns], packed[:, columns : columns + folded].reshape(-1, columns)], axis=0
    )


def whole_lanes(columns):
    return -(-columns // 128) * 128


def pad_lanes(rows):
    return jnp.pad(rows, ((0, 0), (0, whole_lanes(rows.shape[1]) - rows.shape[1])))


def dot(left, right):
    return jnp.dot(left, right, preferred_element_type=full)


def dot_right(left, right):
    return lax.dot_general(left, right, (((1,), (1,)), ((), ())), preferred_element_type=full)


def dot_left(left, right):
    return lax.dot_general(left, right, (((0,), (0,)), ((), ())), preferred_element_type=full)


def iota(shape, axis):
    return lax.broadcasted_iota(jnp.int32, shape, axis)


def mixing_of(feature_ref):
    width = feature_ref.shape[1]
    return (iota((width, width), 0) == feature_ref[...]).astype(full).astype(low)


def fold_pick(rest, main, fold, at):
    row = iota((rest, main), 0)
    per = TILE // fold
    place = (row // per) * TILE + lax.rem(row, per) * fold + at
    return (iota((rest, main), 1) == place).astype(full).astype(low)


def as_row(column):
    return jnp.transpose(jnp.broadcast_to(column, (column.shape[0], 128)))[0:1]


def turn(values, rope, direction):
    half_dim = HEAD_SIZE // 2
    swapped = jnp.concatenate([values[:, half_dim:], values[:, :half_dim]], axis=1)
    return values * rope[:, :HEAD_SIZE] + swapped * (direction * rope[:, HEAD_SIZE:])


def unit_rows(values):
    inverse = lax.rsqrt(jnp.mean(values * values, axis=-1, keepdims=True) + epsilon)
    return values * inverse, inverse


def norm_back(unit, inverse, gain, grad):
    scaled = grad * gain
    return inverse * (scaled - unit * jnp.mean(scaled * unit, axis=-1, keepdims=True))


def query_range(own, rows, axis):
    shape = (rows, 1) if axis == 0 else (1, rows)
    per_head = rows // GROUP
    half = per_head // 2
    row = lax.rem(iota(shape, axis), per_head)
    first = row < half
    last_key = jnp.where(first, own[0] * half + row, own[1] * half + row - half)
    first_key = jnp.where(first, own[2] * half, own[3] * half)
    return first_key.astype(full), last_key.astype(full)


def gains_block(gains):
    high = gains.astype(low).astype(full)
    return jnp.concatenate([high, gains - high], axis=0).astype(low)


def gains_of(block):
    block = block.astype(full)
    return block[:8] + block[8:]


class Call:
    def __init__(self, steps):
        self.steps = steps

    def spec(self, kind, shape):
        if kind == "smem":
            return pl.BlockSpec(memory_space=pltpu.SMEM)
        if self.steps == 1 or kind == "whole":
            return pl.BlockSpec(memory_space=pltpu.VMEM)
        rest = tuple(shape[1:])
        return pl.BlockSpec((shape[0] // self.steps,) + rest, lambda i: (i,) + (0,) * len(rest))

    def __call__(self, kernel, name, ins, outs, scratch, flops, transcendentals=0):
        steps = self.steps

        def run(*refs):
            kernel(pl.program_id(0) if steps > 1 else 0, steps, *refs)

        size = sum(a.size * a.dtype.itemsize for _, a in ins)
        size += sum(np.prod(s.shape) * s.dtype.itemsize for _, s in outs)
        return pl.pallas_call(
            run,
            grid=(steps,) if steps > 1 else (),
            in_specs=[self.spec(kind, a.shape) for kind, a in ins],
            out_specs=[self.spec(kind, s.shape) for kind, s in outs],
            out_shape=[s for _, s in outs],
            scratch_shapes=scratch,
            compiler_params=pltpu.CompilerParams(vmem_limit_bytes=48 * 1024 * 1024),
            cost_estimate=pl.CostEstimate(
                flops=int(flops), bytes_accessed=int(size), transcendentals=int(transcendentals)
            ),
            name=name,
        )(*[a for _, a in ins])


def once(step, steps, at, action):
    if steps == 1:
        action()
    else:
        pl.when(step == at)(action)


def shape_of(shape, dtype):
    return jax.ShapeDtypeStruct(shape, dtype)


def pack_kernel(merged, step, steps, hidden_ref, gain_ref, *rest):
    packed_ref, normed_ref = rest[-2:]
    width = hidden_ref.shape[1]
    unit, _ = unit_rows(hidden_ref[...].astype(full))
    normed_ref[...] = (unit * gain_ref[...]).astype(low)
    groups = hidden_ref.shape[0] // TILE
    for a in range(groups):
        packed_ref[:, a * width : (a + 1) * width] = normed_ref[a * TILE : (a + 1) * TILE, :]
    if merged:
        packed_ref[:, groups * width :] = rest[0][...]


def project_kernel(
    merged, step, steps, feature_ref, normed_ref, rope_ref, rope_own_ref, own_ref, come_ref, *rest
):
    if merged:
        w_own, w_come = own_ref, come_ref
    else:
        w_own, w_come = rest[:2]
        rest = rest[2:]
    query_ref, kv_own_ref, kv_come_ref, weight_ref, mixed = rest
    width = feature_ref.shape[1]
    groups = rope_own_ref.shape[0] // TILE
    base = groups * width if merged else 0
    columns = weight_ref.shape[1]
    half = w_own.shape[0]
    main = 2 * half
    fold = TILE * main // (TILE * (width - main))

    def first():
        mixed[:half, :] = w_own[:, base : base + columns]
        mixed[half:main, :] = w_come[:, base : base + columns]
        part = columns // fold
        folded = slice(base + columns, base + columns + part)
        extra = jnp.concatenate([w_own[:, folded], w_come[:, folded]], axis=0)
        for at in range(fold):
            mixed[main:, at * part : (at + 1) * part] = dot(
                fold_pick(width - main, main, fold, at), extra
            ).astype(low)
        weight_ref[...] = dot(mixing_of(feature_ref), mixed[...]).astype(low)
        queries = dot(normed_ref[...], weight_ref[:, :width])
        rows = normed_ref.shape[0]
        rope = rope_own_ref[...]
        for head in range(HEADS):
            turned = turn(queries[:, head * HEAD_SIZE : (head + 1) * HEAD_SIZE], rope, 1.0)
            turned = turned.astype(low) * low(HEAD_SIZE**-0.5)
            g = head % GROUP
            query_ref[head // GROUP, g * rows : (g + 1) * rows, :] = turned

    once(step, steps, 0, first)
    rows = own_ref.shape[0]
    for a in range(groups):
        normed = jnp.concatenate(
            [own_ref[:, a * width : (a + 1) * width], come_ref[:, a * width : (a + 1) * width]],
            axis=0,
        )
        kv = dot(normed, weight_ref[:, width:])
        rope = rope_ref[a]
        parts = [
            turn(kv[:, head * HEAD_SIZE : (head + 1) * HEAD_SIZE], rope, 1.0)
            for head in range(KV_HEADS)
        ]
        kv = jnp.concatenate(parts + [kv[:, KV_WIDTH:]], axis=1).astype(low)
        kv_own_ref[:, a * 2 * KV_WIDTH : (a + 1) * 2 * KV_WIDTH] = kv[:rows]
        kv_come_ref[:, a * 2 * KV_WIDTH : (a + 1) * 2 * KV_WIDTH] = kv[rows:]


def key_loop(key_ref, kv_own_ref, kv_come_ref, body):
    groups = kv_own_ref.shape[1] // (2 * KV_WIDTH)
    wide = 4 * KV_WIDTH

    def advance(pair, carry):
        lanes = pl.ds(pl.multiple_of(pair * wide, 128), wide)
        own = kv_own_ref[:, lanes]
        come = kv_come_ref[:, lanes]

        def part(c):
            low_at, high_at = c * HEAD_SIZE, 2 * KV_WIDTH + c * HEAD_SIZE
            return jnp.concatenate(
                [
                    own[:, low_at : low_at + HEAD_SIZE],
                    come[:, low_at : low_at + HEAD_SIZE],
                    own[:, high_at : high_at + HEAD_SIZE],
                    come[:, high_at : high_at + HEAD_SIZE],
                ],
                axis=0,
            )

        start = key_ref[pair // (groups // 4)]
        shift = (lax.rem(pair, groups // 4) * (2 * TILE)).astype(full)
        key_index = jnp.concatenate([start + shift, start + (shift + TILE)], axis=1)
        body(pair, key_index, part)
        return carry

    lax.fori_loop(0, groups // 2, advance, 0)


def forward_kernel(
    step, steps, own, key_ref, query_ref, kv_own_ref, kv_come_ref, out_ref, lse_ref, acc, peak, total
):
    rows = query_ref.shape[1]

    def first():
        acc[...] = jnp.zeros_like(acc)
        peak[...] = jnp.full_like(peak, masked_score)
        total[...] = jnp.zeros_like(total)

    once(step, steps, 0, first)
    first_key, last_key = query_range(own, rows, 0)

    def block(pair, key_index, part):
        allowed = (key_index >= first_key) & (key_index <= last_key)
        for head in range(KV_HEADS):
            scores = dot_right(query_ref[head], part(head))
            masked = jnp.where(allowed, scores, masked_score)
            old = peak[head]
            new = jnp.maximum(old, jnp.max(masked, axis=1, keepdims=True))
            weights = jnp.where(allowed, jnp.exp(masked - new), 0.0)
            factor = jnp.exp(old - new)
            peak[head] = new
            total[head] = total[head] * factor + jnp.sum(weights, axis=1, keepdims=True)
            acc[head] = acc[head] * factor + dot(weights.astype(low), part(KV_HEADS + head))

    key_loop(key_ref, kv_own_ref, kv_come_ref, block)

    def last():
        for head in range(KV_HEADS):
            out_ref[head] = acc[head] / total[head]
            lse_ref[head] = as_row(peak[head] + jnp.log(total[head]))

    once(step, steps, steps - 1, last)


def feedforward_kernel(
    step,
    steps,
    source_ref,
    feature_ref,
    attention_ref,
    hidden_ref,
    gain_ref,
    grad_ref,
    own_ref,
    come_ref,
    out_ref,
    grad_middle_ref,
    head_grad_ref,
    delta_ref,
    keep_ref,
    send_ref,
    gain_part_ref,
    attended,
    output_w,
    normed,
    normed_t,
    down_w,
    down_grad,
    total,
    grad_normed,
    extra_grad,
):
    rows, width = hidden_ref.shape
    half = own_ref.shape[0]
    main = 2 * half
    rest = width - main
    fold = main // rest
    places = main // TILE
    ff = down_w.shape[0]
    chunk = 2 * ff // fold
    down_at = 2 * ff + chunk
    device_ff = ff // places
    groups = device_ff // TILE
    out_at = down_at + groups * width
    mixing = mixing_of(feature_ref)

    for h in range(HEADS):
        g = h % GROUP
        attended[:, h * HEAD_SIZE : (h + 1) * HEAD_SIZE] = attention_ref[
            h // GROUP, g * rows : (g + 1) * rows, :
        ].astype(low)
    attended[...] = dot(attended[...], mixing).astype(low)
    output_w[:half, :] = own_ref[:, out_at : out_at + width]
    output_w[half:main, :] = come_ref[:, out_at : out_at + width]
    part = width // fold
    folded = slice(out_at + width, out_at + width + part)
    extra = jnp.concatenate([own_ref[:, folded], come_ref[:, folded]], axis=0)
    for at in range(fold):
        output_w[main:, at * part : (at + 1) * part] = dot(
            fold_pick(rest, main, fold, at), extra
        ).astype(low)
    middle = hidden_ref[...].astype(full) + dot(attended[...], output_w[...])
    gain = gain_ref[...]
    unit, inverse = unit_rows(middle)
    mixed_norm = dot((unit * gain).astype(low), mixing)
    normed[...] = mixed_norm.astype(low)
    normed_t[...] = jnp.transpose(mixed_norm).astype(low)
    for place in range(places):
        held = own_ref if place < places // 2 else come_ref
        row = (place % (places // 2)) * TILE
        for a in range(groups):
            at = pl.multiple_of(source_ref[place] * device_ff + a * TILE, TILE)
            lane = down_at + a * width
            down_w[pl.ds(at, TILE), :] = held[row : row + TILE, lane : lane + width]
    total[...] = jnp.zeros_like(total)
    grad_normed[...] = jnp.zeros_like(grad_normed)
    extra_grad[...] = jnp.zeros_like(extra_grad)
    out_grad = grad_ref[...]

    def advance(c, carry):
        gate_at = pl.ds(pl.multiple_of(c * chunk, 128), chunk)
        up_at = pl.ds(pl.multiple_of(ff + c * chunk, 128), chunk)
        extra = jnp.concatenate(
            [own_ref[:, 2 * ff : down_at], come_ref[:, 2 * ff : down_at]], axis=0
        )

        def columns(lanes, at):
            pick = fold_pick(rest, main, fold, at)
            tail = dot(pick, extra).astype(low)
            value = (
                dot(normed[:, :half], own_ref[:, lanes])
                + dot(normed[:, half:main], come_ref[:, lanes])
                + dot(normed[:, main:], tail)
            )
            return value, tail, pick

        gate, gate_tail, gate_pick = columns(gate_at, c)
        up, up_tail, up_pick = columns(up_at, c + fold // 2)
        down_at_c = pl.ds(pl.multiple_of(c * chunk, 128), chunk)
        down = down_w[down_at_c, :]
        sigma = 1.0 / (1.0 + jnp.exp(-gate))
        silu = gate * sigma
        inner = (silu * up).astype(low)
        total[...] += dot(inner, down)
        grad_inner = dot_right(out_grad, down)
        grad_gate = (grad_inner * up * sigma * (1.0 + gate * (1.0 - sigma))).astype(low)
        grad_up = (grad_inner * silu).astype(low)
        down_grad[down_at_c, :] = dot_left(inner, out_grad).astype(low)
        for grad, lanes, tail, pick in (
            (grad_gate, gate_at, gate_tail, gate_pick),
            (grad_up, up_at, up_tail, up_pick),
        ):
            grad_normed[:, :half] += dot_right(grad, own_ref[:, lanes])
            grad_normed[:, half:main] += dot_right(grad, come_ref[:, lanes])
            grad_normed[:, main:] += dot_right(grad, tail)
            keep_ref[:, lanes] = dot(normed_t[:half], grad).astype(low)
            send_ref[:, lanes] = dot(normed_t[half:main], grad).astype(low)
            extra_grad[...] += dot_left(pick, dot(normed_t[main:], grad).astype(low))
        return carry

    lax.fori_loop(0, ff // chunk, advance, 0)
    out_ref[...] = (middle + total[...]).astype(low)
    keep_ref[:, 2 * ff : down_at] = extra_grad[:half].astype(low)
    send_ref[:, 2 * ff : down_at] = extra_grad[half:].astype(low)
    for place in range(places):
        held = keep_ref if place < places // 2 else send_ref
        row = (place % (places // 2)) * TILE
        for a in range(groups):
            at = pl.multiple_of(source_ref[place] * device_ff + a * TILE, TILE)
            lane = down_at + a * width
            held[row : row + TILE, lane : lane + width] = down_grad[pl.ds(at, TILE), :]

    high = grad_normed[...].astype(low)
    tail = (grad_normed[...] - high.astype(full)).astype(low)
    back = dot_right(high, mixing) + dot_right(tail, mixing)
    gain_part_ref[...] = jnp.sum(back * unit, axis=0, keepdims=True)
    grad_middle = out_grad.astype(full) + norm_back(unit, inverse, gain, back)
    grad_middle_ref[...] = grad_middle
    grad_branch = grad_middle.astype(low)
    output_grad = dot_left(attended[...], grad_branch).astype(low)
    keep_ref[:, out_at : out_at + width] = output_grad[:half]
    send_ref[:, out_at : out_at + width] = output_grad[half:main]
    extra = sum(
        dot_left(
            fold_pick(rest, main, fold, at), output_grad[main:, at * part : (at + 1) * part]
        )
        for at in range(fold)
    ).astype(low)
    unused = jnp.zeros((half, keep_ref.shape[1] - folded.stop), low)
    for held, rows_of_half in ((keep_ref, extra[:half]), (send_ref, extra[half:])):
        held[:, folded] = rows_of_half
        held[:, folded.stop :] = unused
    grad_low = dot_right(grad_branch, output_w[...]).astype(low)
    grad_low = dot_right(grad_low, mixing).astype(low)
    for kv_head in range(KV_HEADS):
        parts = []
        for g in range(GROUP):
            h = kv_head * GROUP + g
            parts.append(grad_low[:, h * HEAD_SIZE : (h + 1) * HEAD_SIZE])
        grads = jnp.concatenate(parts, axis=0)
        head_grad_ref[kv_head] = grads
        delta_ref[kv_head] = as_row(
            jnp.sum(grads.astype(full) * attention_ref[kv_head], axis=1, keepdims=True)
        )


def backward_kernel(
    merged,
    step,
    steps,
    own,
    feature_ref,
    key_ref,
    query_ref,
    grad_ref,
    lse_ref,
    delta_ref,
    kv_own_ref,
    kv_come_ref,
    own_ref,
    come_ref,
    rope_ref,
    rope_own_ref,
    normed_ref,
    weight_ref,
    gain_ref,
    gain_two_ref,
    query_grad_ref,
    gains_ref,
    *rest,
):
    if merged:
        keep_ref, send_ref = rest[:2]
        w_keep, w_send = keep_ref, send_ref
        rest = rest[2:]
    else:
        keep_ref, send_ref, w_keep, w_send = rest[:4]
        rest = rest[4:]
    grad_query, grad_weight = rest
    rows = query_ref.shape[1]
    tokens, width = normed_ref.shape
    groups = tokens // TILE
    half = own_ref.shape[0]
    base = groups * 2 * KV_WIDTH if merged else 0

    def first():
        grad_query[...] = jnp.zeros_like(grad_query)
        grad_weight[...] = jnp.zeros_like(grad_weight)

    once(step, steps, 0, first)
    first_key, last_key = query_range(own, rows, 1)

    def block(pair, key_index, part):
        key_index = jnp.transpose(jnp.broadcast_to(key_index, (128, key_index.shape[1])))[:, 0:1]
        allowed = (key_index >= first_key) & (key_index <= last_key)
        grad_keys, grad_values = [], []
        for head in range(KV_HEADS):
            keys = part(head)
            scores = dot_right(keys, query_ref[head])
            probs = jnp.where(allowed, jnp.exp(scores - lse_ref[head]), 0.0)
            d_probs = dot_right(part(KV_HEADS + head), grad_ref[head])
            d_scores = (probs * (d_probs - delta_ref[head])).astype(low)
            grad_query[head] += dot_left(keys, d_scores)
            grad_keys.append(dot(d_scores, query_ref[head]))
            grad_values.append(dot(probs.astype(low), grad_ref[head]))
        for i in range(2):
            at = slice(i * 2 * half, (i + 1) * 2 * half)
            rope = rope_ref[2 * pair + i]
            turned = jnp.concatenate(
                [turn(part_of[at], rope, -1.0) for part_of in grad_keys]
                + [part_of[at] for part_of in grad_values],
                axis=1,
            ).astype(low)
            lanes = pl.ds(pl.multiple_of((2 * pair + i) * 2 * KV_WIDTH, 128), 2 * KV_WIDTH)
            keep_ref[:, lanes] = turned[:half]
            send_ref[:half, lanes] = turned[half:]
        lanes = pl.ds(pl.multiple_of(pair * 2 * width, 128), 2 * width)
        n_own = own_ref[:, lanes]
        n_come = come_ref[:, lanes]
        for i in range(2):
            cat = slice(i * width, (i + 1) * width)
            kv_lanes = pl.ds(pl.multiple_of((2 * pair + i) * 2 * KV_WIDTH, 128), 2 * KV_WIDTH)
            grad_weight[:, width:] += dot_left(n_own[:, cat], keep_ref[:, kv_lanes])
            grad_weight[:, width:] += dot_left(n_come[:, cat], send_ref[:half, kv_lanes])

    key_loop(key_ref, kv_own_ref, kv_come_ref, block)

    def last():
        rope = rope_own_ref[...]
        for kv_head in range(KV_HEADS):
            rotated = jnp.transpose(grad_query[kv_head]) * HEAD_SIZE**-0.5
            for g in range(GROUP):
                h = kv_head * GROUP + g
                query_grad_ref[:, h * HEAD_SIZE : (h + 1) * HEAD_SIZE] = turn(
                    rotated[g * tokens : (g + 1) * tokens], rope, -1.0
                ).astype(low)
        grad_weight[:, :width] = dot_left(normed_ref[...], query_grad_ref[...])
        natural = grad_weight[...]
        products = natural * weight_ref[...].astype(full)
        gain_part = as_row(jnp.sum(products, axis=1, keepdims=True)) / gain_ref[...]
        pad = jnp.zeros((8, width), full)
        row = iota((8, width), 0)
        gains = jnp.where(row == 0, gain_part, jnp.where(row == 1, gain_two_ref[...], pad))
        gains_ref[...] = gains
        mixed = dot_left(mixing_of(feature_ref), natural.astype(low)).astype(low)
        columns = mixed.shape[1]
        w_rows = w_keep.shape[0]
        main = 2 * w_rows
        fold = main // (width - main)
        part = columns // fold
        extra = sum(
            dot_left(
                fold_pick(width - main, main, fold, at), mixed[main:, at * part : (at + 1) * part]
            )
            for at in range(fold)
        ).astype(low)
        w_keep[:, base : base + columns] = mixed[:w_rows]
        w_send[:w_rows, base : base + columns] = mixed[w_rows:main]
        folded = slice(base + columns, base + columns + part)
        unused = jnp.zeros((w_rows, w_keep.shape[1] - folded.stop), low)
        w_keep[:, folded] = extra[:w_rows]
        w_send[:w_rows, folded] = extra[w_rows:]
        w_keep[:, folded.stop :] = unused
        w_send[:w_rows, folded.stop :] = unused
        if merged:
            send_ref[half:, :width] = gains_block(gains)
            send_ref[half:, width:] = jnp.zeros((TILE, send_ref.shape[1] - width), low)

    once(step, steps, steps - 1, last)


def add_kernel(with_gains, step, steps, keep_ref, come_ref, *rest):
    rows = keep_ref.shape[0]
    if with_gains:
        gains_ref, rest = rest[0], rest[1:]
        rest, gains_out = rest[:-1], rest[-1]
        width = gains_ref.shape[1]
        gains = gains_of(gains_block(gains_ref[...])) + gains_of(come_ref[rows:, :width])
        gains_out[...] = gains

    def tile(at):
        at = pl.ds(at, TILE)
        return keep_ref[at, :].astype(full) + come_ref[at, :].astype(full)

    if rows == TILE:
        rest[0][...] = tile(0)
        return
    keep_out, send_out = rest
    half = rows // 2

    def advance(i, carry):
        at = pl.multiple_of(i * TILE, TILE)
        keep_out[pl.ds(at, TILE), :] = tile(at).astype(low)
        send_out[pl.ds(at, TILE), :] = tile(pl.multiple_of(half + at, TILE)).astype(low)
        return carry

    lax.fori_loop(0, half // TILE, advance, 0)
    if with_gains:
        send_out[half:, :width] = gains_block(gains)
        send_out[half:, width:] = jnp.zeros((TILE, send_out.shape[1] - width), low)


def scatter_halves(keep, leaving, steps, name, gains=None):
    with_gains = gains is not None
    more = TILE if with_gains else 0
    for partner in reversed(steps):
        come = send(leaving, partner)
        rows, columns = keep.shape
        ins = [("whole", keep), ("whole", come)]
        if rows == TILE:
            outs = [("whole", shape_of((rows, columns), full))]
        else:
            outs = [
                ("whole", shape_of((rows // 2, columns), low)),
                ("whole", shape_of((rows // 2 + more, columns), low)),
            ]
        if with_gains:
            ins.append(("whole", gains))
            outs.append(("whole", shape_of(gains.shape, full)))
        result = Call(1)(functools.partial(add_kernel, with_gains), name, ins, outs, [], 0)
        if with_gains:
            gains = result[-1]
        if rows == TILE:
            return result[0], gains
        keep, leaving = result[0], result[1]


def final_kernel(
    step,
    steps,
    sum_ref,
    query_grad_ref,
    weight_ref,
    hidden_ref,
    gain_ref,
    grad_middle_ref,
    rope_ref,
    out_ref,
    grads,
):
    tokens, width = hidden_ref.shape
    grads[:, :width] = query_grad_ref[...]
    for a in range(tokens // TILE):
        rows = slice(a * TILE, (a + 1) * TILE)
        lanes = slice(a * 2 * KV_WIDTH, (a + 1) * 2 * KV_WIDTH)
        grads[rows, width:] = sum_ref[:, lanes].astype(low)
    back = dot_right(grads[...], weight_ref[...])
    unit, inverse = unit_rows(hidden_ref[...].astype(full))
    out_ref[...] = (grad_middle_ref[...] + norm_back(unit, inverse, gain_ref[...], back)).astype(low)


def body(
    hidden_in,
    attention_gain,
    query_weight,
    key_weight,
    value_weight,
    output_weight,
    feedforward_gain,
    gate_weight,
    up_weight,
    down_weight,
    doc_of_block,
    pair_table,
    out_grad,
):
    tokens, width = hidden_in.shape
    half_rows = tokens // 2
    count = lax.axis_size("ctx")
    device = lax.axis_index("ctx")
    ff = gate_weight.shape[1] * count // width
    low_bits = low_bits_of(query_weight.shape[1], width)
    merged = low_bits == 0
    row_steps = exchange_steps(count, low_bits)
    token_steps = exchange_steps(count, 0)
    group_count = count >> low_bits
    group_rows = width // group_count
    groups = tokens // TILE
    steps = max(1, TILE * count // 512)
    places = count // (2 * steps)
    gain_one = attention_gain.reshape(1, width)
    gain_two = feedforward_gain.reshape(1, width)
    columns = width + 2 * KV_WIDTH

    def rows_of(piece, piece_columns):
        return whole_rows(piece, device, low_bits, piece_columns)

    qkv_piece = pad_lanes(
        fold_rows(
            jnp.concatenate(
                [
                    rows_of(query_weight, width),
                    rows_of(key_weight, KV_WIDTH),
                    rows_of(value_weight, KV_WIDTH),
                ],
                axis=1,
            )
        )
    )
    packed, normed = Call(1)(
        functools.partial(pack_kernel, merged),
        "norm_and_pack",
        [("whole", hidden_in), ("whole", gain_one)] + ([("whole", qkv_piece)] if merged else []),
        [
            (
                "whole",
                shape_of((TILE, groups * width + (qkv_piece.shape[1] if merged else 0)), low),
            ),
            ("whole", shape_of((tokens, width), low)),
        ],
        [],
        0,
    )
    token_halves = gather_halves(packed, token_steps)
    qkv_halves = [] if merged else list(gather_halves(qkv_piece, row_steps))
    down_rows = rows_of(down_weight, width)
    late_piece = pad_lanes(jnp.concatenate(
        [
            fold_rows(jnp.concatenate([rows_of(gate_weight, ff), rows_of(up_weight, ff)], axis=1))
        ]
        + [down_rows[a : a + TILE] for a in range(0, down_rows.shape[0], TILE)]
        + [fold_rows(rows_of(output_weight, width))],
        axis=1,
    ))
    late_halves = gather_halves(late_piece, row_steps)

    def table_row(table):
        return lax.dynamic_index_in_dim(jnp.asarray(table), device, 0, keepdims=False)

    sources = table_row(source_table(count, 0))
    group_table = source_table(count, low_bits)
    group_sources = table_row(group_table)
    inside = np.arange(group_rows)[None, None, :]
    features = group_table[:, :, None] * group_rows + inside
    features = np.concatenate(
        [
            features[:, :, :TILE].reshape(count, -1),
            features[:, :, TILE:].reshape(count, -1),
        ],
        axis=1,
    ).astype(np.int32)
    feature_row = table_row(features).reshape(1, width)

    device_iota = jnp.arange(count, dtype=jnp.int32)
    pairs = jnp.sum(
        jnp.where(sources[:, None] == device_iota[None, :], pair_table[None, :], 0), axis=1
    )
    blocks = jnp.stack([pairs, 2 * count - 1 - pairs], axis=1).reshape(-1)
    block_iota = jnp.arange(2 * count, dtype=jnp.int32)
    block_docs = jnp.sum(
        jnp.where(blocks[:, None] == block_iota[None, :], doc_of_block[None, :], 0), axis=1
    )
    doc_start = jnp.min(
        jnp.where(block_docs[:, None] == doc_of_block[None, :], block_iota[None, :], 2 * count),
        axis=1,
    )
    own = jnp.concatenate([blocks[:2], doc_start[:2]])

    def by_step(values):
        return values.reshape(2, steps, places, 2).transpose(1, 3, 0, 2)

    inner = jnp.arange(TILE, dtype=jnp.int32)
    key_index = by_step(blocks)[..., None] * half_rows + inner
    key_index = key_index.astype(full).reshape(2 * steps, 1, -1)
    frequency = rope_base ** (-jnp.arange(HEAD_SIZE // 2, dtype=full) * (2.0 / HEAD_SIZE))
    block_angle = (by_step(blocks - doc_start) * half_rows).astype(full)[..., None] * frequency
    offset = jnp.arange(half_rows, dtype=full).reshape(groups // 2, TILE)
    offset_angle = offset[..., None] * frequency
    cos_in, sin_in = jnp.cos(offset_angle), jnp.sin(offset_angle)
    times_cos = jnp.concatenate([cos_in, cos_in, -sin_in, sin_in], axis=-1)
    times_sin = jnp.concatenate([sin_in, sin_in, cos_in, -cos_in], axis=-1)
    block_cos = jnp.tile(jnp.cos(block_angle), 4)[:, :, None, :, :, None, :]
    block_sin = jnp.tile(jnp.sin(block_angle), 4)[:, :, None, :, :, None, :]
    rope = (
        block_cos * times_cos[None, None, :, None, None, :, :]
        - block_sin * times_sin[None, None, :, None, None, :, :]
    ).reshape(steps * groups, 2 * places * TILE, 2 * HEAD_SIZE)
    rope_own = rope[:groups, :TILE].reshape(tokens, 2 * HEAD_SIZE)

    call = Call(steps)
    rows = GROUP * tokens
    half = TILE * count // 2
    kv_shape = shape_of((half, groups * 2 * KV_WIDTH), low)
    head_shape = (KV_HEADS, rows, HEAD_SIZE)
    key_total = TILE * count * groups
    queries, kv_own, kv_come, qkv_weight = call(
        functools.partial(project_kernel, merged),
        "project",
        [
            ("whole", feature_row),
            ("whole", normed),
            ("rows", rope),
            ("whole", rope_own),
            ("rows", token_halves[0]),
            ("rows", token_halves[1]),
        ]
        + [("whole", a) for a in qkv_halves],
        [
            ("whole", shape_of(head_shape, low)),
            ("rows", kv_shape),
            ("rows", kv_shape),
            ("whole", shape_of((width, columns), low)),
        ],
        [pltpu.VMEM((width, columns), low)],
        2 * key_total * width * 2 * KV_WIDTH,
    )
    attention, lse = call(
        forward_kernel,
        "attention_forward",
        [
            ("smem", own),
            ("rows", key_index),
            ("whole", queries),
            ("rows", kv_own),
            ("rows", kv_come),
        ],
        [
            ("whole", shape_of(head_shape, full)),
            ("whole", shape_of((KV_HEADS, 1, rows), full)),
        ],
        [
            pltpu.VMEM(head_shape, full),
            pltpu.VMEM((KV_HEADS, rows, 1), full),
            pltpu.VMEM((KV_HEADS, rows, 1), full),
        ],
        4 * KV_HEADS * rows * key_total * HEAD_SIZE,
        KV_HEADS * rows * key_total,
    )
    late_shape = late_halves[0].shape
    main = 2 * late_shape[0]
    block_out, grad_middle, head_grads, delta, late_keep, late_send, gain_two_part = Call(1)(
        feedforward_kernel,
        "feedforward",
        [
            ("smem", group_sources),
            ("whole", feature_row),
            ("whole", attention),
            ("whole", hidden_in),
            ("whole", gain_two),
            ("whole", out_grad),
            ("whole", late_halves[0]),
            ("whole", late_halves[1]),
        ],
        [
            ("whole", shape_of((tokens, width), low)),
            ("whole", shape_of((tokens, width), full)),
            ("whole", shape_of(head_shape, low)),
            ("whole", shape_of((KV_HEADS, 1, rows), full)),
            ("whole", shape_of(late_shape, low)),
            ("whole", shape_of(late_shape, low)),
            ("whole", shape_of((1, width), full)),
        ],
        [
            pltpu.VMEM((tokens, width), low),
            pltpu.VMEM((width, width), low),
            pltpu.VMEM((tokens, width), low),
            pltpu.VMEM((width, tokens), low),
            pltpu.VMEM((ff, width), low),
            pltpu.VMEM((ff, width), low),
            pltpu.VMEM((tokens, width), full),
            pltpu.VMEM((tokens, width), full),
            pltpu.VMEM((main, 2 * ff * (width - main) // main), full),
        ],
        6 * tokens * width * (3 * ff + width),
        tokens * ff,
    )
    late_sum, _ = scatter_halves(late_keep, late_send, row_steps, "add_late")

    w_folded = columns * (width - main) // main
    w_columns = whole_lanes(columns + w_folded)
    if merged:
        chain = [
            ("whole", shape_of((half, kv_shape.shape[1] + w_columns), low)),
            ("whole", shape_of((half + TILE, kv_shape.shape[1] + w_columns), low)),
        ]
    else:
        chain = [("rows", kv_shape), ("rows", kv_shape)]
        chain += [("whole", shape_of((main // 2, w_columns), low))] * 2
    query_grad, gains, *chain = call(
        functools.partial(backward_kernel, merged),
        "attention_backward",
        [
            ("smem", own),
            ("whole", feature_row),
            ("rows", key_index),
            ("whole", queries),
            ("whole", head_grads),
            ("whole", lse),
            ("whole", delta),
            ("rows", kv_own),
            ("rows", kv_come),
            ("rows", token_halves[0]),
            ("rows", token_halves[1]),
            ("rows", rope),
            ("whole", rope_own),
            ("whole", normed),
            ("whole", qkv_weight),
            ("whole", gain_one),
            ("whole", gain_two_part),
        ],
        [("whole", shape_of((tokens, width), low)), ("whole", shape_of((8, width), full))] + chain,
        [
            pltpu.VMEM((KV_HEADS, HEAD_SIZE, rows), full),
            pltpu.VMEM((width, columns), full),
        ],
        10 * KV_HEADS * rows * key_total * HEAD_SIZE + 2 * key_total * width * 2 * KV_WIDTH,
        KV_HEADS * rows * key_total,
    )
    if merged:
        own_sum, gains = scatter_halves(chain[0], chain[1], token_steps, "add_chain", gains)
        kv_sum, qkv_sum = own_sum, own_sum[:, kv_shape.shape[1] :]
    else:
        kv_sum, _ = scatter_halves(chain[0], chain[1], token_steps, "add_kv")
        qkv_sum, _ = scatter_halves(chain[2], chain[3], row_steps, "add_qkv")
        gains = lax.psum(gains, "ctx")
    (input_grad,) = Call(1)(
        final_kernel,
        "input_gradient",
        [
            ("whole", kv_sum),
            ("whole", query_grad),
            ("whole", qkv_weight),
            ("whole", hidden_in),
            ("whole", gain_one),
            ("whole", grad_middle),
            ("whole", rope_own),
        ],
        [("whole", shape_of((tokens, width), low))],
        [pltpu.VMEM((tokens, columns), low)],
        2 * tokens * width * columns,
    )

    def piece_of(rows):
        return own_piece(rows, device, low_bits)

    qkv_rows = unfold_rows(qkv_sum, columns, w_folded)
    ff_folded = 2 * ff * (width - main) // main
    down_at = 2 * ff + ff_folded
    ff_rows = unfold_rows(late_sum, 2 * ff, ff_folded)
    device_groups = ff // group_count // TILE
    out_at = down_at + device_groups * width
    down_rows = jnp.concatenate(
        [late_sum[:, down_at + a * width : down_at + (a + 1) * width] for a in range(device_groups)],
        axis=0,
    )
    output_rows = unfold_rows(late_sum[:, out_at:], width, width * (width - main) // main)
    return (
        block_out,
        input_grad,
        gains[0],
        piece_of(qkv_rows[:, :width]),
        piece_of(qkv_rows[:, width : width + KV_WIDTH]),
        piece_of(qkv_rows[:, width + KV_WIDTH :]),
        piece_of(output_rows),
        gains[1],
        piece_of(ff_rows[:, :ff]),
        piece_of(ff_rows[:, ff:]),
        piece_of(down_rows),
    )


def solution(mesh):
    row = P("ctx", None)
    in_specs = (row, P(), row, row, row, row, P(), row, row, row, P(), P(), row)
    out_specs = (row, row, P(), row, row, row, row, P(), row, row, row)
    return jax.shard_map(body, mesh=mesh, in_specs=in_specs, out_specs=out_specs, check_vma=False)
```

```python
import functools

import jax
import jax.numpy as jnp
import numpy as np
from jax import lax
from jax.experimental import pallas as pl
from jax.experimental.pallas import tpu as pltpu
from jax.sharding import PartitionSpec as P

HEADS = 9
KV_HEADS = 3
GROUP = HEADS // KV_HEADS
HEAD_SIZE = 64
KV_WIDTH = KV_HEADS * HEAD_SIZE
TILE = 16

epsilon = 1e-05
rope_base = 100000.0
masked_score = -1e30

low = jnp.bfloat16
full = jnp.float32


def exchange_steps(device_count, low_bits):
    top = device_count.bit_length() - 1
    steps = []
    if low_bits == 0 and top >= 4:
        for bit in range(top - 1, 2, -1):
            steps.append([i ^ (1 << bit) for i in range(device_count)])
        steps.append([i ^ (4 if i & 1 else 2) for i in range(device_count)])
        steps.append([i ^ (2 if i & 1 else 4) for i in range(device_count)])
        steps.append([i ^ 1 for i in range(device_count)])
    else:
        for bit in range(top - 1, low_bits - 1, -1):
            steps.append([i ^ (1 << bit) for i in range(device_count)])
    return steps


def source_table(device_count, low_bits):
    held = [[d >> low_bits] for d in range(device_count)]
    for partner in exchange_steps(device_count, low_bits):
        held = [held[d] + held[partner[d]] for d in range(device_count)]
    return np.array(held, np.int32)


def send(values, partner):
    return lax.ppermute(values, "ctx", [(i, p) for i, p in enumerate(partner)])


def gather_halves(values, steps, name):
    tokens = []
    for partner in steps[:-1]:
        come = send(values, partner)
        values, token = join(values, come, name, [])
        tokens.append(token)
    return values, send(values, steps[-1]), tokens


def whole_rows(flat, device, low_bits, columns):
    for bit in range(low_bits):
        partner = [i ^ (1 << bit) for i in range(lax.axis_size("ctx"))]
        other = send(flat, partner)
        is_high = (device >> bit) & 1
        flat = jnp.concatenate(
            [jnp.where(is_high, other, flat), jnp.where(is_high, flat, other)], axis=1
        )
    return flat.reshape(-1, columns)


def own_piece(rows, device, low_bits):
    flat = rows.reshape(1, -1)
    for bit in range(low_bits - 1, -1, -1):
        partner = [i ^ (1 << bit) for i in range(lax.axis_size("ctx"))]
        half = flat.shape[1] // 2
        is_high = (device >> bit) & 1
        leaving = jnp.where(is_high, flat[:, :half], flat[:, half:]).astype(low)
        staying = jnp.where(is_high, flat[:, half:], flat[:, :half])
        flat = staying + send(leaving, partner).astype(full)
    return flat


def low_bits_of(piece, columns):
    low_bits = 0
    while (piece << low_bits) < TILE * columns:
        low_bits += 1
    return low_bits


def unfold_rows(packed, columns, folded):
    return jnp.concatenate(
        [packed[:, :columns], packed[:, columns : columns + folded].reshape(-1, columns)], axis=0
    )


def whole_lanes(columns):
    return -(-columns // 128) * 128


def dot(left, right):
    return jnp.dot(left, right, preferred_element_type=full)


def dot_right(left, right):
    return lax.dot_general(left, right, (((1,), (1,)), ((), ())), preferred_element_type=full)


def dot_left(left, right):
    return lax.dot_general(left, right, (((0,), (0,)), ((), ())), preferred_element_type=full)


def iota(shape, axis):
    return lax.broadcasted_iota(jnp.int32, shape, axis)


def mixing_of(feature_ref):
    width = feature_ref.shape[1]
    return (iota((width, width), 0) == feature_ref[...]).astype(full).astype(low)


def fold_pick(rest, main, fold, at):
    row = iota((rest, main), 0)
    per = TILE // fold
    place = (row // per) * TILE + lax.rem(row, per) * fold + at
    return (iota((rest, main), 1) == place).astype(full).astype(low)


def as_row(column):
    return jnp.transpose(jnp.broadcast_to(column, (column.shape[0], 128)))[0:1]


def turn(values, rope, direction):
    half_dim = HEAD_SIZE // 2
    swapped = jnp.concatenate([values[:, half_dim:], values[:, :half_dim]], axis=1)
    sine = rope[:, 2 * HEAD_SIZE : 3 * HEAD_SIZE]
    return values * rope[:, :HEAD_SIZE] + swapped * (direction * sine)


def rope_of(cos_ref, sin_ref, times, part, quarter):
    _, places, _, lanes = cos_ref.shape
    value = cos_ref[part] * times[0, quarter] - sin_ref[part] * times[1, quarter]
    return value.reshape(places * TILE, lanes)


def rope_own_of(cos_ref, sin_ref, times):
    _, quarters, rows, lanes = times.shape
    parts = [
        cos_ref[part, 0] * times[0] - sin_ref[part, 0] * times[1] for part in range(2)
    ]
    return jnp.concatenate([part.reshape(quarters * rows, lanes) for part in parts], axis=0)


def unit_rows(values):
    inverse = lax.rsqrt(jnp.mean(values * values, axis=-1, keepdims=True) + epsilon)
    return values * inverse, inverse


def norm_back(unit, inverse, gain, grad):
    scaled = grad * gain
    return inverse * (scaled - unit * jnp.mean(scaled * unit, axis=-1, keepdims=True))


def query_range(own, part, rows, axis):
    shape = (rows, 1) if axis == 0 else (1, rows)
    half = rows // GROUP
    last_key = own[part] * half + lax.rem(iota(shape, axis), half)
    first_key = jnp.zeros(shape, jnp.int32) + own[2 + part] * half
    return first_key.astype(full), last_key.astype(full)


def gains_block(gains):
    high = gains.astype(low).astype(full)
    return jnp.concatenate([high, gains - high], axis=0).astype(low)


def gains_of(block):
    block = block.astype(full)
    return block[:8] + block[8:]


class Call:
    def __init__(self, steps):
        self.steps = steps

    def spec(self, kind, shape):
        if kind == "smem":
            return pl.BlockSpec(memory_space=pltpu.SMEM)
        if kind == "token":
            return pl.BlockSpec(memory_space=pl.ANY)
        if self.steps == 1 or kind == "whole":
            return pl.BlockSpec(memory_space=pltpu.VMEM)
        rest = tuple(shape[1:])
        return pl.BlockSpec((shape[0] // self.steps,) + rest, lambda i: (i,) + (0,) * len(rest))

    def __call__(self, kernel, name, ins, outs, scratch, micros, after=(), vmem=16):
        steps = self.steps
        first, last, end = len(ins), len(ins) + len(after), len(ins) + len(after) + len(outs)

        def run(*refs):
            refs[end][...] = jnp.zeros_like(refs[end])
            used = refs[:first] + refs[last:end] + refs[end + 1 :]
            kernel(pl.program_id(0) if steps > 1 else 0, steps, *used)

        ins = list(ins) + [("token", token) for token in after]
        outs = list(outs) + [("whole", shape_of((8, 128), full))]
        return pl.pallas_call(
            run,
            grid=(steps,) if steps > 1 else (),
            in_specs=[self.spec(kind, a.shape) for kind, a in ins],
            out_specs=[self.spec(kind, s.shape) for kind, s in outs],
            out_shape=[s for _, s in outs],
            scratch_shapes=scratch,
            compiler_params=pltpu.CompilerParams(vmem_limit_bytes=vmem * 1024 * 1024),
            cost_estimate=pl.CostEstimate(
                flops=int(micros * steps * 1e9), bytes_accessed=1024, transcendentals=0
            ),
            name=name,
        )(*[a for _, a in ins])


def once(step, steps, at, action):
    if steps == 1:
        action()
    else:
        pl.when(step == at)(action)


def shape_of(shape, dtype):
    return jax.ShapeDtypeStruct(shape, dtype)


def join_kernel(step, steps, held_ref, come_ref, out_ref):
    rows = held_ref.shape[0]
    out_ref[:rows, :] = held_ref[...]
    out_ref[rows:, :] = come_ref[...]


def join(held, come, name, after):
    rows, columns = held.shape
    if not after and rows > 64:
        return jnp.concatenate([held, come], axis=0), None
    return Call(1)(
        join_kernel,
        "join_" + name,
        [("whole", held), ("whole", come)],
        [("whole", shape_of((2 * rows, columns), held.dtype))],
        [],
        1,
        after,
    )


def pack_kernel(step, steps, hidden_ref, gain_ref, packed_ref, normed_ref):
    width = hidden_ref.shape[1]
    unit, _ = unit_rows(hidden_ref[...].astype(full))
    normed_ref[...] = (unit * gain_ref[...]).astype(low)
    for a in range(hidden_ref.shape[0] // TILE):
        packed_ref[:, a * width : (a + 1) * width] = normed_ref[a * TILE : (a + 1) * TILE, :]


def fold_into(out_ref, at, refs):
    columns = sum(ref.shape[1] for ref in refs)
    lane = at
    for ref in refs:
        out_ref[:, lane : lane + ref.shape[1]] = ref[:TILE, :]
        lane += ref.shape[1]
    tails = [ref[TILE:, :].astype(full) for ref in refs]
    tail = tails[0] if len(tails) == 1 else jnp.concatenate(tails, axis=1)
    fold = TILE // tail.shape[0]
    part = columns // fold
    rows = [
        tail[j : j + 1, block * part : (block + 1) * part]
        for j in range(tail.shape[0])
        for block in range(fold)
    ]
    out_ref[:, lane : lane + part] = jnp.concatenate(rows, axis=0).astype(low)
    return lane + part


def fold_qkv_kernel(step, steps, query_ref, key_ref, value_ref, out_ref):
    end = fold_into(out_ref, 0, [query_ref, key_ref, value_ref])
    out_ref[:, end:] = jnp.zeros((TILE, out_ref.shape[1] - end), low)


def fold_late_kernel(step, steps, gate_ref, up_ref, down_ref, output_ref, out_ref):
    lane = fold_into(out_ref, 0, [gate_ref, up_ref])
    rows, width = down_ref.shape
    for a in range(rows // TILE):
        out_ref[:, lane : lane + width] = down_ref[a * TILE : (a + 1) * TILE, :]
        lane += width
    lane = fold_into(out_ref, lane, [output_ref])
    out_ref[:, lane:] = jnp.zeros((TILE, out_ref.shape[1] - lane), low)


def weights_kernel(step, steps, feature_ref, own_ref, come_ref, weight_ref, key_value_ref, mixed):
    width, columns = weight_ref.shape
    half = own_ref.shape[0]
    main = 2 * half
    fold = main // (width - main)
    part = columns // fold
    mixed[:half, :] = own_ref[:, :columns]
    mixed[half:main, :] = come_ref[:, :columns]
    folded = slice(columns, columns + part)
    extra = jnp.concatenate([own_ref[:, folded], come_ref[:, folded]], axis=0)
    for at in range(fold):
        mixed[main:, at * part : (at + 1) * part] = dot(
            fold_pick(width - main, main, fold, at), extra
        ).astype(low)
    natural = dot(mixing_of(feature_ref), mixed[...])
    weight_ref[...] = natural.astype(low)
    keys = natural[:, width : width + KV_WIDTH]
    key_value_ref[:, :KV_WIDTH] = keys.astype(low)
    half_dim = HEAD_SIZE // 2
    swapped = [
        keys[:, (block ^ 1) * half_dim : ((block ^ 1) + 1) * half_dim]
        for block in range(KV_WIDTH // half_dim)
    ]
    key_value_ref[:, KV_WIDTH : 2 * KV_WIDTH] = jnp.concatenate(swapped, axis=1).astype(low)
    key_value_ref[:, 2 * KV_WIDTH :] = natural[:, width + KV_WIDTH :].astype(low)


def queries_kernel(step, steps, normed_ref, weight_ref, cos_ref, sin_ref, times, query_ref):
    tokens, width = normed_ref.shape
    half = tokens // 2
    queries = dot(normed_ref[...], weight_ref[:, :width])
    rope = rope_own_of(cos_ref, sin_ref, times)
    for head in range(HEADS):
        turned = turn(queries[:, head * HEAD_SIZE : (head + 1) * HEAD_SIZE], rope, 1.0)
        turned = turned.astype(low) * low(HEAD_SIZE**-0.5)
        for part in range(2):
            row = (part * GROUP + head % GROUP) * half
            query_ref[head // GROUP, row : row + half, :] = turned[part * half : (part + 1) * half]


def project_kernel(step, steps, normed_ref, weight_ref, cos_ref, sin_ref, times, kv_ref):
    width = weight_ref.shape[0]
    groups = normed_ref.shape[1] // width
    for a in range(groups):
        kv = dot(normed_ref[:, a * width : (a + 1) * width], weight_ref[...])
        rope = rope_of(cos_ref, sin_ref, times, a // (groups // 2), a % (groups // 2))
        cos, sin = rope[:, : 2 * HEAD_SIZE], rope[:, 2 * HEAD_SIZE :]
        cos = jnp.concatenate([cos, cos[:, :HEAD_SIZE]], axis=1)
        sin = jnp.concatenate([sin, sin[:, :HEAD_SIZE]], axis=1)
        keys = kv[:, :KV_WIDTH] * cos + kv[:, KV_WIDTH : 2 * KV_WIDTH] * sin
        at = a * 2 * KV_WIDTH
        kv_ref[:, at : at + KV_WIDTH] = keys.astype(low)
        kv_ref[:, at + KV_WIDTH : at + 2 * KV_WIDTH] = kv[:, 2 * KV_WIDTH :].astype(low)


def key_part(kv_ref, groups, column):
    lanes = [a * 2 * KV_WIDTH + column * HEAD_SIZE for a in groups]
    return jnp.concatenate([kv_ref[:, at : at + HEAD_SIZE] for at in lanes], axis=0)


def key_row(key_ref, part, groups):
    start = key_ref[part]
    return jnp.concatenate([start + float(i * TILE) for i in range(len(groups))], axis=1)


def reaches_low(own, blocks):
    return own[3] < blocks


def forward_kernel(
    is_first, low_blocks, step, steps, own, key_ref, query_ref, kv_ref, *rest
):
    acc, peak, total = rest[-3:]
    rows = query_ref.shape[1] // 2
    groups = kv_ref.shape[1] // (2 * KV_WIDTH)

    def first():
        if is_first:
            acc[...] = jnp.zeros_like(acc)
            peak[...] = jnp.full_like(peak, masked_score)
            total[...] = jnp.zeros_like(total)
        else:
            for out, held in zip(rest[-3:], rest[:3]):
                out[...] = held[...]

    once(step, steps, 0, first)

    def attend(key_half, query_half):
        members = range(key_half * groups // 2, (key_half + 1) * groups // 2)
        at = slice(query_half * rows, (query_half + 1) * rows)
        key_index = key_row(key_ref, key_half, members)
        first_key, last_key = query_range(own, query_half, rows, 0)
        allowed = (key_index >= first_key) & (key_index <= last_key)
        for head in range(KV_HEADS):
            scores = dot_right(query_ref[head, at], key_part(kv_ref, members, head))
            masked = jnp.where(allowed, scores, masked_score)
            old = peak[head, at]
            new = jnp.maximum(old, jnp.max(masked, axis=1, keepdims=True))
            weights = jnp.where(allowed, jnp.exp(masked - new), 0.0)
            factor = jnp.exp(old - new)
            peak[head, at] = new
            total[head, at] = total[head, at] * factor + jnp.sum(weights, axis=1, keepdims=True)
            acc[head, at] = acc[head, at] * factor + dot(
                weights.astype(low), key_part(kv_ref, members, KV_HEADS + head)
            )

    attend(0, 0)
    pl.when(reaches_low(own, low_blocks))(lambda: attend(0, 1))
    attend(1, 1)


def feedforward_kernel(
    step,
    steps,
    source_ref,
    feature_ref,
    acc_ref,
    peak_ref,
    sum_ref,
    hidden_ref,
    gain_ref,
    grad_ref,
    own_ref,
    come_ref,
    out_ref,
    grad_middle_ref,
    head_grad_ref,
    delta_ref,
    lse_ref,
    keep_ref,
    send_ref,
    gain_part_ref,
    attention,
    attended,
    output_w,
    normed,
    normed_t,
    down_w,
    down_grad,
    total,
    grad_normed,
    extra_grad,
):
    rows, width = hidden_ref.shape
    half = own_ref.shape[0]
    main = 2 * half
    rest = width - main
    fold = main // rest
    places = main // TILE
    ff = down_w.shape[0]
    chunk = 2 * ff // fold
    down_at = 2 * ff + chunk
    device_ff = ff // places
    groups = device_ff // TILE
    out_at = down_at + groups * width
    mixing = mixing_of(feature_ref)

    tokens = rows // 2
    for head in range(KV_HEADS):
        attention[head] = acc_ref[head] / sum_ref[head]
        logs = peak_ref[head] + jnp.log(sum_ref[head])
        for part in range(2):
            lse_ref[2 * head + part] = as_row(
                logs[part * GROUP * tokens : (part + 1) * GROUP * tokens]
            )
    for h in range(HEADS):
        for part in range(2):
            row = (part * GROUP + h % GROUP) * tokens
            attended[
                part * tokens : (part + 1) * tokens, h * HEAD_SIZE : (h + 1) * HEAD_SIZE
            ] = attention[h // GROUP, row : row + tokens, :].astype(low)
    attended[...] = dot(attended[...], mixing).astype(low)
    output_w[:half, :] = own_ref[:, out_at : out_at + width]
    output_w[half:main, :] = come_ref[:, out_at : out_at + width]
    part = width // fold
    folded = slice(out_at + width, out_at + width + part)
    extra = jnp.concatenate([own_ref[:, folded], come_ref[:, folded]], axis=0)
    for at in range(fold):
        output_w[main:, at * part : (at + 1) * part] = dot(
            fold_pick(rest, main, fold, at), extra
        ).astype(low)
    middle = hidden_ref[...].astype(full) + dot(attended[...], output_w[...])
    gain = gain_ref[...]
    unit, inverse = unit_rows(middle)
    mixed_norm = dot((unit * gain).astype(low), mixing)
    normed[...] = mixed_norm.astype(low)
    normed_t[...] = jnp.transpose(mixed_norm).astype(low)
    for place in range(places):
        held = own_ref if place < places // 2 else come_ref
        row = (place % (places // 2)) * TILE
        for a in range(groups):
            at = pl.multiple_of(source_ref[place] * device_ff + a * TILE, TILE)
            lane = down_at + a * width
            down_w[pl.ds(at, TILE), :] = held[row : row + TILE, lane : lane + width]
    total[...] = jnp.zeros_like(total)
    grad_normed[...] = jnp.zeros_like(grad_normed)
    extra_grad[...] = jnp.zeros_like(extra_grad)
    out_grad = grad_ref[...]

    def advance(c, carry):
        gate_at = pl.ds(pl.multiple_of(c * chunk, 128), chunk)
        up_at = pl.ds(pl.multiple_of(ff + c * chunk, 128), chunk)
        extra = jnp.concatenate(
            [own_ref[:, 2 * ff : down_at], come_ref[:, 2 * ff : down_at]], axis=0
        )

        def columns(lanes, at):
            pick = fold_pick(rest, main, fold, at)
            tail = dot(pick, extra).astype(low)
            value = (
                dot(normed[:, :half], own_ref[:, lanes])
                + dot(normed[:, half:main], come_ref[:, lanes])
                + dot(normed[:, main:], tail)
            )
            return value, tail, pick

        gate, gate_tail, gate_pick = columns(gate_at, c)
        up, up_tail, up_pick = columns(up_at, c + fold // 2)
        down_at_c = pl.ds(pl.multiple_of(c * chunk, 128), chunk)
        down = down_w[down_at_c, :]
        sigma = 1.0 / (1.0 + jnp.exp(-gate))
        silu = gate * sigma
        inner = (silu * up).astype(low)
        total[...] += dot(inner, down)
        grad_inner = dot_right(out_grad, down)
        grad_gate = (grad_inner * up * sigma * (1.0 + gate * (1.0 - sigma))).astype(low)
        grad_up = (grad_inner * silu).astype(low)
        down_grad[down_at_c, :] = dot_left(inner, out_grad).astype(low)
        for grad, lanes, tail, pick in (
            (grad_gate, gate_at, gate_tail, gate_pick),
            (grad_up, up_at, up_tail, up_pick),
        ):
            grad_normed[:, :half] += dot_right(grad, own_ref[:, lanes])
            grad_normed[:, half:main] += dot_right(grad, come_ref[:, lanes])
            grad_normed[:, main:] += dot_right(grad, tail)
            keep_ref[:, lanes] = dot(normed_t[:half], grad).astype(low)
            send_ref[:, lanes] = dot(normed_t[half:main], grad).astype(low)
            extra_grad[...] += dot_left(pick, dot(normed_t[main:], grad).astype(low))
        return carry

    lax.fori_loop(0, ff // chunk, advance, 0)
    out_ref[...] = (middle + total[...]).astype(low)
    keep_ref[:, 2 * ff : down_at] = extra_grad[:half].astype(low)
    send_ref[:, 2 * ff : down_at] = extra_grad[half:].astype(low)
    for place in range(places):
        held = keep_ref if place < places // 2 else send_ref
        row = (place % (places // 2)) * TILE
        for a in range(groups):
            at = pl.multiple_of(source_ref[place] * device_ff + a * TILE, TILE)
            lane = down_at + a * width
            held[row : row + TILE, lane : lane + width] = down_grad[pl.ds(at, TILE), :]

    high = grad_normed[...].astype(low)
    tail = (grad_normed[...] - high.astype(full)).astype(low)
    back = dot_right(high, mixing) + dot_right(tail, mixing)
    gain_part_ref[...] = jnp.sum(back * unit, axis=0, keepdims=True)
    grad_middle = out_grad.astype(full) + norm_back(unit, inverse, gain, back)
    grad_middle_ref[...] = grad_middle
    grad_branch = grad_middle.astype(low)
    output_grad = dot_left(attended[...], grad_branch).astype(low)
    keep_ref[:, out_at : out_at + width] = output_grad[:half]
    send_ref[:, out_at : out_at + width] = output_grad[half:main]
    extra = sum(
        dot_left(
            fold_pick(rest, main, fold, at), output_grad[main:, at * part : (at + 1) * part]
        )
        for at in range(fold)
    ).astype(low)
    unused = jnp.zeros((half, keep_ref.shape[1] - folded.stop), low)
    for held, rows_of_half in ((keep_ref, extra[:half]), (send_ref, extra[half:])):
        held[:, folded] = rows_of_half
        held[:, folded.stop :] = unused
    grad_low = dot_right(grad_branch, output_w[...]).astype(low)
    grad_low = dot_right(grad_low, mixing).astype(low)
    for head in range(KV_HEADS):
        for part in range(2):
            grads = jnp.concatenate(
                [
                    grad_low[
                        part * tokens : (part + 1) * tokens, h * HEAD_SIZE : (h + 1) * HEAD_SIZE
                    ]
                    for h in range(head * GROUP, (head + 1) * GROUP)
                ],
                axis=0,
            )
            at = slice(part * GROUP * tokens, (part + 1) * GROUP * tokens)
            head_grad_ref[head, at] = grads
            delta_ref[2 * head + part] = as_row(
                jnp.sum(grads.astype(full) * attention[head, at], axis=1, keepdims=True)
            )


def backward_kernel(
    is_first,
    key_half,
    low_blocks,
    step,
    steps,
    own,
    key_ref,
    query_ref,
    grad_ref,
    lse_ref,
    delta_ref,
    kv_ref,
    tokens_ref,
    cos_ref,
    sin_ref,
    times,
    *rest,
):
    if not is_first:
        held, rest = rest[:2], rest[2:]
    grad_query, grad_weight, out_ref, grad_kv = rest
    rows = query_ref.shape[1] // 2
    groups = kv_ref.shape[1] // (2 * KV_WIDTH)
    key_rows = kv_ref.shape[0]
    width = tokens_ref.shape[1] // groups
    members = range(key_half * groups // 2, (key_half + 1) * groups // 2)

    def first():
        if is_first:
            grad_query[...] = jnp.zeros_like(grad_query)
            grad_weight[...] = jnp.zeros_like(grad_weight)
        else:
            grad_query[...] = held[0][...]
            grad_weight[...] = held[1][...]

    once(step, steps, 0, first)
    key_index = key_row(key_ref, key_half, members)
    key_index = jnp.transpose(jnp.broadcast_to(key_index, (128, key_index.shape[1])))[:, 0:1]

    def attend(query_half, add):
        at = slice(query_half * rows, (query_half + 1) * rows)
        first_key, last_key = query_range(own, query_half, rows, 1)
        allowed = (key_index >= first_key) & (key_index <= last_key)
        for head in range(KV_HEADS):
            keys = key_part(kv_ref, members, head)
            scores = dot_right(keys, query_ref[head, at])
            probs = jnp.where(allowed, jnp.exp(scores - lse_ref[2 * head + query_half]), 0.0)
            d_probs = dot_right(key_part(kv_ref, members, KV_HEADS + head), grad_ref[head, at])
            d_scores = (probs * (d_probs - delta_ref[2 * head + query_half])).astype(low)
            grad_query[2 * head + query_half] += dot_left(keys, d_scores)
            parts = (
                (head, dot(d_scores, query_ref[head, at])),
                (KV_HEADS + head, dot(probs.astype(low), grad_ref[head, at])),
            )
            for column, value in parts:
                lanes = slice(column * HEAD_SIZE, (column + 1) * HEAD_SIZE)
                if add:
                    grad_kv[:, lanes] += value
                else:
                    grad_kv[:, lanes] = value

    if key_half == 0:
        attend(0, False)
        pl.when(reaches_low(own, low_blocks))(lambda: attend(1, True))
    else:
        attend(1, False)
    for i, a in enumerate(members):
        at = slice(i * key_rows, (i + 1) * key_rows)
        rope = rope_of(cos_ref, sin_ref, times, key_half, i)
        turned = jnp.concatenate(
            [
                turn(grad_kv[at, head * HEAD_SIZE : (head + 1) * HEAD_SIZE], rope, -1.0)
                for head in range(KV_HEADS)
            ]
            + [grad_kv[at, KV_WIDTH:]],
            axis=1,
        ).astype(low)
        out_ref[:, i * 2 * KV_WIDTH : (i + 1) * 2 * KV_WIDTH] = turned
        grad_weight[...] += dot_left(turned, tokens_ref[:, a * width : (a + 1) * width])


def qkv_grad_kernel(
    with_gains,
    step,
    steps,
    feature_ref,
    grad_query,
    grad_weight,
    normed_ref,
    weight_ref,
    cos_ref,
    sin_ref,
    times,
    gain_ref,
    gain_two_ref,
    query_grad_ref,
    gains_ref,
    keep_ref,
    send_ref,
    natural,
):
    tokens, width = normed_ref.shape
    half = tokens // 2
    rope = rope_own_of(cos_ref, sin_ref, times)
    for head in range(KV_HEADS):
        rotated = [
            jnp.transpose(grad_query[2 * head + part]) * HEAD_SIZE**-0.5 for part in range(2)
        ]
        for g in range(GROUP):
            h = head * GROUP + g
            value = jnp.concatenate([part[g * half : (g + 1) * half] for part in rotated], axis=0)
            query_grad_ref[:, h * HEAD_SIZE : (h + 1) * HEAD_SIZE] = turn(value, rope, -1.0).astype(
                low
            )
    natural[:, :width] = dot_left(normed_ref[...], query_grad_ref[...])
    natural[:, width:] = jnp.transpose(grad_weight[...])
    products = natural[...] * weight_ref[...].astype(full)
    gain_part = as_row(jnp.sum(products, axis=1, keepdims=True)) / gain_ref[...]
    row = iota((8, width), 0)
    gains = jnp.where(row == 0, gain_part, jnp.where(row == 1, gain_two_ref[...], 0.0))
    gains_ref[...] = gains
    mixed = dot_left(mixing_of(feature_ref), natural[...].astype(low)).astype(low)
    columns = mixed.shape[1]
    rows = keep_ref.shape[0]
    main = 2 * rows
    fold = main // (width - main)
    part = columns // fold
    extra = sum(
        dot_left(fold_pick(width - main, main, fold, at), mixed[main:, at * part : (at + 1) * part])
        for at in range(fold)
    ).astype(low)
    unused = jnp.zeros((rows, keep_ref.shape[1] - columns - part), low)
    for held, at in ((keep_ref, 0), (send_ref, rows)):
        held[:rows, :columns] = mixed[at : at + rows]
        held[:rows, columns : columns + part] = extra[at : at + rows]
        held[:rows, columns + part :] = unused
    if with_gains:
        send_ref[rows:, :width] = gains_block(gains)
        send_ref[rows:, width:] = jnp.zeros((TILE, send_ref.shape[1] - width), low)


def merge_kernel(step, steps, *refs):
    kv_keep, kv_come, w_keep, w_come, gains_ref, keep_out, send_out, gains_out = (
        refs[0:2],
        refs[2:4],
    ) + refs[4:]
    rows = w_keep.shape[0]
    half = rows // 2
    width = gains_ref.shape[1]
    gains = gains_of(gains_block(gains_ref[...])) + gains_of(w_come[rows:, :width])
    gains_out[...] = gains
    lane = 0
    for keep, come in tuple(zip(kv_keep, kv_come)) + ((w_keep, w_come),):
        columns = keep.shape[1]
        lanes = slice(lane, lane + columns)
        for out, at in ((keep_out, 0), (send_out, half)):
            value = keep[at : at + half, :].astype(full) + come[at : at + half, :].astype(full)
            out[:half, lanes] = value.astype(low)
        lane += columns
    send_out[half:, :width] = gains_block(gains)
    send_out[half:, width:] = jnp.zeros((TILE, send_out.shape[1] - width), low)


def add_kernel(with_gains, step, steps, keep_ref, come_ref, *rest):
    rows = keep_ref.shape[0]
    if with_gains:
        gains_ref, rest = rest[0], rest[1:]
        rest, gains_out = rest[:-1], rest[-1]
        width = gains_ref.shape[1]
        gains = gains_of(gains_block(gains_ref[...])) + gains_of(come_ref[rows:, :width])
        gains_out[...] = gains

    def tile(at):
        at = pl.ds(at, TILE)
        return keep_ref[at, :].astype(full) + come_ref[at, :].astype(full)

    if rows == TILE:
        rest[0][...] = tile(0)
        return
    keep_out, send_out = rest
    half = rows // 2

    def advance(i, carry):
        at = pl.multiple_of(i * TILE, TILE)
        keep_out[pl.ds(at, TILE), :] = tile(at).astype(low)
        send_out[pl.ds(at, TILE), :] = tile(pl.multiple_of(half + at, TILE)).astype(low)
        return carry

    lax.fori_loop(0, half // TILE, advance, 0)
    if with_gains:
        send_out[half:, :width] = gains_block(gains)
        send_out[half:, width:] = jnp.zeros((TILE, send_out.shape[1] - width), low)


def scatter_halves(keep, leaving, steps, name, gains=None):
    with_gains = gains is not None
    more = TILE if with_gains else 0
    for at, partner in enumerate(reversed(steps)):
        come = send(leaving, partner)
        rows, columns = keep.shape
        ins = [("whole", keep), ("whole", come)]
        if rows == TILE:
            outs = [("whole", shape_of((rows, columns), full))]
        else:
            outs = [
                ("whole", shape_of((rows // 2, columns), low)),
                ("whole", shape_of((rows // 2 + more, columns), low)),
            ]
        if with_gains:
            ins.append(("whole", gains))
            outs.append(("whole", shape_of(gains.shape, full)))
        result = Call(1)(
            functools.partial(add_kernel, with_gains),
            name,
            ins,
            outs,
            [],
            1,
        )
        if with_gains:
            gains = result[-2]
        if rows == TILE:
            return result[0], gains
        keep, leaving = result[0], result[1]


def final_kernel(
    step,
    steps,
    sum_ref,
    query_grad_ref,
    weight_ref,
    hidden_ref,
    gain_ref,
    grad_middle_ref,
    out_ref,
    grads,
):
    tokens, width = hidden_ref.shape
    grads[:, :width] = query_grad_ref[...]
    for a in range(tokens // TILE):
        rows = slice(a * TILE, (a + 1) * TILE)
        lanes = slice(a * 2 * KV_WIDTH, (a + 1) * 2 * KV_WIDTH)
        grads[rows, width:] = sum_ref[:, lanes].astype(low)
    back = dot_right(grads[...], weight_ref[...])
    unit, inverse = unit_rows(hidden_ref[...].astype(full))
    out_ref[...] = (grad_middle_ref[...] + norm_back(unit, inverse, gain_ref[...], back)).astype(low)


def body(
    hidden_in,
    attention_gain,
    query_weight,
    key_weight,
    value_weight,
    output_weight,
    feedforward_gain,
    gate_weight,
    up_weight,
    down_weight,
    doc_of_block,
    pair_table,
    out_grad,
):
    tokens, width = hidden_in.shape
    half_rows = tokens // 2
    count = lax.axis_size("ctx")
    device = lax.axis_index("ctx")
    ff = gate_weight.shape[1] * count // width
    low_bits = low_bits_of(query_weight.shape[1], width)
    merged = low_bits == 0
    row_steps = exchange_steps(count, low_bits)
    token_steps = exchange_steps(count, 0)
    group_count = count >> low_bits
    group_rows = width // group_count
    groups = tokens // TILE
    steps = max(1, TILE * count // 512)
    places = count // (2 * steps)
    gain_one = attention_gain.reshape(1, width)
    gain_two = feedforward_gain.reshape(1, width)
    columns = width + 2 * KV_WIDTH
    main = TILE * group_count
    fold = main // (width - main)
    w_lanes = whole_lanes(columns + columns // fold)
    ff_folded = 2 * ff // fold
    down_at = 2 * ff + ff_folded
    device_groups = ff // group_count // TILE
    out_at = down_at + device_groups * width
    late_lanes = whole_lanes(out_at + width + width // fold)
    call = Call(steps)
    one = Call(1)

    def rows_of(piece, piece_columns):
        return ("whole", whole_rows(piece, device, low_bits, piece_columns))

    packed, normed, _ = one(
        pack_kernel,
        "norm_and_pack",
        [("whole", hidden_in), ("whole", gain_one)],
        [
            ("whole", shape_of((TILE, groups * width), low)),
            ("whole", shape_of((tokens, width), low)),
        ],
        [],
        1,
    )
    token_own, token_come, token_marks = gather_halves(packed, token_steps, "tokens")
    qkv_piece, _ = one(
        fold_qkv_kernel,
        "fold_qkv",
        [
            rows_of(query_weight, width),
            rows_of(key_weight, KV_WIDTH),
            rows_of(value_weight, KV_WIDTH),
        ],
        [("whole", shape_of((TILE, w_lanes), low))],
        [],
        1,
    )
    w_own, w_come, _ = gather_halves(qkv_piece, row_steps, "qkv")

    def table_row(table):
        return lax.dynamic_index_in_dim(jnp.asarray(table), device, 0, keepdims=False)

    sources = table_row(source_table(count, 0))
    group_table = source_table(count, low_bits)
    group_sources = table_row(group_table)
    inside = np.arange(group_rows)[None, None, :]
    features = group_table[:, :, None] * group_rows + inside
    features = np.concatenate(
        [
            features[:, :, :TILE].reshape(count, -1),
            features[:, :, TILE:].reshape(count, -1),
        ],
        axis=1,
    ).astype(np.int32)
    feature_row = table_row(features).reshape(1, width)

    device_iota = jnp.arange(count, dtype=jnp.int32)
    pairs = jnp.sum(
        jnp.where(sources[:, None] == device_iota[None, :], pair_table[None, :], 0), axis=1
    )
    blocks = jnp.stack([pairs, 2 * count - 1 - pairs], axis=1).reshape(-1)
    block_iota = jnp.arange(2 * count, dtype=jnp.int32)
    block_docs = jnp.sum(
        jnp.where(blocks[:, None] == block_iota[None, :], doc_of_block[None, :], 0), axis=1
    )
    doc_start = jnp.min(
        jnp.where(block_docs[:, None] == doc_of_block[None, :], block_iota[None, :], 2 * count),
        axis=1,
    )
    own = jnp.concatenate([blocks[:2], doc_start[:2]])

    def by_step(values):
        return values.reshape(2, steps, places, 2).transpose(0, 1, 3, 2)

    inner = jnp.arange(TILE, dtype=jnp.int32)
    key_index = by_step(blocks)[..., None] * half_rows + inner
    key_index = key_index.astype(full).reshape(2, 2 * steps, 1, -1)
    frequency = rope_base ** (-jnp.arange(HEAD_SIZE // 2, dtype=full) * (2.0 / HEAD_SIZE))
    block_angle = (by_step(blocks - doc_start) * half_rows).astype(full)[..., None] * frequency
    offset = jnp.arange(half_rows, dtype=full).reshape(groups // 2, TILE)
    offset_angle = offset[..., None] * frequency
    cos_in, sin_in = jnp.cos(offset_angle), jnp.sin(offset_angle)
    times_cos = jnp.concatenate([cos_in] * 4 + [-sin_in, sin_in] * 2, axis=-1)
    times_sin = jnp.concatenate([sin_in] * 4 + [cos_in, -cos_in] * 2, axis=-1)
    times = jnp.stack([times_cos, times_sin])
    block_cos = jnp.tile(jnp.cos(block_angle), 8).reshape(2, 2 * steps, places, 1, 4 * HEAD_SIZE)
    block_sin = jnp.tile(jnp.sin(block_angle), 8).reshape(2, 2 * steps, places, 1, 4 * HEAD_SIZE)
    rope_own = [
        ("whole", block_cos[0, :2, :1]),
        ("whole", block_sin[0, :2, :1]),
        ("whole", times),
    ]
    halves = [
        (
            held,
            key_index[place],
            [("rows", block_cos[place]), ("rows", block_sin[place]), ("whole", times)],
        )
        for place, held in enumerate((token_own, token_come))
    ]

    rows = GROUP * tokens
    half = TILE * count // 2
    kv_shape = shape_of((half, groups * 2 * KV_WIDTH), low)
    head_shape = (KV_HEADS, rows, HEAD_SIZE)
    weight, kv_weight, _ = one(
        weights_kernel,
        "qkv_weights",
        [("whole", feature_row), ("whole", w_own), ("whole", w_come)],
        [
            ("whole", shape_of((width, columns), low)),
            ("whole", shape_of((width, 3 * KV_WIDTH), low)),
        ],
        [pltpu.VMEM((width, columns), low)],
        3,
    )
    queries, _ = one(
        queries_kernel,
        "queries",
        [("whole", normed), ("whole", weight)] + rope_own,
        [("whole", shape_of(head_shape, low))],
        [],
        2,
    )

    def project(place, after):
        token_rows, _, turns = halves[place]
        return call(
            project_kernel,
            "project",
            [("rows", token_rows), ("whole", kv_weight)] + turns,
            [("rows", kv_shape)],
            [],
            5,
            after,
        )

    state_shapes = [
        ("whole", shape_of(head_shape, full)),
        ("whole", shape_of((KV_HEADS, rows, 1), full)),
        ("whole", shape_of((KV_HEADS, rows, 1), full)),
    ]

    def attend(place, kv, state, after):
        return call(
            functools.partial(forward_kernel, not state, count),
            "attention_forward",
            [
                ("smem", own),
                ("rows", halves[place][1]),
                ("whole", queries),
                ("rows", kv),
            ]
            + [("whole", held) for held in state],
            state_shapes,
            [],
            6,
            after,
        )

    kv_own, mark = project(0, [])
    *state, own_mark = attend(0, kv_own, [], [])

    late_piece, _ = one(
        fold_late_kernel,
        "fold_late",
        [
            rows_of(gate_weight, ff),
            rows_of(up_weight, ff),
            rows_of(down_weight, width),
            rows_of(output_weight, width),
        ],
        [("whole", shape_of((TILE, late_lanes), low))],
        [],
        1,
        [token_marks[1]],
    )
    late = late_piece
    for at, partner in enumerate(row_steps[:-1]):
        come = send(late, partner)
        before = [own_mark] if at == len(row_steps) - 3 else []
        if at == len(row_steps) - 2:
            kv_come, come_mark = project(1, [late_mark])
            *state, mark = attend(1, kv_come, state, [])
            before = [mark]
        late, late_mark = join(late, come, "late", before)
    late_own, late_come = late, send(late, row_steps[-1])

    late_shape = late_own.shape
    row_shape = shape_of((2 * KV_HEADS, 1, rows // 2), full)
    block_out, grad_middle, head_grads, delta, lse, late_keep, late_send, gain_two_part, _ = one(
        feedforward_kernel,
        "feedforward",
        [
            ("smem", group_sources),
            ("whole", feature_row),
        ]
        + [("whole", held) for held in state]
        + [
            ("whole", hidden_in),
            ("whole", gain_two),
            ("whole", out_grad),
            ("whole", late_own),
            ("whole", late_come),
        ],
        [
            ("whole", shape_of((tokens, width), low)),
            ("whole", shape_of((tokens, width), full)),
            ("whole", shape_of(head_shape, low)),
            ("whole", row_shape),
            ("whole", row_shape),
            ("whole", shape_of(late_shape, low)),
            ("whole", shape_of(late_shape, low)),
            ("whole", shape_of((1, width), full)),
        ],
        [
            pltpu.VMEM(head_shape, full),
            pltpu.VMEM((tokens, width), low),
            pltpu.VMEM((width, width), low),
            pltpu.VMEM((tokens, width), low),
            pltpu.VMEM((width, tokens), low),
            pltpu.VMEM((ff, width), low),
            pltpu.VMEM((ff, width), low),
            pltpu.VMEM((tokens, width), full),
            pltpu.VMEM((tokens, width), full),
            pltpu.VMEM((main, ff_folded), full),
        ],
        16,
        vmem=28,
    )

    def attend_back(place, key_half, kv, carried, after):
        token_rows, keys, turns = halves[place]
        return call(
            functools.partial(backward_kernel, not carried, key_half, count),
            "attention_backward",
            [
                ("smem", own),
                ("rows", keys),
                ("whole", queries),
                ("whole", head_grads),
                ("whole", lse),
                ("whole", delta),
                ("rows", kv),
                ("rows", token_rows),
            ]
            + turns
            + [("whole", held) for held in carried],
            [
                ("whole", shape_of((2 * KV_HEADS, HEAD_SIZE, rows // 2), full)),
                ("whole", shape_of((2 * KV_WIDTH, width), full)),
                ("rows", shape_of((half, groups * KV_WIDTH), low)),
            ],
            [pltpu.VMEM((groups // 2 * places * TILE, 2 * KV_WIDTH), full)],
            6,
            after,
        )

    late_steps = row_steps[::-1]
    keep, leaving = late_keep, late_send

    def add_late(at, after):
        come = send(leaving, late_steps[at])
        part = shape_of((keep.shape[0] // 2, late_lanes), low)
        outs = [part, part] if keep.shape[0] > TILE else [shape_of((TILE, late_lanes), full)]
        return one(
            functools.partial(add_kernel, False),
            "add_late",
            [("whole", keep), ("whole", come)],
            [("whole", out) for out in outs],
            [],
            1,
            after,
        )

    *carried, send_low, mark = attend_back(1, 0, kv_come, [], [])
    keep, leaving, late_mark = add_late(0, [mark])
    *carried, send_high, mark = attend_back(1, 1, kv_come, carried, [late_mark])
    *carried, keep_low, mark = attend_back(0, 0, kv_own, carried, [])
    keep, leaving, late_mark = add_late(1, [mark])
    *carried, keep_high, mark = attend_back(0, 1, kv_own, carried, [late_mark])
    keep, leaving, late_mark = add_late(2, [mark])
    query_grad, gains, w_keep, w_send, mark = one(
        functools.partial(qkv_grad_kernel, merged),
        "qkv_gradients",
        [
            ("whole", feature_row),
            ("whole", carried[0]),
            ("whole", carried[1]),
            ("whole", normed),
            ("whole", weight),
        ]
        + rope_own
        + [
            ("whole", gain_one),
            ("whole", gain_two_part),
        ],
        [
            ("whole", shape_of((tokens, width), low)),
            ("whole", shape_of((8, width), full)),
            ("whole", shape_of((main // 2, w_lanes), low)),
            ("whole", shape_of((main // 2 + (TILE if merged else 0), w_lanes), low)),
        ],
        [pltpu.VMEM((width, columns), full)],
        3,
        [late_mark],
    )
    for at in range(3, len(late_steps)):
        result = add_late(at, [mark] if at == 3 else [])
        keep, leaving = result[0], result[1]
    late_sum = keep

    if merged:
        come = [send(part, token_steps[-1]) for part in (send_low, send_high, w_send)]
        lanes = 2 * send_low.shape[1] + w_lanes
        keep, leaving, gains, _ = one(
            merge_kernel,
            "add_first",
            [
                ("whole", keep_low),
                ("whole", keep_high),
                ("whole", come[0]),
                ("whole", come[1]),
                ("whole", w_keep),
                ("whole", come[2]),
                ("whole", gains),
            ],
            [
                ("whole", shape_of((half // 2, lanes), low)),
                ("whole", shape_of((half // 2 + TILE, lanes), low)),
                ("whole", shape_of(gains.shape, full)),
            ],
            [],
            2,
        )
        kv_sum, gains = scatter_halves(keep, leaving, token_steps[:-1], "add_chain", gains)
        qkv_sum = kv_sum[:, 2 * send_low.shape[1] :]
    else:
        kv_keep = jnp.concatenate([keep_low, keep_high], axis=1)
        kv_send = jnp.concatenate([send_low, send_high], axis=1)
        kv_sum, _ = scatter_halves(kv_keep, kv_send, token_steps, "add_kv")
        qkv_sum, _ = scatter_halves(w_keep, w_send, row_steps, "add_qkv")
        gains = lax.psum(gains, "ctx")
    input_grad, _ = one(
        final_kernel,
        "input_gradient",
        [
            ("whole", kv_sum),
            ("whole", query_grad),
            ("whole", weight),
            ("whole", hidden_in),
            ("whole", gain_one),
            ("whole", grad_middle),
        ],
        [("whole", shape_of((tokens, width), low))],
        [pltpu.VMEM((tokens, columns), low)],
        1,
    )

    def piece_of(piece_rows):
        return own_piece(piece_rows, device, low_bits)

    qkv_rows = unfold_rows(qkv_sum, columns, columns // fold)
    ff_rows = unfold_rows(late_sum, 2 * ff, ff_folded)
    down_rows = jnp.concatenate(
        [late_sum[:, down_at + a * width : down_at + (a + 1) * width] for a in range(device_groups)],
        axis=0,
    )
    output_rows = unfold_rows(late_sum[:, out_at:], width, width // fold)
    return (
        block_out,
        input_grad,
        gains[0],
        piece_of(qkv_rows[:, :width]),
        piece_of(qkv_rows[:, width : width + KV_WIDTH]),
        piece_of(qkv_rows[:, width + KV_WIDTH :]),
        piece_of(output_rows),
        gains[1],
        piece_of(ff_rows[:, :ff]),
        piece_of(ff_rows[:, ff:]),
        piece_of(down_rows),
    )


def solution(mesh):
    row = P("ctx", None)
    in_specs = (row, P(), row, row, row, row, P(), row, row, row, P(), P(), row)
    out_specs = (row, row, P(), row, row, row, row, P(), row, row, row)
    return jax.shard_map(body, mesh=mesh, in_specs=in_specs, out_specs=out_specs, check_vma=False)
```

```python
import functools

import jax
import jax.numpy as jnp
import numpy as np
from jax import lax
from jax.experimental import pallas as pl
from jax.experimental.pallas import tpu as pltpu
from jax.sharding import PartitionSpec as P

HEADS = 9
KV_HEADS = 3
GROUP = HEADS // KV_HEADS
HEAD_SIZE = 64
KV_WIDTH = KV_HEADS * HEAD_SIZE
TILE = 16
TOTAL, PEAK = HEAD_SIZE, HEAD_SIZE + 1

epsilon = 1e-05
rope_base = 100000.0
masked_score = -1e30

low = jnp.bfloat16
full = jnp.float32


def exchange_steps(device_count, low_bits):
    top = device_count.bit_length() - 1
    steps = []
    if low_bits == 0 and top >= 4:
        for bit in range(top - 1, 2, -1):
            steps.append([i ^ (1 << bit) for i in range(device_count)])
        steps.append([i ^ (4 if i & 1 else 2) for i in range(device_count)])
        steps.append([i ^ (2 if i & 1 else 4) for i in range(device_count)])
        steps.append([i ^ 1 for i in range(device_count)])
    else:
        for bit in range(top - 1, low_bits - 1, -1):
            steps.append([i ^ (1 << bit) for i in range(device_count)])
    return steps


def source_table(device_count, low_bits):
    held = [[d >> low_bits] for d in range(device_count)]
    for partner in exchange_steps(device_count, low_bits):
        held = [held[d] + held[partner[d]] for d in range(device_count)]
    return np.array(held, np.int32)


def send(values, partner):
    return lax.ppermute(values, "ctx", [(i, p) for i, p in enumerate(partner)])


def gather_halves(values, steps, name):
    for partner in steps[:-1]:
        values, _ = join(values, send(values, partner), name, [])
    return values, send(values, steps[-1])


def whole_rows(flat, device, low_bits, columns):
    for bit in range(low_bits):
        partner = [i ^ (1 << bit) for i in range(lax.axis_size("ctx"))]
        other = send(flat, partner)
        is_high = (device >> bit) & 1
        flat = jnp.concatenate(
            [jnp.where(is_high, other, flat), jnp.where(is_high, flat, other)], axis=1
        )
    return flat.reshape(-1, columns)


def own_piece(rows, device, low_bits):
    flat = rows.reshape(1, -1)
    for bit in range(low_bits - 1, -1, -1):
        partner = [i ^ (1 << bit) for i in range(lax.axis_size("ctx"))]
        half = flat.shape[1] // 2
        is_high = (device >> bit) & 1
        leaving = jnp.where(is_high, flat[:, :half], flat[:, half:]).astype(low)
        staying = jnp.where(is_high, flat[:, half:], flat[:, :half])
        flat = staying + send(leaving, partner).astype(full)
    return flat


def low_bits_of(piece, columns):
    low_bits = 0
    while (piece << low_bits) < TILE * columns:
        low_bits += 1
    return low_bits


def unfold_rows(packed, columns, folded):
    return jnp.concatenate(
        [packed[:, :columns], packed[:, columns : columns + folded].reshape(-1, columns)], axis=0
    )


def whole_lanes(columns):
    return -(-columns // 128) * 128


def dot(left, right):
    return jnp.dot(left, right, preferred_element_type=full)


def dot_right(left, right):
    return lax.dot_general(left, right, (((1,), (1,)), ((), ())), preferred_element_type=full)


def dot_left(left, right):
    return lax.dot_general(left, right, (((0,), (0,)), ((), ())), preferred_element_type=full)


def iota(shape, axis):
    return lax.broadcasted_iota(jnp.int32, shape, axis)


def mixing_of(feature_ref):
    width = feature_ref.shape[1]
    return (iota((width, width), 0) == feature_ref[...]).astype(full).astype(low)


def fold_scratch(main, part):
    return pltpu.VMEM((-(-part // 128), main, 128), full)


def fold_write(scratch, extra):
    for block in range(scratch.shape[0]):
        lanes = slice(block * 128, min(block * 128 + 128, extra.shape[1]))
        scratch[block, :, : lanes.stop - lanes.start] = extra[:, lanes].astype(full)


def fold_read(scratch, part):
    parts = [scratch[block] for block in range(scratch.shape[0])]
    return jnp.concatenate(parts, axis=1)[:, :part].astype(low)


def fold_get(scratch, at, fold, part):
    rows = pl.ds(at, scratch.shape[1] // fold, stride=fold)
    parts = [scratch.at[block][rows, :] for block in range(scratch.shape[0])]
    return jnp.concatenate(parts, axis=1)[:, :part].astype(low)


def fold_put(scratch, at, fold, value):
    rows = pl.ds(at, scratch.shape[1] // fold, stride=fold)
    missing = scratch.shape[0] * 128 - value.shape[1]
    if missing:
        value = jnp.concatenate([value, jnp.zeros((value.shape[0], missing), full)], axis=1)
    for block in range(scratch.shape[0]):
        scratch.at[block][rows, :] = value[:, block * 128 : (block + 1) * 128]


def as_row(column):
    return jnp.transpose(jnp.broadcast_to(column, (column.shape[0], 128)))[0:1]


def turn(values, rope, direction):
    half_dim = HEAD_SIZE // 2
    swapped = jnp.concatenate([values[:, half_dim:], values[:, :half_dim]], axis=1)
    sine = rope[:, 2 * HEAD_SIZE : 3 * HEAD_SIZE]
    return values * rope[:, :HEAD_SIZE] + swapped * (direction * sine)


def rope_of(cos_ref, sin_ref, times, part, quarter):
    _, places, _, lanes = cos_ref.shape
    value = cos_ref[part] * times[0, quarter] - sin_ref[part] * times[1, quarter]
    return value.reshape(places * TILE, lanes)


def rope_own_of(cos_ref, sin_ref, times):
    _, quarters, rows, lanes = times.shape
    parts = [
        cos_ref[part, 0] * times[0] - sin_ref[part, 0] * times[1] for part in range(2)
    ]
    return jnp.concatenate([part.reshape(quarters * rows, lanes) for part in parts], axis=0)


def unit_rows(values):
    inverse = lax.rsqrt(jnp.mean(values * values, axis=-1, keepdims=True) + epsilon)
    return values * inverse, inverse


def norm_back(unit, inverse, gain, grad):
    scaled = grad * gain
    return inverse * (scaled - unit * jnp.mean(scaled * unit, axis=-1, keepdims=True))


def query_range(own, part, rows, axis):
    shape = (rows, 1) if axis == 0 else (1, rows)
    half = rows // GROUP
    last_key = own[part] * half + lax.rem(iota(shape, axis), half)
    first_key = jnp.zeros(shape, jnp.int32) + own[2 + part] * half
    return first_key.astype(full), last_key.astype(full)


def gains_block(gains):
    high = gains.astype(low).astype(full)
    return jnp.concatenate([high, gains - high], axis=0).astype(low)


def gains_of(block):
    block = block.astype(full)
    return block[:8] + block[8:]


class Call:
    def __init__(self, steps):
        self.steps = steps

    def spec(self, kind, shape):
        if kind == "smem":
            return pl.BlockSpec(memory_space=pltpu.SMEM)
        if kind == "token":
            return pl.BlockSpec(memory_space=pl.ANY)
        if self.steps == 1 or kind == "whole":
            return pl.BlockSpec(memory_space=pltpu.VMEM)
        rest = tuple(shape[1:])
        return pl.BlockSpec((shape[0] // self.steps,) + rest, lambda i: (i,) + (0,) * len(rest))

    def __call__(self, kernel, name, ins, outs, scratch, micros, after=(), vmem=16):
        steps = self.steps
        first, last, end = len(ins), len(ins) + len(after), len(ins) + len(after) + len(outs)

        def run(*refs):
            refs[end][...] = jnp.zeros_like(refs[end])
            used = refs[:first] + refs[last:end] + refs[end + 1 :]
            kernel(pl.program_id(0) if steps > 1 else 0, steps, *used)

        ins = list(ins) + [("token", token) for token in after]
        outs = list(outs) + [("whole", shape_of((8, 128), full))]
        return pl.pallas_call(
            run,
            grid=(steps,) if steps > 1 else (),
            in_specs=[self.spec(kind, a.shape) for kind, a in ins],
            out_specs=[self.spec(kind, s.shape) for kind, s in outs],
            out_shape=[s for _, s in outs],
            scratch_shapes=scratch,
            compiler_params=pltpu.CompilerParams(vmem_limit_bytes=vmem * 1024 * 1024),
            cost_estimate=pl.CostEstimate(
                flops=int(micros * steps * 1e9), bytes_accessed=1024, transcendentals=0
            ),
            name=name,
        )(*[a for _, a in ins])


one_call = Call(1)


def once(step, steps, at, action):
    if steps == 1:
        action()
    else:
        pl.when(step == at)(action)


def shape_of(shape, dtype):
    return jax.ShapeDtypeStruct(shape, dtype)


def join_kernel(step, steps, held_ref, come_ref, *outs):
    rows = held_ref.shape[0]
    lane = 0
    for out_ref in outs:
        lanes = slice(lane, lane + out_ref.shape[1])
        out_ref[:rows, :] = held_ref[:, lanes]
        out_ref[rows:, :] = come_ref[:, lanes]
        lane = lanes.stop


def join(held, come, name, after, parts=()):
    rows, columns = held.shape
    if rows * columns > 2 << 20:
        return jnp.concatenate([held, come], axis=0), None
    return one_call(
        join_kernel,
        "join_" + name,
        [("whole", held), ("whole", come)],
        [("whole", shape_of((2 * rows, part), held.dtype)) for part in parts or (columns,)],
        [],
        1,
        after,
    )


def pack_kernel(step, steps, hidden_ref, gain_ref, *refs):
    packed_ref, normed_ref = refs[-2:]
    width = hidden_ref.shape[1]
    unit, _ = unit_rows(hidden_ref[...].astype(full))
    normed_ref[...] = (unit * gain_ref[...]).astype(low)
    for a in range(hidden_ref.shape[0] // TILE):
        packed_ref[:, a * width : (a + 1) * width] = normed_ref[a * TILE : (a + 1) * TILE, :]
    if len(refs) > 2:
        packed_ref[:, (a + 1) * width :] = refs[0][...]


def fold_into(out_ref, at, refs):
    columns = sum(ref.shape[1] for ref in refs)
    lane = at
    for ref in refs:
        out_ref[:, lane : lane + ref.shape[1]] = ref[:TILE, :]
        lane += ref.shape[1]
    tails = [ref[TILE:, :].astype(full) for ref in refs]
    tail = tails[0] if len(tails) == 1 else jnp.concatenate(tails, axis=1)
    fold = TILE // tail.shape[0]
    part = columns // fold
    rows = [
        tail[j : j + 1, block * part : (block + 1) * part]
        for j in range(tail.shape[0])
        for block in range(fold)
    ]
    out_ref[:, lane : lane + part] = jnp.concatenate(rows, axis=0).astype(low)
    return lane + part


def fold_qkv_kernel(step, steps, query_ref, key_ref, value_ref, out_ref):
    end = fold_into(out_ref, 0, [query_ref, key_ref, value_ref])
    out_ref[:, end:] = jnp.zeros((TILE, out_ref.shape[1] - end), low)


def fold_late_kernel(step, steps, gate_ref, up_ref, down_ref, output_ref, out_ref):
    lane = fold_into(out_ref, 0, [gate_ref, up_ref])
    rows, width = down_ref.shape
    for a in range(rows // TILE):
        out_ref[:, lane : lane + width] = down_ref[a * TILE : (a + 1) * TILE, :]
        lane += width
    lane = fold_into(out_ref, lane, [output_ref])
    out_ref[:, lane:] = jnp.zeros((TILE, out_ref.shape[1] - lane), low)


def weights_kernel(step, steps, feature_ref, own_ref, come_ref, weight_ref, key_value_ref, mixed, folds):
    width, columns = weight_ref.shape
    half = own_ref.shape[0]
    main = 2 * half
    fold = main // (width - main)
    part = columns // fold
    mixed[:half, :] = own_ref[:, :columns]
    mixed[half:main, :] = come_ref[:, :columns]
    folded = slice(columns, columns + part)
    extra = jnp.concatenate([own_ref[:, folded], come_ref[:, folded]], axis=0)
    fold_write(folds, extra)
    for at in range(fold):
        mixed[main:, at * part : (at + 1) * part] = fold_get(folds, at, fold, part)
    natural = dot(mixing_of(feature_ref), mixed[...])
    weight_ref[...] = natural.astype(low)
    keys = natural[:, width : width + KV_WIDTH]
    key_value_ref[:, :KV_WIDTH] = keys.astype(low)
    half_dim = HEAD_SIZE // 2
    swapped = [
        keys[:, (block ^ 1) * half_dim : ((block ^ 1) + 1) * half_dim]
        for block in range(KV_WIDTH // half_dim)
    ]
    key_value_ref[:, KV_WIDTH : 2 * KV_WIDTH] = jnp.concatenate(swapped, axis=1).astype(low)
    key_value_ref[:, 2 * KV_WIDTH :] = natural[:, width + KV_WIDTH :].astype(low)


def queries_kernel(step, steps, normed_ref, weight_ref, cos_ref, sin_ref, times, query_ref):
    tokens, width = normed_ref.shape
    half = tokens // 2
    queries = dot(normed_ref[...], weight_ref[:, :width])
    rope = rope_own_of(cos_ref, sin_ref, times)
    for head in range(HEADS):
        turned = turn(queries[:, head * HEAD_SIZE : (head + 1) * HEAD_SIZE], rope, 1.0)
        turned = turned.astype(low) * low(HEAD_SIZE**-0.5)
        for part in range(2):
            row = (part * GROUP + head % GROUP) * half
            query_ref[head // GROUP, row : row + half, :] = turned[part * half : (part + 1) * half]


def project_kernel(step, steps, normed_ref, weight_ref, cos_ref, sin_ref, times, kv_ref):
    width = weight_ref.shape[0]
    groups = normed_ref.shape[1] // width
    for a in range(groups):
        kv = dot(normed_ref[:, a * width : (a + 1) * width], weight_ref[...])
        rope = rope_of(cos_ref, sin_ref, times, a // (groups // 2), a % (groups // 2))
        cos, sin = rope[:, : 2 * HEAD_SIZE], rope[:, 2 * HEAD_SIZE :]
        cos = jnp.concatenate([cos, cos[:, :HEAD_SIZE]], axis=1)
        sin = jnp.concatenate([sin, sin[:, :HEAD_SIZE]], axis=1)
        keys = kv[:, :KV_WIDTH] * cos + kv[:, KV_WIDTH : 2 * KV_WIDTH] * sin
        at = a * 2 * KV_WIDTH
        kv_ref[:, at : at + KV_WIDTH] = keys.astype(low)
        kv_ref[:, at + KV_WIDTH : at + 2 * KV_WIDTH] = kv[:, 2 * KV_WIDTH :].astype(low)


def key_part(kv_ref, groups, column):
    lanes = [a * 2 * KV_WIDTH + column * HEAD_SIZE for a in groups]
    return jnp.concatenate([kv_ref[:, at : at + HEAD_SIZE] for at in lanes], axis=0)


def key_row(key_ref, part, groups):
    start = key_ref[part]
    return jnp.concatenate([start + float(i * TILE) for i in range(len(groups))], axis=1)


def reaches_low(own, blocks):
    return own[3] < blocks


def forward_kernel(
    is_first, low_blocks, step, steps, own, key_ref, query_ref, kv_ref, *rest
):
    state = rest[-1]
    rows = query_ref.shape[1] // 2
    groups = kv_ref.shape[1] // (2 * KV_WIDTH)

    def first():
        if is_first:
            lane = lax.broadcasted_iota(jnp.int32, state.shape, 2)
            state[...] = jnp.where(lane == PEAK, masked_score, 0.0)
        else:
            state[...] = rest[0][...]

    once(step, steps, 0, first)

    def attend(key_half, query_half):
        members = range(key_half * groups // 2, (key_half + 1) * groups // 2)
        at = slice(query_half * rows, (query_half + 1) * rows)
        key_index = key_row(key_ref, key_half, members)
        first_key, last_key = query_range(own, query_half, rows, 0)
        allowed = (key_index >= first_key) & (key_index <= last_key)
        for head in range(KV_HEADS):
            scores = dot_right(query_ref[head, at], key_part(kv_ref, members, head))
            masked = jnp.where(allowed, scores, masked_score)
            old = state[head, at, PEAK : PEAK + 1]
            new = jnp.maximum(old, jnp.max(masked, axis=1, keepdims=True))
            weights = jnp.where(allowed, jnp.exp(masked - new), 0.0)
            factor = jnp.exp(old - new)
            state[head, at, PEAK : PEAK + 1] = new
            state[head, at, TOTAL : TOTAL + 1] = state[
                head, at, TOTAL : TOTAL + 1
            ] * factor + jnp.sum(weights, axis=1, keepdims=True)
            state[head, at, :HEAD_SIZE] = state[head, at, :HEAD_SIZE] * factor + dot(
                weights.astype(low), key_part(kv_ref, members, KV_HEADS + head)
            )

    attend(0, 0)
    pl.when(reaches_low(own, low_blocks))(lambda: attend(0, 1))
    attend(1, 1)


def feedforward_kernel(
    step,
    steps,
    source_ref,
    feature_ref,
    state_ref,
    hidden_ref,
    gain_ref,
    grad_ref,
    own_ref,
    come_ref,
    out_ref,
    grad_middle_ref,
    head_grad_ref,
    delta_ref,
    lse_ref,
    keep_ref,
    send_ref,
    gain_part_ref,
    attention,
    attended,
    output_w,
    normed,
    normed_t,
    down_w,
    down_grad,
    total,
    grad_normed,
    extra_grad,
    output_folds,
    late_folds,
):
    rows, width = hidden_ref.shape
    half = own_ref.shape[0]
    main = 2 * half
    rest = width - main
    fold = main // rest
    places = main // TILE
    ff = down_w.shape[0]
    chunk = 2 * ff // fold
    down_at = 2 * ff + chunk
    device_ff = ff // places
    groups = device_ff // TILE
    out_at = down_at + groups * width
    mixing = mixing_of(feature_ref)

    tokens = rows // 2
    for head in range(KV_HEADS):
        sums = state_ref[head, :, TOTAL : TOTAL + 1]
        attention[head] = state_ref[head, :, :HEAD_SIZE] / sums
        logs = state_ref[head, :, PEAK : PEAK + 1] + jnp.log(sums)
        for part in range(2):
            lse_ref[2 * head + part] = as_row(
                logs[part * GROUP * tokens : (part + 1) * GROUP * tokens]
            )
    for h in range(HEADS):
        for part in range(2):
            row = (part * GROUP + h % GROUP) * tokens
            attended[
                part * tokens : (part + 1) * tokens, h * HEAD_SIZE : (h + 1) * HEAD_SIZE
            ] = attention[h // GROUP, row : row + tokens, :].astype(low)
    attended[...] = dot(attended[...], mixing).astype(low)
    output_w[:half, :] = own_ref[:, out_at : out_at + width]
    output_w[half:main, :] = come_ref[:, out_at : out_at + width]
    part = width // fold
    folded = slice(out_at + width, out_at + width + part)
    extra = jnp.concatenate([own_ref[:, folded], come_ref[:, folded]], axis=0)
    fold_write(output_folds, extra)
    for at in range(fold):
        output_w[main:, at * part : (at + 1) * part] = fold_get(output_folds, at, fold, part)
    middle = hidden_ref[...].astype(full) + dot(attended[...], output_w[...])
    gain = gain_ref[...]
    unit, inverse = unit_rows(middle)
    mixed_norm = dot((unit * gain).astype(low), mixing)
    normed[...] = mixed_norm.astype(low)
    normed_t[...] = jnp.transpose(mixed_norm).astype(low)
    for place in range(places):
        held = own_ref if place < places // 2 else come_ref
        row = (place % (places // 2)) * TILE
        for a in range(groups):
            at = pl.multiple_of(source_ref[place] * device_ff + a * TILE, TILE)
            lane = down_at + a * width
            down_w[pl.ds(at, TILE), :] = held[row : row + TILE, lane : lane + width]
    total[...] = jnp.zeros_like(total)
    grad_normed[...] = jnp.zeros_like(grad_normed)
    out_grad = grad_ref[...]
    fold_write(
        late_folds,
        jnp.concatenate([own_ref[:, 2 * ff : down_at], come_ref[:, 2 * ff : down_at]], axis=0),
    )

    def advance(c, carry):
        gate_at = pl.ds(pl.multiple_of(c * chunk, 128), chunk)
        up_at = pl.ds(pl.multiple_of(ff + c * chunk, 128), chunk)

        def columns(lanes, at):
            tail = fold_get(late_folds, at, fold, chunk)
            value = (
                dot(normed[:, :half], own_ref[:, lanes])
                + dot(normed[:, half:main], come_ref[:, lanes])
                + dot(normed[:, main:], tail)
            )
            return value, tail

        gate, gate_tail = columns(gate_at, c)
        up, up_tail = columns(up_at, c + fold // 2)
        down_at_c = pl.ds(pl.multiple_of(c * chunk, 128), chunk)
        down = down_w[down_at_c, :]
        sigma = 1.0 / (1.0 + jnp.exp(-gate))
        silu = gate * sigma
        inner = (silu * up).astype(low)
        total[...] += dot(inner, down)
        grad_inner = dot_right(out_grad, down)
        grad_gate = (grad_inner * up * sigma * (1.0 + gate * (1.0 - sigma))).astype(low)
        grad_up = (grad_inner * silu).astype(low)
        down_grad[down_at_c, :] = dot_left(inner, out_grad).astype(low)
        for grad, lanes, tail, at in (
            (grad_gate, gate_at, gate_tail, c),
            (grad_up, up_at, up_tail, c + fold // 2),
        ):
            grad_normed[:, :half] += dot_right(grad, own_ref[:, lanes])
            grad_normed[:, half:main] += dot_right(grad, come_ref[:, lanes])
            grad_normed[:, main:] += dot_right(grad, tail)
            keep_ref[:, lanes] = dot(normed_t[:half], grad).astype(low)
            send_ref[:, lanes] = dot(normed_t[half:main], grad).astype(low)
            fold_put(extra_grad, at, fold, dot(normed_t[main:], grad))
        return carry

    lax.fori_loop(0, ff // chunk, advance, 0)
    out_ref[...] = (middle + total[...]).astype(low)
    extra = fold_read(extra_grad, chunk)
    keep_ref[:, 2 * ff : down_at] = extra[:half]
    send_ref[:, 2 * ff : down_at] = extra[half:]
    for place in range(places):
        held = keep_ref if place < places // 2 else send_ref
        row = (place % (places // 2)) * TILE
        for a in range(groups):
            at = pl.multiple_of(source_ref[place] * device_ff + a * TILE, TILE)
            lane = down_at + a * width
            held[row : row + TILE, lane : lane + width] = down_grad[pl.ds(at, TILE), :]

    high = grad_normed[...].astype(low)
    tail = (grad_normed[...] - high.astype(full)).astype(low)
    back = dot_right(high, mixing) + dot_right(tail, mixing)
    gain_part_ref[...] = jnp.sum(back * unit, axis=0, keepdims=True)
    grad_middle = out_grad.astype(full) + norm_back(unit, inverse, gain, back)
    grad_middle_ref[...] = grad_middle
    grad_branch = grad_middle.astype(low)
    output_grad = dot_left(attended[...], grad_branch)
    keep_ref[:, out_at : out_at + width] = output_grad[:half].astype(low)
    send_ref[:, out_at : out_at + width] = output_grad[half:main].astype(low)
    for at in range(fold):
        fold_put(output_folds, at, fold, output_grad[main:, at * part : (at + 1) * part])
    extra = fold_read(output_folds, part)
    unused = jnp.zeros((half, keep_ref.shape[1] - folded.stop), low)
    for held, rows_of_half in ((keep_ref, extra[:half]), (send_ref, extra[half:])):
        held[:, folded] = rows_of_half
        held[:, folded.stop :] = unused
    grad_low = dot_right(grad_branch, output_w[...]).astype(low)
    grad_low = dot_right(grad_low, mixing).astype(low)
    for head in range(KV_HEADS):
        for part in range(2):
            grads = jnp.concatenate(
                [
                    grad_low[
                        part * tokens : (part + 1) * tokens, h * HEAD_SIZE : (h + 1) * HEAD_SIZE
                    ]
                    for h in range(head * GROUP, (head + 1) * GROUP)
                ],
                axis=0,
            )
            at = slice(part * GROUP * tokens, (part + 1) * GROUP * tokens)
            head_grad_ref[head, at] = grads
            delta_ref[2 * head + part] = as_row(
                jnp.sum(grads.astype(full) * attention[head, at], axis=1, keepdims=True)
            )


def backward_kernel(
    is_first,
    key_half,
    low_blocks,
    step,
    steps,
    own,
    key_ref,
    query_ref,
    grad_ref,
    lse_ref,
    delta_ref,
    kv_ref,
    tokens_ref,
    cos_ref,
    sin_ref,
    times,
    *rest,
):
    if not is_first:
        held, rest = rest[:2], rest[2:]
    grad_query, grad_weight, out_ref, grad_kv = rest
    rows = query_ref.shape[1] // 2
    groups = kv_ref.shape[1] // (2 * KV_WIDTH)
    key_rows = kv_ref.shape[0]
    width = tokens_ref.shape[1] // groups
    members = range(key_half * groups // 2, (key_half + 1) * groups // 2)

    def first():
        if is_first:
            grad_query[...] = jnp.zeros_like(grad_query)
            grad_weight[...] = jnp.zeros_like(grad_weight)
        else:
            grad_query[...] = held[0][...]
            grad_weight[...] = held[1][...]

    once(step, steps, 0, first)
    key_index = key_row(key_ref, key_half, members)
    key_index = jnp.transpose(jnp.broadcast_to(key_index, (128, key_index.shape[1])))[:, 0:1]

    def attend(query_half, add):
        at = slice(query_half * rows, (query_half + 1) * rows)
        first_key, last_key = query_range(own, query_half, rows, 1)
        allowed = (key_index >= first_key) & (key_index <= last_key)
        for head in range(KV_HEADS):
            keys = key_part(kv_ref, members, head)
            scores = dot_right(keys, query_ref[head, at])
            probs = jnp.where(allowed, jnp.exp(scores - lse_ref[2 * head + query_half]), 0.0)
            d_probs = dot_right(key_part(kv_ref, members, KV_HEADS + head), grad_ref[head, at])
            d_scores = (probs * (d_probs - delta_ref[2 * head + query_half])).astype(low)
            grad_query[2 * head + query_half] += dot_left(keys, d_scores)
            parts = (
                (head, dot(d_scores, query_ref[head, at])),
                (KV_HEADS + head, dot(probs.astype(low), grad_ref[head, at])),
            )
            for column, value in parts:
                lanes = slice(column * HEAD_SIZE, (column + 1) * HEAD_SIZE)
                if add:
                    grad_kv[:, lanes] += value
                else:
                    grad_kv[:, lanes] = value

    if key_half == 0:
        attend(0, False)
        pl.when(reaches_low(own, low_blocks))(lambda: attend(1, True))
    else:
        attend(1, False)
    for i, a in enumerate(members):
        at = slice(i * key_rows, (i + 1) * key_rows)
        rope = rope_of(cos_ref, sin_ref, times, key_half, i)
        turned = jnp.concatenate(
            [
                turn(grad_kv[at, head * HEAD_SIZE : (head + 1) * HEAD_SIZE], rope, -1.0)
                for head in range(KV_HEADS)
            ]
            + [grad_kv[at, KV_WIDTH:]],
            axis=1,
        ).astype(low)
        out_ref[:, i * 2 * KV_WIDTH : (i + 1) * 2 * KV_WIDTH] = turned
        grad_weight[...] += dot_left(turned, tokens_ref[:, a * width : (a + 1) * width])


def qkv_grad_kernel(
    with_gains,
    step,
    steps,
    feature_ref,
    grad_query,
    grad_weight,
    normed_ref,
    weight_ref,
    cos_ref,
    sin_ref,
    times,
    gain_ref,
    gain_two_ref,
    query_grad_ref,
    gains_ref,
    keep_ref,
    send_ref,
    natural,
    folds,
):
    tokens, width = normed_ref.shape
    half = tokens // 2
    rope = rope_own_of(cos_ref, sin_ref, times)
    for head in range(KV_HEADS):
        rotated = [
            jnp.transpose(grad_query[2 * head + part]) * HEAD_SIZE**-0.5 for part in range(2)
        ]
        for g in range(GROUP):
            h = head * GROUP + g
            value = jnp.concatenate([part[g * half : (g + 1) * half] for part in rotated], axis=0)
            query_grad_ref[:, h * HEAD_SIZE : (h + 1) * HEAD_SIZE] = turn(value, rope, -1.0).astype(
                low
            )
    natural[:, :width] = dot_left(normed_ref[...], query_grad_ref[...])
    natural[:, width:] = jnp.transpose(grad_weight[...])
    products = natural[...] * weight_ref[...].astype(full)
    gain_part = as_row(jnp.sum(products, axis=1, keepdims=True)) / gain_ref[...]
    row = iota((8, width), 0)
    gains = jnp.where(row == 0, gain_part, jnp.where(row == 1, gain_two_ref[...], 0.0))
    gains_ref[...] = gains
    mixed = dot_left(mixing_of(feature_ref), natural[...].astype(low)).astype(low)
    columns = mixed.shape[1]
    rows = keep_ref.shape[0]
    main = 2 * rows
    fold = main // (width - main)
    part = columns // fold
    for at in range(fold):
        fold_put(folds, at, fold, mixed[main:, at * part : (at + 1) * part].astype(full))
    extra = fold_read(folds, part)
    unused = jnp.zeros((rows, keep_ref.shape[1] - columns - part), low)
    for held, at in ((keep_ref, 0), (send_ref, rows)):
        held[:rows, :columns] = mixed[at : at + rows]
        held[:rows, columns : columns + part] = extra[at : at + rows]
        held[:rows, columns + part :] = unused
    if with_gains:
        send_ref[rows:, :width] = gains_block(gains)
        send_ref[rows:, width:] = jnp.zeros((TILE, send_ref.shape[1] - width), low)


def merge_kernel(step, steps, *refs):
    kv_keep, kv_come, w_keep, w_come, gains_ref, keep_out, send_out, gains_out = (
        refs[0:2],
        refs[2:4],
    ) + refs[4:]
    rows = w_keep.shape[0]
    half = rows // 2
    width = gains_ref.shape[1]
    gains = gains_of(gains_block(gains_ref[...])) + gains_of(w_come[rows:, :width])
    gains_out[...] = gains
    lane = 0
    for keep, come in tuple(zip(kv_keep, kv_come)) + ((w_keep, w_come),):
        columns = keep.shape[1]
        lanes = slice(lane, lane + columns)
        for out, at in ((keep_out, 0), (send_out, half)):
            value = keep[at : at + half, :].astype(full) + come[at : at + half, :].astype(full)
            out[:half, lanes] = value.astype(low)
        lane += columns
    send_out[half:, :width] = gains_block(gains)
    send_out[half:, width:] = jnp.zeros((TILE, send_out.shape[1] - width), low)


def add_kernel(with_gains, step, steps, keep_ref, come_ref, *rest):
    rows = keep_ref.shape[0]
    if with_gains:
        gains_ref, rest = rest[0], rest[1:]
        rest, gains_out = rest[:-1], rest[-1]
        width = gains_ref.shape[1]
        gains = gains_of(gains_block(gains_ref[...])) + gains_of(come_ref[rows:, :width])
        gains_out[...] = gains

    def tile(at):
        at = pl.ds(at, TILE)
        return keep_ref[at, :].astype(full) + come_ref[at, :].astype(full)

    if rows == TILE:
        rest[0][...] = tile(0)
        return
    keep_out, send_out = rest
    half = rows // 2

    def advance(i, carry):
        at = pl.multiple_of(i * TILE, TILE)
        keep_out[pl.ds(at, TILE), :] = tile(at).astype(low)
        send_out[pl.ds(at, TILE), :] = tile(pl.multiple_of(half + at, TILE)).astype(low)
        return carry

    lax.fori_loop(0, half // TILE, advance, 0)
    if with_gains:
        send_out[half:, :width] = gains_block(gains)
        send_out[half:, width:] = jnp.zeros((TILE, send_out.shape[1] - width), low)


def scatter_halves(keep, leaving, steps, name, gains=None, after=()):
    with_gains = gains is not None
    more = TILE if with_gains else 0
    for at, partner in enumerate(reversed(steps)):
        come = send(leaving, partner)
        rows, columns = keep.shape
        ins = [("whole", keep), ("whole", come)]
        if rows == TILE:
            outs = [("whole", shape_of((rows, columns), full))]
        else:
            outs = [
                ("whole", shape_of((rows // 2, columns), low)),
                ("whole", shape_of((rows // 2 + more, columns), low)),
            ]
        if with_gains:
            ins.append(("whole", gains))
            outs.append(("whole", shape_of(gains.shape, full)))
        result = Call(1)(
            functools.partial(add_kernel, with_gains),
            name,
            ins,
            outs,
            [],
            1,
            after[at] if at < len(after) else (),
        )
        if with_gains:
            gains = result[-2]
        if rows == TILE:
            return result[0], gains
        keep, leaving = result[0], result[1]


def final_kernel(
    step,
    steps,
    sum_ref,
    query_grad_ref,
    weight_ref,
    hidden_ref,
    gain_ref,
    grad_middle_ref,
    out_ref,
    grads,
):
    tokens, width = hidden_ref.shape
    grads[:, :width] = query_grad_ref[...]
    for a in range(tokens // TILE):
        rows = slice(a * TILE, (a + 1) * TILE)
        lanes = slice(a * 2 * KV_WIDTH, (a + 1) * 2 * KV_WIDTH)
        grads[rows, width:] = sum_ref[:, lanes].astype(low)
    back = dot_right(grads[...], weight_ref[...])
    unit, inverse = unit_rows(hidden_ref[...].astype(full))
    out_ref[...] = (grad_middle_ref[...] + norm_back(unit, inverse, gain_ref[...], back)).astype(low)


def body(
    hidden_in,
    attention_gain,
    query_weight,
    key_weight,
    value_weight,
    output_weight,
    feedforward_gain,
    gate_weight,
    up_weight,
    down_weight,
    doc_of_block,
    pair_table,
    out_grad,
):
    tokens, width = hidden_in.shape
    half_rows = tokens // 2
    count = lax.axis_size("ctx")
    device = lax.axis_index("ctx")
    ff = gate_weight.shape[1] * count // width
    low_bits = low_bits_of(query_weight.shape[1], width)
    merged = low_bits == 0
    row_steps = exchange_steps(count, low_bits)
    token_steps = exchange_steps(count, 0)
    group_count = count >> low_bits
    group_rows = width // group_count
    groups = tokens // TILE
    steps = max(1, TILE * count // 512)
    places = count // (2 * steps)
    gain_one = attention_gain.reshape(1, width)
    gain_two = feedforward_gain.reshape(1, width)
    columns = width + 2 * KV_WIDTH
    main = TILE * group_count
    fold = main // (width - main)
    w_lanes = whole_lanes(columns + columns // fold)
    ff_folded = 2 * ff // fold
    down_at = 2 * ff + ff_folded
    device_groups = ff // group_count // TILE
    out_at = down_at + device_groups * width
    late_lanes = whole_lanes(out_at + width + width // fold)
    call = Call(steps)
    one = Call(1)

    def rows_of(piece, piece_columns):
        return ("whole", whole_rows(piece, device, low_bits, piece_columns))

    qkv_piece, _ = one(
        fold_qkv_kernel,
        "fold_qkv",
        [
            rows_of(query_weight, width),
            rows_of(key_weight, KV_WIDTH),
            rows_of(value_weight, KV_WIDTH),
        ],
        [("whole", shape_of((TILE, w_lanes), low))],
        [],
        1,
    )
    token_parts = (groups * width, w_lanes) if merged else (groups * width,)
    packed, normed, _ = one(
        pack_kernel,
        "norm_and_pack",
        [("whole", hidden_in), ("whole", gain_one)] + ([("whole", qkv_piece)] if merged else []),
        [
            ("whole", shape_of((TILE, sum(token_parts)), low)),
            ("whole", shape_of((tokens, width), low)),
        ],
        [],
        1,
    )

    late_at = 2
    late_mark = None
    for at, partner in enumerate(token_steps[:-1]):
        if at == late_at:
            late, _ = one(
                fold_late_kernel,
                "fold_late",
                [
                    rows_of(gate_weight, ff),
                    rows_of(up_weight, ff),
                    rows_of(down_weight, width),
                    rows_of(output_weight, width),
                ],
                [("whole", shape_of((TILE, late_lanes), low))],
                [],
                1,
                [mark],
            )
        if late_at <= at < late_at + 2:
            late, late_mark = join(late, send(late, row_steps[at - late_at]), "late", [])
        last = at == len(token_steps) - 2
        *held, mark = join(
            packed,
            send(packed, partner),
            "tokens",
            [late_mark] if late_mark is not None else [],
            token_parts if last else (),
        )
        packed = held[0]
    token_own = packed
    if merged:
        w_own, w_come = held[1], send(held[1], token_steps[-1])
    else:
        w_own, w_come = gather_halves(qkv_piece, row_steps, "qkv")
    token_come = send(token_own, token_steps[-1])

    def table_row(table):
        return lax.dynamic_index_in_dim(jnp.asarray(table), device, 0, keepdims=False)

    sources = table_row(source_table(count, 0))
    group_table = source_table(count, low_bits)
    group_sources = table_row(group_table)
    inside = np.arange(group_rows)[None, None, :]
    features = group_table[:, :, None] * group_rows + inside
    features = np.concatenate(
        [
            features[:, :, :TILE].reshape(count, -1),
            features[:, :, TILE:].reshape(count, -1),
        ],
        axis=1,
    ).astype(np.int32)
    feature_row = table_row(features).reshape(1, width)

    device_iota = jnp.arange(count, dtype=jnp.int32)
    pairs = jnp.sum(
        jnp.where(sources[:, None] == device_iota[None, :], pair_table[None, :], 0), axis=1
    )
    blocks = jnp.stack([pairs, 2 * count - 1 - pairs], axis=1).reshape(-1)
    block_iota = jnp.arange(2 * count, dtype=jnp.int32)
    block_docs = jnp.sum(
        jnp.where(blocks[:, None] == block_iota[None, :], doc_of_block[None, :], 0), axis=1
    )
    doc_start = jnp.min(
        jnp.where(block_docs[:, None] == doc_of_block[None, :], block_iota[None, :], 2 * count),
        axis=1,
    )
    own = jnp.concatenate([blocks[:2], doc_start[:2]])

    def by_step(values):
        return values.reshape(2, steps, places, 2).transpose(0, 1, 3, 2)

    inner = jnp.arange(TILE, dtype=jnp.int32)
    key_index = by_step(blocks)[..., None] * half_rows + inner
    key_index = key_index.astype(full).reshape(2, 2 * steps, 1, -1)
    frequency = rope_base ** (-jnp.arange(HEAD_SIZE // 2, dtype=full) * (2.0 / HEAD_SIZE))
    block_angle = (by_step(blocks - doc_start) * half_rows).astype(full)[..., None] * frequency
    offset = jnp.arange(half_rows, dtype=full).reshape(groups // 2, TILE)
    offset_angle = offset[..., None] * frequency
    cos_in, sin_in = jnp.cos(offset_angle), jnp.sin(offset_angle)
    times_cos = jnp.concatenate([cos_in] * 4 + [-sin_in, sin_in] * 2, axis=-1)
    times_sin = jnp.concatenate([sin_in] * 4 + [cos_in, -cos_in] * 2, axis=-1)
    times = jnp.stack([times_cos, times_sin])
    block_cos = jnp.tile(jnp.cos(block_angle), 8).reshape(2, 2 * steps, places, 1, 4 * HEAD_SIZE)
    block_sin = jnp.tile(jnp.sin(block_angle), 8).reshape(2, 2 * steps, places, 1, 4 * HEAD_SIZE)
    rope_own = [
        ("whole", block_cos[0, :2, :1]),
        ("whole", block_sin[0, :2, :1]),
        ("whole", times),
    ]
    halves = [
        (
            held,
            key_index[place],
            [("rows", block_cos[place]), ("rows", block_sin[place]), ("whole", times)],
        )
        for place, held in enumerate((token_own, token_come))
    ]

    rows = GROUP * tokens
    half = TILE * count // 2
    kv_shape = shape_of((half, groups * 2 * KV_WIDTH), low)
    head_shape = (KV_HEADS, rows, HEAD_SIZE)
    weight, kv_weight, _ = one(
        weights_kernel,
        "qkv_weights",
        [("whole", feature_row), ("whole", w_own), ("whole", w_come)],
        [
            ("whole", shape_of((width, columns), low)),
            ("whole", shape_of((width, 3 * KV_WIDTH), low)),
        ],
        [pltpu.VMEM((width, columns), low), fold_scratch(main, columns // fold)],
        3,
    )
    queries, _ = one(
        queries_kernel,
        "queries",
        [("whole", normed), ("whole", weight)] + rope_own,
        [("whole", shape_of(head_shape, low))],
        [],
        2,
    )

    def project(place, after):
        token_rows, _, turns = halves[place]
        return call(
            project_kernel,
            "project",
            [("rows", token_rows), ("whole", kv_weight)] + turns,
            [("rows", kv_shape)],
            [],
            5,
            after,
        )

    state_shapes = [("whole", shape_of((KV_HEADS, rows, 2 * HEAD_SIZE), full))]

    def attend(place, kv, state, after):
        return call(
            functools.partial(forward_kernel, not state, count),
            "attention_forward",
            [
                ("smem", own),
                ("rows", halves[place][1]),
                ("whole", queries),
                ("rows", kv),
            ]
            + [("whole", held) for held in state],
            state_shapes,
            [],
            6,
            after,
        )

    kv_own, mark = project(0, [])

    for at in range(2, len(row_steps) - 1):
        come = send(late, row_steps[at])
        before = [mark] if at == len(row_steps) - 3 else []
        if at == len(row_steps) - 2:
            *state, mark = attend(0, kv_own, [], [late_mark])
            kv_come, mark = project(1, [mark])
            *state, mark = attend(1, kv_come, state, [])
            before = [mark]
        late, late_mark = join(late, come, "late", before)
    late_own, late_come = late, send(late, row_steps[-1])

    late_shape = late_own.shape
    row_shape = shape_of((2 * KV_HEADS, 1, rows // 2), full)
    block_out, grad_middle, head_grads, delta, lse, late_keep, late_send, gain_two_part, _ = one(
        feedforward_kernel,
        "feedforward",
        [
            ("smem", group_sources),
            ("whole", feature_row),
        ]
        + [("whole", held) for held in state]
        + [
            ("whole", hidden_in),
            ("whole", gain_two),
            ("whole", out_grad),
            ("whole", late_own),
            ("whole", late_come),
        ],
        [
            ("whole", shape_of((tokens, width), low)),
            ("whole", shape_of((tokens, width), full)),
            ("whole", shape_of(head_shape, low)),
            ("whole", row_shape),
            ("whole", row_shape),
            ("whole", shape_of(late_shape, low)),
            ("whole", shape_of(late_shape, low)),
            ("whole", shape_of((1, width), full)),
        ],
        [
            pltpu.VMEM(head_shape, full),
            pltpu.VMEM((tokens, width), low),
            pltpu.VMEM((width, width), low),
            pltpu.VMEM((tokens, width), low),
            pltpu.VMEM((width, tokens), low),
            pltpu.VMEM((ff, width), low),
            pltpu.VMEM((ff, width), low),
            pltpu.VMEM((tokens, width), full),
            pltpu.VMEM((tokens, width), full),
            fold_scratch(main, ff_folded),
            fold_scratch(main, width // fold),
            fold_scratch(main, ff_folded),
        ],
        16,
        vmem=28,
    )

    def attend_back(place, key_half, kv, carried, after):
        token_rows, keys, turns = halves[place]
        return call(
            functools.partial(backward_kernel, not carried, key_half, count),
            "attention_backward",
            [
                ("smem", own),
                ("rows", keys),
                ("whole", queries),
                ("whole", head_grads),
                ("whole", lse),
                ("whole", delta),
                ("rows", kv),
                ("rows", token_rows),
            ]
            + turns
            + [("whole", held) for held in carried],
            [
                ("whole", shape_of((2 * KV_HEADS, HEAD_SIZE, rows // 2), full)),
                ("whole", shape_of((2 * KV_WIDTH, width), full)),
                ("rows", shape_of((half, groups * KV_WIDTH), low)),
            ],
            [pltpu.VMEM((groups // 2 * places * TILE, 2 * KV_WIDTH), full)],
            6,
            after,
        )

    late_steps = row_steps[::-1]
    keep, leaving = late_keep, late_send

    def add_late(at, after):
        come = send(leaving, late_steps[at])
        part = shape_of((keep.shape[0] // 2, late_lanes), low)
        outs = [part, part] if keep.shape[0] > TILE else [shape_of((TILE, late_lanes), full)]
        return one(
            functools.partial(add_kernel, False),
            "add_late",
            [("whole", keep), ("whole", come)],
            [("whole", out) for out in outs],
            [],
            1,
            after,
        )

    *carried, send_low, mark = attend_back(1, 0, kv_come, [], [])
    keep, leaving, late_mark = add_late(0, [mark])
    *carried, send_high, mark = attend_back(1, 1, kv_come, carried, [late_mark])
    *carried, keep_low, mark = attend_back(0, 0, kv_own, carried, [])
    *carried, keep_high, mark = attend_back(0, 1, kv_own, carried, [])
    query_grad, gains, w_keep, w_send, mark = one(
        functools.partial(qkv_grad_kernel, merged),
        "qkv_gradients",
        [
            ("whole", feature_row),
            ("whole", carried[0]),
            ("whole", carried[1]),
            ("whole", normed),
            ("whole", weight),
        ]
        + rope_own
        + [
            ("whole", gain_one),
            ("whole", gain_two_part),
        ],
        [
            ("whole", shape_of((tokens, width), low)),
            ("whole", shape_of((8, width), full)),
            ("whole", shape_of((main // 2, w_lanes), low)),
            ("whole", shape_of((main // 2 + (TILE if merged else 0), w_lanes), low)),
        ],
        [pltpu.VMEM((width, columns), full), fold_scratch(main, columns // fold)],
        3,
    )
    late_marks = []
    for at in range(1, len(late_steps)):
        result = add_late(at, [mark] if at == 1 else [])
        keep, leaving = result[0], result[1]
        late_marks.append([result[-1]])
    late_sum = keep

    if merged:
        come = [send(part, token_steps[-1]) for part in (send_low, send_high, w_send)]
        lanes = 2 * send_low.shape[1] + w_lanes
        keep, leaving, gains, _ = one(
            merge_kernel,
            "add_first",
            [
                ("whole", keep_low),
                ("whole", keep_high),
                ("whole", come[0]),
                ("whole", come[1]),
                ("whole", w_keep),
                ("whole", come[2]),
                ("whole", gains),
            ],
            [
                ("whole", shape_of((half // 2, lanes), low)),
                ("whole", shape_of((half // 2 + TILE, lanes), low)),
                ("whole", shape_of(gains.shape, full)),
            ],
            [],
            2,
            late_marks[0],
        )
        kv_sum, gains = scatter_halves(
            keep, leaving, token_steps[:-1], "add_chain", gains, late_marks[1:]
        )
        qkv_sum = kv_sum[:, 2 * send_low.shape[1] :]
    else:
        kv_keep = jnp.concatenate([keep_low, keep_high], axis=1)
        kv_send = jnp.concatenate([send_low, send_high], axis=1)
        kv_sum, _ = scatter_halves(kv_keep, kv_send, token_steps, "add_kv")
        qkv_sum, _ = scatter_halves(w_keep, w_send, row_steps, "add_qkv")
        gains = lax.psum(gains, "ctx")
    input_grad, _ = one(
        final_kernel,
        "input_gradient",
        [
            ("whole", kv_sum),
            ("whole", query_grad),
            ("whole", weight),
            ("whole", hidden_in),
            ("whole", gain_one),
            ("whole", grad_middle),
        ],
        [("whole", shape_of((tokens, width), low))],
        [pltpu.VMEM((tokens, columns), low)],
        1,
    )

    def piece_of(piece_rows):
        return own_piece(piece_rows, device, low_bits)

    qkv_rows = unfold_rows(qkv_sum, columns, columns // fold)
    ff_rows = unfold_rows(late_sum, 2 * ff, ff_folded)
    down_rows = jnp.concatenate(
        [late_sum[:, down_at + a * width : down_at + (a + 1) * width] for a in range(device_groups)],
        axis=0,
    )
    output_rows = unfold_rows(late_sum[:, out_at:], width, width // fold)
    return (
        block_out,
        input_grad,
        gains[0],
        piece_of(qkv_rows[:, :width]),
        piece_of(qkv_rows[:, width : width + KV_WIDTH]),
        piece_of(qkv_rows[:, width + KV_WIDTH :]),
        piece_of(output_rows),
        gains[1],
        piece_of(ff_rows[:, :ff]),
        piece_of(ff_rows[:, ff:]),
        piece_of(down_rows),
    )


def solution(mesh):
    row = P("ctx", None)
    in_specs = (row, P(), row, row, row, row, P(), row, row, row, P(), P(), row)
    out_specs = (row, row, P(), row, row, row, row, P(), row, row, row)
    return jax.shard_map(body, mesh=mesh, in_specs=in_specs, out_specs=out_specs, check_vma=False)
```

```python
import functools

import jax
import jax.numpy as jnp
import numpy as np
from jax import lax
from jax.experimental import pallas as pl
from jax.experimental.pallas import tpu as pltpu
from jax.sharding import PartitionSpec as P

HEADS = 9
KV_HEADS = 3
GROUP = HEADS // KV_HEADS
HEAD_SIZE = 64
KV_WIDTH = KV_HEADS * HEAD_SIZE
TILE = 16
TOTAL, PEAK = HEAD_SIZE, HEAD_SIZE + 1

epsilon = 1e-05
rope_base = 100000.0
masked_score = -1e30

low = jnp.bfloat16
full = jnp.float32


def exchange_steps(device_count, low_bits):
    top = device_count.bit_length() - 1
    steps = []
    if low_bits == 0 and top >= 4:
        for bit in range(top - 1, 2, -1):
            steps.append([i ^ (1 << bit) for i in range(device_count)])
        steps.append([i ^ (4 if i & 1 else 2) for i in range(device_count)])
        steps.append([i ^ (2 if i & 1 else 4) for i in range(device_count)])
        steps.append([i ^ 1 for i in range(device_count)])
    else:
        for bit in range(top - 1, low_bits - 1, -1):
            steps.append([i ^ (1 << bit) for i in range(device_count)])
    return steps


def source_table(device_count, low_bits):
    held = [[d >> low_bits] for d in range(device_count)]
    for partner in exchange_steps(device_count, low_bits):
        held = [held[d] + held[partner[d]] for d in range(device_count)]
    return np.array(held, np.int32)


def send(values, partner):
    return lax.ppermute(values, "ctx", [(i, p) for i, p in enumerate(partner)])


def gather_halves(values, steps, name):
    for partner in steps[:-1]:
        values, _ = join(values, send(values, partner), name, [])
    return values, send(values, steps[-1])


def whole_rows(flat, device, low_bits, columns):
    for bit in range(low_bits):
        partner = [i ^ (1 << bit) for i in range(lax.axis_size("ctx"))]
        other = send(flat, partner)
        is_high = (device >> bit) & 1
        flat = jnp.concatenate(
            [jnp.where(is_high, other, flat), jnp.where(is_high, flat, other)], axis=1
        )
    return flat.reshape(-1, columns)


def own_piece(rows, device, low_bits):
    flat = rows.reshape(1, -1)
    for bit in range(low_bits - 1, -1, -1):
        partner = [i ^ (1 << bit) for i in range(lax.axis_size("ctx"))]
        half = flat.shape[1] // 2
        is_high = (device >> bit) & 1
        leaving = jnp.where(is_high, flat[:, :half], flat[:, half:]).astype(low)
        staying = jnp.where(is_high, flat[:, half:], flat[:, :half])
        flat = staying + send(leaving, partner).astype(full)
    return flat


def low_bits_of(piece, columns):
    low_bits = 0
    while (piece << low_bits) < TILE * columns:
        low_bits += 1
    return low_bits


def unfold_rows(packed, columns, folded):
    return jnp.concatenate(
        [packed[:, :columns], packed[:, columns : columns + folded].reshape(-1, columns)], axis=0
    )


def whole_lanes(columns):
    return -(-columns // 128) * 128


def dot(left, right):
    return jnp.dot(left, right, preferred_element_type=full)


def dot_right(left, right):
    return lax.dot_general(left, right, (((1,), (1,)), ((), ())), preferred_element_type=full)


def dot_left(left, right):
    return lax.dot_general(left, right, (((0,), (0,)), ((), ())), preferred_element_type=full)


def iota(shape, axis):
    return lax.broadcasted_iota(jnp.int32, shape, axis)


def mixing_of(feature_ref):
    width = feature_ref.shape[1]
    return (iota((width, width), 0) == feature_ref[...]).astype(full).astype(low)


def fold_scratch(main, part):
    return pltpu.VMEM((-(-part // 128), main, 128), full)


def fold_write(scratch, extra):
    for block in range(scratch.shape[0]):
        lanes = slice(block * 128, min(block * 128 + 128, extra.shape[1]))
        scratch[block, :, : lanes.stop - lanes.start] = extra[:, lanes].astype(full)


def fold_read(scratch, part):
    parts = [scratch[block] for block in range(scratch.shape[0])]
    return jnp.concatenate(parts, axis=1)[:, :part].astype(low)


def fold_get(scratch, at, fold, part):
    rows = pl.ds(at, scratch.shape[1] // fold, stride=fold)
    parts = [scratch.at[block][rows, :] for block in range(scratch.shape[0])]
    return jnp.concatenate(parts, axis=1)[:, :part].astype(low)


def fold_put(scratch, at, fold, value):
    rows = pl.ds(at, scratch.shape[1] // fold, stride=fold)
    missing = scratch.shape[0] * 128 - value.shape[1]
    if missing:
        value = jnp.concatenate([value, jnp.zeros((value.shape[0], missing), full)], axis=1)
    for block in range(scratch.shape[0]):
        scratch.at[block][rows, :] = value[:, block * 128 : (block + 1) * 128]


def as_row(column):
    return jnp.transpose(jnp.broadcast_to(column, (column.shape[0], 128)))[0:1]


def turn(values, rope, direction):
    half_dim = HEAD_SIZE // 2
    swapped = jnp.concatenate([values[:, half_dim:], values[:, :half_dim]], axis=1)
    sine = rope[:, 2 * HEAD_SIZE : 3 * HEAD_SIZE]
    return values * rope[:, :HEAD_SIZE] + swapped * (direction * sine)


def rope_of(cos_ref, sin_ref, times, part, quarter):
    _, places, _, lanes = cos_ref.shape
    value = cos_ref[part] * times[0, quarter] - sin_ref[part] * times[1, quarter]
    return value.reshape(places * TILE, lanes)


def rope_own_of(cos_ref, sin_ref, times):
    _, quarters, rows, lanes = times.shape
    parts = [
        cos_ref[part, 0] * times[0] - sin_ref[part, 0] * times[1] for part in range(2)
    ]
    return jnp.concatenate([part.reshape(quarters * rows, lanes) for part in parts], axis=0)


def unit_rows(values):
    inverse = lax.rsqrt(jnp.mean(values * values, axis=-1, keepdims=True) + epsilon)
    return values * inverse, inverse


def norm_back(unit, inverse, gain, grad):
    scaled = grad * gain
    return inverse * (scaled - unit * jnp.mean(scaled * unit, axis=-1, keepdims=True))


def query_range(own, part, rows, axis):
    shape = (rows, 1) if axis == 0 else (1, rows)
    half = rows // GROUP
    last_key = own[part] * half + lax.rem(iota(shape, axis), half)
    first_key = jnp.zeros(shape, jnp.int32) + own[2 + part] * half
    return first_key.astype(full), last_key.astype(full)


def fold_gains(rows):
    part = len(rows) * rows[0].shape[1] // TILE
    pieces = [
        row[:, at : at + part] for row in rows for at in range(0, row.shape[1], part)
    ]
    return jnp.concatenate(pieces, axis=0)


def sum_gains(gains, come):
    return gains.astype(low).astype(full) + come.astype(full)


class Call:
    def __init__(self, steps):
        self.steps = steps

    def spec(self, kind, shape):
        if kind == "smem":
            return pl.BlockSpec(memory_space=pltpu.SMEM)
        if kind == "token":
            return pl.BlockSpec(memory_space=pl.ANY)
        if self.steps == 1 or kind == "whole":
            return pl.BlockSpec(memory_space=pltpu.VMEM)
        rest = tuple(shape[1:])
        return pl.BlockSpec((shape[0] // self.steps,) + rest, lambda i: (i,) + (0,) * len(rest))

    def __call__(self, kernel, name, ins, outs, scratch, micros, after=(), vmem=16):
        steps = self.steps
        first, last, end = len(ins), len(ins) + len(after), len(ins) + len(after) + len(outs)

        def run(*refs):
            refs[end][...] = jnp.zeros_like(refs[end])
            used = refs[:first] + refs[last:end] + refs[end + 1 :]
            kernel(pl.program_id(0) if steps > 1 else 0, steps, *used)

        ins = list(ins) + [("token", token) for token in after]
        outs = list(outs) + [("whole", shape_of((8, 128), full))]
        return pl.pallas_call(
            run,
            grid=(steps,) if steps > 1 else (),
            in_specs=[self.spec(kind, a.shape) for kind, a in ins],
            out_specs=[self.spec(kind, s.shape) for kind, s in outs],
            out_shape=[s for _, s in outs],
            scratch_shapes=scratch,
            compiler_params=pltpu.CompilerParams(vmem_limit_bytes=vmem * 1024 * 1024),
            cost_estimate=pl.CostEstimate(
                flops=int(micros * steps * 1e9), bytes_accessed=1024, transcendentals=0
            ),
            name=name,
        )(*[a for _, a in ins])


one_call = Call(1)


def once(step, steps, at, action):
    if steps == 1:
        action()
    else:
        pl.when(step == at)(action)


def shape_of(shape, dtype):
    return jax.ShapeDtypeStruct(shape, dtype)


def join_kernel(step, steps, held_ref, come_ref, *outs):
    rows = held_ref.shape[0]
    lane = 0
    for out_ref in outs:
        lanes = slice(lane, lane + out_ref.shape[1])
        out_ref[:rows, :] = held_ref[:, lanes]
        out_ref[rows:, :] = come_ref[:, lanes]
        lane = lanes.stop


def copy_kernel(step, steps, held_ref, out_ref):
    out_ref[...] = held_ref[...]


def join(held, come, name, after, parts=()):
    rows, columns = held.shape
    if rows * columns > 2 << 20:
        return jnp.concatenate([held, come], axis=0), None
    return one_call(
        join_kernel,
        "join_" + name,
        [("whole", held), ("whole", come)],
        [("whole", shape_of((2 * rows, part), held.dtype)) for part in parts or (columns,)],
        [],
        1,
        after,
    )


def pack_kernel(step, steps, hidden_ref, gain_ref, *refs):
    packed_ref, normed_ref = refs[-2:]
    width = hidden_ref.shape[1]
    unit, _ = unit_rows(hidden_ref[...].astype(full))
    normed_ref[...] = (unit * gain_ref[...]).astype(low)
    for a in range(hidden_ref.shape[0] // TILE):
        packed_ref[:, a * width : (a + 1) * width] = normed_ref[a * TILE : (a + 1) * TILE, :]
    if len(refs) > 2:
        fold_qkv(packed_ref, (a + 1) * width, width, refs[:-2])


def rows_in(ref, columns):
    value = ref[...].astype(full)
    if value.shape[1] == columns:
        return value
    pieces = [value[:, at : at + columns] for at in range(0, value.shape[1], columns)]
    return jnp.concatenate(pieces, axis=0)


def fold_into(out_ref, at, pieces):
    columns = sum(piece.shape[1] for piece in pieces)
    lane = at
    for piece in pieces:
        out_ref[:, lane : lane + piece.shape[1]] = piece[:TILE, :].astype(low)
        lane += piece.shape[1]
    tails = [piece[TILE:, :] for piece in pieces]
    tail = tails[0] if len(tails) == 1 else jnp.concatenate(tails, axis=1)
    fold = TILE // tail.shape[0]
    part = columns // fold
    rows = [
        tail[j : j + 1, block * part : (block + 1) * part]
        for j in range(tail.shape[0])
        for block in range(fold)
    ]
    out_ref[:, lane : lane + part] = jnp.concatenate(rows, axis=0).astype(low)
    return lane + part


def fold_qkv(out_ref, at, width, refs):
    query_ref, key_ref, value_ref = refs
    pieces = [rows_in(query_ref, width), rows_in(key_ref, KV_WIDTH), rows_in(value_ref, KV_WIDTH)]
    end = fold_into(out_ref, at, pieces)
    out_ref[:, end:] = jnp.zeros((TILE, out_ref.shape[1] - end), low)


def fold_qkv_kernel(width, step, steps, *refs):
    fold_qkv(refs[-1], 0, width, refs[:-1])


def fold_late_kernel(width, ff, step, steps, gate_ref, up_ref, down_ref, output_ref, out_ref):
    lane = fold_into(out_ref, 0, [rows_in(gate_ref, ff), rows_in(up_ref, ff)])
    down = rows_in(down_ref, width)
    for a in range(down.shape[0] // TILE):
        out_ref[:, lane : lane + width] = down[a * TILE : (a + 1) * TILE].astype(low)
        lane += width
    lane = fold_into(out_ref, lane, [rows_in(output_ref, width)])
    out_ref[:, lane:] = jnp.zeros((TILE, out_ref.shape[1] - lane), low)


def weights_kernel(step, steps, feature_ref, own_ref, come_ref, weight_ref, key_value_ref, mixed, folds):
    width, columns = weight_ref.shape
    half = own_ref.shape[0]
    main = 2 * half
    fold = main // (width - main)
    part = columns // fold
    mixed[:half, :] = own_ref[:, :columns]
    mixed[half:main, :] = come_ref[:, :columns]
    folded = slice(columns, columns + part)
    extra = jnp.concatenate([own_ref[:, folded], come_ref[:, folded]], axis=0)
    fold_write(folds, extra)
    for at in range(fold):
        mixed[main:, at * part : (at + 1) * part] = fold_get(folds, at, fold, part)
    natural = dot(mixing_of(feature_ref), mixed[...])
    weight_ref[...] = natural.astype(low)
    keys = natural[:, width : width + KV_WIDTH]
    key_value_ref[:, :KV_WIDTH] = keys.astype(low)
    half_dim = HEAD_SIZE // 2
    swapped = [
        keys[:, (block ^ 1) * half_dim : ((block ^ 1) + 1) * half_dim]
        for block in range(KV_WIDTH // half_dim)
    ]
    key_value_ref[:, KV_WIDTH : 2 * KV_WIDTH] = jnp.concatenate(swapped, axis=1).astype(low)
    key_value_ref[:, 2 * KV_WIDTH :] = natural[:, width + KV_WIDTH :].astype(low)


def queries_kernel(step, steps, normed_ref, weight_ref, cos_ref, sin_ref, times, query_ref):
    tokens, width = normed_ref.shape
    half = tokens // 2
    queries = dot(normed_ref[...], weight_ref[:, :width])
    rope = rope_own_of(cos_ref, sin_ref, times)
    for head in range(HEADS):
        turned = turn(queries[:, head * HEAD_SIZE : (head + 1) * HEAD_SIZE], rope, 1.0)
        turned = turned.astype(low) * low(HEAD_SIZE**-0.5)
        for part in range(2):
            row = (part * GROUP + head % GROUP) * half
            query_ref[head // GROUP, row : row + half, :] = turned[part * half : (part + 1) * half]


def project_kernel(step, steps, normed_ref, weight_ref, cos_ref, sin_ref, times, kv_ref):
    width = weight_ref.shape[0]
    groups = normed_ref.shape[1] // width
    for a in range(groups):
        kv = dot(normed_ref[:, a * width : (a + 1) * width], weight_ref[...])
        rope = rope_of(cos_ref, sin_ref, times, a // (groups // 2), a % (groups // 2))
        cos, sin = rope[:, : 2 * HEAD_SIZE], rope[:, 2 * HEAD_SIZE :]
        cos = jnp.concatenate([cos, cos[:, :HEAD_SIZE]], axis=1)
        sin = jnp.concatenate([sin, sin[:, :HEAD_SIZE]], axis=1)
        keys = kv[:, :KV_WIDTH] * cos + kv[:, KV_WIDTH : 2 * KV_WIDTH] * sin
        at = a * 2 * KV_WIDTH
        kv_ref[:, at : at + KV_WIDTH] = keys.astype(low)
        kv_ref[:, at + KV_WIDTH : at + 2 * KV_WIDTH] = kv[:, 2 * KV_WIDTH :].astype(low)


def key_part(kv_ref, groups, column):
    lanes = [a * 2 * KV_WIDTH + column * HEAD_SIZE for a in groups]
    return jnp.concatenate([kv_ref[:, at : at + HEAD_SIZE] for at in lanes], axis=0)


def key_row(key_ref, part, groups):
    start = key_ref[part]
    return jnp.concatenate([start + float(i * TILE) for i in range(len(groups))], axis=1)


def reaches_low(own, blocks):
    return own[3] < blocks


def forward_kernel(
    is_first, low_blocks, step, steps, own, key_ref, query_ref, kv_ref, *rest
):
    state = rest[-1]
    rows = query_ref.shape[1] // 2
    groups = kv_ref.shape[1] // (2 * KV_WIDTH)

    def first():
        if is_first:
            lane = lax.broadcasted_iota(jnp.int32, state.shape, 2)
            state[...] = jnp.where(lane == PEAK, masked_score, 0.0)
        else:
            state[...] = rest[0][...]

    once(step, steps, 0, first)

    def attend(key_half, query_half):
        members = range(key_half * groups // 2, (key_half + 1) * groups // 2)
        at = slice(query_half * rows, (query_half + 1) * rows)
        key_index = key_row(key_ref, key_half, members)
        first_key, last_key = query_range(own, query_half, rows, 0)
        allowed = (key_index >= first_key) & (key_index <= last_key)
        for head in range(KV_HEADS):
            scores = dot_right(query_ref[head, at], key_part(kv_ref, members, head))
            masked = jnp.where(allowed, scores, masked_score)
            old = state[head, at, PEAK : PEAK + 1]
            new = jnp.maximum(old, jnp.max(masked, axis=1, keepdims=True))
            weights = jnp.where(allowed, jnp.exp(masked - new), 0.0)
            factor = jnp.exp(old - new)
            state[head, at, PEAK : PEAK + 1] = new
            state[head, at, TOTAL : TOTAL + 1] = state[
                head, at, TOTAL : TOTAL + 1
            ] * factor + jnp.sum(weights, axis=1, keepdims=True)
            state[head, at, :HEAD_SIZE] = state[head, at, :HEAD_SIZE] * factor + dot(
                weights.astype(low), key_part(kv_ref, members, KV_HEADS + head)
            )

    attend(0, 0)
    pl.when(reaches_low(own, low_blocks))(lambda: attend(0, 1))
    attend(1, 1)


def feedforward_kernel(
    step,
    steps,
    source_ref,
    feature_ref,
    state_ref,
    hidden_ref,
    gain_ref,
    grad_ref,
    own_ref,
    come_ref,
    out_ref,
    grad_middle_ref,
    head_grad_ref,
    delta_ref,
    lse_ref,
    keep_ref,
    send_ref,
    gain_part_ref,
    attention,
    attended,
    output_w,
    normed,
    normed_t,
    down_w,
    down_grad,
    total,
    grad_normed,
    extra_grad,
    output_folds,
    late_folds,
):
    rows, width = hidden_ref.shape
    half = own_ref.shape[0]
    main = 2 * half
    rest = width - main
    fold = main // rest
    places = main // TILE
    ff = down_w.shape[0]
    chunk = 2 * ff // fold
    down_at = 2 * ff + chunk
    device_ff = ff // places
    groups = device_ff // TILE
    out_at = down_at + groups * width
    mixing = mixing_of(feature_ref)

    tokens = rows // 2
    for head in range(KV_HEADS):
        sums = state_ref[head, :, TOTAL : TOTAL + 1]
        attention[head] = state_ref[head, :, :HEAD_SIZE] / sums
        logs = state_ref[head, :, PEAK : PEAK + 1] + jnp.log(sums)
        for part in range(2):
            lse_ref[2 * head + part] = as_row(
                logs[part * GROUP * tokens : (part + 1) * GROUP * tokens]
            )
    for h in range(HEADS):
        for part in range(2):
            row = (part * GROUP + h % GROUP) * tokens
            attended[
                part * tokens : (part + 1) * tokens, h * HEAD_SIZE : (h + 1) * HEAD_SIZE
            ] = attention[h // GROUP, row : row + tokens, :].astype(low)
    attended[...] = dot(attended[...], mixing).astype(low)
    output_w[:half, :] = own_ref[:, out_at : out_at + width]
    output_w[half:main, :] = come_ref[:, out_at : out_at + width]
    part = width // fold
    folded = slice(out_at + width, out_at + width + part)
    extra = jnp.concatenate([own_ref[:, folded], come_ref[:, folded]], axis=0)
    fold_write(output_folds, extra)
    for at in range(fold):
        output_w[main:, at * part : (at + 1) * part] = fold_get(output_folds, at, fold, part)
    middle = hidden_ref[...].astype(full) + dot(attended[...], output_w[...])
    gain = gain_ref[...]
    unit, inverse = unit_rows(middle)
    mixed_norm = dot((unit * gain).astype(low), mixing)
    normed[...] = mixed_norm.astype(low)
    normed_t[...] = jnp.transpose(mixed_norm).astype(low)
    for place in range(places):
        held = own_ref if place < places // 2 else come_ref
        row = (place % (places // 2)) * TILE
        for a in range(groups):
            at = pl.multiple_of(source_ref[place] * device_ff + a * TILE, TILE)
            lane = down_at + a * width
            down_w[pl.ds(at, TILE), :] = held[row : row + TILE, lane : lane + width]
    total[...] = jnp.zeros_like(total)
    grad_normed[...] = jnp.zeros_like(grad_normed)
    out_grad = grad_ref[...]
    fold_write(
        late_folds,
        jnp.concatenate([own_ref[:, 2 * ff : down_at], come_ref[:, 2 * ff : down_at]], axis=0),
    )

    def advance(c, carry):
        gate_at = pl.ds(pl.multiple_of(c * chunk, 128), chunk)
        up_at = pl.ds(pl.multiple_of(ff + c * chunk, 128), chunk)

        def columns(lanes, at):
            tail = fold_get(late_folds, at, fold, chunk)
            value = (
                dot(normed[:, :half], own_ref[:, lanes])
                + dot(normed[:, half:main], come_ref[:, lanes])
                + dot(normed[:, main:], tail)
            )
            return value, tail

        gate, gate_tail = columns(gate_at, c)
        up, up_tail = columns(up_at, c + fold // 2)
        down_at_c = pl.ds(pl.multiple_of(c * chunk, 128), chunk)
        down = down_w[down_at_c, :]
        sigma = 1.0 / (1.0 + jnp.exp(-gate))
        silu = gate * sigma
        inner = (silu * up).astype(low)
        total[...] += dot(inner, down)
        grad_inner = dot_right(out_grad, down)
        grad_gate = (grad_inner * up * sigma * (1.0 + gate * (1.0 - sigma))).astype(low)
        grad_up = (grad_inner * silu).astype(low)
        down_grad[down_at_c, :] = dot_left(inner, out_grad).astype(low)
        for grad, lanes, tail, at in (
            (grad_gate, gate_at, gate_tail, c),
            (grad_up, up_at, up_tail, c + fold // 2),
        ):
            grad_normed[:, :half] += dot_right(grad, own_ref[:, lanes])
            grad_normed[:, half:main] += dot_right(grad, come_ref[:, lanes])
            grad_normed[:, main:] += dot_right(grad, tail)
            keep_ref[:, lanes] = dot(normed_t[:half], grad).astype(low)
            send_ref[:, lanes] = dot(normed_t[half:main], grad).astype(low)
            fold_put(extra_grad, at, fold, dot(normed_t[main:], grad))
        return carry

    lax.fori_loop(0, ff // chunk, advance, 0)
    out_ref[...] = (middle + total[...]).astype(low)
    extra = fold_read(extra_grad, chunk)
    keep_ref[:, 2 * ff : down_at] = extra[:half]
    send_ref[:, 2 * ff : down_at] = extra[half:]
    for place in range(places):
        held = keep_ref if place < places // 2 else send_ref
        row = (place % (places // 2)) * TILE
        for a in range(groups):
            at = pl.multiple_of(source_ref[place] * device_ff + a * TILE, TILE)
            lane = down_at + a * width
            held[row : row + TILE, lane : lane + width] = down_grad[pl.ds(at, TILE), :]

    high = grad_normed[...].astype(low)
    tail = (grad_normed[...] - high.astype(full)).astype(low)
    back = dot_right(high, mixing) + dot_right(tail, mixing)
    gain_part_ref[...] = jnp.sum(back * unit, axis=0, keepdims=True)
    grad_middle = out_grad.astype(full) + norm_back(unit, inverse, gain, back)
    grad_middle_ref[...] = grad_middle
    grad_branch = grad_middle.astype(low)
    output_grad = dot_left(attended[...], grad_branch)
    keep_ref[:, out_at : out_at + width] = output_grad[:half].astype(low)
    send_ref[:, out_at : out_at + width] = output_grad[half:main].astype(low)
    for at in range(fold):
        fold_put(output_folds, at, fold, output_grad[main:, at * part : (at + 1) * part])
    extra = fold_read(output_folds, part)
    unused = jnp.zeros((half, keep_ref.shape[1] - folded.stop), low)
    for held, rows_of_half in ((keep_ref, extra[:half]), (send_ref, extra[half:])):
        held[:, folded] = rows_of_half
        held[:, folded.stop :] = unused
    grad_low = dot_right(grad_branch, output_w[...]).astype(low)
    grad_low = dot_right(grad_low, mixing).astype(low)
    for head in range(KV_HEADS):
        for part in range(2):
            grads = jnp.concatenate(
                [
                    grad_low[
                        part * tokens : (part + 1) * tokens, h * HEAD_SIZE : (h + 1) * HEAD_SIZE
                    ]
                    for h in range(head * GROUP, (head + 1) * GROUP)
                ],
                axis=0,
            )
            at = slice(part * GROUP * tokens, (part + 1) * GROUP * tokens)
            head_grad_ref[head, at] = grads
            delta_ref[2 * head + part] = as_row(
                jnp.sum(grads.astype(full) * attention[head, at], axis=1, keepdims=True)
            )


def backward_kernel(
    is_first,
    key_half,
    low_blocks,
    joined,
    step,
    steps,
    own,
    key_ref,
    query_ref,
    grad_ref,
    lse_ref,
    delta_ref,
    kv_ref,
    tokens_ref,
    cos_ref,
    sin_ref,
    times,
    *rest,
):
    if not is_first:
        held, rest = rest[:2], rest[2:]
    base = 0
    if joined:
        low_ref, rest = rest[0], rest[1:]
        base = low_ref.shape[1]
        rest[2][:, :base] = low_ref[...]
    grad_query, grad_weight, out_ref, grad_kv = rest
    rows = query_ref.shape[1] // 2
    groups = kv_ref.shape[1] // (2 * KV_WIDTH)
    key_rows = kv_ref.shape[0]
    width = tokens_ref.shape[1] // groups
    members = range(key_half * groups // 2, (key_half + 1) * groups // 2)

    def first():
        if is_first:
            grad_query[...] = jnp.zeros_like(grad_query)
            grad_weight[...] = jnp.zeros_like(grad_weight)
        else:
            grad_query[...] = held[0][...]
            grad_weight[...] = held[1][...]

    once(step, steps, 0, first)
    key_index = key_row(key_ref, key_half, members)
    key_index = jnp.transpose(jnp.broadcast_to(key_index, (128, key_index.shape[1])))[:, 0:1]

    def attend(query_half, add):
        at = slice(query_half * rows, (query_half + 1) * rows)
        first_key, last_key = query_range(own, query_half, rows, 1)
        allowed = (key_index >= first_key) & (key_index <= last_key)
        for head in range(KV_HEADS):
            keys = key_part(kv_ref, members, head)
            scores = dot_right(keys, query_ref[head, at])
            probs = jnp.where(allowed, jnp.exp(scores - lse_ref[2 * head + query_half]), 0.0)
            d_probs = dot_right(key_part(kv_ref, members, KV_HEADS + head), grad_ref[head, at])
            d_scores = (probs * (d_probs - delta_ref[2 * head + query_half])).astype(low)
            grad_query[2 * head + query_half] += dot_left(keys, d_scores)
            parts = (
                (head, dot(d_scores, query_ref[head, at])),
                (KV_HEADS + head, dot(probs.astype(low), grad_ref[head, at])),
            )
            for column, value in parts:
                lanes = slice(column * HEAD_SIZE, (column + 1) * HEAD_SIZE)
                if add:
                    grad_kv[:, lanes] += value
                else:
                    grad_kv[:, lanes] = value

    if key_half == 0:
        attend(0, False)
        pl.when(reaches_low(own, low_blocks))(lambda: attend(1, True))
    else:
        attend(1, False)
    for i, a in enumerate(members):
        at = slice(i * key_rows, (i + 1) * key_rows)
        rope = rope_of(cos_ref, sin_ref, times, key_half, i)
        turned = jnp.concatenate(
            [
                turn(grad_kv[at, head * HEAD_SIZE : (head + 1) * HEAD_SIZE], rope, -1.0)
                for head in range(KV_HEADS)
            ]
            + [grad_kv[at, KV_WIDTH:]],
            axis=1,
        ).astype(low)
        lane = base + i * 2 * KV_WIDTH
        out_ref[:, lane : lane + 2 * KV_WIDTH] = turned
        grad_weight[...] += dot_left(turned, tokens_ref[:, a * width : (a + 1) * width])


def qkv_grad_kernel(
    step,
    steps,
    feature_ref,
    grad_query,
    grad_weight,
    normed_ref,
    weight_ref,
    cos_ref,
    sin_ref,
    times,
    gain_ref,
    gain_two_ref,
    query_grad_ref,
    gains_ref,
    keep_ref,
    send_ref,
    natural,
    folds,
):
    tokens, width = normed_ref.shape
    half = tokens // 2
    rope = rope_own_of(cos_ref, sin_ref, times)
    for head in range(KV_HEADS):
        rotated = [
            jnp.transpose(grad_query[2 * head + part]) * HEAD_SIZE**-0.5 for part in range(2)
        ]
        for g in range(GROUP):
            h = head * GROUP + g
            value = jnp.concatenate([part[g * half : (g + 1) * half] for part in rotated], axis=0)
            query_grad_ref[:, h * HEAD_SIZE : (h + 1) * HEAD_SIZE] = turn(value, rope, -1.0).astype(
                low
            )
    natural[:, :width] = dot_left(normed_ref[...], query_grad_ref[...])
    natural[:, width:] = jnp.transpose(grad_weight[...])
    products = natural[...] * weight_ref[...].astype(full)
    gain_part = as_row(jnp.sum(products, axis=1, keepdims=True)) / gain_ref[...]
    gains = fold_gains([gain_part, gain_two_ref[...]])
    gains_ref[...] = gains
    mixed = dot_left(mixing_of(feature_ref), natural[...].astype(low)).astype(low)
    columns = mixed.shape[1]
    rows = keep_ref.shape[0]
    main = 2 * rows
    fold = main // (width - main)
    part = columns // fold
    for at in range(fold):
        fold_put(folds, at, fold, mixed[main:, at * part : (at + 1) * part].astype(full))
    extra = fold_read(folds, part)
    unused = jnp.zeros((rows, keep_ref.shape[1] - columns - part), low)
    for held, at in ((keep_ref, 0), (send_ref, rows)):
        held[:rows, :columns] = mixed[at : at + rows]
        held[:rows, columns : columns + part] = extra[at : at + rows]
        held[:rows, columns + part :] = unused
    send_ref[:TILE, columns + part : columns + part + gains.shape[1]] = gains.astype(low)


def merge_kernel(gain_at, step, steps, *refs):
    keep_low, keep_high, kv_come, w_keep, w_come, gains_ref, keep_out, send_out, gains_out = refs
    half = w_keep.shape[0] // 2
    part = keep_low.shape[1]
    base = 2 * part
    lane = 0
    for keep, come, first in (
        (keep_low, kv_come, 0),
        (keep_high, kv_come, part),
        (w_keep, w_come, 0),
    ):
        columns = keep.shape[1]
        for out, at in ((keep_out, 0), (send_out, half)):
            value = keep[at : at + half, :].astype(full) + come[
                at : at + half, first : first + columns
            ].astype(full)
            out[:, lane : lane + columns] = value.astype(low)
        lane += columns
    lanes = slice(gain_at, gain_at + gains_ref.shape[1])
    gains = sum_gains(gains_ref[...], w_come[:TILE, lanes])
    gains_out[...] = gains
    send_out[:TILE, base + lanes.start : base + lanes.stop] = gains.astype(low)


def add_kernel(gain_at, step, steps, keep_ref, come_ref, *rest):
    rows = keep_ref.shape[0]
    if gain_at is not None:
        gains_ref, keep_out, send_out, gains_out = rest
        lanes = slice(gain_at, gain_at + gains_ref.shape[1])
        gains = sum_gains(gains_ref[...], come_ref[:TILE, lanes])
        gains_out[...] = gains
        rest = rest[1:-1]

    def tile(at):
        at = pl.ds(at, TILE)
        return keep_ref[at, :].astype(full) + come_ref[at, :].astype(full)

    if rows == TILE:
        rest[0][...] = tile(0)
        return
    keep_out, send_out = rest
    half = rows // 2

    def advance(i, carry):
        at = pl.multiple_of(i * TILE, TILE)
        keep_out[pl.ds(at, TILE), :] = tile(at).astype(low)
        send_out[pl.ds(at, TILE), :] = tile(pl.multiple_of(half + at, TILE)).astype(low)
        return carry

    lax.fori_loop(0, half // TILE, advance, 0)
    if gain_at is not None:
        send_out[:TILE, lanes] = gains.astype(low)


def scatter_halves(keep, leaving, steps, name, gains=None, gain_at=None, after=()):
    for at, partner in enumerate(reversed(steps)):
        come = send(leaving, partner)
        rows, columns = keep.shape
        ins = [("whole", keep), ("whole", come)]
        if rows == TILE:
            if gains is not None:
                return keep, come, gains
            outs = [("whole", shape_of((rows, columns), full))]
        else:
            outs = [("whole", shape_of((rows // 2, columns), low))] * 2
        if gains is not None:
            ins.append(("whole", gains))
            outs.append(("whole", shape_of(gains.shape, full)))
        result = one_call(
            functools.partial(add_kernel, gain_at),
            name,
            ins,
            outs,
            [],
            1,
            after[at] if at < len(after) else (),
        )
        if gains is not None:
            gains = result[-2]
        if rows == TILE:
            return result[0]
        keep, leaving = result[0], result[1]


def final_kernel(
    base,
    step,
    steps,
    keep_ref,
    come_ref,
    query_grad_ref,
    weight_ref,
    hidden_ref,
    gain_ref,
    grad_middle_ref,
    *rest,
):
    grads = rest[-1]
    tokens, width = hidden_ref.shape
    grads[:, :width] = query_grad_ref[...]
    for a in range(tokens // TILE):
        rows = slice(a * TILE, (a + 1) * TILE)
        lanes = slice(a * 2 * KV_WIDTH, (a + 1) * 2 * KV_WIDTH)
        value = keep_ref[:, lanes].astype(full) + come_ref[:, lanes].astype(full)
        grads[rows, width:] = value.astype(low)
    back = dot_right(grads[...], weight_ref[...])
    unit, inverse = unit_rows(hidden_ref[...].astype(full))
    out_ref = rest[-6] if base else rest[-2]
    out_ref[...] = (grad_middle_ref[...] + norm_back(unit, inverse, gain_ref[...], back)).astype(low)
    if not base:
        return
    gains_ref, _, query_out, key_out, value_out, gains_out, _ = rest
    columns = weight_ref.shape[1]
    total = keep_ref[:, base:].astype(full) + come_ref[:, base:].astype(full)
    fold = gains_ref.shape[0] // 2
    part = columns // fold
    for row in range(TILE + TILE // fold):
        if row < TILE:
            value = total[row : row + 1, :columns]
        else:
            at = (row - TILE) * fold
            value = jnp.concatenate(
                [total[at + i : at + i + 1, columns : columns + part] for i in range(fold)], axis=1
            )
        query_out[:, row * width : (row + 1) * width] = value[:, :width]
        for out, first in ((key_out, width), (value_out, width + KV_WIDTH)):
            out[:, row * KV_WIDTH : (row + 1) * KV_WIDTH] = value[:, first : first + KV_WIDTH]
    at = columns + part
    lanes = slice(at, at + gains_ref.shape[1])
    gains = sum_gains(gains_ref[...], come_ref[:TILE, base + lanes.start : base + lanes.stop])
    for k in range(2):
        gains_out[k : k + 1, :] = jnp.concatenate(
            [gains[k * fold + i : k * fold + i + 1] for i in range(fold)], axis=1
        )


def body(
    hidden_in,
    attention_gain,
    query_weight,
    key_weight,
    value_weight,
    output_weight,
    feedforward_gain,
    gate_weight,
    up_weight,
    down_weight,
    doc_of_block,
    pair_table,
    out_grad,
):
    tokens, width = hidden_in.shape
    half_rows = tokens // 2
    count = lax.axis_size("ctx")
    device = lax.axis_index("ctx")
    ff = gate_weight.shape[1] * count // width
    low_bits = low_bits_of(query_weight.shape[1], width)
    merged = low_bits == 0
    row_steps = exchange_steps(count, low_bits)
    token_steps = exchange_steps(count, 0)
    group_count = count >> low_bits
    group_rows = width // group_count
    groups = tokens // TILE
    steps = max(1, TILE * count // 512)
    places = count // (2 * steps)
    gain_one = attention_gain.reshape(1, width)
    gain_two = feedforward_gain.reshape(1, width)
    columns = width + 2 * KV_WIDTH
    main = TILE * group_count
    fold = main // (width - main)
    w_lanes = whole_lanes(columns + columns // fold + 2 * width // TILE)
    ff_folded = 2 * ff // fold
    down_at = 2 * ff + ff_folded
    device_groups = ff // group_count // TILE
    out_at = down_at + device_groups * width
    late_lanes = whole_lanes(out_at + width + width // fold)
    call = Call(steps)
    one = Call(1)

    def rows_of(piece, piece_columns):
        if low_bits:
            piece = whole_rows(piece, device, low_bits, piece_columns)
        return ("whole", piece)

    qkv_pieces = [
        rows_of(query_weight, width),
        rows_of(key_weight, KV_WIDTH),
        rows_of(value_weight, KV_WIDTH),
    ]
    token_parts = (groups * width, w_lanes) if merged else (groups * width,)
    packed, normed, pack_mark = one(
        pack_kernel,
        "norm_and_pack",
        [("whole", hidden_in), ("whole", gain_one)] + (qkv_pieces if merged else []),
        [
            ("whole", shape_of((TILE, sum(token_parts)), low)),
            ("whole", shape_of((tokens, width), low)),
        ],
        [],
        1,
    )

    late_at = 2
    late, before = one(
        functools.partial(fold_late_kernel, width, ff),
        "fold_late",
        [
            rows_of(gate_weight, ff),
            rows_of(up_weight, ff),
            rows_of(down_weight, width),
            rows_of(output_weight, width),
        ],
        [("whole", shape_of((TILE, late_lanes), low))],
        [],
        1,
        [pack_mark],
    )
    for at, partner in enumerate(token_steps[:-1]):
        if late_at <= at < late_at + 2:
            late, before = join(late, send(late, row_steps[at - late_at]), "late", [])
        last = at == len(token_steps) - 2
        *held, mark = join(
            packed,
            send(packed, partner),
            "tokens",
            [before] if late_at - 1 <= at < late_at + 2 else [],
            token_parts if last else (),
        )
        packed = held[0]
        if at == late_at - 1:
            late, _ = one(
                copy_kernel,
                "release_late",
                [("whole", late)],
                [("whole", shape_of(late.shape, low))],
                [],
                1,
                [mark],
            )
    token_own = packed
    if merged:
        w_own, w_come = held[1], send(held[1], token_steps[-1])
    else:
        qkv_piece, _ = one(
            functools.partial(fold_qkv_kernel, width),
            "fold_qkv",
            qkv_pieces,
            [("whole", shape_of((TILE, w_lanes), low))],
            [],
            1,
        )
        w_own, w_come = gather_halves(qkv_piece, row_steps, "qkv")
    token_come = send(token_own, token_steps[-1])

    def table_row(table):
        return lax.dynamic_index_in_dim(jnp.asarray(table), device, 0, keepdims=False)

    sources = table_row(source_table(count, 0))
    group_table = source_table(count, low_bits)
    group_sources = table_row(group_table)
    inside = np.arange(group_rows)[None, None, :]
    features = group_table[:, :, None] * group_rows + inside
    features = np.concatenate(
        [
            features[:, :, :TILE].reshape(count, -1),
            features[:, :, TILE:].reshape(count, -1),
        ],
        axis=1,
    ).astype(np.int32)
    feature_row = table_row(features).reshape(1, width)

    device_iota = jnp.arange(count, dtype=jnp.int32)
    pairs = jnp.sum(
        jnp.where(sources[:, None] == device_iota[None, :], pair_table[None, :], 0), axis=1
    )
    blocks = jnp.stack([pairs, 2 * count - 1 - pairs], axis=1).reshape(-1)
    block_iota = jnp.arange(2 * count, dtype=jnp.int32)
    block_docs = jnp.sum(
        jnp.where(blocks[:, None] == block_iota[None, :], doc_of_block[None, :], 0), axis=1
    )
    doc_start = jnp.min(
        jnp.where(block_docs[:, None] == doc_of_block[None, :], block_iota[None, :], 2 * count),
        axis=1,
    )
    own = jnp.concatenate([blocks[:2], doc_start[:2]])

    def by_step(values):
        return values.reshape(2, steps, places, 2).transpose(0, 1, 3, 2)

    inner = jnp.arange(TILE, dtype=jnp.int32)
    key_index = by_step(blocks)[..., None] * half_rows + inner
    key_index = key_index.astype(full).reshape(2, 2 * steps, 1, -1)
    frequency = rope_base ** (-jnp.arange(HEAD_SIZE // 2, dtype=full) * (2.0 / HEAD_SIZE))
    block_angle = (by_step(blocks - doc_start) * half_rows).astype(full)[..., None] * frequency
    offset = jnp.arange(half_rows, dtype=full).reshape(groups // 2, TILE)
    offset_angle = offset[..., None] * frequency
    cos_in, sin_in = jnp.cos(offset_angle), jnp.sin(offset_angle)
    times_cos = jnp.concatenate([cos_in] * 4 + [-sin_in, sin_in] * 2, axis=-1)
    times_sin = jnp.concatenate([sin_in] * 4 + [cos_in, -cos_in] * 2, axis=-1)
    times = jnp.stack([times_cos, times_sin])
    block_cos = jnp.tile(jnp.cos(block_angle), 8).reshape(2, 2 * steps, places, 1, 4 * HEAD_SIZE)
    block_sin = jnp.tile(jnp.sin(block_angle), 8).reshape(2, 2 * steps, places, 1, 4 * HEAD_SIZE)
    rope_own = [
        ("whole", block_cos[0, :2, :1]),
        ("whole", block_sin[0, :2, :1]),
        ("whole", times),
    ]
    halves = [
        (
            held,
            key_index[place],
            [("rows", block_cos[place]), ("rows", block_sin[place]), ("whole", times)],
        )
        for place, held in enumerate((token_own, token_come))
    ]

    rows = GROUP * tokens
    half = TILE * count // 2
    kv_shape = shape_of((half, groups * 2 * KV_WIDTH), low)
    head_shape = (KV_HEADS, rows, HEAD_SIZE)
    late, before = join(late, send(late, row_steps[late_at]), "late", [])
    weight, kv_weight, _ = one(
        weights_kernel,
        "qkv_weights",
        [("whole", feature_row), ("whole", w_own), ("whole", w_come)],
        [
            ("whole", shape_of((width, columns), low)),
            ("whole", shape_of((width, 3 * KV_WIDTH), low)),
        ],
        [pltpu.VMEM((width, columns), low), fold_scratch(main, columns // fold)],
        3,
        [before],
    )
    queries, _ = one(
        queries_kernel,
        "queries",
        [("whole", normed), ("whole", weight)] + rope_own,
        [("whole", shape_of(head_shape, low))],
        [],
        2,
    )

    def project(place, after):
        token_rows, _, turns = halves[place]
        return call(
            project_kernel,
            "project",
            [("rows", token_rows), ("whole", kv_weight)] + turns,
            [("rows", kv_shape)],
            [],
            5,
            after,
        )

    state_shapes = [("whole", shape_of((KV_HEADS, rows, 2 * HEAD_SIZE), full))]

    def attend(place, kv, state, after):
        return call(
            functools.partial(forward_kernel, not state, count),
            "attention_forward",
            [
                ("smem", own),
                ("rows", halves[place][1]),
                ("whole", queries),
                ("rows", kv),
            ]
            + [("whole", held) for held in state],
            state_shapes,
            [],
            6,
            after,
        )

    kv_own, mark = project(0, [])

    *state, mark = attend(0, kv_own, [], [])
    kv_come, mark = project(1, [mark])
    *state, mark = attend(1, kv_come, state, [])
    for partner in row_steps[late_at + 1 : -1]:
        late, late_mark = join(late, send(late, partner), "late", [mark])
    late_own, late_come = late, send(late, row_steps[-1])

    late_shape = late_own.shape
    row_shape = shape_of((2 * KV_HEADS, 1, rows // 2), full)
    block_out, grad_middle, head_grads, delta, lse, late_keep, late_send, gain_two_part, _ = one(
        feedforward_kernel,
        "feedforward",
        [
            ("smem", group_sources),
            ("whole", feature_row),
        ]
        + [("whole", held) for held in state]
        + [
            ("whole", hidden_in),
            ("whole", gain_two),
            ("whole", out_grad),
            ("whole", late_own),
            ("whole", late_come),
        ],
        [
            ("whole", shape_of((tokens, width), low)),
            ("whole", shape_of((tokens, width), full)),
            ("whole", shape_of(head_shape, low)),
            ("whole", row_shape),
            ("whole", row_shape),
            ("whole", shape_of(late_shape, low)),
            ("whole", shape_of(late_shape, low)),
            ("whole", shape_of((1, width), full)),
        ],
        [
            pltpu.VMEM(head_shape, full),
            pltpu.VMEM((tokens, width), low),
            pltpu.VMEM((width, width), low),
            pltpu.VMEM((tokens, width), low),
            pltpu.VMEM((width, tokens), low),
            pltpu.VMEM((ff, width), low),
            pltpu.VMEM((ff, width), low),
            pltpu.VMEM((tokens, width), full),
            pltpu.VMEM((tokens, width), full),
            fold_scratch(main, ff_folded),
            fold_scratch(main, width // fold),
            fold_scratch(main, ff_folded),
        ],
        16,
        vmem=28,
    )

    def attend_back(place, key_half, kv, carried, after, joined=()):
        token_rows, keys, turns = halves[place]
        return call(
            functools.partial(backward_kernel, not carried, key_half, count, bool(joined)),
            "attention_backward",
            [
                ("smem", own),
                ("rows", keys),
                ("whole", queries),
                ("whole", head_grads),
                ("whole", lse),
                ("whole", delta),
                ("rows", kv),
                ("rows", token_rows),
            ]
            + turns
            + [("whole", held) for held in carried]
            + [("rows", part) for part in joined],
            [
                ("whole", shape_of((2 * KV_HEADS, HEAD_SIZE, rows // 2), full)),
                ("whole", shape_of((2 * KV_WIDTH, width), full)),
                ("rows", shape_of((half, groups * KV_WIDTH * (1 + len(joined))), low)),
            ],
            [pltpu.VMEM((groups // 2 * places * TILE, 2 * KV_WIDTH), full)],
            6,
            after,
        )

    late_steps = row_steps[::-1]
    keep, leaving = late_keep, late_send

    def add_late(at, after):
        come = send(leaving, late_steps[at])
        part = shape_of((keep.shape[0] // 2, late_lanes), low)
        outs = [part, part] if keep.shape[0] > TILE else [shape_of((TILE, late_lanes), full)]
        return one(
            functools.partial(add_kernel, None),
            "add_late",
            [("whole", keep), ("whole", come)],
            [("whole", out) for out in outs],
            [],
            1,
            after,
        )

    *carried, send_low, mark = attend_back(1, 0, kv_come, [], [])
    keep, leaving, late_mark = add_late(0, [mark])
    *carried, kv_send, mark = attend_back(1, 1, kv_come, carried, [late_mark], [send_low])
    *carried, keep_low, mark = attend_back(0, 0, kv_own, carried, [])
    *carried, keep_high, mark = attend_back(0, 1, kv_own, carried, [])
    query_grad, gains, w_keep, w_send, mark = one(
        qkv_grad_kernel,
        "qkv_gradients",
        [
            ("whole", feature_row),
            ("whole", carried[0]),
            ("whole", carried[1]),
            ("whole", normed),
            ("whole", weight),
        ]
        + rope_own
        + [
            ("whole", gain_one),
            ("whole", gain_two_part),
        ],
        [
            ("whole", shape_of((tokens, width), low)),
            ("whole", shape_of((TILE, 2 * width // TILE), full)),
            ("whole", shape_of((main // 2, w_lanes), low)),
            ("whole", shape_of((main // 2, w_lanes), low)),
        ],
        [pltpu.VMEM((width, columns), full), fold_scratch(main, columns // fold)],
        3,
    )
    late_marks = []
    for at in range(1, len(late_steps)):
        result = add_late(at, [mark] if at == 1 else [])
        keep, leaving = result[0], result[1]
        late_marks.append([result[-1]])
    late_sum = keep

    ends = [
        ("whole", query_grad),
        ("whole", weight),
        ("whole", hidden_in),
        ("whole", gain_one),
        ("whole", grad_middle),
    ]
    end_scratch = [pltpu.VMEM((tokens, columns), low)]
    input_shape = ("whole", shape_of((tokens, width), low))
    if merged:
        gain_at = columns + columns // fold
        base = kv_send.shape[1]
        lanes = base + w_lanes
        keep, leaving, gains, _ = one(
            functools.partial(merge_kernel, gain_at),
            "add_first",
            [
                ("whole", keep_low),
                ("whole", keep_high),
                ("whole", send(kv_send, token_steps[-1])),
                ("whole", w_keep),
                ("whole", send(w_send, token_steps[-1])),
                ("whole", gains),
            ],
            [
                ("whole", shape_of((half // 2, lanes), low)),
                ("whole", shape_of((half // 2, lanes), low)),
                ("whole", shape_of(gains.shape, full)),
            ],
            [],
            2,
            late_marks[0],
        )
        keep, come, gains = scatter_halves(
            keep, leaving, token_steps[:-1], "add_chain", gains, base + gain_at, late_marks[1:]
        )
        input_grad, query_w_grad, key_w_grad, value_w_grad, gains, _ = one(
            functools.partial(final_kernel, base),
            "last_gradients",
            [("whole", keep), ("whole", come)] + ends + [("whole", gains)],
            [
                input_shape,
                ("whole", shape_of((1, query_weight.shape[1]), full)),
                ("whole", shape_of((1, key_weight.shape[1]), full)),
                ("whole", shape_of((1, value_weight.shape[1]), full)),
                ("whole", shape_of((2, width), full)),
            ],
            end_scratch,
            1,
        )
        gain_sums = (gains[0], gains[1])
    else:
        kv_keep = jnp.concatenate([keep_low, keep_high], axis=1)
        kv_sum = scatter_halves(kv_keep, kv_send, token_steps, "add_kv")
        qkv_sum = scatter_halves(w_keep, w_send, row_steps, "add_qkv")
        gains = lax.psum(gains, "ctx").reshape(2, width)
        gain_sums = (gains[0], gains[1])
        input_grad, _ = one(
            functools.partial(final_kernel, 0),
            "input_gradient",
            [("whole", kv_sum), ("whole", jnp.zeros_like(kv_sum))] + ends,
            [input_shape],
            end_scratch,
            1,
        )
        qkv_rows = unfold_rows(qkv_sum, columns, columns // fold)
        query_w_grad, key_w_grad, value_w_grad = (
            own_piece(qkv_rows[:, first:last], device, low_bits)
            for first, last in (
                (0, width),
                (width, width + KV_WIDTH),
                (width + KV_WIDTH, columns),
            )
        )

    def piece_of(piece_rows):
        return own_piece(piece_rows, device, low_bits)

    ff_rows = unfold_rows(late_sum, 2 * ff, ff_folded)
    down_rows = jnp.concatenate(
        [late_sum[:, down_at + a * width : down_at + (a + 1) * width] for a in range(device_groups)],
        axis=0,
    )
    output_rows = unfold_rows(late_sum[:, out_at:], width, width // fold)
    return (
        block_out,
        input_grad,
        gain_sums[0],
        query_w_grad,
        key_w_grad,
        value_w_grad,
        piece_of(output_rows),
        gain_sums[1],
        piece_of(ff_rows[:, :ff]),
        piece_of(ff_rows[:, ff:]),
        piece_of(down_rows),
    )


def solution(mesh):
    row = P("ctx", None)
    in_specs = (row, P(), row, row, row, row, P(), row, row, row, P(), P(), row)
    out_specs = (row, row, P(), row, row, row, row, P(), row, row, row)
    return jax.shard_map(body, mesh=mesh, in_specs=in_specs, out_specs=out_specs, check_vma=False)
```

```python
import functools

import jax
import jax.numpy as jnp
import numpy as np
from jax import lax
from jax.experimental import pallas as pl
from jax.experimental.pallas import tpu as pltpu
from jax.sharding import PartitionSpec as P

HEADS = 9
KV_HEADS = 3
GROUP = HEADS // KV_HEADS
HEAD_SIZE = 64
KV_WIDTH = KV_HEADS * HEAD_SIZE
TILE = 16
TOTAL, PEAK = HEAD_SIZE, HEAD_SIZE + 1

epsilon = 1e-05
rope_base = 100000.0
masked_score = -1e30

low = jnp.bfloat16
full = jnp.float32


def exchange_steps(device_count, low_bits):
    top = device_count.bit_length() - 1
    steps = []
    if low_bits == 0 and top >= 4:
        for bit in range(top - 1, 2, -1):
            steps.append([i ^ (1 << bit) for i in range(device_count)])
        steps.append([i ^ (4 if i & 1 else 2) for i in range(device_count)])
        steps.append([i ^ (2 if i & 1 else 4) for i in range(device_count)])
        steps.append([i ^ 1 for i in range(device_count)])
    else:
        for bit in range(top - 1, low_bits - 1, -1):
            steps.append([i ^ (1 << bit) for i in range(device_count)])
    return steps


def source_table(device_count, low_bits):
    held = [[d >> low_bits] for d in range(device_count)]
    for partner in exchange_steps(device_count, low_bits):
        held = [held[d] + held[partner[d]] for d in range(device_count)]
    return np.array(held, np.int32)


def send(values, partner):
    return lax.ppermute(values, "ctx", [(i, p) for i, p in enumerate(partner)])


def gather_halves(values, steps, name):
    for partner in steps[:-1]:
        values, _ = join(values, send(values, partner), name, [])
    return values, send(values, steps[-1])


def whole_rows(flat, device, low_bits, columns):
    for bit in range(low_bits):
        partner = [i ^ (1 << bit) for i in range(lax.axis_size("ctx"))]
        other = send(flat, partner)
        is_high = (device >> bit) & 1
        flat = jnp.concatenate(
            [jnp.where(is_high, other, flat), jnp.where(is_high, flat, other)], axis=1
        )
    return flat.reshape(-1, columns)


def own_piece(rows, device, low_bits):
    flat = rows.reshape(1, -1)
    for bit in range(low_bits - 1, -1, -1):
        partner = [i ^ (1 << bit) for i in range(lax.axis_size("ctx"))]
        half = flat.shape[1] // 2
        is_high = (device >> bit) & 1
        leaving = jnp.where(is_high, flat[:, :half], flat[:, half:]).astype(low)
        staying = jnp.where(is_high, flat[:, half:], flat[:, :half])
        flat = staying + send(leaving, partner).astype(full)
    return flat


def low_bits_of(piece, columns):
    low_bits = 0
    while (piece << low_bits) < TILE * columns:
        low_bits += 1
    return low_bits


def unfold_rows(packed, columns, folded):
    return jnp.concatenate(
        [packed[:, :columns], packed[:, columns : columns + folded].reshape(-1, columns)], axis=0
    )


def whole_lanes(columns):
    return -(-columns // 128) * 128


def dot(left, right):
    return jnp.dot(left, right, preferred_element_type=full)


def dot_right(left, right):
    return lax.dot_general(left, right, (((1,), (1,)), ((), ())), preferred_element_type=full)


def dot_left(left, right):
    return lax.dot_general(left, right, (((0,), (0,)), ((), ())), preferred_element_type=full)


def iota(shape, axis):
    return lax.broadcasted_iota(jnp.int32, shape, axis)


def mixing_of(feature_ref):
    width = feature_ref.shape[1]
    return (iota((width, width), 0) == feature_ref[...]).astype(full).astype(low)


def fold_scratch(main, part):
    return pltpu.VMEM((-(-part // 128), main, 128), full)


def fold_write(scratch, extra):
    for block in range(scratch.shape[0]):
        lanes = slice(block * 128, min(block * 128 + 128, extra.shape[1]))
        scratch[block, :, : lanes.stop - lanes.start] = extra[:, lanes].astype(full)


def fold_read(scratch, part):
    parts = [scratch[block] for block in range(scratch.shape[0])]
    return jnp.concatenate(parts, axis=1)[:, :part].astype(low)


def fold_get(scratch, at, fold, part):
    rows = pl.ds(at, scratch.shape[1] // fold, stride=fold)
    parts = [scratch.at[block][rows, :] for block in range(scratch.shape[0])]
    return jnp.concatenate(parts, axis=1)[:, :part].astype(low)


def fold_put(scratch, at, fold, value):
    rows = pl.ds(at, scratch.shape[1] // fold, stride=fold)
    missing = scratch.shape[0] * 128 - value.shape[1]
    if missing:
        value = jnp.concatenate([value, jnp.zeros((value.shape[0], missing), full)], axis=1)
    for block in range(scratch.shape[0]):
        scratch.at[block][rows, :] = value[:, block * 128 : (block + 1) * 128]


def as_row(column):
    return jnp.transpose(jnp.broadcast_to(column, (column.shape[0], 128)))[0:1]


def turn(values, rope, direction):
    half_dim = HEAD_SIZE // 2
    swapped = jnp.concatenate([values[:, half_dim:], values[:, :half_dim]], axis=1)
    sine = rope[:, 2 * HEAD_SIZE : 3 * HEAD_SIZE]
    return values * rope[:, :HEAD_SIZE] + swapped * (direction * sine)


def rope_of(cos_ref, sin_ref, times, part, quarter):
    _, places, _, lanes = cos_ref.shape
    value = cos_ref[part] * times[0, quarter] - sin_ref[part] * times[1, quarter]
    return value.reshape(places * TILE, lanes)


def rope_own_of(cos_ref, sin_ref, times):
    _, quarters, rows, lanes = times.shape
    parts = [
        cos_ref[part, 0] * times[0] - sin_ref[part, 0] * times[1] for part in range(2)
    ]
    return jnp.concatenate([part.reshape(quarters * rows, lanes) for part in parts], axis=0)


def unit_rows(values):
    inverse = lax.rsqrt(jnp.mean(values * values, axis=-1, keepdims=True) + epsilon)
    return values * inverse, inverse


def norm_back(unit, inverse, gain, grad):
    scaled = grad * gain
    return inverse * (scaled - unit * jnp.mean(scaled * unit, axis=-1, keepdims=True))


def query_range(own, part, rows, axis):
    shape = (rows, 1) if axis == 0 else (1, rows)
    half = rows // GROUP
    last_key = own[part] * half + lax.rem(iota(shape, axis), half)
    first_key = jnp.zeros(shape, jnp.int32) + own[2 + part] * half
    return first_key.astype(full), last_key.astype(full)


def fold_gains(rows):
    part = len(rows) * rows[0].shape[1] // TILE
    pieces = [
        row[:, at : at + part] for row in rows for at in range(0, row.shape[1], part)
    ]
    return jnp.concatenate(pieces, axis=0)


def sum_gains(gains, come):
    return gains.astype(low).astype(full) + come.astype(full)


class Call:
    def __init__(self, steps):
        self.steps = steps

    def spec(self, kind, shape):
        if kind == "smem":
            return pl.BlockSpec(memory_space=pltpu.SMEM)
        if kind == "token":
            return pl.BlockSpec(memory_space=pl.ANY)
        if self.steps == 1 or kind == "whole":
            return pl.BlockSpec(memory_space=pltpu.VMEM)
        rest = tuple(shape[1:])
        return pl.BlockSpec((shape[0] // self.steps,) + rest, lambda i: (i,) + (0,) * len(rest))

    def __call__(self, kernel, name, ins, outs, scratch, micros, after=(), vmem=16):
        steps = self.steps
        first, last, end = len(ins), len(ins) + len(after), len(ins) + len(after) + len(outs)

        def run(*refs):
            refs[end][...] = jnp.zeros_like(refs[end])
            used = refs[:first] + refs[last:end] + refs[end + 1 :]
            kernel(pl.program_id(0) if steps > 1 else 0, steps, *used)

        ins = list(ins) + [("token", token) for token in after]
        outs = list(outs) + [("whole", shape_of((8, 128), full))]
        return pl.pallas_call(
            run,
            grid=(steps,) if steps > 1 else (),
            in_specs=[self.spec(kind, a.shape) for kind, a in ins],
            out_specs=[self.spec(kind, s.shape) for kind, s in outs],
            out_shape=[s for _, s in outs],
            scratch_shapes=scratch,
            compiler_params=pltpu.CompilerParams(vmem_limit_bytes=vmem * 1024 * 1024),
            cost_estimate=pl.CostEstimate(
                flops=int(micros * steps * 1e9), bytes_accessed=1024, transcendentals=0
            ),
            name=name,
        )(*[a for _, a in ins])


one_call = Call(1)


def once(step, steps, at, action):
    if steps == 1:
        action()
    else:
        pl.when(step == at)(action)


def shape_of(shape, dtype):
    return jax.ShapeDtypeStruct(shape, dtype)


def join_kernel(step, steps, held_ref, come_ref, *outs):
    rows = held_ref.shape[0]
    lane = 0
    for out_ref in outs:
        lanes = slice(lane, lane + out_ref.shape[1])
        out_ref[:rows, :] = held_ref[:, lanes]
        out_ref[rows:, :] = come_ref[:, lanes]
        lane = lanes.stop


def copy_kernel(step, steps, held_ref, out_ref):
    out_ref[...] = held_ref[...]


def join(held, come, name, after, parts=()):
    rows, columns = held.shape
    if rows * columns > 2 << 20:
        return jnp.concatenate([held, come], axis=0), None
    return one_call(
        join_kernel,
        "join_" + name,
        [("whole", held), ("whole", come)],
        [("whole", shape_of((2 * rows, part), held.dtype)) for part in parts or (columns,)],
        [],
        1,
        after,
    )


def pack_kernel(step, steps, hidden_ref, gain_ref, *refs):
    packed_ref, normed_ref = refs[-2:]
    width = hidden_ref.shape[1]
    unit, _ = unit_rows(hidden_ref[...].astype(full))
    normed_ref[...] = (unit * gain_ref[...]).astype(low)
    for a in range(hidden_ref.shape[0] // TILE):
        packed_ref[:, a * width : (a + 1) * width] = normed_ref[a * TILE : (a + 1) * TILE, :]
    if len(refs) > 2:
        fold_projections(packed_ref, (a + 1) * width, width, refs[:-2])


def rows_in(ref, columns):
    value = ref[...].astype(full)
    if value.shape[1] == columns:
        return value
    pieces = [value[:, at : at + columns] for at in range(0, value.shape[1], columns)]
    return jnp.concatenate(pieces, axis=0)


def fold_into(out_ref, at, pieces):
    columns = sum(piece.shape[1] for piece in pieces)
    lane = at
    for piece in pieces:
        out_ref[:, lane : lane + piece.shape[1]] = piece[:TILE, :].astype(low)
        lane += piece.shape[1]
    tails = [piece[TILE:, :] for piece in pieces]
    tail = tails[0] if len(tails) == 1 else jnp.concatenate(tails, axis=1)
    fold = TILE // tail.shape[0]
    part = columns // fold
    rows = [
        tail[j : j + 1, block * part : (block + 1) * part]
        for j in range(tail.shape[0])
        for block in range(fold)
    ]
    out_ref[:, lane : lane + part] = jnp.concatenate(rows, axis=0).astype(low)
    return lane + part


def fold_projections(out_ref, at, width, refs):
    query_ref, key_ref, value_ref, output_ref = refs
    pieces = [rows_in(query_ref, width), rows_in(key_ref, KV_WIDTH), rows_in(value_ref, KV_WIDTH)]
    end = fold_into(out_ref, at, pieces)
    end = fold_into(out_ref, end, [rows_in(output_ref, width)])
    out_ref[:, end:] = jnp.zeros((TILE, out_ref.shape[1] - end), low)


def fold_projections_kernel(width, step, steps, *refs):
    fold_projections(refs[-1], 0, width, refs[:-1])


def fold_late_kernel(width, ff, step, steps, gate_ref, up_ref, down_ref, out_ref):
    lane = fold_into(out_ref, 0, [rows_in(gate_ref, ff), rows_in(up_ref, ff)])
    down = rows_in(down_ref, width)
    for a in range(down.shape[0] // TILE):
        out_ref[:, lane : lane + width] = down[a * TILE : (a + 1) * TILE].astype(low)
        lane += width
    out_ref[:, lane:] = jnp.zeros((TILE, out_ref.shape[1] - lane), low)


def weights_kernel(
    step, steps, feature_ref, own_ref, come_ref, weight_ref, key_value_ref, output_ref, mixed, *folds
):
    width, columns = weight_ref.shape
    half = own_ref.shape[0]
    main = 2 * half
    fold = main // (width - main)
    lane, first = 0, 0
    for scratch, count in zip(folds, (columns, width)):
        part = count // fold
        mixed[:half, first : first + count] = own_ref[:, lane : lane + count]
        mixed[half:main, first : first + count] = come_ref[:, lane : lane + count]
        lane += count
        folded = slice(lane, lane + part)
        fold_write(scratch, jnp.concatenate([own_ref[:, folded], come_ref[:, folded]], axis=0))
        for at in range(fold):
            lanes = slice(first + at * part, first + (at + 1) * part)
            mixed[main:, lanes] = fold_get(scratch, at, fold, part)
        lane += part
        first += count
    natural = dot(mixing_of(feature_ref), mixed[...])
    weight_ref[...] = natural[:, :columns].astype(low)
    output_ref[...] = natural[:, columns:].astype(low)
    keys = natural[:, width : width + KV_WIDTH]
    key_value_ref[:, :KV_WIDTH] = keys.astype(low)
    half_dim = HEAD_SIZE // 2
    swapped = [
        keys[:, (block ^ 1) * half_dim : ((block ^ 1) + 1) * half_dim]
        for block in range(KV_WIDTH // half_dim)
    ]
    key_value_ref[:, KV_WIDTH : 2 * KV_WIDTH] = jnp.concatenate(swapped, axis=1).astype(low)
    key_value_ref[:, 2 * KV_WIDTH :] = natural[:, width + KV_WIDTH : columns].astype(low)


def queries_kernel(step, steps, normed_ref, weight_ref, cos_ref, sin_ref, times, query_ref):
    tokens, width = normed_ref.shape
    half = tokens // 2
    queries = dot(normed_ref[...], weight_ref[:, :width])
    rope = rope_own_of(cos_ref, sin_ref, times)
    for head in range(HEADS):
        turned = turn(queries[:, head * HEAD_SIZE : (head + 1) * HEAD_SIZE], rope, 1.0)
        turned = turned.astype(low) * low(HEAD_SIZE**-0.5)
        for part in range(2):
            row = (part * GROUP + head % GROUP) * half
            query_ref[head // GROUP, row : row + half, :] = turned[part * half : (part + 1) * half]


def project_kernel(step, steps, normed_ref, weight_ref, cos_ref, sin_ref, times, kv_ref):
    width = weight_ref.shape[0]
    groups = normed_ref.shape[1] // width
    for a in range(groups):
        kv = dot(normed_ref[:, a * width : (a + 1) * width], weight_ref[...])
        rope = rope_of(cos_ref, sin_ref, times, a // (groups // 2), a % (groups // 2))
        cos, sin = rope[:, : 2 * HEAD_SIZE], rope[:, 2 * HEAD_SIZE :]
        cos = jnp.concatenate([cos, cos[:, :HEAD_SIZE]], axis=1)
        sin = jnp.concatenate([sin, sin[:, :HEAD_SIZE]], axis=1)
        keys = kv[:, :KV_WIDTH] * cos + kv[:, KV_WIDTH : 2 * KV_WIDTH] * sin
        at = a * 2 * KV_WIDTH
        kv_ref[:, at : at + KV_WIDTH] = keys.astype(low)
        kv_ref[:, at + KV_WIDTH : at + 2 * KV_WIDTH] = kv[:, 2 * KV_WIDTH :].astype(low)


def key_part(kv_ref, groups, column):
    lanes = [a * 2 * KV_WIDTH + column * HEAD_SIZE for a in groups]
    return jnp.concatenate([kv_ref[:, at : at + HEAD_SIZE] for at in lanes], axis=0)


def key_row(key_ref, part, groups):
    start = key_ref[part]
    return jnp.concatenate([start + float(i * TILE) for i in range(len(groups))], axis=1)


def reaches_low(own, blocks):
    return own[3] < blocks


def forward_kernel(
    is_first, low_blocks, step, steps, own, key_ref, query_ref, kv_ref, *rest
):
    state = rest[-1]
    rows = query_ref.shape[1] // 2
    groups = kv_ref.shape[1] // (2 * KV_WIDTH)

    def first():
        if is_first:
            lane = lax.broadcasted_iota(jnp.int32, state.shape, 2)
            state[...] = jnp.where(lane == PEAK, masked_score, 0.0)
        else:
            state[...] = rest[0][...]

    once(step, steps, 0, first)

    def attend(key_half, query_half):
        members = range(key_half * groups // 2, (key_half + 1) * groups // 2)
        at = slice(query_half * rows, (query_half + 1) * rows)
        key_index = key_row(key_ref, key_half, members)
        first_key, last_key = query_range(own, query_half, rows, 0)
        allowed = (key_index >= first_key) & (key_index <= last_key)
        for head in range(KV_HEADS):
            scores = dot_right(query_ref[head, at], key_part(kv_ref, members, head))
            masked = jnp.where(allowed, scores, masked_score)
            old = state[head, at, PEAK : PEAK + 1]
            new = jnp.maximum(old, jnp.max(masked, axis=1, keepdims=True))
            weights = jnp.where(allowed, jnp.exp(masked - new), 0.0)
            factor = jnp.exp(old - new)
            state[head, at, PEAK : PEAK + 1] = new
            state[head, at, TOTAL : TOTAL + 1] = state[
                head, at, TOTAL : TOTAL + 1
            ] * factor + jnp.sum(weights, axis=1, keepdims=True)
            state[head, at, :HEAD_SIZE] = state[head, at, :HEAD_SIZE] * factor + dot(
                weights.astype(low), key_part(kv_ref, members, KV_HEADS + head)
            )

    attend(0, 0)
    pl.when(reaches_low(own, low_blocks))(lambda: attend(0, 1))
    attend(1, 1)


def middle_kernel(
    step,
    steps,
    feature_ref,
    state_ref,
    hidden_ref,
    output_w,
    gain_ref,
    attention,
    attended,
    middle_ref,
    normed,
    normed_t,
    lse_ref,
    natural,
):
    mixing = mixing_of(feature_ref)
    tokens = hidden_ref.shape[0] // 2
    for head in range(KV_HEADS):
        sums = state_ref[head, :, TOTAL : TOTAL + 1]
        attention[head] = state_ref[head, :, :HEAD_SIZE] / sums
        logs = state_ref[head, :, PEAK : PEAK + 1] + jnp.log(sums)
        for part in range(2):
            lse_ref[2 * head + part] = as_row(
                logs[part * GROUP * tokens : (part + 1) * GROUP * tokens]
            )
    for h in range(HEADS):
        for part in range(2):
            row = (part * GROUP + h % GROUP) * tokens
            natural[
                part * tokens : (part + 1) * tokens, h * HEAD_SIZE : (h + 1) * HEAD_SIZE
            ] = attention[h // GROUP, row : row + tokens, :].astype(low)
    middle = hidden_ref[...].astype(full) + dot(natural[...], output_w[...])
    middle_ref[...] = middle
    unit, _ = unit_rows(middle)
    mixed_norm = dot((unit * gain_ref[...]).astype(low), mixing)
    normed[...] = mixed_norm.astype(low)
    normed_t[...] = jnp.transpose(mixed_norm).astype(low)
    attended[...] = dot(natural[...], mixing).astype(low)


def feedforward_kernel(
    step,
    steps,
    source_ref,
    feature_ref,
    attention,
    attended,
    middle_ref,
    normed,
    normed_t,
    output_w,
    gain_ref,
    grad_ref,
    own_ref,
    come_low_ref,
    come_high_ref,
    out_ref,
    grad_middle_ref,
    head_grad_ref,
    delta_ref,
    keep_ref,
    send_ref,
    gain_part_ref,
    come_ref,
    down_w,
    down_grad,
    total,
    grad_normed,
    extra_grad,
    output_folds,
    late_folds,
):
    rows, width = middle_ref.shape
    half = own_ref.shape[0]
    main = 2 * half
    rest = width - main
    fold = main // rest
    places = main // TILE
    ff = down_w.shape[0]
    chunk = 2 * ff // fold
    down_at = 2 * ff + chunk
    device_ff = ff // places
    groups = device_ff // TILE
    out_at = down_at + groups * width
    mixing = mixing_of(feature_ref)
    tokens = rows // 2
    part = width // fold
    folded = slice(out_at + width, out_at + width + part)
    come_ref[: half // 2, :] = come_low_ref[...]
    come_ref[half // 2 :, :] = come_high_ref[...]
    middle = middle_ref[...]
    gain = gain_ref[...]
    unit, inverse = unit_rows(middle)
    for place in range(places):
        held = own_ref if place < places // 2 else come_ref
        row = (place % (places // 2)) * TILE
        for a in range(groups):
            at = pl.multiple_of(source_ref[place] * device_ff + a * TILE, TILE)
            lane = down_at + a * width
            down_w[pl.ds(at, TILE), :] = held[row : row + TILE, lane : lane + width]
    total[...] = jnp.zeros_like(total)
    grad_normed[...] = jnp.zeros_like(grad_normed)
    out_grad = grad_ref[...]
    fold_write(
        late_folds,
        jnp.concatenate([own_ref[:, 2 * ff : down_at], come_ref[:, 2 * ff : down_at]], axis=0),
    )

    def advance(c, carry):
        gate_at = pl.ds(pl.multiple_of(c * chunk, 128), chunk)
        up_at = pl.ds(pl.multiple_of(ff + c * chunk, 128), chunk)

        def columns(lanes, at):
            tail = fold_get(late_folds, at, fold, chunk)
            value = (
                dot(normed[:, :half], own_ref[:, lanes])
                + dot(normed[:, half:main], come_ref[:, lanes])
                + dot(normed[:, main:], tail)
            )
            return value, tail

        gate, gate_tail = columns(gate_at, c)
        up, up_tail = columns(up_at, c + fold // 2)
        down_at_c = pl.ds(pl.multiple_of(c * chunk, 128), chunk)
        down = down_w[down_at_c, :]
        sigma = 1.0 / (1.0 + jnp.exp(-gate))
        silu = gate * sigma
        inner = (silu * up).astype(low)
        total[...] += dot(inner, down)
        grad_inner = dot_right(out_grad, down)
        grad_gate = (grad_inner * up * sigma * (1.0 + gate * (1.0 - sigma))).astype(low)
        grad_up = (grad_inner * silu).astype(low)
        down_grad[down_at_c, :] = dot_left(inner, out_grad).astype(low)
        for grad, lanes, tail, at in (
            (grad_gate, gate_at, gate_tail, c),
            (grad_up, up_at, up_tail, c + fold // 2),
        ):
            grad_normed[:, :half] += dot_right(grad, own_ref[:, lanes])
            grad_normed[:, half:main] += dot_right(grad, come_ref[:, lanes])
            grad_normed[:, main:] += dot_right(grad, tail)
            keep_ref[:, lanes] = dot(normed_t[:half], grad).astype(low)
            send_ref[:, lanes] = dot(normed_t[half:main], grad).astype(low)
            fold_put(extra_grad, at, fold, dot(normed_t[main:], grad))
        return carry

    lax.fori_loop(0, ff // chunk, advance, 0)
    out_ref[...] = (middle + total[...]).astype(low)
    extra = fold_read(extra_grad, chunk)
    keep_ref[:, 2 * ff : down_at] = extra[:half]
    send_ref[:, 2 * ff : down_at] = extra[half:]
    for place in range(places):
        held = keep_ref if place < places // 2 else send_ref
        row = (place % (places // 2)) * TILE
        for a in range(groups):
            at = pl.multiple_of(source_ref[place] * device_ff + a * TILE, TILE)
            lane = down_at + a * width
            held[row : row + TILE, lane : lane + width] = down_grad[pl.ds(at, TILE), :]

    high = grad_normed[...].astype(low)
    tail = (grad_normed[...] - high.astype(full)).astype(low)
    back = dot_right(high, mixing) + dot_right(tail, mixing)
    gain_part_ref[...] = jnp.sum(back * unit, axis=0, keepdims=True)
    grad_middle = out_grad.astype(full) + norm_back(unit, inverse, gain, back)
    grad_middle_ref[...] = grad_middle
    grad_branch = grad_middle.astype(low)
    output_grad = dot_left(attended[...], grad_branch)
    keep_ref[:, out_at : out_at + width] = output_grad[:half].astype(low)
    send_ref[:, out_at : out_at + width] = output_grad[half:main].astype(low)
    for at in range(fold):
        fold_put(output_folds, at, fold, output_grad[main:, at * part : (at + 1) * part])
    extra = fold_read(output_folds, part)
    unused = jnp.zeros((half, keep_ref.shape[1] - folded.stop), low)
    for held, rows_of_half in ((keep_ref, extra[:half]), (send_ref, extra[half:])):
        held[:, folded] = rows_of_half
        held[:, folded.stop :] = unused
    grad_low = dot_right(grad_branch, output_w[...]).astype(low)
    for head in range(KV_HEADS):
        for part in range(2):
            grads = jnp.concatenate(
                [
                    grad_low[
                        part * tokens : (part + 1) * tokens, h * HEAD_SIZE : (h + 1) * HEAD_SIZE
                    ]
                    for h in range(head * GROUP, (head + 1) * GROUP)
                ],
                axis=0,
            )
            at = slice(part * GROUP * tokens, (part + 1) * GROUP * tokens)
            head_grad_ref[head, at] = grads
            delta_ref[2 * head + part] = as_row(
                jnp.sum(grads.astype(full) * attention[head, at], axis=1, keepdims=True)
            )


def backward_kernel(
    is_first,
    key_half,
    low_blocks,
    joined,
    step,
    steps,
    own,
    key_ref,
    query_ref,
    grad_ref,
    lse_ref,
    delta_ref,
    kv_ref,
    tokens_ref,
    cos_ref,
    sin_ref,
    times,
    *rest,
):
    if not is_first:
        held, rest = rest[:2], rest[2:]
    base = 0
    if joined:
        low_ref, rest = rest[0], rest[1:]
        base = low_ref.shape[1]
        rest[2][:, :base] = low_ref[...]
    grad_query, grad_weight, out_ref, grad_kv = rest
    rows = query_ref.shape[1] // 2
    groups = kv_ref.shape[1] // (2 * KV_WIDTH)
    key_rows = kv_ref.shape[0]
    width = tokens_ref.shape[1] // groups
    members = range(key_half * groups // 2, (key_half + 1) * groups // 2)

    def first():
        if is_first:
            grad_query[...] = jnp.zeros_like(grad_query)
            grad_weight[...] = jnp.zeros_like(grad_weight)
        else:
            grad_query[...] = held[0][...]
            grad_weight[...] = held[1][...]

    once(step, steps, 0, first)
    key_index = key_row(key_ref, key_half, members)
    key_index = jnp.transpose(jnp.broadcast_to(key_index, (128, key_index.shape[1])))[:, 0:1]

    def attend(query_half, add):
        at = slice(query_half * rows, (query_half + 1) * rows)
        first_key, last_key = query_range(own, query_half, rows, 1)
        allowed = (key_index >= first_key) & (key_index <= last_key)
        for head in range(KV_HEADS):
            keys = key_part(kv_ref, members, head)
            scores = dot_right(keys, query_ref[head, at])
            probs = jnp.where(allowed, jnp.exp(scores - lse_ref[2 * head + query_half]), 0.0)
            d_probs = dot_right(key_part(kv_ref, members, KV_HEADS + head), grad_ref[head, at])
            d_scores = (probs * (d_probs - delta_ref[2 * head + query_half])).astype(low)
            grad_query[2 * head + query_half] += dot_left(keys, d_scores)
            parts = (
                (head, dot(d_scores, query_ref[head, at])),
                (KV_HEADS + head, dot(probs.astype(low), grad_ref[head, at])),
            )
            for column, value in parts:
                lanes = slice(column * HEAD_SIZE, (column + 1) * HEAD_SIZE)
                if add:
                    grad_kv[:, lanes] += value
                else:
                    grad_kv[:, lanes] = value

    if key_half == 0:
        attend(0, False)
        pl.when(reaches_low(own, low_blocks))(lambda: attend(1, True))
    else:
        attend(1, False)
    for i, a in enumerate(members):
        at = slice(i * key_rows, (i + 1) * key_rows)
        rope = rope_of(cos_ref, sin_ref, times, key_half, i)
        turned = jnp.concatenate(
            [
                turn(grad_kv[at, head * HEAD_SIZE : (head + 1) * HEAD_SIZE], rope, -1.0)
                for head in range(KV_HEADS)
            ]
            + [grad_kv[at, KV_WIDTH:]],
            axis=1,
        ).astype(low)
        lane = base + i * 2 * KV_WIDTH
        out_ref[:, lane : lane + 2 * KV_WIDTH] = turned
        grad_weight[...] += dot_left(turned, tokens_ref[:, a * width : (a + 1) * width])


def qkv_grad_kernel(
    step,
    steps,
    feature_ref,
    grad_query,
    grad_weight,
    normed_ref,
    weight_ref,
    cos_ref,
    sin_ref,
    times,
    gain_ref,
    gain_two_ref,
    query_grad_ref,
    gains_ref,
    keep_ref,
    send_ref,
    natural,
    folds,
):
    tokens, width = normed_ref.shape
    half = tokens // 2
    rope = rope_own_of(cos_ref, sin_ref, times)
    for head in range(KV_HEADS):
        rotated = [
            jnp.transpose(grad_query[2 * head + part]) * HEAD_SIZE**-0.5 for part in range(2)
        ]
        for g in range(GROUP):
            h = head * GROUP + g
            value = jnp.concatenate([part[g * half : (g + 1) * half] for part in rotated], axis=0)
            query_grad_ref[:, h * HEAD_SIZE : (h + 1) * HEAD_SIZE] = turn(value, rope, -1.0).astype(
                low
            )
    natural[:, :width] = dot_left(normed_ref[...], query_grad_ref[...])
    natural[:, width:] = jnp.transpose(grad_weight[...])
    products = natural[...] * weight_ref[...].astype(full)
    gain_part = as_row(jnp.sum(products, axis=1, keepdims=True)) / gain_ref[...]
    gains = fold_gains([gain_part, gain_two_ref[...]])
    gains_ref[...] = gains
    mixed = dot_left(mixing_of(feature_ref), natural[...].astype(low)).astype(low)
    columns = mixed.shape[1]
    rows = keep_ref.shape[0]
    main = 2 * rows
    fold = main // (width - main)
    part = columns // fold
    for at in range(fold):
        fold_put(folds, at, fold, mixed[main:, at * part : (at + 1) * part].astype(full))
    extra = fold_read(folds, part)
    unused = jnp.zeros((rows, keep_ref.shape[1] - columns - part), low)
    for held, at in ((keep_ref, 0), (send_ref, rows)):
        held[:rows, :columns] = mixed[at : at + rows]
        held[:rows, columns : columns + part] = extra[at : at + rows]
        held[:rows, columns + part :] = unused
    send_ref[:TILE, columns + part : columns + part + gains.shape[1]] = gains.astype(low)


def merge_kernel(gain_at, step, steps, *refs):
    keep_low, keep_high, kv_come, w_keep, w_come, gains_ref, keep_out, send_out, gains_out = refs
    half = w_keep.shape[0] // 2
    part = keep_low.shape[1]
    base = 2 * part
    lane = 0
    for keep, come, first in (
        (keep_low, kv_come, 0),
        (keep_high, kv_come, part),
        (w_keep, w_come, 0),
    ):
        columns = keep.shape[1]
        for out, at in ((keep_out, 0), (send_out, half)):
            value = keep[at : at + half, :].astype(full) + come[
                at : at + half, first : first + columns
            ].astype(full)
            out[:, lane : lane + columns] = value.astype(low)
        lane += columns
    lanes = slice(gain_at, gain_at + gains_ref.shape[1])
    gains = sum_gains(gains_ref[...], w_come[:TILE, lanes])
    gains_out[...] = gains
    send_out[:TILE, base + lanes.start : base + lanes.stop] = gains.astype(low)


def add_kernel(gain_at, step, steps, keep_ref, come_ref, *rest):
    rows = keep_ref.shape[0]
    if gain_at is not None:
        gains_ref, keep_out, send_out, gains_out = rest
        lanes = slice(gain_at, gain_at + gains_ref.shape[1])
        gains = sum_gains(gains_ref[...], come_ref[:TILE, lanes])
        gains_out[...] = gains
        rest = rest[1:-1]

    def tile(at):
        at = pl.ds(at, TILE)
        return keep_ref[at, :].astype(full) + come_ref[at, :].astype(full)

    if rows == TILE:
        rest[0][...] = tile(0)
        return
    keep_out, send_out = rest
    half = rows // 2

    def advance(i, carry):
        at = pl.multiple_of(i * TILE, TILE)
        keep_out[pl.ds(at, TILE), :] = tile(at).astype(low)
        send_out[pl.ds(at, TILE), :] = tile(pl.multiple_of(half + at, TILE)).astype(low)
        return carry

    lax.fori_loop(0, half // TILE, advance, 0)
    if gain_at is not None:
        send_out[:TILE, lanes] = gains.astype(low)


def scatter_halves(keep, leaving, steps, name, gains=None, gain_at=None, after=()):
    for at, partner in enumerate(reversed(steps)):
        come = send(leaving, partner)
        rows, columns = keep.shape
        ins = [("whole", keep), ("whole", come)]
        if rows == TILE:
            if gains is not None:
                return keep, come, gains
            outs = [("whole", shape_of((rows, columns), full))]
        else:
            outs = [("whole", shape_of((rows // 2, columns), low))] * 2
        if gains is not None:
            ins.append(("whole", gains))
            outs.append(("whole", shape_of(gains.shape, full)))
        result = one_call(
            functools.partial(add_kernel, gain_at),
            name,
            ins,
            outs,
            [],
            1,
            after[at] if at < len(after) else (),
        )
        if gains is not None:
            gains = result[-2]
        if rows == TILE:
            return result[0]
        keep, leaving = result[0], result[1]


def final_kernel(
    base,
    step,
    steps,
    keep_ref,
    come_ref,
    query_grad_ref,
    weight_ref,
    hidden_ref,
    gain_ref,
    grad_middle_ref,
    *rest,
):
    grads = rest[-1]
    tokens, width = hidden_ref.shape
    grads[:, :width] = query_grad_ref[...]
    for a in range(tokens // TILE):
        rows = slice(a * TILE, (a + 1) * TILE)
        lanes = slice(a * 2 * KV_WIDTH, (a + 1) * 2 * KV_WIDTH)
        value = keep_ref[:, lanes].astype(full) + come_ref[:, lanes].astype(full)
        grads[rows, width:] = value.astype(low)
    back = dot_right(grads[...], weight_ref[...])
    unit, inverse = unit_rows(hidden_ref[...].astype(full))
    out_ref = rest[-6] if base else rest[-2]
    out_ref[...] = (grad_middle_ref[...] + norm_back(unit, inverse, gain_ref[...], back)).astype(low)
    if not base:
        return
    gains_ref, _, query_out, key_out, value_out, gains_out, _ = rest
    columns = weight_ref.shape[1]
    total = keep_ref[:, base:].astype(full) + come_ref[:, base:].astype(full)
    fold = gains_ref.shape[0] // 2
    part = columns // fold
    for row in range(TILE + TILE // fold):
        if row < TILE:
            value = total[row : row + 1, :columns]
        else:
            at = (row - TILE) * fold
            value = jnp.concatenate(
                [total[at + i : at + i + 1, columns : columns + part] for i in range(fold)], axis=1
            )
        query_out[:, row * width : (row + 1) * width] = value[:, :width]
        for out, first in ((key_out, width), (value_out, width + KV_WIDTH)):
            out[:, row * KV_WIDTH : (row + 1) * KV_WIDTH] = value[:, first : first + KV_WIDTH]
    at = columns + part
    lanes = slice(at, at + gains_ref.shape[1])
    gains = sum_gains(gains_ref[...], come_ref[:TILE, base + lanes.start : base + lanes.stop])
    for k in range(2):
        gains_out[k : k + 1, :] = jnp.concatenate(
            [gains[k * fold + i : k * fold + i + 1] for i in range(fold)], axis=1
        )


def body(
    hidden_in,
    attention_gain,
    query_weight,
    key_weight,
    value_weight,
    output_weight,
    feedforward_gain,
    gate_weight,
    up_weight,
    down_weight,
    doc_of_block,
    pair_table,
    out_grad,
):
    tokens, width = hidden_in.shape
    half_rows = tokens // 2
    count = lax.axis_size("ctx")
    device = lax.axis_index("ctx")
    ff = gate_weight.shape[1] * count // width
    low_bits = low_bits_of(query_weight.shape[1], width)
    merged = low_bits == 0
    row_steps = exchange_steps(count, low_bits)
    token_steps = exchange_steps(count, 0)
    group_count = count >> low_bits
    group_rows = width // group_count
    groups = tokens // TILE
    steps = max(1, TILE * count // 512)
    places = count // (2 * steps)
    gain_one = attention_gain.reshape(1, width)
    gain_two = feedforward_gain.reshape(1, width)
    columns = width + 2 * KV_WIDTH
    main = TILE * group_count
    fold = main // (width - main)
    w_lanes = whole_lanes(columns + columns // fold + 2 * width // TILE)
    projection_lanes = whole_lanes((columns + width) + (columns + width) // fold)
    ff_folded = 2 * ff // fold
    down_at = 2 * ff + ff_folded
    device_groups = ff // group_count // TILE
    out_at = down_at + device_groups * width
    late_lanes = whole_lanes(out_at + width + width // fold)
    ff_lanes = whole_lanes(out_at)
    call = Call(steps)
    one = Call(1)

    def rows_of(piece, piece_columns):
        if low_bits:
            piece = whole_rows(piece, device, low_bits, piece_columns)
        return ("whole", piece)

    projections = [
        rows_of(query_weight, width),
        rows_of(key_weight, KV_WIDTH),
        rows_of(value_weight, KV_WIDTH),
        rows_of(output_weight, width),
    ]
    token_parts = (groups * width, projection_lanes) if merged else (groups * width,)
    packed, normed, pack_mark = one(
        pack_kernel,
        "norm_and_pack",
        [("whole", hidden_in), ("whole", gain_one)] + (projections if merged else []),
        [
            ("whole", shape_of((TILE, sum(token_parts)), low)),
            ("whole", shape_of((tokens, width), low)),
        ],
        [],
        1,
    )

    def table_row(table):
        return lax.dynamic_index_in_dim(jnp.asarray(table), device, 0, keepdims=False)

    sources = table_row(source_table(count, 0))
    group_table = source_table(count, low_bits)
    group_sources = table_row(group_table)
    inside = np.arange(group_rows)[None, None, :]
    features = group_table[:, :, None] * group_rows + inside
    features = np.concatenate(
        [
            features[:, :, :TILE].reshape(count, -1),
            features[:, :, TILE:].reshape(count, -1),
        ],
        axis=1,
    ).astype(np.int32)
    feature_row = table_row(features).reshape(1, width)

    device_iota = jnp.arange(count, dtype=jnp.int32)
    pairs = jnp.sum(
        jnp.where(sources[:, None] == device_iota[None, :], pair_table[None, :], 0), axis=1
    )
    blocks = jnp.stack([pairs, 2 * count - 1 - pairs], axis=1).reshape(-1)
    block_iota = jnp.arange(2 * count, dtype=jnp.int32)
    block_docs = jnp.sum(
        jnp.where(blocks[:, None] == block_iota[None, :], doc_of_block[None, :], 0), axis=1
    )
    doc_start = jnp.min(
        jnp.where(block_docs[:, None] == doc_of_block[None, :], block_iota[None, :], 2 * count),
        axis=1,
    )
    own = jnp.concatenate([blocks[:2], doc_start[:2]])

    def by_step(values):
        return values.reshape(2, steps, places, 2).transpose(0, 1, 3, 2)

    inner = jnp.arange(TILE, dtype=jnp.int32)
    key_index = by_step(blocks)[..., None] * half_rows + inner
    key_index = key_index.astype(full).reshape(2, 2 * steps, 1, -1)
    frequency = rope_base ** (-jnp.arange(HEAD_SIZE // 2, dtype=full) * (2.0 / HEAD_SIZE))
    block_angle = (by_step(blocks - doc_start) * half_rows).astype(full)[..., None] * frequency
    offset = jnp.arange(half_rows, dtype=full).reshape(groups // 2, TILE)
    offset_angle = offset[..., None] * frequency
    cos_in, sin_in = jnp.cos(offset_angle), jnp.sin(offset_angle)
    times_cos = jnp.concatenate([cos_in] * 4 + [-sin_in, sin_in] * 2, axis=-1)
    times_sin = jnp.concatenate([sin_in] * 4 + [cos_in, -cos_in] * 2, axis=-1)
    times = jnp.stack([times_cos, times_sin])
    block_cos = jnp.tile(jnp.cos(block_angle), 8).reshape(2, 2 * steps, places, 1, 4 * HEAD_SIZE)
    block_sin = jnp.tile(jnp.sin(block_angle), 8).reshape(2, 2 * steps, places, 1, 4 * HEAD_SIZE)
    rope_own = [
        ("whole", block_cos[0, :2, :1]),
        ("whole", block_sin[0, :2, :1]),
        ("whole", times),
    ]
    tables = [key_index, block_cos, block_sin, times, feature_row]
    late_at = 2
    late, before = one(
        functools.partial(fold_late_kernel, width, ff),
        "fold_late",
        [
            rows_of(gate_weight, ff),
            rows_of(up_weight, ff),
            rows_of(down_weight, width),
        ],
        [("whole", shape_of((TILE, ff_lanes), low))],
        [],
        1,
        [pack_mark],
    )
    for at, partner in enumerate(token_steps[:-1]):
        if late_at <= at < late_at + 2:
            late, before = join(late, send(late, row_steps[at - late_at]), "late", [])
        last = at == len(token_steps) - 2
        *held, mark = join(
            packed,
            send(packed, partner),
            "tokens",
            [before] if late_at <= at < late_at + 2 else [before] + tables if at == 1 else [],
            token_parts if last else (),
        )
        packed = held[0]
        if at == late_at - 1:
            late, _ = one(
                copy_kernel,
                "release_late",
                [("whole", late)],
                [("whole", shape_of(late.shape, low))],
                [],
                1,
                [mark],
            )
    token_own = packed
    if merged:
        w_own, w_come = held[1], send(held[1], token_steps[-1])
    else:
        qkv_piece, _ = one(
            functools.partial(fold_projections_kernel, width),
            "fold_projections",
            projections,
            [("whole", shape_of((TILE, projection_lanes), low))],
            [],
            1,
        )
        w_own, w_come = gather_halves(qkv_piece, row_steps, "qkv")
    token_come = send(token_own, token_steps[-1])

    halves = [
        (
            held,
            key_index[place],
            [("rows", block_cos[place]), ("rows", block_sin[place]), ("whole", times)],
        )
        for place, held in enumerate((token_own, token_come))
    ]

    rows = GROUP * tokens
    half = TILE * count // 2
    kv_shape = shape_of((half, groups * 2 * KV_WIDTH), low)
    head_shape = (KV_HEADS, rows, HEAD_SIZE)
    late, before = join(late, send(late, row_steps[late_at]), "late", [])
    weight, kv_weight, output_w, _ = one(
        weights_kernel,
        "qkv_weights",
        [("whole", feature_row), ("whole", w_own), ("whole", w_come)],
        [
            ("whole", shape_of((width, columns), low)),
            ("whole", shape_of((width, 3 * KV_WIDTH), low)),
            ("whole", shape_of((width, width), low)),
        ],
        [
            pltpu.VMEM((width, columns + width), low),
            fold_scratch(main, columns // fold),
            fold_scratch(main, width // fold),
        ],
        3,
    )
    queries, _ = one(
        queries_kernel,
        "queries",
        [("whole", normed), ("whole", weight)] + rope_own,
        [("whole", shape_of(head_shape, low))],
        [],
        2,
    )

    def project(place, after):
        token_rows, _, turns = halves[place]
        return call(
            project_kernel,
            "project",
            [("rows", token_rows), ("whole", kv_weight)] + turns,
            [("rows", kv_shape)],
            [],
            5,
            after,
        )

    state_shapes = [("whole", shape_of((KV_HEADS, rows, 2 * HEAD_SIZE), full))]

    def attend(place, kv, state, after):
        return call(
            functools.partial(forward_kernel, not state, count),
            "attention_forward",
            [
                ("smem", own),
                ("rows", halves[place][1]),
                ("whole", queries),
                ("rows", kv),
            ]
            + [("whole", held) for held in state],
            state_shapes,
            [],
            6,
            after,
        )

    kv_own, mark = project(0, [])

    *state, mark = attend(0, kv_own, [], [before])
    kv_come, mark = project(1, [mark])
    *state, mark = attend(1, kv_come, state, [])
    come_low = send(late, row_steps[-1])
    late_high, _ = one(
        copy_kernel,
        "release_high",
        [("whole", send(late, row_steps[-2]))],
        [("whole", shape_of(late.shape, low))],
        [],
        1,
        [mark],
    )
    come_high = send(late_high, row_steps[-1])
    late_own, mark = join(late, late_high, "late", [])

    row_shape = ("whole", shape_of((2 * KV_HEADS, 1, rows // 2), full))
    token_low = ("whole", shape_of((tokens, width), low))
    token_full = ("whole", shape_of((tokens, width), full))
    *inner_values, lse, _ = one(
        middle_kernel,
        "middle",
        [
            ("whole", feature_row),
            ("whole", state[0]),
            ("whole", hidden_in),
            ("whole", output_w),
            ("whole", gain_two),
        ],
        [
            ("whole", shape_of(head_shape, full)),
            token_low,
            token_full,
            token_low,
            ("whole", shape_of((width, tokens), low)),
            row_shape,
        ],
        [pltpu.VMEM((tokens, width), low)],
        3,
        [mark],
    )
    late_shape = shape_of((late_own.shape[0], late_lanes), low)
    block_out, grad_middle, head_grads, delta, late_keep, late_send, gain_two_part, _ = one(
        feedforward_kernel,
        "feedforward",
        [
            ("smem", group_sources),
            ("whole", feature_row),
        ]
        + [("whole", held) for held in inner_values]
        + [
            ("whole", output_w),
            ("whole", gain_two),
            ("whole", out_grad),
            ("whole", late_own),
            ("whole", come_low),
            ("whole", come_high),
        ],
        [
            token_low,
            token_full,
            ("whole", shape_of(head_shape, low)),
            row_shape,
            ("whole", late_shape),
            ("whole", late_shape),
            ("whole", shape_of((1, width), full)),
        ],
        [
            pltpu.VMEM(late_own.shape, low),
            pltpu.VMEM((ff, width), low),
            pltpu.VMEM((ff, width), low),
            pltpu.VMEM((tokens, width), full),
            pltpu.VMEM((tokens, width), full),
            fold_scratch(main, ff_folded),
            fold_scratch(main, width // fold),
            fold_scratch(main, ff_folded),
        ],
        11,
        vmem=24,
    )

    def attend_back(place, key_half, kv, carried, after, joined=()):
        token_rows, keys, turns = halves[place]
        return call(
            functools.partial(backward_kernel, not carried, key_half, count, bool(joined)),
            "attention_backward",
            [
                ("smem", own),
                ("rows", keys),
                ("whole", queries),
                ("whole", head_grads),
                ("whole", lse),
                ("whole", delta),
                ("rows", kv),
                ("rows", token_rows),
            ]
            + turns
            + [("whole", held) for held in carried]
            + [("rows", part) for part in joined],
            [
                ("whole", shape_of((2 * KV_HEADS, HEAD_SIZE, rows // 2), full)),
                ("whole", shape_of((2 * KV_WIDTH, width), full)),
                ("rows", shape_of((half, groups * KV_WIDTH * (1 + len(joined))), low)),
            ],
            [pltpu.VMEM((groups // 2 * places * TILE, 2 * KV_WIDTH), full)],
            6,
            after,
        )

    late_steps = row_steps[::-1]
    keep, leaving = late_keep, late_send

    def add_late(at, after):
        come = send(leaving, late_steps[at])
        part = shape_of((keep.shape[0] // 2, late_lanes), low)
        outs = [part, part] if keep.shape[0] > TILE else [shape_of((TILE, late_lanes), full)]
        return one(
            functools.partial(add_kernel, None),
            "add_late",
            [("whole", keep), ("whole", come)],
            [("whole", out) for out in outs],
            [],
            1,
            after,
        )

    *carried, send_low, mark = attend_back(1, 0, kv_come, [], [])
    keep, leaving, late_mark = add_late(0, [mark])
    *carried, kv_send, mark = attend_back(1, 1, kv_come, carried, [late_mark], [send_low])
    *carried, keep_low, mark = attend_back(0, 0, kv_own, carried, [])
    *carried, keep_high, mark = attend_back(0, 1, kv_own, carried, [])
    query_grad, gains, w_keep, w_send, mark = one(
        qkv_grad_kernel,
        "qkv_gradients",
        [
            ("whole", feature_row),
            ("whole", carried[0]),
            ("whole", carried[1]),
            ("whole", normed),
            ("whole", weight),
        ]
        + rope_own
        + [
            ("whole", gain_one),
            ("whole", gain_two_part),
        ],
        [
            ("whole", shape_of((tokens, width), low)),
            ("whole", shape_of((TILE, 2 * width // TILE), full)),
            ("whole", shape_of((main // 2, w_lanes), low)),
            ("whole", shape_of((main // 2, w_lanes), low)),
        ],
        [pltpu.VMEM((width, columns), full), fold_scratch(main, columns // fold)],
        3,
    )
    late_marks = []
    for at in range(1, len(late_steps)):
        result = add_late(at, [mark] if at == 1 else [])
        keep, leaving = result[0], result[1]
        late_marks.append([result[-1]])
    late_sum = keep

    ends = [
        ("whole", query_grad),
        ("whole", weight),
        ("whole", hidden_in),
        ("whole", gain_one),
        ("whole", grad_middle),
    ]
    end_scratch = [pltpu.VMEM((tokens, columns), low)]
    input_shape = ("whole", shape_of((tokens, width), low))
    if merged:
        gain_at = columns + columns // fold
        base = kv_send.shape[1]
        lanes = base + w_lanes
        keep, leaving, gains, _ = one(
            functools.partial(merge_kernel, gain_at),
            "add_first",
            [
                ("whole", keep_low),
                ("whole", keep_high),
                ("whole", send(kv_send, token_steps[-1])),
                ("whole", w_keep),
                ("whole", send(w_send, token_steps[-1])),
                ("whole", gains),
            ],
            [
                ("whole", shape_of((half // 2, lanes), low)),
                ("whole", shape_of((half // 2, lanes), low)),
                ("whole", shape_of(gains.shape, full)),
            ],
            [],
            2,
            late_marks[1],
        )
        keep, come, gains = scatter_halves(
            keep, leaving, token_steps[:-1], "add_chain", gains, base + gain_at, late_marks[2:]
        )
        input_grad, query_w_grad, key_w_grad, value_w_grad, gains, _ = one(
            functools.partial(final_kernel, base),
            "last_gradients",
            [("whole", keep), ("whole", come)] + ends + [("whole", gains)],
            [
                input_shape,
                ("whole", shape_of((1, query_weight.shape[1]), full)),
                ("whole", shape_of((1, key_weight.shape[1]), full)),
                ("whole", shape_of((1, value_weight.shape[1]), full)),
                ("whole", shape_of((2, width), full)),
            ],
            end_scratch,
            1,
        )
        gain_sums = (gains[0], gains[1])
    else:
        kv_keep = jnp.concatenate([keep_low, keep_high], axis=1)
        kv_sum = scatter_halves(kv_keep, kv_send, token_steps, "add_kv")
        qkv_sum = scatter_halves(w_keep, w_send, row_steps, "add_qkv")
        gains = lax.psum(gains, "ctx").reshape(2, width)
        gain_sums = (gains[0], gains[1])
        input_grad, _ = one(
            functools.partial(final_kernel, 0),
            "input_gradient",
            [("whole", kv_sum), ("whole", jnp.zeros_like(kv_sum))] + ends,
            [input_shape],
            end_scratch,
            1,
        )
        qkv_rows = unfold_rows(qkv_sum, columns, columns // fold)
        query_w_grad, key_w_grad, value_w_grad = (
            own_piece(qkv_rows[:, first:last], device, low_bits)
            for first, last in (
                (0, width),
                (width, width + KV_WIDTH),
                (width + KV_WIDTH, columns),
            )
        )

    def piece_of(piece_rows):
        return own_piece(piece_rows, device, low_bits)

    ff_rows = unfold_rows(late_sum, 2 * ff, ff_folded)
    down_rows = jnp.concatenate(
        [late_sum[:, down_at + a * width : down_at + (a + 1) * width] for a in range(device_groups)],
        axis=0,
    )
    output_rows = unfold_rows(late_sum[:, out_at:], width, width // fold)
    return (
        block_out,
        input_grad,
        gain_sums[0],
        query_w_grad,
        key_w_grad,
        value_w_grad,
        piece_of(output_rows),
        gain_sums[1],
        piece_of(ff_rows[:, :ff]),
        piece_of(ff_rows[:, ff:]),
        piece_of(down_rows),
    )


def solution(mesh):
    row = P("ctx", None)
    in_specs = (row, P(), row, row, row, row, P(), row, row, row, P(), P(), row)
    out_specs = (row, row, P(), row, row, row, row, P(), row, row, row)
    return jax.shard_map(body, mesh=mesh, in_specs=in_specs, out_specs=out_specs, check_vma=False)
```

```python
import functools

import jax
import jax.numpy as jnp
import numpy as np
from jax import lax
from jax.experimental import pallas as pl
from jax.experimental.pallas import tpu as pltpu
from jax.sharding import PartitionSpec as P

HEADS = 9
KV_HEADS = 3
GROUP = HEADS // KV_HEADS
HEAD_SIZE = 64
KV_WIDTH = KV_HEADS * HEAD_SIZE
TILE = 16
TOTAL, PEAK = HEAD_SIZE, HEAD_SIZE + 1

epsilon = 1e-05
rope_base = 100000.0
masked_score = -1e30

low = jnp.bfloat16
full = jnp.float32


def exchange_steps(device_count, low_bits):
    top = device_count.bit_length() - 1
    steps = []
    if low_bits == 0 and top >= 4:
        for bit in range(top - 1, 2, -1):
            steps.append([i ^ (1 << bit) for i in range(device_count)])
        steps.append([i ^ (4 if i & 1 else 2) for i in range(device_count)])
        steps.append([i ^ (2 if i & 1 else 4) for i in range(device_count)])
        steps.append([i ^ 1 for i in range(device_count)])
    else:
        for bit in range(top - 1, low_bits - 1, -1):
            steps.append([i ^ (1 << bit) for i in range(device_count)])
    return steps


def source_table(device_count, low_bits, steps):
    held = [[d >> low_bits] for d in range(device_count)]
    for partner in steps:
        held = [held[d] + held[partner[d]] for d in range(device_count)]
    return np.array(held, np.int32)


def send(values, partner):
    return lax.ppermute(values, "ctx", [(i, p) for i, p in enumerate(partner)])


def gather_halves(values, steps, name):
    for partner in steps[:-1]:
        values, _ = join(values, send(values, partner), name, [])
    return values, send(values, steps[-1])


def whole_rows(flat, device, low_bits, columns):
    for bit in range(low_bits):
        partner = [i ^ (1 << bit) for i in range(lax.axis_size("ctx"))]
        other = send(flat, partner)
        is_high = (device >> bit) & 1
        flat = jnp.concatenate(
            [jnp.where(is_high, other, flat), jnp.where(is_high, flat, other)], axis=1
        )
    return flat.reshape(-1, columns)


def own_piece(rows, device, low_bits):
    flat = rows.reshape(1, -1)
    for bit in range(low_bits - 1, -1, -1):
        partner = [i ^ (1 << bit) for i in range(lax.axis_size("ctx"))]
        half = flat.shape[1] // 2
        is_high = (device >> bit) & 1
        leaving = jnp.where(is_high, flat[:, :half], flat[:, half:]).astype(low)
        staying = jnp.where(is_high, flat[:, half:], flat[:, :half])
        flat = staying + send(leaving, partner).astype(full)
    return flat


def low_bits_of(piece, columns):
    low_bits = 0
    while (piece << low_bits) < TILE * columns:
        low_bits += 1
    return low_bits


def unfold_rows(packed, columns, folded):
    return jnp.concatenate(
        [packed[:, :columns], packed[:, columns : columns + folded].reshape(-1, columns)], axis=0
    )


def whole_lanes(columns):
    return -(-columns // 128) * 128


def dot(left, right):
    return jnp.dot(left, right, preferred_element_type=full)


def dot_right(left, right):
    return lax.dot_general(left, right, (((1,), (1,)), ((), ())), preferred_element_type=full)


def dot_left(left, right):
    return lax.dot_general(left, right, (((0,), (0,)), ((), ())), preferred_element_type=full)


def iota(shape, axis):
    return lax.broadcasted_iota(jnp.int32, shape, axis)


def mixing_of(feature_ref):
    width = feature_ref.shape[1]
    return (iota((width, width), 0) == feature_ref[...]).astype(full).astype(low)


def fold_scratch(main, part):
    return pltpu.VMEM((-(-part // 128), main, 128), full)


def fold_write(scratch, extra):
    for block in range(scratch.shape[0]):
        lanes = slice(block * 128, min(block * 128 + 128, extra.shape[1]))
        scratch[block, :, : lanes.stop - lanes.start] = extra[:, lanes].astype(full)


def fold_read(scratch, part):
    parts = [scratch[block] for block in range(scratch.shape[0])]
    return jnp.concatenate(parts, axis=1)[:, :part].astype(low)


def fold_get(scratch, at, fold, part):
    rows = pl.ds(at, scratch.shape[1] // fold, stride=fold)
    parts = [scratch.at[block][rows, :] for block in range(scratch.shape[0])]
    return jnp.concatenate(parts, axis=1)[:, :part].astype(low)


def fold_put(scratch, at, fold, value):
    rows = pl.ds(at, scratch.shape[1] // fold, stride=fold)
    missing = scratch.shape[0] * 128 - value.shape[1]
    if missing:
        value = jnp.concatenate([value, jnp.zeros((value.shape[0], missing), full)], axis=1)
    for block in range(scratch.shape[0]):
        scratch.at[block][rows, :] = value[:, block * 128 : (block + 1) * 128]


def as_row(column):
    return jnp.transpose(jnp.broadcast_to(column, (column.shape[0], 128)))[0:1]


def turn(values, rope, direction):
    half_dim = HEAD_SIZE // 2
    swapped = jnp.concatenate([values[:, half_dim:], values[:, :half_dim]], axis=1)
    sine = rope[:, 2 * HEAD_SIZE : 3 * HEAD_SIZE]
    return values * rope[:, :HEAD_SIZE] + swapped * (direction * sine)


def rope_of(cos_ref, sin_ref, times, part, quarter):
    _, places, _, lanes = cos_ref.shape
    value = cos_ref[part] * times[0, quarter] - sin_ref[part] * times[1, quarter]
    return value.reshape(places * TILE, lanes)


def rope_own_of(cos_ref, sin_ref, times):
    _, quarters, rows, lanes = times.shape
    parts = [
        cos_ref[part, 0] * times[0] - sin_ref[part, 0] * times[1] for part in range(2)
    ]
    return jnp.concatenate([part.reshape(quarters * rows, lanes) for part in parts], axis=0)


def unit_rows(values):
    inverse = lax.rsqrt(jnp.mean(values * values, axis=-1, keepdims=True) + epsilon)
    return values * inverse, inverse


def norm_back(unit, inverse, gain, grad):
    scaled = grad * gain
    return inverse * (scaled - unit * jnp.mean(scaled * unit, axis=-1, keepdims=True))


def query_range(own, part, rows, axis):
    shape = (rows, 1) if axis == 0 else (1, rows)
    half = rows // GROUP
    last_key = own[part] * half + lax.rem(iota(shape, axis), half)
    first_key = jnp.zeros(shape, jnp.int32) + own[2 + part] * half
    return first_key.astype(full), last_key.astype(full)


def fold_gains(rows):
    part = len(rows) * rows[0].shape[1] // TILE
    pieces = [
        row[:, at : at + part] for row in rows for at in range(0, row.shape[1], part)
    ]
    return jnp.concatenate(pieces, axis=0)


def sum_gains(gains, come):
    return gains.astype(low).astype(full) + come.astype(full)


class Call:
    def __init__(self, steps):
        self.steps = steps

    def spec(self, kind, shape):
        if kind == "smem":
            return pl.BlockSpec(memory_space=pltpu.SMEM)
        if kind == "token":
            return pl.BlockSpec(memory_space=pl.ANY)
        if self.steps == 1 or kind == "whole":
            return pl.BlockSpec(memory_space=pltpu.VMEM)
        rest = tuple(shape[1:])
        return pl.BlockSpec((shape[0] // self.steps,) + rest, lambda i: (i,) + (0,) * len(rest))

    def __call__(self, kernel, name, ins, outs, scratch, micros, after=(), vmem=16):
        steps = self.steps
        first, last, end = len(ins), len(ins) + len(after), len(ins) + len(after) + len(outs)

        def run(*refs):
            refs[end][...] = jnp.zeros_like(refs[end])
            used = refs[:first] + refs[last:end] + refs[end + 1 :]
            kernel(pl.program_id(0) if steps > 1 else 0, steps, *used)

        ins = list(ins) + [("token", token) for token in after]
        outs = list(outs) + [("whole", shape_of((8, 128), full))]
        return pl.pallas_call(
            run,
            grid=(steps,) if steps > 1 else (),
            in_specs=[self.spec(kind, a.shape) for kind, a in ins],
            out_specs=[self.spec(kind, s.shape) for kind, s in outs],
            out_shape=[s for _, s in outs],
            scratch_shapes=scratch,
            compiler_params=pltpu.CompilerParams(vmem_limit_bytes=vmem * 1024 * 1024),
            cost_estimate=pl.CostEstimate(
                flops=int(micros * steps * 1e9), bytes_accessed=1024, transcendentals=0
            ),
            name=name,
        )(*[a for _, a in ins])


one_call = Call(1)


def once(step, steps, at, action):
    if steps == 1:
        action()
    else:
        pl.when(step == at)(action)


def shape_of(shape, dtype):
    return jax.ShapeDtypeStruct(shape, dtype)


def join_kernel(step, steps, held_ref, come_ref, *outs):
    rows = held_ref.shape[0]
    lane = 0
    for out_ref in outs:
        lanes = slice(lane, lane + out_ref.shape[1])
        out_ref[:rows, :] = held_ref[:, lanes]
        out_ref[rows:, :] = come_ref[:, lanes]
        lane = lanes.stop


def copy_kernel(step, steps, held_ref, out_ref):
    out_ref[...] = held_ref[...]


def join(held, come, name, after, parts=()):
    rows, columns = held.shape
    if rows * columns > 2 << 20:
        return jnp.concatenate([held, come], axis=0), None
    return one_call(
        join_kernel,
        "join_" + name,
        [("whole", held), ("whole", come)],
        [("whole", shape_of((2 * rows, part), held.dtype)) for part in parts or (columns,)],
        [],
        1,
        after,
    )


def pack_kernel(step, steps, hidden_ref, gain_ref, *refs):
    packed_ref, normed_ref = refs[-2:]
    width = hidden_ref.shape[1]
    unit, _ = unit_rows(hidden_ref[...].astype(full))
    normed_ref[...] = (unit * gain_ref[...]).astype(low)
    for a in range(hidden_ref.shape[0] // TILE):
        packed_ref[:, a * width : (a + 1) * width] = normed_ref[a * TILE : (a + 1) * TILE, :]
    if len(refs) > 2:
        fold_projections(packed_ref, (a + 1) * width, width, refs[:-2])


def rows_in(ref, columns):
    value = ref[...].astype(full)
    if value.shape[1] == columns:
        return value
    pieces = [value[:, at : at + columns] for at in range(0, value.shape[1], columns)]
    return jnp.concatenate(pieces, axis=0)


def fold_into(out_ref, at, pieces):
    columns = sum(piece.shape[1] for piece in pieces)
    lane = at
    for piece in pieces:
        out_ref[:, lane : lane + piece.shape[1]] = piece[:TILE, :].astype(low)
        lane += piece.shape[1]
    tails = [piece[TILE:, :] for piece in pieces]
    tail = tails[0] if len(tails) == 1 else jnp.concatenate(tails, axis=1)
    fold = TILE // tail.shape[0]
    part = columns // fold
    rows = [
        tail[j : j + 1, block * part : (block + 1) * part]
        for j in range(tail.shape[0])
        for block in range(fold)
    ]
    out_ref[:, lane : lane + part] = jnp.concatenate(rows, axis=0).astype(low)
    return lane + part


def fold_projections(out_ref, at, width, refs):
    query_ref, key_ref, value_ref, output_ref = refs
    pieces = [rows_in(query_ref, width), rows_in(key_ref, KV_WIDTH), rows_in(value_ref, KV_WIDTH)]
    end = fold_into(out_ref, at, pieces)
    end = fold_into(out_ref, end, [rows_in(output_ref, width)])
    out_ref[:, end:] = jnp.zeros((TILE, out_ref.shape[1] - end), low)


def fold_projections_kernel(width, step, steps, *refs):
    fold_projections(refs[-1], 0, width, refs[:-1])


def fold_gates_kernel(ff, step, steps, gate_ref, up_ref, out_ref):
    lane = fold_into(out_ref, 0, [rows_in(gate_ref, ff), rows_in(up_ref, ff)])
    if lane < out_ref.shape[1]:
        out_ref[:, lane:] = jnp.zeros((TILE, out_ref.shape[1] - lane), low)


def fold_down_kernel(width, step, steps, down_ref, out_ref):
    down = rows_in(down_ref, width)
    lane = 0
    for a in range(down.shape[0] // TILE):
        out_ref[:, lane : lane + width] = down[a * TILE : (a + 1) * TILE].astype(low)
        lane += width
    out_ref[:, lane:] = jnp.zeros((TILE, out_ref.shape[1] - lane), low)


def weights_kernel(
    step, steps, feature_ref, own_ref, come_ref, weight_ref, key_value_ref, output_ref, mixed, *folds
):
    width, columns = weight_ref.shape
    half = own_ref.shape[0]
    main = 2 * half
    fold = main // (width - main)
    lane, first = 0, 0
    for scratch, count in zip(folds, (columns, width)):
        part = count // fold
        mixed[:half, first : first + count] = own_ref[:, lane : lane + count]
        mixed[half:main, first : first + count] = come_ref[:, lane : lane + count]
        lane += count
        folded = slice(lane, lane + part)
        fold_write(scratch, jnp.concatenate([own_ref[:, folded], come_ref[:, folded]], axis=0))
        for at in range(fold):
            lanes = slice(first + at * part, first + (at + 1) * part)
            mixed[main:, lanes] = fold_get(scratch, at, fold, part)
        lane += part
        first += count
    natural = dot(mixing_of(feature_ref), mixed[...])
    weight_ref[...] = natural[:, :columns].astype(low)
    output_ref[...] = natural[:, columns:].astype(low)
    keys = natural[:, width : width + KV_WIDTH]
    key_value_ref[:, :KV_WIDTH] = keys.astype(low)
    half_dim = HEAD_SIZE // 2
    swapped = [
        keys[:, (block ^ 1) * half_dim : ((block ^ 1) + 1) * half_dim]
        for block in range(KV_WIDTH // half_dim)
    ]
    key_value_ref[:, KV_WIDTH : 2 * KV_WIDTH] = jnp.concatenate(swapped, axis=1).astype(low)
    key_value_ref[:, 2 * KV_WIDTH :] = natural[:, width + KV_WIDTH : columns].astype(low)


def queries_kernel(step, steps, normed_ref, weight_ref, cos_ref, sin_ref, times, query_ref):
    tokens, width = normed_ref.shape
    half = tokens // 2
    queries = dot(normed_ref[...], weight_ref[:, :width])
    rope = rope_own_of(cos_ref, sin_ref, times)
    for head in range(HEADS):
        turned = turn(queries[:, head * HEAD_SIZE : (head + 1) * HEAD_SIZE], rope, 1.0)
        turned = turned.astype(low) * low(HEAD_SIZE**-0.5)
        for part in range(2):
            row = (part * GROUP + head % GROUP) * half
            query_ref[head // GROUP, row : row + half, :] = turned[part * half : (part + 1) * half]


def project_kernel(step, steps, normed_ref, weight_ref, cos_ref, sin_ref, times, kv_ref):
    width = weight_ref.shape[0]
    groups = normed_ref.shape[1] // width
    for a in range(groups):
        kv = dot(normed_ref[:, a * width : (a + 1) * width], weight_ref[...])
        rope = rope_of(cos_ref, sin_ref, times, a // (groups // 2), a % (groups // 2))
        cos, sin = rope[:, : 2 * HEAD_SIZE], rope[:, 2 * HEAD_SIZE :]
        cos = jnp.concatenate([cos, cos[:, :HEAD_SIZE]], axis=1)
        sin = jnp.concatenate([sin, sin[:, :HEAD_SIZE]], axis=1)
        keys = kv[:, :KV_WIDTH] * cos + kv[:, KV_WIDTH : 2 * KV_WIDTH] * sin
        at = a * 2 * KV_WIDTH
        kv_ref[:, at : at + KV_WIDTH] = keys.astype(low)
        kv_ref[:, at + KV_WIDTH : at + 2 * KV_WIDTH] = kv[:, 2 * KV_WIDTH :].astype(low)


def key_part(kv_ref, groups, column):
    lanes = [a * 2 * KV_WIDTH + column * HEAD_SIZE for a in groups]
    return jnp.concatenate([kv_ref[:, at : at + HEAD_SIZE] for at in lanes], axis=0)


def key_row(key_ref, part, groups):
    start = key_ref[part]
    return jnp.concatenate([start + float(i * TILE) for i in range(len(groups))], axis=1)


def reaches_low(own, blocks):
    return own[3] < blocks


def forward_kernel(
    is_first, low_blocks, step, steps, own, key_ref, query_ref, kv_ref, *rest
):
    state = rest[-1]
    rows = query_ref.shape[1] // 2
    groups = kv_ref.shape[1] // (2 * KV_WIDTH)

    def first():
        if is_first:
            lane = lax.broadcasted_iota(jnp.int32, state.shape, 2)
            state[...] = jnp.where(lane == PEAK, masked_score, 0.0)
        else:
            state[...] = rest[0][...]

    once(step, steps, 0, first)

    def attend(key_half, query_half):
        members = range(key_half * groups // 2, (key_half + 1) * groups // 2)
        at = slice(query_half * rows, (query_half + 1) * rows)
        key_index = key_row(key_ref, key_half, members)
        first_key, last_key = query_range(own, query_half, rows, 0)
        allowed = (key_index >= first_key) & (key_index <= last_key)
        for head in range(KV_HEADS):
            scores = dot_right(query_ref[head, at], key_part(kv_ref, members, head))
            masked = jnp.where(allowed, scores, masked_score)
            old = state[head, at, PEAK : PEAK + 1]
            new = jnp.maximum(old, jnp.max(masked, axis=1, keepdims=True))
            weights = jnp.where(allowed, jnp.exp(masked - new), 0.0)
            factor = jnp.exp(old - new)
            state[head, at, PEAK : PEAK + 1] = new
            state[head, at, TOTAL : TOTAL + 1] = state[
                head, at, TOTAL : TOTAL + 1
            ] * factor + jnp.sum(weights, axis=1, keepdims=True)
            state[head, at, :HEAD_SIZE] = state[head, at, :HEAD_SIZE] * factor + dot(
                weights.astype(low), key_part(kv_ref, members, KV_HEADS + head)
            )

    attend(0, 0)
    pl.when(reaches_low(own, low_blocks))(lambda: attend(0, 1))
    attend(1, 1)


def middle_kernel(
    step,
    steps,
    feature_ref,
    state_ref,
    hidden_ref,
    output_w,
    gain_ref,
    attention,
    attended,
    middle_ref,
    normed,
    normed_t,
    lse_ref,
    natural,
):
    mixing = mixing_of(feature_ref)
    tokens = hidden_ref.shape[0] // 2
    for head in range(KV_HEADS):
        sums = state_ref[head, :, TOTAL : TOTAL + 1]
        attention[head] = state_ref[head, :, :HEAD_SIZE] / sums
        logs = state_ref[head, :, PEAK : PEAK + 1] + jnp.log(sums)
        for part in range(2):
            lse_ref[2 * head + part] = as_row(
                logs[part * GROUP * tokens : (part + 1) * GROUP * tokens]
            )
    for h in range(HEADS):
        for part in range(2):
            row = (part * GROUP + h % GROUP) * tokens
            natural[
                part * tokens : (part + 1) * tokens, h * HEAD_SIZE : (h + 1) * HEAD_SIZE
            ] = attention[h // GROUP, row : row + tokens, :].astype(low)
    middle = hidden_ref[...].astype(full) + dot(natural[...], output_w[...])
    middle_ref[...] = middle
    unit, _ = unit_rows(middle)
    mixed_norm = dot((unit * gain_ref[...]).astype(low), mixing)
    normed[...] = mixed_norm.astype(low)
    normed_t[...] = jnp.transpose(mixed_norm).astype(low)
    attended[...] = dot(natural[...], mixing).astype(low)


def feedforward_kernel(
    step,
    steps,
    source_ref,
    feature_ref,
    attention,
    attended,
    middle_ref,
    normed,
    normed_t,
    output_w,
    gain_ref,
    grad_ref,
    own_ref,
    come_low_ref,
    come_high_ref,
    down_own_ref,
    down_come_ref,
    out_ref,
    grad_middle_ref,
    head_grad_ref,
    delta_ref,
    keep_ref,
    send_ref,
    down_keep_ref,
    down_send_ref,
    gain_part_ref,
    come_ref,
    down_w,
    down_grad,
    total,
    grad_normed,
    extra_grad,
    output_folds,
    late_folds,
):
    rows, width = middle_ref.shape
    half = own_ref.shape[0]
    main = 2 * half
    rest = width - main
    fold = main // rest
    places = main // TILE
    ff = down_w.shape[0]
    chunk = 2 * ff // fold
    down_at = 2 * ff + chunk
    device_ff = ff // places
    groups = device_ff // TILE
    out_at = down_at
    mixing = mixing_of(feature_ref)
    tokens = rows // 2
    part = width // fold
    folded = slice(out_at + width, out_at + width + part)
    come_ref[: half // 2, :] = come_low_ref[...]
    come_ref[half // 2 :, :] = come_high_ref[...]
    middle = middle_ref[...]
    gain = gain_ref[...]
    unit, inverse = unit_rows(middle)
    for place in range(places):
        held = down_own_ref if place < places // 2 else down_come_ref
        row = (place % (places // 2)) * TILE
        for a in range(groups):
            at = pl.multiple_of(source_ref[place] * device_ff + a * TILE, TILE)
            lane = a * width
            down_w[pl.ds(at, TILE), :] = held[row : row + TILE, lane : lane + width]
    total[...] = jnp.zeros_like(total)
    grad_normed[...] = jnp.zeros_like(grad_normed)
    out_grad = grad_ref[...]
    fold_write(
        late_folds,
        jnp.concatenate([own_ref[:, 2 * ff : down_at], come_ref[:, 2 * ff : down_at]], axis=0),
    )

    def advance(c, carry):
        gate_at = pl.ds(pl.multiple_of(c * chunk, 128), chunk)
        up_at = pl.ds(pl.multiple_of(ff + c * chunk, 128), chunk)

        def columns(lanes, at):
            tail = fold_get(late_folds, at, fold, chunk)
            value = (
                dot(normed[:, :half], own_ref[:, lanes])
                + dot(normed[:, half:main], come_ref[:, lanes])
                + dot(normed[:, main:], tail)
            )
            return value, tail

        gate, gate_tail = columns(gate_at, c)
        up, up_tail = columns(up_at, c + fold // 2)
        down_at_c = pl.ds(pl.multiple_of(c * chunk, 128), chunk)
        down = down_w[down_at_c, :]
        sigma = 1.0 / (1.0 + jnp.exp(-gate))
        silu = gate * sigma
        inner = (silu * up).astype(low)
        total[...] += dot(inner, down)
        grad_inner = dot_right(out_grad, down)
        grad_gate = (grad_inner * up * sigma * (1.0 + gate * (1.0 - sigma))).astype(low)
        grad_up = (grad_inner * silu).astype(low)
        down_grad[down_at_c, :] = dot_left(inner, out_grad).astype(low)
        for grad, lanes, tail, at in (
            (grad_gate, gate_at, gate_tail, c),
            (grad_up, up_at, up_tail, c + fold // 2),
        ):
            grad_normed[:, :half] += dot_right(grad, own_ref[:, lanes])
            grad_normed[:, half:main] += dot_right(grad, come_ref[:, lanes])
            grad_normed[:, main:] += dot_right(grad, tail)
            keep_ref[:, lanes] = dot(normed_t[:half], grad).astype(low)
            send_ref[:, lanes] = dot(normed_t[half:main], grad).astype(low)
            fold_put(extra_grad, at, fold, dot(normed_t[main:], grad))
        return carry

    lax.fori_loop(0, ff // chunk, advance, 0)
    out_ref[...] = (middle + total[...]).astype(low)
    extra = fold_read(extra_grad, chunk)
    keep_ref[:, 2 * ff : down_at] = extra[:half]
    send_ref[:, 2 * ff : down_at] = extra[half:]
    for place in range(places):
        held = down_keep_ref if place < places // 2 else down_send_ref
        row = (place % (places // 2)) * TILE
        for a in range(groups):
            at = pl.multiple_of(source_ref[place] * device_ff + a * TILE, TILE)
            lane = a * width
            held[row : row + TILE, lane : lane + width] = down_grad[pl.ds(at, TILE), :]
    unused = jnp.zeros((half, down_keep_ref.shape[1] - groups * width), low)
    down_keep_ref[:, groups * width :] = unused
    down_send_ref[:, groups * width :] = unused

    high = grad_normed[...].astype(low)
    tail = (grad_normed[...] - high.astype(full)).astype(low)
    back = dot_right(high, mixing) + dot_right(tail, mixing)
    gain_part_ref[...] = jnp.sum(back * unit, axis=0, keepdims=True)
    grad_middle = out_grad.astype(full) + norm_back(unit, inverse, gain, back)
    grad_middle_ref[...] = grad_middle
    grad_branch = grad_middle.astype(low)
    output_grad = dot_left(attended[...], grad_branch)
    keep_ref[:, out_at : out_at + width] = output_grad[:half].astype(low)
    send_ref[:, out_at : out_at + width] = output_grad[half:main].astype(low)
    for at in range(fold):
        fold_put(output_folds, at, fold, output_grad[main:, at * part : (at + 1) * part])
    extra = fold_read(output_folds, part)
    unused = jnp.zeros((half, keep_ref.shape[1] - folded.stop), low)
    for held, rows_of_half in ((keep_ref, extra[:half]), (send_ref, extra[half:])):
        held[:, folded] = rows_of_half
        held[:, folded.stop :] = unused
    grad_low = dot_right(grad_branch, output_w[...]).astype(low)
    for head in range(KV_HEADS):
        for part in range(2):
            grads = jnp.concatenate(
                [
                    grad_low[
                        part * tokens : (part + 1) * tokens, h * HEAD_SIZE : (h + 1) * HEAD_SIZE
                    ]
                    for h in range(head * GROUP, (head + 1) * GROUP)
                ],
                axis=0,
            )
            at = slice(part * GROUP * tokens, (part + 1) * GROUP * tokens)
            head_grad_ref[head, at] = grads
            delta_ref[2 * head + part] = as_row(
                jnp.sum(grads.astype(full) * attention[head, at], axis=1, keepdims=True)
            )


def backward_kernel(
    is_first,
    key_half,
    low_blocks,
    joined,
    step,
    steps,
    own,
    key_ref,
    query_ref,
    grad_ref,
    lse_ref,
    delta_ref,
    kv_ref,
    tokens_ref,
    cos_ref,
    sin_ref,
    times,
    *rest,
):
    if not is_first:
        held, rest = rest[:2], rest[2:]
    base = 0
    if joined:
        low_ref, rest = rest[0], rest[1:]
        base = low_ref.shape[1]
        rest[2][:, :base] = low_ref[...]
    grad_query, grad_weight, out_ref, grad_kv = rest
    rows = query_ref.shape[1] // 2
    groups = kv_ref.shape[1] // (2 * KV_WIDTH)
    key_rows = kv_ref.shape[0]
    width = tokens_ref.shape[1] // groups
    members = range(key_half * groups // 2, (key_half + 1) * groups // 2)

    def first():
        if is_first:
            grad_query[...] = jnp.zeros_like(grad_query)
            grad_weight[...] = jnp.zeros_like(grad_weight)
        else:
            grad_query[...] = held[0][...]
            grad_weight[...] = held[1][...]

    once(step, steps, 0, first)
    key_index = key_row(key_ref, key_half, members)
    key_index = jnp.transpose(jnp.broadcast_to(key_index, (128, key_index.shape[1])))[:, 0:1]

    def attend(query_half, add):
        at = slice(query_half * rows, (query_half + 1) * rows)
        first_key, last_key = query_range(own, query_half, rows, 1)
        allowed = (key_index >= first_key) & (key_index <= last_key)
        for head in range(KV_HEADS):
            keys = key_part(kv_ref, members, head)
            scores = dot_right(keys, query_ref[head, at])
            probs = jnp.where(allowed, jnp.exp(scores - lse_ref[2 * head + query_half]), 0.0)
            d_probs = dot_right(key_part(kv_ref, members, KV_HEADS + head), grad_ref[head, at])
            d_scores = (probs * (d_probs - delta_ref[2 * head + query_half])).astype(low)
            grad_query[2 * head + query_half] += dot_left(keys, d_scores)
            parts = (
                (head, dot(d_scores, query_ref[head, at])),
                (KV_HEADS + head, dot(probs.astype(low), grad_ref[head, at])),
            )
            for column, value in parts:
                lanes = slice(column * HEAD_SIZE, (column + 1) * HEAD_SIZE)
                if add:
                    grad_kv[:, lanes] += value
                else:
                    grad_kv[:, lanes] = value

    if key_half == 0:
        attend(0, False)
        pl.when(reaches_low(own, low_blocks))(lambda: attend(1, True))
    else:
        attend(1, False)
    for i, a in enumerate(members):
        at = slice(i * key_rows, (i + 1) * key_rows)
        rope = rope_of(cos_ref, sin_ref, times, key_half, i)
        turned = jnp.concatenate(
            [
                turn(grad_kv[at, head * HEAD_SIZE : (head + 1) * HEAD_SIZE], rope, -1.0)
                for head in range(KV_HEADS)
            ]
            + [grad_kv[at, KV_WIDTH:]],
            axis=1,
        ).astype(low)
        lane = base + i * 2 * KV_WIDTH
        out_ref[:, lane : lane + 2 * KV_WIDTH] = turned
        grad_weight[...] += dot_left(turned, tokens_ref[:, a * width : (a + 1) * width])


def qkv_grad_kernel(
    step,
    steps,
    feature_ref,
    grad_query,
    grad_weight,
    normed_ref,
    weight_ref,
    cos_ref,
    sin_ref,
    times,
    gain_ref,
    gain_two_ref,
    query_grad_ref,
    gains_ref,
    keep_ref,
    send_ref,
    natural,
    folds,
):
    tokens, width = normed_ref.shape
    half = tokens // 2
    rope = rope_own_of(cos_ref, sin_ref, times)
    for head in range(KV_HEADS):
        rotated = [
            jnp.transpose(grad_query[2 * head + part]) * HEAD_SIZE**-0.5 for part in range(2)
        ]
        for g in range(GROUP):
            h = head * GROUP + g
            value = jnp.concatenate([part[g * half : (g + 1) * half] for part in rotated], axis=0)
            query_grad_ref[:, h * HEAD_SIZE : (h + 1) * HEAD_SIZE] = turn(value, rope, -1.0).astype(
                low
            )
    natural[:, :width] = dot_left(normed_ref[...], query_grad_ref[...])
    natural[:, width:] = jnp.transpose(grad_weight[...])
    products = natural[...] * weight_ref[...].astype(full)
    gain_part = as_row(jnp.sum(products, axis=1, keepdims=True)) / gain_ref[...]
    gains = fold_gains([gain_part, gain_two_ref[...]])
    gains_ref[...] = gains
    mixed = dot_left(mixing_of(feature_ref), natural[...].astype(low)).astype(low)
    columns = mixed.shape[1]
    rows = keep_ref.shape[0]
    main = 2 * rows
    fold = main // (width - main)
    part = columns // fold
    for at in range(fold):
        fold_put(folds, at, fold, mixed[main:, at * part : (at + 1) * part].astype(full))
    extra = fold_read(folds, part)
    unused = jnp.zeros((rows, keep_ref.shape[1] - columns - part), low)
    for held, at in ((keep_ref, 0), (send_ref, rows)):
        held[:rows, :columns] = mixed[at : at + rows]
        held[:rows, columns : columns + part] = extra[at : at + rows]
        held[:rows, columns + part :] = unused
    send_ref[:TILE, columns + part : columns + part + gains.shape[1]] = gains.astype(low)


def merge_kernel(gain_at, step, steps, *refs):
    keep_low, keep_high, kv_come, w_keep, w_come, gains_ref, keep_out, send_out, gains_out = refs
    half = w_keep.shape[0] // 2
    part = keep_low.shape[1]
    base = 2 * part
    lane = 0
    for keep, come, first in (
        (keep_low, kv_come, 0),
        (keep_high, kv_come, part),
        (w_keep, w_come, 0),
    ):
        columns = keep.shape[1]
        for out, at in ((keep_out, 0), (send_out, half)):
            value = keep[at : at + half, :].astype(full) + come[
                at : at + half, first : first + columns
            ].astype(full)
            out[:, lane : lane + columns] = value.astype(low)
        lane += columns
    lanes = slice(gain_at, gain_at + gains_ref.shape[1])
    gains = sum_gains(gains_ref[...], w_come[:TILE, lanes])
    gains_out[...] = gains
    send_out[:TILE, base + lanes.start : base + lanes.stop] = gains.astype(low)


def add_kernel(gain_at, step, steps, keep_ref, come_ref, *rest):
    rows = keep_ref.shape[0]
    if gain_at is not None:
        gains_ref, keep_out, send_out, gains_out = rest
        lanes = slice(gain_at, gain_at + gains_ref.shape[1])
        gains = sum_gains(gains_ref[...], come_ref[:TILE, lanes])
        gains_out[...] = gains
        rest = rest[1:-1]

    def tile(at):
        at = pl.ds(at, TILE)
        return keep_ref[at, :].astype(full) + come_ref[at, :].astype(full)

    if rows == TILE:
        rest[0][...] = tile(0)
        return
    keep_out, send_out = rest
    half = rows // 2

    def advance(i, carry):
        at = pl.multiple_of(i * TILE, TILE)
        keep_out[pl.ds(at, TILE), :] = tile(at).astype(low)
        send_out[pl.ds(at, TILE), :] = tile(pl.multiple_of(half + at, TILE)).astype(low)
        return carry

    lax.fori_loop(0, half // TILE, advance, 0)
    if gain_at is not None:
        send_out[:TILE, lanes] = gains.astype(low)


def scatter_halves(keep, leaving, steps, name, gains=None, gain_at=None, after=()):
    for at, partner in enumerate(reversed(steps)):
        come = send(leaving, partner)
        rows, columns = keep.shape
        ins = [("whole", keep), ("whole", come)]
        if rows == TILE:
            if gains is not None:
                return keep, come, gains
            outs = [("whole", shape_of((rows, columns), full))]
        else:
            outs = [("whole", shape_of((rows // 2, columns), low))] * 2
        if gains is not None:
            ins.append(("whole", gains))
            outs.append(("whole", shape_of(gains.shape, full)))
        result = one_call(
            functools.partial(add_kernel, gain_at),
            name,
            ins,
            outs,
            [],
            1,
            after[at] if at < len(after) else (),
        )
        if gains is not None:
            gains = result[-2]
        if rows == TILE:
            return result[0]
        keep, leaving = result[0], result[1]


def final_kernel(
    base,
    step,
    steps,
    keep_ref,
    come_ref,
    query_grad_ref,
    weight_ref,
    hidden_ref,
    gain_ref,
    grad_middle_ref,
    *rest,
):
    grads = rest[-1]
    tokens, width = hidden_ref.shape
    grads[:, :width] = query_grad_ref[...]
    for a in range(tokens // TILE):
        rows = slice(a * TILE, (a + 1) * TILE)
        lanes = slice(a * 2 * KV_WIDTH, (a + 1) * 2 * KV_WIDTH)
        value = keep_ref[:, lanes].astype(full) + come_ref[:, lanes].astype(full)
        grads[rows, width:] = value.astype(low)
    back = dot_right(grads[...], weight_ref[...])
    unit, inverse = unit_rows(hidden_ref[...].astype(full))
    out_ref = rest[-6] if base else rest[-2]
    out_ref[...] = (grad_middle_ref[...] + norm_back(unit, inverse, gain_ref[...], back)).astype(low)
    if not base:
        return
    gains_ref, _, query_out, key_out, value_out, gains_out, _ = rest
    columns = weight_ref.shape[1]
    total = keep_ref[:, base:].astype(full) + come_ref[:, base:].astype(full)
    fold = gains_ref.shape[0] // 2
    part = columns // fold
    for row in range(TILE + TILE // fold):
        if row < TILE:
            value = total[row : row + 1, :columns]
        else:
            at = (row - TILE) * fold
            value = jnp.concatenate(
                [total[at + i : at + i + 1, columns : columns + part] for i in range(fold)], axis=1
            )
        query_out[:, row * width : (row + 1) * width] = value[:, :width]
        for out, first in ((key_out, width), (value_out, width + KV_WIDTH)):
            out[:, row * KV_WIDTH : (row + 1) * KV_WIDTH] = value[:, first : first + KV_WIDTH]
    at = columns + part
    lanes = slice(at, at + gains_ref.shape[1])
    gains = sum_gains(gains_ref[...], come_ref[:TILE, base + lanes.start : base + lanes.stop])
    for k in range(2):
        gains_out[k : k + 1, :] = jnp.concatenate(
            [gains[k * fold + i : k * fold + i + 1] for i in range(fold)], axis=1
        )


def body(
    hidden_in,
    attention_gain,
    query_weight,
    key_weight,
    value_weight,
    output_weight,
    feedforward_gain,
    gate_weight,
    up_weight,
    down_weight,
    doc_of_block,
    pair_table,
    out_grad,
):
    tokens, width = hidden_in.shape
    half_rows = tokens // 2
    count = lax.axis_size("ctx")
    device = lax.axis_index("ctx")
    ff = gate_weight.shape[1] * count // width
    low_bits = low_bits_of(query_weight.shape[1], width)
    merged = low_bits == 0
    row_steps = exchange_steps(count, low_bits)
    token_steps = exchange_steps(count, 0)
    down_steps = row_steps[2:4] + row_steps[:2] + row_steps[4:] if merged else row_steps
    group_count = count >> low_bits
    group_rows = width // group_count
    groups = tokens // TILE
    steps = max(1, TILE * count // 512)
    places = count // (2 * steps)
    gain_one = attention_gain.reshape(1, width)
    gain_two = feedforward_gain.reshape(1, width)
    columns = width + 2 * KV_WIDTH
    main = TILE * group_count
    fold = main // (width - main)
    w_lanes = whole_lanes(columns + columns // fold + 2 * width // TILE)
    projection_lanes = whole_lanes((columns + width) + (columns + width) // fold)
    ff_folded = 2 * ff // fold
    out_at = 2 * ff + ff_folded
    device_groups = ff // group_count // TILE
    late_lanes = whole_lanes(out_at + width + width // fold)
    gate_lanes = whole_lanes(out_at)
    down_lanes = whole_lanes(device_groups * width)
    call = Call(steps)
    one = Call(1)

    def rows_of(piece, piece_columns):
        if low_bits:
            piece = whole_rows(piece, device, low_bits, piece_columns)
        return ("whole", piece)

    projections = [
        rows_of(query_weight, width),
        rows_of(key_weight, KV_WIDTH),
        rows_of(value_weight, KV_WIDTH),
        rows_of(output_weight, width),
    ]
    token_parts = (groups * width, projection_lanes) if merged else (groups * width,)
    packed, normed, pack_mark = one(
        pack_kernel,
        "norm_and_pack",
        [("whole", hidden_in), ("whole", gain_one)] + (projections if merged else []),
        [
            ("whole", shape_of((TILE, sum(token_parts)), low)),
            ("whole", shape_of((tokens, width), low)),
        ],
        [],
        1,
    )

    def table_row(table):
        return lax.dynamic_index_in_dim(jnp.asarray(table), device, 0, keepdims=False)

    sources = table_row(source_table(count, 0, token_steps))
    down_sources = table_row(source_table(count, low_bits, down_steps))
    group_table = source_table(count, low_bits, row_steps)
    inside = np.arange(group_rows)[None, None, :]
    features = group_table[:, :, None] * group_rows + inside
    features = np.concatenate(
        [
            features[:, :, :TILE].reshape(count, -1),
            features[:, :, TILE:].reshape(count, -1),
        ],
        axis=1,
    ).astype(np.int32)
    feature_row = table_row(features).reshape(1, width)

    device_iota = jnp.arange(count, dtype=jnp.int32)
    pairs = jnp.sum(
        jnp.where(sources[:, None] == device_iota[None, :], pair_table[None, :], 0), axis=1
    )
    blocks = jnp.stack([pairs, 2 * count - 1 - pairs], axis=1).reshape(-1)
    block_iota = jnp.arange(2 * count, dtype=jnp.int32)
    block_docs = jnp.sum(
        jnp.where(blocks[:, None] == block_iota[None, :], doc_of_block[None, :], 0), axis=1
    )
    doc_start = jnp.min(
        jnp.where(block_docs[:, None] == doc_of_block[None, :], block_iota[None, :], 2 * count),
        axis=1,
    )
    own = jnp.concatenate([blocks[:2], doc_start[:2]])

    def by_step(values):
        return values.reshape(2, steps, places, 2).transpose(0, 1, 3, 2)

    inner = jnp.arange(TILE, dtype=jnp.int32)
    key_index = by_step(blocks)[..., None] * half_rows + inner
    key_index = key_index.astype(full).reshape(2, 2 * steps, 1, -1)
    frequency = rope_base ** (-jnp.arange(HEAD_SIZE // 2, dtype=full) * (2.0 / HEAD_SIZE))
    block_angle = (by_step(blocks - doc_start) * half_rows).astype(full)[..., None] * frequency
    offset = jnp.arange(half_rows, dtype=full).reshape(groups // 2, TILE)
    offset_angle = offset[..., None] * frequency
    cos_in, sin_in = jnp.cos(offset_angle), jnp.sin(offset_angle)
    times_cos = jnp.concatenate([cos_in] * 4 + [-sin_in, sin_in] * 2, axis=-1)
    times_sin = jnp.concatenate([sin_in] * 4 + [cos_in, -cos_in] * 2, axis=-1)
    times = jnp.stack([times_cos, times_sin])
    block_cos = jnp.tile(jnp.cos(block_angle), 8).reshape(2, 2 * steps, places, 1, 4 * HEAD_SIZE)
    block_sin = jnp.tile(jnp.sin(block_angle), 8).reshape(2, 2 * steps, places, 1, 4 * HEAD_SIZE)
    rope_own = [
        ("whole", block_cos[0, :2, :1]),
        ("whole", block_sin[0, :2, :1]),
        ("whole", times),
    ]
    tables = [key_index, block_cos, block_sin, times, feature_row]
    late_at = 2
    down, down_mark = one(
        functools.partial(fold_down_kernel, width),
        "fold_down",
        [rows_of(down_weight, width)],
        [("whole", shape_of((TILE, down_lanes), low))],
        [],
        1,
        [pack_mark],
    )
    late, late_mark = one(
        functools.partial(fold_gates_kernel, ff),
        "fold_gates",
        [rows_of(gate_weight, ff), rows_of(up_weight, ff)],
        [("whole", shape_of((TILE, gate_lanes), low))],
        [],
        1,
        [pack_mark],
    )

    def release(values, name, after):
        return one(
            copy_kernel,
            "release_" + name,
            [("whole", values)],
            [("whole", shape_of(values.shape, low))],
            [],
            1,
            after,
        )[0]

    mark = None
    for at, partner in enumerate(token_steps[:-1]):
        after = []
        if at < 2:
            down, down_mark = join(down, send(down, down_steps[at]), "down", [])
            after = [down_mark] + ([late_mark] + tables if at == 1 else [])
        elif at == late_at:
            late = release(late, "gates", [mark])
            late, late_mark = join(late, send(late, row_steps[0]), "gates", [])
            after = [late_mark]
        elif at == late_at + 1:
            late, late_mark = join(late, send(late, row_steps[1]), "gates", [])
            down = release(down, "down", [late_mark])
            down, down_mark = join(down, send(down, down_steps[2]), "down", [])
            after = [down_mark]
        last = at == len(token_steps) - 2
        *held, mark = join(
            packed,
            send(packed, partner),
            "tokens",
            after,
            token_parts if last else (),
        )
        packed = held[0]
    token_own = packed
    if merged:
        w_own, w_come = held[1], send(held[1], token_steps[-1])
    else:
        qkv_piece, _ = one(
            functools.partial(fold_projections_kernel, width),
            "fold_projections",
            projections,
            [("whole", shape_of((TILE, projection_lanes), low))],
            [],
            1,
        )
        w_own, w_come = gather_halves(qkv_piece, row_steps, "qkv")
    token_come = send(token_own, token_steps[-1])

    halves = [
        (
            held,
            key_index[place],
            [("rows", block_cos[place]), ("rows", block_sin[place]), ("whole", times)],
        )
        for place, held in enumerate((token_own, token_come))
    ]

    rows = GROUP * tokens
    half = TILE * count // 2
    kv_shape = shape_of((half, groups * 2 * KV_WIDTH), low)
    head_shape = (KV_HEADS, rows, HEAD_SIZE)
    weight, kv_weight, output_w, _ = one(
        weights_kernel,
        "qkv_weights",
        [("whole", feature_row), ("whole", w_own), ("whole", w_come)],
        [
            ("whole", shape_of((width, columns), low)),
            ("whole", shape_of((width, 3 * KV_WIDTH), low)),
            ("whole", shape_of((width, width), low)),
        ],
        [
            pltpu.VMEM((width, columns + width), low),
            fold_scratch(main, columns // fold),
            fold_scratch(main, width // fold),
        ],
        3,
    )
    queries, _ = one(
        queries_kernel,
        "queries",
        [("whole", normed), ("whole", weight)] + rope_own,
        [("whole", shape_of(head_shape, low))],
        [],
        2,
    )

    def project(place, after):
        token_rows, _, turns = halves[place]
        return call(
            project_kernel,
            "project",
            [("rows", token_rows), ("whole", kv_weight)] + turns,
            [("rows", kv_shape)],
            [],
            5,
            after,
        )

    state_shapes = [("whole", shape_of((KV_HEADS, rows, 2 * HEAD_SIZE), full))]

    def attend(place, kv, state, after):
        return call(
            functools.partial(forward_kernel, not state, count),
            "attention_forward",
            [
                ("smem", own),
                ("rows", halves[place][1]),
                ("whole", queries),
                ("rows", kv),
            ]
            + [("whole", held) for held in state],
            state_shapes,
            [],
            6,
            after,
        )

    kv_own, mark = project(0, [])
    late, late_mark = join(late, send(late, row_steps[2]), "gates", [mark])
    down, down_mark = join(down, send(down, down_steps[3]), "down", [mark])
    come_low = send(late, row_steps[4])
    down_come = send(down, down_steps[4])
    *state, mark = attend(0, kv_own, [], [late_mark, down_mark])
    kv_come, mark = project(1, [mark])
    *state, mark = attend(1, kv_come, state, [])
    late_high = release(send(late, row_steps[3]), "high", [mark])
    come_high = send(late_high, row_steps[4])
    late_own, mark = join(late, late_high, "gates", [])

    row_shape = ("whole", shape_of((2 * KV_HEADS, 1, rows // 2), full))
    token_low = ("whole", shape_of((tokens, width), low))
    token_full = ("whole", shape_of((tokens, width), full))
    *inner_values, lse, _ = one(
        middle_kernel,
        "middle",
        [
            ("whole", feature_row),
            ("whole", state[0]),
            ("whole", hidden_in),
            ("whole", output_w),
            ("whole", gain_two),
        ],
        [
            ("whole", shape_of(head_shape, full)),
            token_low,
            token_full,
            token_low,
            ("whole", shape_of((width, tokens), low)),
            row_shape,
        ],
        [pltpu.VMEM((tokens, width), low)],
        3,
        [mark],
    )
    late_shape = shape_of((late_own.shape[0], late_lanes), low)
    down_shape = shape_of(down.shape, low)
    (
        block_out,
        grad_middle,
        head_grads,
        delta,
        late_keep,
        late_send,
        down_keep,
        down_send,
        gain_two_part,
        _,
    ) = one(
        feedforward_kernel,
        "feedforward",
        [
            ("smem", down_sources),
            ("whole", feature_row),
        ]
        + [("whole", held) for held in inner_values]
        + [
            ("whole", output_w),
            ("whole", gain_two),
            ("whole", out_grad),
            ("whole", late_own),
            ("whole", come_low),
            ("whole", come_high),
            ("whole", down),
            ("whole", down_come),
        ],
        [
            token_low,
            token_full,
            ("whole", shape_of(head_shape, low)),
            row_shape,
            ("whole", late_shape),
            ("whole", late_shape),
            ("whole", down_shape),
            ("whole", down_shape),
            ("whole", shape_of((1, width), full)),
        ],
        [
            pltpu.VMEM(late_own.shape, low),
            pltpu.VMEM((ff, width), low),
            pltpu.VMEM((ff, width), low),
            pltpu.VMEM((tokens, width), full),
            pltpu.VMEM((tokens, width), full),
            fold_scratch(main, ff_folded),
            fold_scratch(main, width // fold),
            fold_scratch(main, ff_folded),
        ],
        11,
        vmem=24,
    )

    def attend_back(place, key_half, kv, carried, after, joined=()):
        token_rows, keys, turns = halves[place]
        return call(
            functools.partial(backward_kernel, not carried, key_half, count, bool(joined)),
            "attention_backward",
            [
                ("smem", own),
                ("rows", keys),
                ("whole", queries),
                ("whole", head_grads),
                ("whole", lse),
                ("whole", delta),
                ("rows", kv),
                ("rows", token_rows),
            ]
            + turns
            + [("whole", held) for held in carried]
            + [("rows", part) for part in joined],
            [
                ("whole", shape_of((2 * KV_HEADS, HEAD_SIZE, rows // 2), full)),
                ("whole", shape_of((2 * KV_WIDTH, width), full)),
                ("rows", shape_of((half, groups * KV_WIDTH * (1 + len(joined))), low)),
            ],
            [pltpu.VMEM((groups // 2 * places * TILE, 2 * KV_WIDTH), full)],
            6,
            after,
        )

    class Adding:
        def __init__(self, keep, leaving, steps, name):
            self.keep, self.leaving, self.steps, self.name = keep, leaving, steps[::-1], name

        def step(self, after):
            come = send(self.leaving, self.steps[0])
            self.steps = self.steps[1:]
            rows, columns = self.keep.shape
            outs = [shape_of((rows // 2, columns), low)] * 2
            if rows == TILE:
                outs = [shape_of((rows, columns), full)]
            *result, token = one(
                functools.partial(add_kernel, None),
                self.name,
                [("whole", self.keep), ("whole", come)],
                [("whole", out) for out in outs],
                [],
                1,
                after,
            )
            self.keep, self.leaving = result[0], result[-1]
            return token

    late_chain = Adding(late_keep, late_send, row_steps, "add_late")
    down_chain = Adding(down_keep, down_send, down_steps, "add_down")
    *carried, send_low, mark = attend_back(1, 0, kv_come, [], [])
    marks = [late_chain.step([mark]), down_chain.step([mark])]
    *carried, kv_send, mark = attend_back(1, 1, kv_come, carried, marks, [send_low])
    *carried, keep_low, mark = attend_back(0, 0, kv_own, carried, [])
    marks = [late_chain.step([mark]), down_chain.step([mark])]
    *carried, keep_high, mark = attend_back(0, 1, kv_own, carried, marks)
    query_grad, gains, w_keep, w_send, mark = one(
        qkv_grad_kernel,
        "qkv_gradients",
        [
            ("whole", feature_row),
            ("whole", carried[0]),
            ("whole", carried[1]),
            ("whole", normed),
            ("whole", weight),
        ]
        + rope_own
        + [
            ("whole", gain_one),
            ("whole", gain_two_part),
        ],
        [
            ("whole", shape_of((tokens, width), low)),
            ("whole", shape_of((TILE, 2 * width // TILE), full)),
            ("whole", shape_of((main // 2, w_lanes), low)),
            ("whole", shape_of((main // 2, w_lanes), low)),
        ],
        [pltpu.VMEM((width, columns), full), fold_scratch(main, columns // fold)],
        3,
    )
    late_mark = late_chain.step([mark])
    ends = [
        ("whole", query_grad),
        ("whole", weight),
        ("whole", hidden_in),
        ("whole", gain_one),
        ("whole", grad_middle),
    ]
    end_scratch = [pltpu.VMEM((tokens, columns), low)]
    input_shape = ("whole", shape_of((tokens, width), low))
    if merged:
        gain_at = columns + columns // fold
        base = kv_send.shape[1]
        lanes = base + w_lanes
        keep, leaving, gains, mark = one(
            functools.partial(merge_kernel, gain_at),
            "add_first",
            [
                ("whole", keep_low),
                ("whole", keep_high),
                ("whole", send(kv_send, token_steps[-1])),
                ("whole", w_keep),
                ("whole", send(w_send, token_steps[-1])),
                ("whole", gains),
            ],
            [
                ("whole", shape_of((half // 2, lanes), low)),
                ("whole", shape_of((half // 2, lanes), low)),
                ("whole", shape_of(gains.shape, full)),
            ],
            [],
            2,
            [late_mark],
        )
        marks = [down_chain.step([mark])]
        marks = [[late_chain.step(marks), down_chain.step(marks)]]
        marks.append([late_chain.step(marks[0]), down_chain.step(marks[0])])
        keep, come, gains = scatter_halves(
            keep, leaving, token_steps[:-1], "add_chain", gains, base + gain_at, marks
        )
        input_grad, query_w_grad, key_w_grad, value_w_grad, gains, _ = one(
            functools.partial(final_kernel, base),
            "last_gradients",
            [("whole", keep), ("whole", come)] + ends + [("whole", gains)],
            [
                input_shape,
                ("whole", shape_of((1, query_weight.shape[1]), full)),
                ("whole", shape_of((1, key_weight.shape[1]), full)),
                ("whole", shape_of((1, value_weight.shape[1]), full)),
                ("whole", shape_of((2, width), full)),
            ],
            end_scratch,
            1,
        )
        gain_sums = (gains[0], gains[1])
    else:
        for _ in range(2):
            late_chain.step([])
        for _ in range(3):
            down_chain.step([])
        kv_keep = jnp.concatenate([keep_low, keep_high], axis=1)
        kv_sum = scatter_halves(kv_keep, kv_send, token_steps, "add_kv")
        qkv_sum = scatter_halves(w_keep, w_send, row_steps, "add_qkv")
        gains = lax.psum(gains, "ctx").reshape(2, width)
        gain_sums = (gains[0], gains[1])
        input_grad, _ = one(
            functools.partial(final_kernel, 0),
            "input_gradient",
            [("whole", kv_sum), ("whole", jnp.zeros_like(kv_sum))] + ends,
            [input_shape],
            end_scratch,
            1,
        )
        qkv_rows = unfold_rows(qkv_sum, columns, columns // fold)
        query_w_grad, key_w_grad, value_w_grad = (
            own_piece(qkv_rows[:, first:last], device, low_bits)
            for first, last in (
                (0, width),
                (width, width + KV_WIDTH),
                (width + KV_WIDTH, columns),
            )
        )

    def piece_of(piece_rows):
        return own_piece(piece_rows, device, low_bits)

    late_sum, down_sum = late_chain.keep, down_chain.keep
    ff_rows = unfold_rows(late_sum, 2 * ff, ff_folded)
    down_rows = jnp.concatenate(
        [down_sum[:, a * width : (a + 1) * width] for a in range(device_groups)], axis=0
    )
    output_rows = unfold_rows(late_sum[:, out_at:], width, width // fold)
    return (
        block_out,
        input_grad,
        gain_sums[0],
        query_w_grad,
        key_w_grad,
        value_w_grad,
        piece_of(output_rows),
        gain_sums[1],
        piece_of(ff_rows[:, :ff]),
        piece_of(ff_rows[:, ff:]),
        piece_of(down_rows),
    )


def solution(mesh):
    row = P("ctx", None)
    in_specs = (row, P(), row, row, row, row, P(), row, row, row, P(), P(), row)
    out_specs = (row, row, P(), row, row, row, row, P(), row, row, row)
    return jax.shard_map(body, mesh=mesh, in_specs=in_specs, out_specs=out_specs, check_vma=False)
```

```python
import functools

import jax
import jax.numpy as jnp
import numpy as np
from jax import lax
from jax.experimental import pallas as pl
from jax.experimental.pallas import tpu as pltpu
from jax.sharding import PartitionSpec as P

HEADS = 9
KV_HEADS = 3
GROUP = HEADS // KV_HEADS
HEAD_SIZE = 64
KV_WIDTH = KV_HEADS * HEAD_SIZE
TILE = 16
TOTAL, PEAK = HEAD_SIZE, HEAD_SIZE + 1

epsilon = 1e-05
rope_base = 100000.0
masked_score = -1e30

low = jnp.bfloat16
full = jnp.float32


def exchange_steps(device_count, low_bits):
    top = device_count.bit_length() - 1
    steps = []
    if low_bits == 0 and top >= 4:
        for bit in range(top - 1, 2, -1):
            steps.append([i ^ (1 << bit) for i in range(device_count)])
        steps.append([i ^ (4 if i & 1 else 2) for i in range(device_count)])
        steps.append([i ^ (2 if i & 1 else 4) for i in range(device_count)])
        steps.append([i ^ 1 for i in range(device_count)])
    else:
        for bit in range(top - 1, low_bits - 1, -1):
            steps.append([i ^ (1 << bit) for i in range(device_count)])
    return steps


def source_table(device_count, low_bits, steps):
    held = [[d >> low_bits] for d in range(device_count)]
    for partner in steps:
        held = [held[d] + held[partner[d]] for d in range(device_count)]
    return np.array(held, np.int32)


def send(values, partner):
    return lax.ppermute(values, "ctx", [(i, p) for i, p in enumerate(partner)])


def gather_halves(values, steps, name):
    for partner in steps[:-1]:
        values, _ = join(values, send(values, partner), name, [])
    return values, send(values, steps[-1])


def whole_rows(flat, device, low_bits, columns):
    for bit in range(low_bits):
        partner = [i ^ (1 << bit) for i in range(lax.axis_size("ctx"))]
        other = send(flat, partner)
        is_high = (device >> bit) & 1
        flat = jnp.concatenate(
            [jnp.where(is_high, other, flat), jnp.where(is_high, flat, other)], axis=1
        )
    return flat.reshape(-1, columns)


def own_piece(rows, device, low_bits):
    flat = rows.reshape(1, -1)
    for bit in range(low_bits - 1, -1, -1):
        partner = [i ^ (1 << bit) for i in range(lax.axis_size("ctx"))]
        half = flat.shape[1] // 2
        is_high = (device >> bit) & 1
        leaving = jnp.where(is_high, flat[:, :half], flat[:, half:]).astype(low)
        staying = jnp.where(is_high, flat[:, half:], flat[:, :half])
        flat = staying + send(leaving, partner).astype(full)
    return flat


def low_bits_of(piece, columns):
    low_bits = 0
    while (piece << low_bits) < TILE * columns:
        low_bits += 1
    return low_bits


def unfold_rows(packed, columns, folded):
    return jnp.concatenate(
        [packed[:, :columns], packed[:, columns : columns + folded].reshape(-1, columns)], axis=0
    )


def whole_lanes(columns):
    return -(-columns // 128) * 128


def dot(left, right):
    return jnp.dot(left, right, preferred_element_type=full)


def dot_right(left, right):
    return lax.dot_general(left, right, (((1,), (1,)), ((), ())), preferred_element_type=full)


def dot_left(left, right):
    return lax.dot_general(left, right, (((0,), (0,)), ((), ())), preferred_element_type=full)


def iota(shape, axis):
    return lax.broadcasted_iota(jnp.int32, shape, axis)


def mixing_of(feature_ref):
    width = feature_ref.shape[1]
    return (iota((width, width), 0) == feature_ref[...]).astype(full).astype(low)


def fold_scratch(main, part):
    return pltpu.VMEM((-(-part // 128), main, 128), full)


def fold_write(scratch, extra):
    for block in range(scratch.shape[0]):
        lanes = slice(block * 128, min(block * 128 + 128, extra.shape[1]))
        scratch[block, :, : lanes.stop - lanes.start] = extra[:, lanes].astype(full)


def fold_read(scratch, part):
    parts = [scratch[block] for block in range(scratch.shape[0])]
    return jnp.concatenate(parts, axis=1)[:, :part].astype(low)


def fold_get(scratch, at, fold, part):
    rows = pl.ds(at, scratch.shape[1] // fold, stride=fold)
    parts = [scratch.at[block][rows, :] for block in range(scratch.shape[0])]
    return jnp.concatenate(parts, axis=1)[:, :part].astype(low)


def fold_put(scratch, at, fold, value):
    rows = pl.ds(at, scratch.shape[1] // fold, stride=fold)
    missing = scratch.shape[0] * 128 - value.shape[1]
    if missing:
        value = jnp.concatenate([value, jnp.zeros((value.shape[0], missing), full)], axis=1)
    for block in range(scratch.shape[0]):
        scratch.at[block][rows, :] = value[:, block * 128 : (block + 1) * 128]


def as_row(column):
    return jnp.transpose(jnp.broadcast_to(column, (column.shape[0], 128)))[0:1]


def turn(values, rope, direction):
    half_dim = HEAD_SIZE // 2
    swapped = jnp.concatenate([values[:, half_dim:], values[:, :half_dim]], axis=1)
    sine = rope[:, 2 * HEAD_SIZE : 3 * HEAD_SIZE]
    return values * rope[:, :HEAD_SIZE] + swapped * (direction * sine)


def rope_of(cos_ref, sin_ref, times, part, quarter):
    _, places, _, lanes = cos_ref.shape
    value = cos_ref[part] * times[0, quarter] - sin_ref[part] * times[1, quarter]
    return value.reshape(places * TILE, lanes)


def rope_own_of(cos_ref, sin_ref, times):
    _, quarters, rows, lanes = times.shape
    parts = [
        cos_ref[part, 0] * times[0] - sin_ref[part, 0] * times[1] for part in range(2)
    ]
    return jnp.concatenate([part.reshape(quarters * rows, lanes) for part in parts], axis=0)


def unit_rows(values):
    inverse = lax.rsqrt(jnp.mean(values * values, axis=-1, keepdims=True) + epsilon)
    return values * inverse, inverse


def norm_back(unit, inverse, gain, grad):
    scaled = grad * gain
    return inverse * (scaled - unit * jnp.mean(scaled * unit, axis=-1, keepdims=True))


def query_range(own, part, rows, axis):
    shape = (rows, 1) if axis == 0 else (1, rows)
    half = rows // GROUP
    last_key = own[part] * half + lax.rem(iota(shape, axis), half)
    first_key = jnp.zeros(shape, jnp.int32) + own[2 + part] * half
    return first_key.astype(full), last_key.astype(full)


def fold_gains(rows):
    part = len(rows) * rows[0].shape[1] // TILE
    pieces = [
        row[:, at : at + part] for row in rows for at in range(0, row.shape[1], part)
    ]
    return jnp.concatenate(pieces, axis=0)


def sum_gains(gains, come):
    return gains.astype(low).astype(full) + come.astype(full)


class Call:
    def __init__(self, steps):
        self.steps = steps

    def spec(self, kind, shape):
        if kind == "smem":
            return pl.BlockSpec(memory_space=pltpu.SMEM)
        if kind == "token":
            return pl.BlockSpec(memory_space=pl.ANY)
        if self.steps == 1 or kind == "whole":
            return pl.BlockSpec(memory_space=pltpu.VMEM)
        rest = tuple(shape[1:])
        return pl.BlockSpec((shape[0] // self.steps,) + rest, lambda i: (i,) + (0,) * len(rest))

    def __call__(self, kernel, name, ins, outs, scratch, micros, after=(), vmem=16):
        steps = self.steps
        first, last, end = len(ins), len(ins) + len(after), len(ins) + len(after) + len(outs)

        def run(*refs):
            refs[end][...] = jnp.zeros_like(refs[end])
            used = refs[:first] + refs[last:end] + refs[end + 1 :]
            kernel(pl.program_id(0) if steps > 1 else 0, steps, *used)

        ins = list(ins) + [("token", token) for token in after]
        outs = list(outs) + [("whole", shape_of((8, 128), full))]
        return pl.pallas_call(
            run,
            grid=(steps,) if steps > 1 else (),
            in_specs=[self.spec(kind, a.shape) for kind, a in ins],
            out_specs=[self.spec(kind, s.shape) for kind, s in outs],
            out_shape=[s for _, s in outs],
            scratch_shapes=scratch,
            compiler_params=pltpu.CompilerParams(vmem_limit_bytes=vmem * 1024 * 1024),
            cost_estimate=pl.CostEstimate(
                flops=int(micros * steps * 1e9), bytes_accessed=1024, transcendentals=0
            ),
            name=name,
        )(*[a for _, a in ins])


one_call = Call(1)


def once(step, steps, at, action):
    if steps == 1:
        action()
    else:
        pl.when(step == at)(action)


def shape_of(shape, dtype):
    return jax.ShapeDtypeStruct(shape, dtype)


def join_kernel(step, steps, held_ref, come_ref, *outs):
    rows = held_ref.shape[0]
    lane = 0
    for out_ref in outs:
        lanes = slice(lane, lane + out_ref.shape[1])
        out_ref[:rows, :] = held_ref[:, lanes]
        out_ref[rows:, :] = come_ref[:, lanes]
        lane = lanes.stop


def copy_kernel(step, steps, held_ref, out_ref):
    out_ref[...] = held_ref[...]


def join(held, come, name, after, parts=()):
    rows, columns = held.shape
    if rows * columns > 2 << 20:
        return jnp.concatenate([held, come], axis=0), None
    return one_call(
        join_kernel,
        "join_" + name,
        [("whole", held), ("whole", come)],
        [("whole", shape_of((2 * rows, part), held.dtype)) for part in parts or (columns,)],
        [],
        1,
        after,
    )


def pack_kernel(step, steps, hidden_ref, gain_ref, *refs):
    packed_ref, normed_ref = refs[-2:]
    width = hidden_ref.shape[1]
    unit, _ = unit_rows(hidden_ref[...].astype(full))
    normed_ref[...] = (unit * gain_ref[...]).astype(low)
    for a in range(hidden_ref.shape[0] // TILE):
        packed_ref[:, a * width : (a + 1) * width] = normed_ref[a * TILE : (a + 1) * TILE, :]
    if len(refs) > 2:
        fold_projections(packed_ref, (a + 1) * width, width, refs[:-2])


def rows_in(ref, columns):
    value = ref[...].astype(full)
    if value.shape[1] == columns:
        return value
    pieces = [value[:, at : at + columns] for at in range(0, value.shape[1], columns)]
    return jnp.concatenate(pieces, axis=0)


def fold_into(out_ref, at, pieces):
    columns = sum(piece.shape[1] for piece in pieces)
    lane = at
    for piece in pieces:
        out_ref[:, lane : lane + piece.shape[1]] = piece[:TILE, :].astype(low)
        lane += piece.shape[1]
    tails = [piece[TILE:, :] for piece in pieces]
    tail = tails[0] if len(tails) == 1 else jnp.concatenate(tails, axis=1)
    fold = TILE // tail.shape[0]
    part = columns // fold
    rows = [
        tail[j : j + 1, block * part : (block + 1) * part]
        for j in range(tail.shape[0])
        for block in range(fold)
    ]
    out_ref[:, lane : lane + part] = jnp.concatenate(rows, axis=0).astype(low)
    return lane + part


def fold_projections(out_ref, at, width, refs):
    query_ref, key_ref, value_ref, output_ref = refs
    pieces = [rows_in(query_ref, width), rows_in(key_ref, KV_WIDTH), rows_in(value_ref, KV_WIDTH)]
    end = fold_into(out_ref, at, pieces)
    end = fold_into(out_ref, end, [rows_in(output_ref, width)])
    out_ref[:, end:] = jnp.zeros((TILE, out_ref.shape[1] - end), low)


def fold_projections_kernel(width, step, steps, *refs):
    fold_projections(refs[-1], 0, width, refs[:-1])


def fold_gates_kernel(ff, step, steps, gate_ref, up_ref, out_ref):
    lane = fold_into(out_ref, 0, [rows_in(gate_ref, ff), rows_in(up_ref, ff)])
    if lane < out_ref.shape[1]:
        out_ref[:, lane:] = jnp.zeros((TILE, out_ref.shape[1] - lane), low)


def fold_down_kernel(width, step, steps, down_ref, out_ref):
    down = rows_in(down_ref, width)
    lane = 0
    for a in range(down.shape[0] // TILE):
        out_ref[:, lane : lane + width] = down[a * TILE : (a + 1) * TILE].astype(low)
        lane += width
    out_ref[:, lane:] = jnp.zeros((TILE, out_ref.shape[1] - lane), low)


def weights_kernel(
    step, steps, feature_ref, own_ref, come_ref, weight_ref, key_value_ref, output_ref, mixed, *folds
):
    width, columns = weight_ref.shape
    half = own_ref.shape[0]
    main = 2 * half
    fold = main // (width - main)
    lane, first = 0, 0
    for scratch, count in zip(folds, (columns, width)):
        part = count // fold
        mixed[:half, first : first + count] = own_ref[:, lane : lane + count]
        mixed[half:main, first : first + count] = come_ref[:, lane : lane + count]
        lane += count
        folded = slice(lane, lane + part)
        fold_write(scratch, jnp.concatenate([own_ref[:, folded], come_ref[:, folded]], axis=0))
        for at in range(fold):
            lanes = slice(first + at * part, first + (at + 1) * part)
            mixed[main:, lanes] = fold_get(scratch, at, fold, part)
        lane += part
        first += count
    natural = dot(mixing_of(feature_ref), mixed[...])
    weight_ref[...] = natural[:, :columns].astype(low)
    output_ref[...] = natural[:, columns:].astype(low)
    keys = natural[:, width : width + KV_WIDTH]
    key_value_ref[:, :KV_WIDTH] = keys.astype(low)
    half_dim = HEAD_SIZE // 2
    swapped = [
        keys[:, (block ^ 1) * half_dim : ((block ^ 1) + 1) * half_dim]
        for block in range(KV_WIDTH // half_dim)
    ]
    key_value_ref[:, KV_WIDTH : 2 * KV_WIDTH] = jnp.concatenate(swapped, axis=1).astype(low)
    key_value_ref[:, 2 * KV_WIDTH :] = natural[:, width + KV_WIDTH : columns].astype(low)


def queries_kernel(step, steps, normed_ref, weight_ref, cos_ref, sin_ref, times, query_ref):
    tokens, width = normed_ref.shape
    half = tokens // 2
    queries = dot(normed_ref[...], weight_ref[:, :width])
    rope = rope_own_of(cos_ref, sin_ref, times)
    for head in range(HEADS):
        turned = turn(queries[:, head * HEAD_SIZE : (head + 1) * HEAD_SIZE], rope, 1.0)
        turned = turned.astype(low) * low(HEAD_SIZE**-0.5)
        for part in range(2):
            row = (part * GROUP + head % GROUP) * half
            query_ref[head // GROUP, row : row + half, :] = turned[part * half : (part + 1) * half]


def project_kernel(step, steps, normed_ref, weight_ref, cos_ref, sin_ref, times, kv_ref):
    width = weight_ref.shape[0]
    groups = normed_ref.shape[1] // width
    for a in range(groups):
        kv = dot(normed_ref[:, a * width : (a + 1) * width], weight_ref[...])
        rope = rope_of(cos_ref, sin_ref, times, a // (groups // 2), a % (groups // 2))
        cos, sin = rope[:, : 2 * HEAD_SIZE], rope[:, 2 * HEAD_SIZE :]
        cos = jnp.concatenate([cos, cos[:, :HEAD_SIZE]], axis=1)
        sin = jnp.concatenate([sin, sin[:, :HEAD_SIZE]], axis=1)
        keys = kv[:, :KV_WIDTH] * cos + kv[:, KV_WIDTH : 2 * KV_WIDTH] * sin
        at = a * 2 * KV_WIDTH
        kv_ref[:, at : at + KV_WIDTH] = keys.astype(low)
        kv_ref[:, at + KV_WIDTH : at + 2 * KV_WIDTH] = kv[:, 2 * KV_WIDTH :].astype(low)


def key_part(kv_ref, groups, column):
    lanes = [a * 2 * KV_WIDTH + column * HEAD_SIZE for a in groups]
    return jnp.concatenate([kv_ref[:, at : at + HEAD_SIZE] for at in lanes], axis=0)


def key_row(key_ref, part, groups):
    start = key_ref[part]
    return jnp.concatenate([start + float(i * TILE) for i in range(len(groups))], axis=1)


def reaches_low(own, blocks):
    return own[3] < blocks


def forward_kernel(
    is_first, low_blocks, step, steps, own, key_ref, query_ref, kv_ref, *rest
):
    state = rest[-1]
    rows = query_ref.shape[1] // 2
    groups = kv_ref.shape[1] // (2 * KV_WIDTH)

    def first():
        if is_first:
            lane = lax.broadcasted_iota(jnp.int32, state.shape, 2)
            state[...] = jnp.where(lane == PEAK, masked_score, 0.0)
        else:
            state[...] = rest[0][...]

    once(step, steps, 0, first)

    def attend(key_half, query_half):
        members = range(key_half * groups // 2, (key_half + 1) * groups // 2)
        at = slice(query_half * rows, (query_half + 1) * rows)
        key_index = key_row(key_ref, key_half, members)
        first_key, last_key = query_range(own, query_half, rows, 0)
        allowed = (key_index >= first_key) & (key_index <= last_key)
        for head in range(KV_HEADS):
            scores = dot_right(query_ref[head, at], key_part(kv_ref, members, head))
            masked = jnp.where(allowed, scores, masked_score)
            old = state[head, at, PEAK : PEAK + 1]
            new = jnp.maximum(old, jnp.max(masked, axis=1, keepdims=True))
            weights = jnp.where(allowed, jnp.exp(masked - new), 0.0)
            factor = jnp.exp(old - new)
            state[head, at, PEAK : PEAK + 1] = new
            state[head, at, TOTAL : TOTAL + 1] = state[
                head, at, TOTAL : TOTAL + 1
            ] * factor + jnp.sum(weights, axis=1, keepdims=True)
            state[head, at, :HEAD_SIZE] = state[head, at, :HEAD_SIZE] * factor + dot(
                weights.astype(low), key_part(kv_ref, members, KV_HEADS + head)
            )

    attend(0, 0)
    pl.when(reaches_low(own, low_blocks))(lambda: attend(0, 1))
    attend(1, 1)


def middle_kernel(
    step,
    steps,
    feature_ref,
    state_ref,
    hidden_ref,
    output_w,
    gain_ref,
    attention,
    attended,
    middle_ref,
    normed,
    normed_t,
    lse_ref,
    natural,
):
    mixing = mixing_of(feature_ref)
    tokens = hidden_ref.shape[0] // 2
    for head in range(KV_HEADS):
        sums = state_ref[head, :, TOTAL : TOTAL + 1]
        attention[head] = state_ref[head, :, :HEAD_SIZE] / sums
        logs = state_ref[head, :, PEAK : PEAK + 1] + jnp.log(sums)
        for part in range(2):
            lse_ref[2 * head + part] = as_row(
                logs[part * GROUP * tokens : (part + 1) * GROUP * tokens]
            )
    for h in range(HEADS):
        for part in range(2):
            row = (part * GROUP + h % GROUP) * tokens
            natural[
                part * tokens : (part + 1) * tokens, h * HEAD_SIZE : (h + 1) * HEAD_SIZE
            ] = attention[h // GROUP, row : row + tokens, :].astype(low)
    middle = hidden_ref[...].astype(full) + dot(natural[...], output_w[...])
    middle_ref[...] = middle
    unit, _ = unit_rows(middle)
    mixed_norm = dot((unit * gain_ref[...]).astype(low), mixing)
    normed[...] = mixed_norm.astype(low)
    normed_t[...] = jnp.transpose(mixed_norm).astype(low)
    attended[...] = dot(natural[...], mixing).astype(low)


def feedforward_kernel(
    step,
    steps,
    source_ref,
    feature_ref,
    attention,
    attended,
    middle_ref,
    normed,
    normed_t,
    output_w,
    gain_ref,
    grad_ref,
    own_ref,
    come_low_ref,
    come_high_ref,
    down_own_ref,
    down_come_ref,
    out_ref,
    grad_middle_ref,
    head_grad_ref,
    delta_ref,
    keep_ref,
    send_ref,
    down_keep_ref,
    down_send_ref,
    gain_part_ref,
    come_ref,
    down_w,
    down_grad,
    total,
    grad_normed,
    extra_grad,
    output_folds,
    late_folds,
):
    rows, width = middle_ref.shape
    half = own_ref.shape[0]
    main = 2 * half
    rest = width - main
    fold = main // rest
    places = main // TILE
    ff = down_w.shape[0]
    chunk = 2 * ff // fold
    down_at = 2 * ff + chunk
    device_ff = ff // places
    groups = device_ff // TILE
    out_at = down_at
    mixing = mixing_of(feature_ref)
    tokens = rows // 2
    part = width // fold
    folded = slice(out_at + width, out_at + width + part)
    come_ref[: half // 2, :] = come_low_ref[...]
    come_ref[half // 2 :, :] = come_high_ref[...]
    middle = middle_ref[...]
    gain = gain_ref[...]
    unit, inverse = unit_rows(middle)
    for place in range(places):
        held = down_own_ref if place < places // 2 else down_come_ref
        row = (place % (places // 2)) * TILE
        for a in range(groups):
            at = pl.multiple_of(source_ref[place] * device_ff + a * TILE, TILE)
            lane = a * width
            down_w[pl.ds(at, TILE), :] = held[row : row + TILE, lane : lane + width]
    total[...] = jnp.zeros_like(total)
    grad_normed[...] = jnp.zeros_like(grad_normed)
    out_grad = grad_ref[...]
    fold_write(
        late_folds,
        jnp.concatenate([own_ref[:, 2 * ff : down_at], come_ref[:, 2 * ff : down_at]], axis=0),
    )

    def advance(c, carry):
        gate_at = pl.ds(pl.multiple_of(c * chunk, 128), chunk)
        up_at = pl.ds(pl.multiple_of(ff + c * chunk, 128), chunk)

        def columns(lanes, at):
            tail = fold_get(late_folds, at, fold, chunk)
            value = (
                dot(normed[:, :half], own_ref[:, lanes])
                + dot(normed[:, half:main], come_ref[:, lanes])
                + dot(normed[:, main:], tail)
            )
            return value, tail

        gate, gate_tail = columns(gate_at, c)
        up, up_tail = columns(up_at, c + fold // 2)
        down_at_c = pl.ds(pl.multiple_of(c * chunk, 128), chunk)
        down = down_w[down_at_c, :]
        sigma = 1.0 / (1.0 + jnp.exp(-gate))
        silu = gate * sigma
        inner = (silu * up).astype(low)
        total[...] += dot(inner, down)
        grad_inner = dot_right(out_grad, down)
        grad_gate = (grad_inner * up * sigma * (1.0 + gate * (1.0 - sigma))).astype(low)
        grad_up = (grad_inner * silu).astype(low)
        down_grad[down_at_c, :] = dot_left(inner, out_grad).astype(low)
        for grad, lanes, tail, at in (
            (grad_gate, gate_at, gate_tail, c),
            (grad_up, up_at, up_tail, c + fold // 2),
        ):
            grad_normed[:, :half] += dot_right(grad, own_ref[:, lanes])
            grad_normed[:, half:main] += dot_right(grad, come_ref[:, lanes])
            grad_normed[:, main:] += dot_right(grad, tail)
            keep_ref[:, lanes] = dot(normed_t[:half], grad).astype(low)
            send_ref[:, lanes] = dot(normed_t[half:main], grad).astype(low)
            fold_put(extra_grad, at, fold, dot(normed_t[main:], grad))
        return carry

    lax.fori_loop(0, ff // chunk, advance, 0)
    out_ref[...] = (middle + total[...]).astype(low)
    extra = fold_read(extra_grad, chunk)
    keep_ref[:, 2 * ff : down_at] = extra[:half]
    send_ref[:, 2 * ff : down_at] = extra[half:]
    for place in range(places):
        held = down_keep_ref if place < places // 2 else down_send_ref
        row = (place % (places // 2)) * TILE
        for a in range(groups):
            at = pl.multiple_of(source_ref[place] * device_ff + a * TILE, TILE)
            lane = a * width
            held[row : row + TILE, lane : lane + width] = down_grad[pl.ds(at, TILE), :]
    unused = jnp.zeros((half, down_keep_ref.shape[1] - groups * width), low)
    down_keep_ref[:, groups * width :] = unused
    down_send_ref[:, groups * width :] = unused

    high = grad_normed[...].astype(low)
    tail = (grad_normed[...] - high.astype(full)).astype(low)
    back = dot_right(high, mixing) + dot_right(tail, mixing)
    gain_part_ref[...] = jnp.sum(back * unit, axis=0, keepdims=True)
    grad_middle = out_grad.astype(full) + norm_back(unit, inverse, gain, back)
    grad_middle_ref[...] = grad_middle
    grad_branch = grad_middle.astype(low)
    output_grad = dot_left(attended[...], grad_branch)
    keep_ref[:, out_at : out_at + width] = output_grad[:half].astype(low)
    send_ref[:, out_at : out_at + width] = output_grad[half:main].astype(low)
    for at in range(fold):
        fold_put(output_folds, at, fold, output_grad[main:, at * part : (at + 1) * part])
    extra = fold_read(output_folds, part)
    unused = jnp.zeros((half, keep_ref.shape[1] - folded.stop), low)
    for held, rows_of_half in ((keep_ref, extra[:half]), (send_ref, extra[half:])):
        held[:, folded] = rows_of_half
        held[:, folded.stop :] = unused
    grad_low = dot_right(grad_branch, output_w[...]).astype(low)
    for head in range(KV_HEADS):
        for part in range(2):
            grads = jnp.concatenate(
                [
                    grad_low[
                        part * tokens : (part + 1) * tokens, h * HEAD_SIZE : (h + 1) * HEAD_SIZE
                    ]
                    for h in range(head * GROUP, (head + 1) * GROUP)
                ],
                axis=0,
            )
            at = slice(part * GROUP * tokens, (part + 1) * GROUP * tokens)
            head_grad_ref[head, at] = grads
            delta_ref[2 * head + part] = as_row(
                jnp.sum(grads.astype(full) * attention[head, at], axis=1, keepdims=True)
            )


def backward_kernel(
    is_first,
    key_half,
    low_blocks,
    joined,
    step,
    steps,
    own,
    key_ref,
    query_ref,
    grad_ref,
    lse_ref,
    delta_ref,
    kv_ref,
    tokens_ref,
    cos_ref,
    sin_ref,
    times,
    *rest,
):
    if not is_first:
        held, rest = rest[:2], rest[2:]
    if joined:
        high_ref, rest = rest[0], rest[1:]
        rest[2][:, high_ref.shape[1] :] = high_ref[...]
    grad_query, grad_weight, out_ref, grad_kv = rest
    rows = query_ref.shape[1] // 2
    groups = kv_ref.shape[1] // (2 * KV_WIDTH)
    key_rows = kv_ref.shape[0]
    width = tokens_ref.shape[1] // groups
    members = range(key_half * groups // 2, (key_half + 1) * groups // 2)

    def first():
        if is_first:
            grad_query[...] = jnp.zeros_like(grad_query)
            grad_weight[...] = jnp.zeros_like(grad_weight)
        else:
            grad_query[...] = held[0][...]
            grad_weight[...] = held[1][...]

    once(step, steps, 0, first)
    key_index = key_row(key_ref, key_half, members)
    key_index = jnp.transpose(jnp.broadcast_to(key_index, (128, key_index.shape[1])))[:, 0:1]

    def attend(query_half, add):
        at = slice(query_half * rows, (query_half + 1) * rows)
        first_key, last_key = query_range(own, query_half, rows, 1)
        allowed = (key_index >= first_key) & (key_index <= last_key)
        for head in range(KV_HEADS):
            keys = key_part(kv_ref, members, head)
            scores = dot_right(keys, query_ref[head, at])
            probs = jnp.where(allowed, jnp.exp(scores - lse_ref[2 * head + query_half]), 0.0)
            d_probs = dot_right(key_part(kv_ref, members, KV_HEADS + head), grad_ref[head, at])
            d_scores = (probs * (d_probs - delta_ref[2 * head + query_half])).astype(low)
            grad_query[2 * head + query_half] += dot_left(keys, d_scores)
            parts = (
                (head, dot(d_scores, query_ref[head, at])),
                (KV_HEADS + head, dot(probs.astype(low), grad_ref[head, at])),
            )
            for column, value in parts:
                lanes = slice(column * HEAD_SIZE, (column + 1) * HEAD_SIZE)
                if add:
                    grad_kv[:, lanes] += value
                else:
                    grad_kv[:, lanes] = value

    if key_half == 0:
        attend(0, False)
        pl.when(reaches_low(own, low_blocks))(lambda: attend(1, True))
    else:
        attend(1, False)
    for i, a in enumerate(members):
        at = slice(i * key_rows, (i + 1) * key_rows)
        rope = rope_of(cos_ref, sin_ref, times, key_half, i)
        turned = jnp.concatenate(
            [
                turn(grad_kv[at, head * HEAD_SIZE : (head + 1) * HEAD_SIZE], rope, -1.0)
                for head in range(KV_HEADS)
            ]
            + [grad_kv[at, KV_WIDTH:]],
            axis=1,
        ).astype(low)
        lane = i * 2 * KV_WIDTH
        out_ref[:, lane : lane + 2 * KV_WIDTH] = turned
        grad_weight[...] += dot_left(turned, tokens_ref[:, a * width : (a + 1) * width])


def qkv_grad_kernel(
    step,
    steps,
    feature_ref,
    grad_query,
    grad_weight,
    normed_ref,
    weight_ref,
    cos_ref,
    sin_ref,
    times,
    gain_ref,
    gain_two_ref,
    query_grad_ref,
    gains_ref,
    keep_ref,
    send_ref,
    natural,
    folds,
):
    tokens, width = normed_ref.shape
    half = tokens // 2
    rope = rope_own_of(cos_ref, sin_ref, times)
    for head in range(KV_HEADS):
        rotated = [
            jnp.transpose(grad_query[2 * head + part]) * HEAD_SIZE**-0.5 for part in range(2)
        ]
        for g in range(GROUP):
            h = head * GROUP + g
            value = jnp.concatenate([part[g * half : (g + 1) * half] for part in rotated], axis=0)
            query_grad_ref[:, h * HEAD_SIZE : (h + 1) * HEAD_SIZE] = turn(value, rope, -1.0).astype(
                low
            )
    natural[:, :width] = dot_left(normed_ref[...], query_grad_ref[...])
    natural[:, width:] = jnp.transpose(grad_weight[...])
    products = natural[...] * weight_ref[...].astype(full)
    gain_part = as_row(jnp.sum(products, axis=1, keepdims=True)) / gain_ref[...]
    gains = fold_gains([gain_part, gain_two_ref[...]])
    gains_ref[...] = gains
    mixed = dot_left(mixing_of(feature_ref), natural[...].astype(low)).astype(low)
    columns = mixed.shape[1]
    rows = keep_ref.shape[0]
    main = 2 * rows
    fold = main // (width - main)
    part = columns // fold
    for at in range(fold):
        fold_put(folds, at, fold, mixed[main:, at * part : (at + 1) * part].astype(full))
    extra = fold_read(folds, part)
    unused = jnp.zeros((rows, keep_ref.shape[1] - columns - part), low)
    for held, at in ((keep_ref, 0), (send_ref, rows)):
        held[:rows, :columns] = mixed[at : at + rows]
        held[:rows, columns : columns + part] = extra[at : at + rows]
        held[:rows, columns + part :] = unused
    send_ref[:TILE, columns + part : columns + part + gains.shape[1]] = gains.astype(low)


def merge_kernel(gain_at, step, steps, *refs):
    keep_low, keep_high, kv_come, w_keep, w_come, gains_ref, keep_out, send_out, gains_out = refs
    half = w_keep.shape[0] // 2
    part = keep_low.shape[1]
    base = 2 * part
    lane = 0
    for keep, come, first in (
        (keep_low, kv_come, 0),
        (keep_high, kv_come, part),
        (w_keep, w_come, 0),
    ):
        columns = keep.shape[1]
        for out, at in ((keep_out, 0), (send_out, half)):
            value = keep[at : at + half, :].astype(full) + come[
                at : at + half, first : first + columns
            ].astype(full)
            out[:, lane : lane + columns] = value.astype(low)
        lane += columns
    lanes = slice(gain_at, gain_at + gains_ref.shape[1])
    gains = sum_gains(gains_ref[...], w_come[:TILE, lanes])
    gains_out[...] = gains
    send_out[:TILE, base + lanes.start : base + lanes.stop] = gains.astype(low)


def add_kernel(gain_at, step, steps, keep_ref, come_ref, *rest):
    rows = keep_ref.shape[0]
    if gain_at is not None:
        gains_ref, keep_out, send_out, gains_out = rest
        lanes = slice(gain_at, gain_at + gains_ref.shape[1])
        gains = sum_gains(gains_ref[...], come_ref[:TILE, lanes])
        gains_out[...] = gains
        rest = rest[1:-1]

    def tile(at):
        at = pl.ds(at, TILE)
        return keep_ref[at, :].astype(full) + come_ref[at, :].astype(full)

    if rows == TILE:
        rest[0][...] = tile(0)
        return
    keep_out, send_out = rest
    half = rows // 2

    def advance(i, carry):
        at = pl.multiple_of(i * TILE, TILE)
        keep_out[pl.ds(at, TILE), :] = tile(at).astype(low)
        send_out[pl.ds(at, TILE), :] = tile(pl.multiple_of(half + at, TILE)).astype(low)
        return carry

    lax.fori_loop(0, half // TILE, advance, 0)
    if gain_at is not None:
        send_out[:TILE, lanes] = gains.astype(low)


def scatter_halves(
    keep, leaving, steps, name, gains=None, gain_at=None, after=None, between=None
):
    for at, partner in enumerate(reversed(steps)):
        come = send(leaving, partner)
        rows, columns = keep.shape
        ins = [("whole", keep), ("whole", come)]
        if rows == TILE:
            if gains is not None:
                return keep, come, gains
            outs = [("whole", shape_of((rows, columns), full))]
        else:
            outs = [("whole", shape_of((rows // 2, columns), low))] * 2
        if gains is not None:
            ins.append(("whole", gains))
            outs.append(("whole", shape_of(gains.shape, full)))
        result = one_call(
            functools.partial(add_kernel, gain_at),
            name,
            ins,
            outs,
            [],
            1,
            (after or {}).get(at, ()),
        )
        if between:
            between(at, result[-1])
        if gains is not None:
            gains = result[-2]
        if rows == TILE:
            return result[0]
        keep, leaving = result[0], result[1]


def final_kernel(
    base,
    step,
    steps,
    keep_ref,
    come_ref,
    query_grad_ref,
    weight_ref,
    hidden_ref,
    gain_ref,
    grad_middle_ref,
    *rest,
):
    grads = rest[-1]
    tokens, width = hidden_ref.shape
    grads[:, :width] = query_grad_ref[...]
    for a in range(tokens // TILE):
        rows = slice(a * TILE, (a + 1) * TILE)
        lanes = slice(a * 2 * KV_WIDTH, (a + 1) * 2 * KV_WIDTH)
        value = keep_ref[:, lanes].astype(full) + come_ref[:, lanes].astype(full)
        grads[rows, width:] = value.astype(low)
    back = dot_right(grads[...], weight_ref[...])
    unit, inverse = unit_rows(hidden_ref[...].astype(full))
    out_ref = rest[-6] if base else rest[-2]
    out_ref[...] = (grad_middle_ref[...] + norm_back(unit, inverse, gain_ref[...], back)).astype(low)
    if not base:
        return
    gains_ref, _, query_out, key_out, value_out, gains_out, _ = rest
    columns = weight_ref.shape[1]
    total = keep_ref[:, base:].astype(full) + come_ref[:, base:].astype(full)
    fold = gains_ref.shape[0] // 2
    part = columns // fold
    for row in range(TILE + TILE // fold):
        if row < TILE:
            value = total[row : row + 1, :columns]
        else:
            at = (row - TILE) * fold
            value = jnp.concatenate(
                [total[at + i : at + i + 1, columns : columns + part] for i in range(fold)], axis=1
            )
        query_out[:, row * width : (row + 1) * width] = value[:, :width]
        for out, first in ((key_out, width), (value_out, width + KV_WIDTH)):
            out[:, row * KV_WIDTH : (row + 1) * KV_WIDTH] = value[:, first : first + KV_WIDTH]
    at = columns + part
    lanes = slice(at, at + gains_ref.shape[1])
    gains = sum_gains(gains_ref[...], come_ref[:TILE, base + lanes.start : base + lanes.stop])
    for k in range(2):
        gains_out[k : k + 1, :] = jnp.concatenate(
            [gains[k * fold + i : k * fold + i + 1] for i in range(fold)], axis=1
        )


def body(
    hidden_in,
    attention_gain,
    query_weight,
    key_weight,
    value_weight,
    output_weight,
    feedforward_gain,
    gate_weight,
    up_weight,
    down_weight,
    doc_of_block,
    pair_table,
    out_grad,
):
    tokens, width = hidden_in.shape
    half_rows = tokens // 2
    count = lax.axis_size("ctx")
    device = lax.axis_index("ctx")
    ff = gate_weight.shape[1] * count // width
    low_bits = low_bits_of(query_weight.shape[1], width)
    merged = low_bits == 0
    row_steps = exchange_steps(count, low_bits)
    token_steps = exchange_steps(count, 0)
    down_steps = row_steps[2:4] + row_steps[:2] + row_steps[4:] if merged else row_steps
    group_count = count >> low_bits
    group_rows = width // group_count
    groups = tokens // TILE
    steps = max(1, TILE * count // 512)
    places = count // (2 * steps)
    gain_one = attention_gain.reshape(1, width)
    gain_two = feedforward_gain.reshape(1, width)
    columns = width + 2 * KV_WIDTH
    main = TILE * group_count
    fold = main // (width - main)
    w_lanes = whole_lanes(columns + columns // fold + 2 * width // TILE)
    projection_lanes = whole_lanes((columns + width) + (columns + width) // fold)
    ff_folded = 2 * ff // fold
    out_at = 2 * ff + ff_folded
    device_groups = ff // group_count // TILE
    late_lanes = whole_lanes(out_at + width + width // fold)
    gate_lanes = whole_lanes(out_at)
    down_lanes = whole_lanes(device_groups * width)
    call = Call(steps)
    one = Call(1)

    def rows_of(piece, piece_columns):
        if low_bits:
            piece = whole_rows(piece, device, low_bits, piece_columns)
        return ("whole", piece)

    projections = [
        rows_of(query_weight, width),
        rows_of(key_weight, KV_WIDTH),
        rows_of(value_weight, KV_WIDTH),
        rows_of(output_weight, width),
    ]
    token_parts = (groups * width, projection_lanes) if merged else (groups * width,)
    packed, normed, pack_mark = one(
        pack_kernel,
        "norm_and_pack",
        [("whole", hidden_in), ("whole", gain_one)] + (projections if merged else []),
        [
            ("whole", shape_of((TILE, sum(token_parts)), low)),
            ("whole", shape_of((tokens, width), low)),
        ],
        [],
        1,
    )

    def table_row(table):
        return lax.dynamic_index_in_dim(jnp.asarray(table), device, 0, keepdims=False)

    sources = table_row(source_table(count, 0, token_steps))
    down_sources = table_row(source_table(count, low_bits, down_steps))
    group_table = source_table(count, low_bits, row_steps)
    inside = np.arange(group_rows)[None, None, :]
    features = group_table[:, :, None] * group_rows + inside
    features = np.concatenate(
        [
            features[:, :, :TILE].reshape(count, -1),
            features[:, :, TILE:].reshape(count, -1),
        ],
        axis=1,
    ).astype(np.int32)
    feature_row = table_row(features).reshape(1, width)

    device_iota = jnp.arange(count, dtype=jnp.int32)
    pairs = jnp.sum(
        jnp.where(sources[:, None] == device_iota[None, :], pair_table[None, :], 0), axis=1
    )
    blocks = jnp.stack([pairs, 2 * count - 1 - pairs], axis=1).reshape(-1)
    block_iota = jnp.arange(2 * count, dtype=jnp.int32)
    block_docs = jnp.sum(
        jnp.where(blocks[:, None] == block_iota[None, :], doc_of_block[None, :], 0), axis=1
    )
    doc_start = jnp.min(
        jnp.where(block_docs[:, None] == doc_of_block[None, :], block_iota[None, :], 2 * count),
        axis=1,
    )
    own = jnp.concatenate([blocks[:2], doc_start[:2]])

    def by_step(values):
        return values.reshape(2, steps, places, 2).transpose(0, 1, 3, 2)

    inner = jnp.arange(TILE, dtype=jnp.int32)
    key_index = by_step(blocks)[..., None] * half_rows + inner
    key_index = key_index.astype(full).reshape(2, 2 * steps, 1, -1)
    frequency = rope_base ** (-jnp.arange(HEAD_SIZE // 2, dtype=full) * (2.0 / HEAD_SIZE))
    block_angle = (by_step(blocks - doc_start) * half_rows).astype(full)[..., None] * frequency
    offset = jnp.arange(half_rows, dtype=full).reshape(groups // 2, TILE)
    offset_angle = offset[..., None] * frequency
    cos_in, sin_in = jnp.cos(offset_angle), jnp.sin(offset_angle)
    times_cos = jnp.concatenate([cos_in] * 4 + [-sin_in, sin_in] * 2, axis=-1)
    times_sin = jnp.concatenate([sin_in] * 4 + [cos_in, -cos_in] * 2, axis=-1)
    times = jnp.stack([times_cos, times_sin])
    block_cos = jnp.tile(jnp.cos(block_angle), 8).reshape(2, 2 * steps, places, 1, 4 * HEAD_SIZE)
    block_sin = jnp.tile(jnp.sin(block_angle), 8).reshape(2, 2 * steps, places, 1, 4 * HEAD_SIZE)
    own_cos, own_sin = block_cos[0, :2, :1], block_sin[0, :2, :1]
    rope_own = [("whole", own_cos), ("whole", own_sin), ("whole", times)]
    key_index, block_cos, block_sin = (
        [values[0], values[1]] for values in (key_index, block_cos, block_sin)
    )
    tables = key_index + block_cos + block_sin + [own, own_cos, own_sin, times, feature_row]
    late_at = 2
    down, down_mark = one(
        functools.partial(fold_down_kernel, width),
        "fold_down",
        [rows_of(down_weight, width)],
        [("whole", shape_of((TILE, down_lanes), low))],
        [],
        1,
        [pack_mark],
    )
    late, late_mark = one(
        functools.partial(fold_gates_kernel, ff),
        "fold_gates",
        [rows_of(gate_weight, ff), rows_of(up_weight, ff)],
        [("whole", shape_of((TILE, gate_lanes), low))],
        [],
        1,
        [pack_mark],
    )

    def release(values, name, after):
        return one(
            copy_kernel,
            "release_" + name,
            [("whole", values)],
            [("whole", shape_of(values.shape, low))],
            [],
            1,
            after,
        )[0]

    mark = None
    for at, partner in enumerate(token_steps[:-1]):
        after = []
        if at == 0:
            after = [down_mark]
        elif at == 1:
            down = release(down, "down", [mark])
            down, down_mark = join(down, send(down, down_steps[0]), "down", [])
            after = [down_mark, late_mark] + tables
        elif at == late_at:
            late = release(late, "gates", [mark])
            late, late_mark = join(late, send(late, row_steps[0]), "gates", [])
            down, down_mark = join(down, send(down, down_steps[1]), "down", [])
            after = [late_mark, down_mark]
        elif at == late_at + 1:
            late, late_mark = join(late, send(late, row_steps[1]), "gates", [])
            down = release(down, "down", [late_mark])
            down, down_mark = join(down, send(down, down_steps[2]), "down", [])
            after = [down_mark]
        last = at == len(token_steps) - 2
        *held, mark = join(
            packed,
            send(packed, partner),
            "tokens",
            after,
            token_parts if last else (),
        )
        packed = held[0]
    token_own = packed
    if merged:
        w_own, w_come = held[1], send(held[1], token_steps[-1])
    else:
        qkv_piece, _ = one(
            functools.partial(fold_projections_kernel, width),
            "fold_projections",
            projections,
            [("whole", shape_of((TILE, projection_lanes), low))],
            [],
            1,
        )
        w_own, w_come = gather_halves(qkv_piece, row_steps, "qkv")
    token_come = send(token_own, token_steps[-1])

    halves = [
        (
            held,
            key_index[place],
            [("rows", block_cos[place]), ("rows", block_sin[place]), ("whole", times)],
        )
        for place, held in enumerate((token_own, token_come))
    ]

    rows = GROUP * tokens
    half = TILE * count // 2
    kv_shape = shape_of((half, groups * 2 * KV_WIDTH), low)
    head_shape = (KV_HEADS, rows, HEAD_SIZE)
    weight, kv_weight, output_w, _ = one(
        weights_kernel,
        "qkv_weights",
        [("whole", feature_row), ("whole", w_own), ("whole", w_come)],
        [
            ("whole", shape_of((width, columns), low)),
            ("whole", shape_of((width, 3 * KV_WIDTH), low)),
            ("whole", shape_of((width, width), low)),
        ],
        [
            pltpu.VMEM((width, columns + width), low),
            fold_scratch(main, columns // fold),
            fold_scratch(main, width // fold),
        ],
        3,
    )
    queries, _ = one(
        queries_kernel,
        "queries",
        [("whole", normed), ("whole", weight)] + rope_own,
        [("whole", shape_of(head_shape, low))],
        [],
        2,
    )

    def project(place, after):
        token_rows, _, turns = halves[place]
        return call(
            project_kernel,
            "project",
            [("rows", token_rows), ("whole", kv_weight)] + turns,
            [("rows", kv_shape)],
            [],
            5,
            after,
        )

    state_shapes = [("whole", shape_of((KV_HEADS, rows, 2 * HEAD_SIZE), full))]

    def attend(place, kv, state, after):
        return call(
            functools.partial(forward_kernel, not state, count),
            "attention_forward",
            [
                ("smem", own),
                ("rows", halves[place][1]),
                ("whole", queries),
                ("rows", kv),
            ]
            + [("whole", held) for held in state],
            state_shapes,
            [],
            6,
            after,
        )

    kv_own, mark = project(0, [])
    late, late_mark = join(late, send(late, row_steps[2]), "gates", [mark])
    down, down_mark = join(down, send(down, down_steps[3]), "down", [mark])
    come_low = send(late, row_steps[4])
    down_come = send(down, down_steps[4])
    *state, mark = attend(0, kv_own, [], [late_mark, down_mark])
    kv_come, mark = project(1, [mark])
    *state, mark = attend(1, kv_come, state, [])
    late_high = release(send(late, row_steps[3]), "high", [mark])
    come_high = send(late_high, row_steps[4])
    late_own, mark = join(late, late_high, "gates", [])

    row_shape = ("whole", shape_of((2 * KV_HEADS, 1, rows // 2), full))
    token_low = ("whole", shape_of((tokens, width), low))
    token_full = ("whole", shape_of((tokens, width), full))
    *inner_values, lse, _ = one(
        middle_kernel,
        "middle",
        [
            ("whole", feature_row),
            ("whole", state[0]),
            ("whole", hidden_in),
            ("whole", output_w),
            ("whole", gain_two),
        ],
        [
            ("whole", shape_of(head_shape, full)),
            token_low,
            token_full,
            token_low,
            ("whole", shape_of((width, tokens), low)),
            row_shape,
        ],
        [pltpu.VMEM((tokens, width), low)],
        3,
        [mark],
    )
    late_shape = shape_of((late_own.shape[0], late_lanes), low)
    down_shape = shape_of(down.shape, low)
    (
        block_out,
        grad_middle,
        head_grads,
        delta,
        late_keep,
        late_send,
        down_keep,
        down_send,
        gain_two_part,
        _,
    ) = one(
        feedforward_kernel,
        "feedforward",
        [
            ("smem", down_sources),
            ("whole", feature_row),
        ]
        + [("whole", held) for held in inner_values]
        + [
            ("whole", output_w),
            ("whole", gain_two),
            ("whole", out_grad),
            ("whole", late_own),
            ("whole", come_low),
            ("whole", come_high),
            ("whole", down),
            ("whole", down_come),
        ],
        [
            token_low,
            token_full,
            ("whole", shape_of(head_shape, low)),
            row_shape,
            ("whole", late_shape),
            ("whole", late_shape),
            ("whole", down_shape),
            ("whole", down_shape),
            ("whole", shape_of((1, width), full)),
        ],
        [
            pltpu.VMEM(late_own.shape, low),
            pltpu.VMEM((ff, width), low),
            pltpu.VMEM((ff, width), low),
            pltpu.VMEM((tokens, width), full),
            pltpu.VMEM((tokens, width), full),
            fold_scratch(main, ff_folded),
            fold_scratch(main, width // fold),
            fold_scratch(main, ff_folded),
        ],
        11,
        vmem=24,
    )

    def attend_back(place, key_half, kv, carried, after, joined=()):
        token_rows, keys, turns = halves[place]
        return call(
            functools.partial(backward_kernel, not carried, key_half, count, bool(joined)),
            "attention_backward",
            [
                ("smem", own),
                ("rows", keys),
                ("whole", queries),
                ("whole", head_grads),
                ("whole", lse),
                ("whole", delta),
                ("rows", kv),
                ("rows", token_rows),
            ]
            + turns
            + [("whole", held) for held in carried]
            + [("rows", part) for part in joined],
            [
                ("whole", shape_of((2 * KV_HEADS, HEAD_SIZE, rows // 2), full)),
                ("whole", shape_of((2 * KV_WIDTH, width), full)),
                ("rows", shape_of((half, groups * KV_WIDTH * (1 + len(joined))), low)),
            ],
            [pltpu.VMEM((groups // 2 * places * TILE, 2 * KV_WIDTH), full)],
            6,
            after,
        )

    class Adding:
        def __init__(self, keep, leaving, steps, name):
            self.keep, self.leaving, self.steps, self.name = keep, leaving, steps[::-1], name

        def step(self, after):
            come = send(self.leaving, self.steps[0])
            self.steps = self.steps[1:]
            rows, columns = self.keep.shape
            outs = [shape_of((rows // 2, columns), low)] * 2
            if rows == TILE:
                outs = [shape_of((rows, columns), full)]
            *result, token = one(
                functools.partial(add_kernel, None),
                self.name,
                [("whole", self.keep), ("whole", come)],
                [("whole", out) for out in outs],
                [],
                1,
                after,
            )
            self.keep, self.leaving = result[0], result[-1]
            return token

    late_chain = Adding(late_keep, late_send, row_steps, "add_late")
    down_chain = Adding(down_keep, down_send, down_steps, "add_down")
    *carried, send_high, mark = attend_back(1, 1, kv_come, [], [])
    marks = [late_chain.step([mark]), down_chain.step([mark])]
    *carried, kv_send, mark = attend_back(1, 0, kv_come, carried, marks, [send_high])
    *carried, keep_high, mark = attend_back(0, 1, kv_own, carried, [])
    marks = [late_chain.step([mark]), down_chain.step([mark])]
    *carried, keep_low, mark = attend_back(0, 0, kv_own, carried, marks)
    query_grad, gains, w_keep, w_send, mark = one(
        qkv_grad_kernel,
        "qkv_gradients",
        [
            ("whole", feature_row),
            ("whole", carried[0]),
            ("whole", carried[1]),
            ("whole", normed),
            ("whole", weight),
        ]
        + rope_own
        + [
            ("whole", gain_one),
            ("whole", gain_two_part),
        ],
        [
            ("whole", shape_of((tokens, width), low)),
            ("whole", shape_of((TILE, 2 * width // TILE), full)),
            ("whole", shape_of((main // 2, w_lanes), low)),
            ("whole", shape_of((main // 2, w_lanes), low)),
        ],
        [pltpu.VMEM((width, columns), full), fold_scratch(main, columns // fold)],
        3,
    )
    late_mark = late_chain.step([mark])
    ends = [
        ("whole", query_grad),
        ("whole", weight),
        ("whole", hidden_in),
        ("whole", gain_one),
        ("whole", grad_middle),
    ]
    end_scratch = [pltpu.VMEM((tokens, columns), low)]
    input_shape = ("whole", shape_of((tokens, width), low))
    if merged:
        gain_at = columns + columns // fold
        base = kv_send.shape[1]
        lanes = base + w_lanes
        keep, leaving, gains, mark = one(
            functools.partial(merge_kernel, gain_at),
            "add_first",
            [
                ("whole", keep_low),
                ("whole", keep_high),
                ("whole", send(kv_send, token_steps[-1])),
                ("whole", w_keep),
                ("whole", send(w_send, token_steps[-1])),
                ("whole", gains),
            ],
            [
                ("whole", shape_of((half // 2, lanes), low)),
                ("whole", shape_of((half // 2, lanes), low)),
                ("whole", shape_of(gains.shape, full)),
            ],
            [],
            2,
            [late_mark],
        )
        others = {0: [down_chain.step([mark])]}

        def between(at, token):
            if at < 2:
                others[at + 1] = [late_chain.step([token]), down_chain.step([token])]

        keep, come, gains = scatter_halves(
            keep, leaving, token_steps[:-1], "add_chain", gains, base + gain_at, others, between
        )
        input_grad, query_w_grad, key_w_grad, value_w_grad, gains, _ = one(
            functools.partial(final_kernel, base),
            "last_gradients",
            [("whole", keep), ("whole", come)] + ends + [("whole", gains)],
            [
                input_shape,
                ("whole", shape_of((1, query_weight.shape[1]), full)),
                ("whole", shape_of((1, key_weight.shape[1]), full)),
                ("whole", shape_of((1, value_weight.shape[1]), full)),
                ("whole", shape_of((2, width), full)),
            ],
            end_scratch,
            1,
        )
        gain_sums = (gains[0], gains[1])
    else:
        for _ in range(2):
            late_chain.step([])
        for _ in range(3):
            down_chain.step([])
        kv_keep = jnp.concatenate([keep_low, keep_high], axis=1)
        kv_sum = scatter_halves(kv_keep, kv_send, token_steps, "add_kv")
        qkv_sum = scatter_halves(w_keep, w_send, row_steps, "add_qkv")
        gains = lax.psum(gains, "ctx").reshape(2, width)
        gain_sums = (gains[0], gains[1])
        input_grad, _ = one(
            functools.partial(final_kernel, 0),
            "input_gradient",
            [("whole", kv_sum), ("whole", jnp.zeros_like(kv_sum))] + ends,
            [input_shape],
            end_scratch,
            1,
        )
        qkv_rows = unfold_rows(qkv_sum, columns, columns // fold)
        query_w_grad, key_w_grad, value_w_grad = (
            own_piece(qkv_rows[:, first:last], device, low_bits)
            for first, last in (
                (0, width),
                (width, width + KV_WIDTH),
                (width + KV_WIDTH, columns),
            )
        )

    def piece_of(piece_rows):
        return own_piece(piece_rows, device, low_bits)

    late_sum, down_sum = late_chain.keep, down_chain.keep
    ff_rows = unfold_rows(late_sum, 2 * ff, ff_folded)
    down_rows = jnp.concatenate(
        [down_sum[:, a * width : (a + 1) * width] for a in range(device_groups)], axis=0
    )
    output_rows = unfold_rows(late_sum[:, out_at:], width, width // fold)
    return (
        block_out,
        input_grad,
        gain_sums[0],
        query_w_grad,
        key_w_grad,
        value_w_grad,
        piece_of(output_rows),
        gain_sums[1],
        piece_of(ff_rows[:, :ff]),
        piece_of(ff_rows[:, ff:]),
        piece_of(down_rows),
    )


def solution(mesh):
    row = P("ctx", None)
    in_specs = (row, P(), row, row, row, row, P(), row, row, row, P(), P(), row)
    out_specs = (row, row, P(), row, row, row, row, P(), row, row, row)
    return jax.shard_map(body, mesh=mesh, in_specs=in_specs, out_specs=out_specs, check_vma=False)
```

```python
import functools

import jax
import jax.numpy as jnp
import numpy as np
from jax import lax
from jax.experimental import pallas as pl
from jax.experimental.pallas import tpu as pltpu
from jax.sharding import PartitionSpec as P

HEADS = 9
KV_HEADS = 3
GROUP = HEADS // KV_HEADS
HEAD_SIZE = 64
KV_WIDTH = KV_HEADS * HEAD_SIZE
TILE = 16
TOTAL, PEAK = HEAD_SIZE, HEAD_SIZE + 1

epsilon = 1e-05
rope_base = 100000.0
masked_score = -1e30

low = jnp.bfloat16
full = jnp.float32


def exchange_steps(device_count, low_bits):
    top = device_count.bit_length() - 1
    steps = []
    if low_bits == 0 and top >= 4:
        for bit in range(top - 1, 2, -1):
            steps.append([i ^ (1 << bit) for i in range(device_count)])
        steps.append([i ^ (4 if i & 1 else 2) for i in range(device_count)])
        steps.append([i ^ (2 if i & 1 else 4) for i in range(device_count)])
        steps.append([i ^ 1 for i in range(device_count)])
    else:
        for bit in range(top - 1, low_bits - 1, -1):
            steps.append([i ^ (1 << bit) for i in range(device_count)])
    return steps


def source_table(device_count, low_bits, steps):
    held = [[d >> low_bits] for d in range(device_count)]
    for partner in steps:
        held = [held[d] + held[partner[d]] for d in range(device_count)]
    return np.array(held, np.int32)


def send(values, partner):
    return lax.ppermute(values, "ctx", [(i, p) for i, p in enumerate(partner)])


def gather_halves(values, steps, name):
    for partner in steps[:-1]:
        values, _ = join(values, send(values, partner), name, [])
    return values, send(values, steps[-1])


def whole_rows(flat, device, low_bits, columns):
    for bit in range(low_bits):
        partner = [i ^ (1 << bit) for i in range(lax.axis_size("ctx"))]
        other = send(flat, partner)
        is_high = (device >> bit) & 1
        flat = jnp.concatenate(
            [jnp.where(is_high, other, flat), jnp.where(is_high, flat, other)], axis=1
        )
    return flat.reshape(-1, columns)


def own_piece(rows, device, low_bits):
    flat = rows.reshape(1, -1)
    for bit in range(low_bits - 1, -1, -1):
        partner = [i ^ (1 << bit) for i in range(lax.axis_size("ctx"))]
        half = flat.shape[1] // 2
        is_high = (device >> bit) & 1
        leaving = jnp.where(is_high, flat[:, :half], flat[:, half:]).astype(low)
        staying = jnp.where(is_high, flat[:, half:], flat[:, :half])
        flat = staying + send(leaving, partner).astype(full)
    return flat


def low_bits_of(piece, columns):
    low_bits = 0
    while (piece << low_bits) < TILE * columns:
        low_bits += 1
    return low_bits


def unfold_rows(packed, columns, folded):
    return jnp.concatenate(
        [packed[:, :columns], packed[:, columns : columns + folded].reshape(-1, columns)], axis=0
    )


def whole_lanes(columns):
    return -(-columns // 128) * 128


def dot(left, right):
    return jnp.dot(left, right, preferred_element_type=full)


def dot_right(left, right):
    return lax.dot_general(left, right, (((1,), (1,)), ((), ())), preferred_element_type=full)


def dot_left(left, right):
    return lax.dot_general(left, right, (((0,), (0,)), ((), ())), preferred_element_type=full)


def iota(shape, axis):
    return lax.broadcasted_iota(jnp.int32, shape, axis)


def mixing_of(feature_ref):
    width = feature_ref.shape[1]
    return (iota((width, width), 0) == feature_ref[...]).astype(full).astype(low)


def fold_scratch(main, part):
    return pltpu.VMEM((-(-part // 128), main, 128), full)


def fold_write(scratch, extra):
    for block in range(scratch.shape[0]):
        lanes = slice(block * 128, min(block * 128 + 128, extra.shape[1]))
        scratch[block, :, : lanes.stop - lanes.start] = extra[:, lanes].astype(full)


def fold_read(scratch, part):
    parts = [scratch[block] for block in range(scratch.shape[0])]
    return jnp.concatenate(parts, axis=1)[:, :part].astype(low)


def fold_get(scratch, at, fold, part):
    rows = pl.ds(at, scratch.shape[1] // fold, stride=fold)
    parts = [scratch.at[block][rows, :] for block in range(scratch.shape[0])]
    return jnp.concatenate(parts, axis=1)[:, :part].astype(low)


def fold_put(scratch, at, fold, value):
    rows = pl.ds(at, scratch.shape[1] // fold, stride=fold)
    missing = scratch.shape[0] * 128 - value.shape[1]
    if missing:
        value = jnp.concatenate([value, jnp.zeros((value.shape[0], missing), full)], axis=1)
    for block in range(scratch.shape[0]):
        scratch.at[block][rows, :] = value[:, block * 128 : (block + 1) * 128]


def as_row(column):
    return jnp.transpose(jnp.broadcast_to(column, (column.shape[0], 128)))[0:1]


def turn(values, rope, direction):
    half_dim = HEAD_SIZE // 2
    swapped = jnp.concatenate([values[:, half_dim:], values[:, :half_dim]], axis=1)
    sine = rope[:, 2 * HEAD_SIZE : 3 * HEAD_SIZE]
    return values * rope[:, :HEAD_SIZE] + swapped * (direction * sine)


def rope_of(cos_ref, sin_ref, times, part, quarter):
    _, places, _, lanes = cos_ref.shape
    value = cos_ref[part] * times[0, quarter] - sin_ref[part] * times[1, quarter]
    return value.reshape(places * TILE, lanes)


def rope_own_of(cos_ref, sin_ref, times):
    _, quarters, rows, lanes = times.shape
    parts = [
        cos_ref[part, 0] * times[0] - sin_ref[part, 0] * times[1] for part in range(2)
    ]
    return jnp.concatenate([part.reshape(quarters * rows, lanes) for part in parts], axis=0)


def unit_rows(values):
    inverse = lax.rsqrt(jnp.mean(values * values, axis=-1, keepdims=True) + epsilon)
    return values * inverse, inverse


def norm_back(unit, inverse, gain, grad):
    scaled = grad * gain
    return inverse * (scaled - unit * jnp.mean(scaled * unit, axis=-1, keepdims=True))


def query_range(own, part, rows, axis):
    shape = (rows, 1) if axis == 0 else (1, rows)
    half = rows // GROUP
    last_key = own[part] * half + lax.rem(iota(shape, axis), half)
    first_key = jnp.zeros(shape, jnp.int32) + own[2 + part] * half
    return first_key.astype(full), last_key.astype(full)


def fold_gains(rows):
    part = len(rows) * rows[0].shape[1] // TILE
    pieces = [
        row[:, at : at + part] for row in rows for at in range(0, row.shape[1], part)
    ]
    return jnp.concatenate(pieces, axis=0)


def sum_gains(gains, come):
    return gains.astype(low).astype(full) + come.astype(full)


class Call:
    def __init__(self, steps):
        self.steps = steps

    def spec(self, kind, shape):
        if kind == "smem":
            return pl.BlockSpec(memory_space=pltpu.SMEM)
        if kind == "token":
            return pl.BlockSpec(memory_space=pl.ANY)
        if self.steps == 1 or kind == "whole":
            return pl.BlockSpec(memory_space=pltpu.VMEM)
        rest = tuple(shape[1:])
        return pl.BlockSpec((shape[0] // self.steps,) + rest, lambda i: (i,) + (0,) * len(rest))

    def __call__(self, kernel, name, ins, outs, scratch, micros, after=(), vmem=14):
        steps = self.steps
        first, last, end = len(ins), len(ins) + len(after), len(ins) + len(after) + len(outs)

        def run(*refs):
            refs[end][...] = jnp.zeros_like(refs[end])
            used = refs[:first] + refs[last:end] + refs[end + 1 :]
            kernel(pl.program_id(0) if steps > 1 else 0, steps, *used)

        ins = list(ins) + [("token", token) for token in after]
        outs = list(outs) + [("whole", shape_of((8, 128), full))]
        size = sum(a.size * a.dtype.itemsize for kind, a in ins if kind != "token")
        size += sum(int(np.prod(a.shape)) * a.dtype.itemsize for _, a in outs)
        if steps > 1 or size > 16 << 20:
            vmem = 40
        return pl.pallas_call(
            run,
            grid=(steps,) if steps > 1 else (),
            in_specs=[self.spec(kind, a.shape) for kind, a in ins],
            out_specs=[self.spec(kind, s.shape) for kind, s in outs],
            out_shape=[s for _, s in outs],
            scratch_shapes=scratch,
            compiler_params=pltpu.CompilerParams(vmem_limit_bytes=vmem * 1024 * 1024),
            cost_estimate=pl.CostEstimate(
                flops=int(micros * steps * 1e9), bytes_accessed=1024, transcendentals=0
            ),
            name=name,
        )(*[a for _, a in ins])


one_call = Call(1)


def once(step, steps, at, action):
    if steps == 1:
        action()
    else:
        pl.when(step == at)(action)


def shape_of(shape, dtype):
    return jax.ShapeDtypeStruct(shape, dtype)


def join_kernel(step, steps, held_ref, come_ref, *outs):
    rows = held_ref.shape[0]
    lane = 0
    for out_ref in outs:
        lanes = slice(lane, lane + out_ref.shape[1])
        out_ref[:rows, :] = held_ref[:, lanes]
        out_ref[rows:, :] = come_ref[:, lanes]
        lane = lanes.stop


def copy_kernel(step, steps, held_ref, out_ref):
    out_ref[...] = held_ref[...]


def join(held, come, name, after, parts=()):
    rows, columns = held.shape
    if rows * columns > 2 << 20:
        return jnp.concatenate([held, come], axis=0), None
    return one_call(
        join_kernel,
        "join_" + name,
        [("whole", held), ("whole", come)],
        [("whole", shape_of((2 * rows, part), held.dtype)) for part in parts or (columns,)],
        [],
        1,
        after,
    )


def pack_kernel(step, steps, turned_ref, gain_ref, *refs):
    packed_ref, normed_ref, hidden_ref = refs[-3:]
    hidden = jnp.transpose(turned_ref[...].astype(full))
    hidden_ref[...] = hidden.astype(low)
    width = hidden_ref.shape[1]
    unit, _ = unit_rows(hidden)
    normed_ref[...] = (unit * gain_ref[...]).astype(low)
    for a in range(hidden_ref.shape[0] // TILE):
        packed_ref[:, a * width : (a + 1) * width] = normed_ref[a * TILE : (a + 1) * TILE, :]
    if len(refs) > 3:
        fold_projections(packed_ref, (a + 1) * width, width, refs[:-3])


def rows_in(ref, columns):
    value = ref[...].astype(full)
    if value.shape[1] == columns:
        return value
    pieces = [value[:, at : at + columns] for at in range(0, value.shape[1], columns)]
    return jnp.concatenate(pieces, axis=0)


def fold_into(out_ref, at, pieces):
    columns = sum(piece.shape[1] for piece in pieces)
    lane = at
    for piece in pieces:
        out_ref[:, lane : lane + piece.shape[1]] = piece[:TILE, :].astype(low)
        lane += piece.shape[1]
    tails = [piece[TILE:, :] for piece in pieces]
    tail = tails[0] if len(tails) == 1 else jnp.concatenate(tails, axis=1)
    fold = TILE // tail.shape[0]
    part = columns // fold
    rows = [
        tail[j : j + 1, block * part : (block + 1) * part]
        for j in range(tail.shape[0])
        for block in range(fold)
    ]
    out_ref[:, lane : lane + part] = jnp.concatenate(rows, axis=0).astype(low)
    return lane + part


def fold_projections(out_ref, at, width, refs):
    query_ref, key_ref, value_ref, output_ref = refs
    pieces = [rows_in(query_ref, width), rows_in(key_ref, KV_WIDTH), rows_in(value_ref, KV_WIDTH)]
    end = fold_into(out_ref, at, pieces)
    end = fold_into(out_ref, end, [rows_in(output_ref, width)])
    out_ref[:, end:] = jnp.zeros((TILE, out_ref.shape[1] - end), low)


def fold_projections_kernel(width, step, steps, *refs):
    fold_projections(refs[-1], 0, width, refs[:-1])


def fold_gates_kernel(ff, step, steps, gate_ref, up_ref, out_ref):
    lane = fold_into(out_ref, 0, [rows_in(gate_ref, ff), rows_in(up_ref, ff)])
    if lane < out_ref.shape[1]:
        out_ref[:, lane:] = jnp.zeros((TILE, out_ref.shape[1] - lane), low)


def fold_down_kernel(width, step, steps, down_ref, out_ref):
    down = rows_in(down_ref, width)
    lane = 0
    for a in range(down.shape[0] // TILE):
        out_ref[:, lane : lane + width] = down[a * TILE : (a + 1) * TILE].astype(low)
        lane += width
    out_ref[:, lane:] = jnp.zeros((TILE, out_ref.shape[1] - lane), low)


def weights_kernel(
    step, steps, feature_ref, own_ref, come_ref, weight_ref, key_value_ref, output_ref, mixed, *folds
):
    width, columns = weight_ref.shape
    half = own_ref.shape[0]
    main = 2 * half
    fold = main // (width - main)
    lane, first = 0, 0
    for scratch, count in zip(folds, (columns, width)):
        part = count // fold
        mixed[:half, first : first + count] = own_ref[:, lane : lane + count]
        mixed[half:main, first : first + count] = come_ref[:, lane : lane + count]
        lane += count
        folded = slice(lane, lane + part)
        fold_write(scratch, jnp.concatenate([own_ref[:, folded], come_ref[:, folded]], axis=0))
        for at in range(fold):
            lanes = slice(first + at * part, first + (at + 1) * part)
            mixed[main:, lanes] = fold_get(scratch, at, fold, part)
        lane += part
        first += count
    natural = dot(mixing_of(feature_ref), mixed[...])
    weight_ref[...] = natural[:, :columns].astype(low)
    output_ref[...] = natural[:, columns:].astype(low)
    keys = natural[:, width : width + KV_WIDTH]
    key_value_ref[:, :KV_WIDTH] = keys.astype(low)
    half_dim = HEAD_SIZE // 2
    swapped = [
        keys[:, (block ^ 1) * half_dim : ((block ^ 1) + 1) * half_dim]
        for block in range(KV_WIDTH // half_dim)
    ]
    key_value_ref[:, KV_WIDTH : 2 * KV_WIDTH] = jnp.concatenate(swapped, axis=1).astype(low)
    key_value_ref[:, 2 * KV_WIDTH :] = natural[:, width + KV_WIDTH : columns].astype(low)


def queries_kernel(step, steps, normed_ref, weight_ref, cos_ref, sin_ref, times, query_ref):
    tokens, width = normed_ref.shape
    half = tokens // 2
    queries = dot(normed_ref[...], weight_ref[:, :width])
    rope = rope_own_of(cos_ref, sin_ref, times)
    for head in range(HEADS):
        turned = turn(queries[:, head * HEAD_SIZE : (head + 1) * HEAD_SIZE], rope, 1.0)
        turned = turned.astype(low) * low(HEAD_SIZE**-0.5)
        for part in range(2):
            row = (part * GROUP + head % GROUP) * half
            query_ref[head // GROUP, row : row + half, :] = turned[part * half : (part + 1) * half]


def project_kernel(step, steps, normed_ref, weight_ref, cos_ref, sin_ref, times, kv_ref):
    width = weight_ref.shape[0]
    groups = normed_ref.shape[1] // width
    for a in range(groups):
        kv = dot(normed_ref[:, a * width : (a + 1) * width], weight_ref[...])
        rope = rope_of(cos_ref, sin_ref, times, a // (groups // 2), a % (groups // 2))
        cos, sin = rope[:, : 2 * HEAD_SIZE], rope[:, 2 * HEAD_SIZE :]
        cos = jnp.concatenate([cos, cos[:, :HEAD_SIZE]], axis=1)
        sin = jnp.concatenate([sin, sin[:, :HEAD_SIZE]], axis=1)
        keys = kv[:, :KV_WIDTH] * cos + kv[:, KV_WIDTH : 2 * KV_WIDTH] * sin
        at = a * 2 * KV_WIDTH
        kv_ref[:, at : at + KV_WIDTH] = keys.astype(low)
        kv_ref[:, at + KV_WIDTH : at + 2 * KV_WIDTH] = kv[:, 2 * KV_WIDTH :].astype(low)


def key_part(kv_ref, groups, column):
    lanes = [a * 2 * KV_WIDTH + column * HEAD_SIZE for a in groups]
    return jnp.concatenate([kv_ref[:, at : at + HEAD_SIZE] for at in lanes], axis=0)


def key_row(key_ref, part, groups):
    start = key_ref[part]
    return jnp.concatenate([start + float(i * TILE) for i in range(len(groups))], axis=1)


def reaches_low(own, blocks):
    return own[3] < blocks


def forward_kernel(
    is_first, low_blocks, step, steps, own, key_ref, query_ref, kv_ref, *rest
):
    state = rest[-1]
    rows = query_ref.shape[1] // 2
    groups = kv_ref.shape[1] // (2 * KV_WIDTH)

    def first():
        if is_first:
            lane = lax.broadcasted_iota(jnp.int32, state.shape, 2)
            state[...] = jnp.where(lane == PEAK, masked_score, 0.0)
        else:
            state[...] = rest[0][...]

    once(step, steps, 0, first)

    def attend(key_half, query_half):
        members = range(key_half * groups // 2, (key_half + 1) * groups // 2)
        at = slice(query_half * rows, (query_half + 1) * rows)
        key_index = key_row(key_ref, key_half, members)
        first_key, last_key = query_range(own, query_half, rows, 0)
        allowed = (key_index >= first_key) & (key_index <= last_key)
        for head in range(KV_HEADS):
            scores = dot_right(query_ref[head, at], key_part(kv_ref, members, head))
            masked = jnp.where(allowed, scores, masked_score)
            old = state[head, at, PEAK : PEAK + 1]
            new = jnp.maximum(old, jnp.max(masked, axis=1, keepdims=True))
            weights = jnp.where(allowed, jnp.exp(masked - new), 0.0)
            factor = jnp.exp(old - new)
            state[head, at, PEAK : PEAK + 1] = new
            state[head, at, TOTAL : TOTAL + 1] = state[
                head, at, TOTAL : TOTAL + 1
            ] * factor + jnp.sum(weights, axis=1, keepdims=True)
            state[head, at, :HEAD_SIZE] = state[head, at, :HEAD_SIZE] * factor + dot(
                weights.astype(low), key_part(kv_ref, members, KV_HEADS + head)
            )

    attend(0, 0)
    pl.when(reaches_low(own, low_blocks))(lambda: attend(0, 1))
    attend(1, 1)


def middle_kernel(
    step,
    steps,
    feature_ref,
    state_ref,
    hidden_ref,
    output_w,
    gain_ref,
    attention,
    attended,
    middle_ref,
    normed,
    normed_t,
    lse_ref,
    natural,
):
    mixing = mixing_of(feature_ref)
    tokens = hidden_ref.shape[0] // 2
    for head in range(KV_HEADS):
        sums = state_ref[head, :, TOTAL : TOTAL + 1]
        attention[head] = state_ref[head, :, :HEAD_SIZE] / sums
        logs = state_ref[head, :, PEAK : PEAK + 1] + jnp.log(sums)
        for part in range(2):
            lse_ref[2 * head + part] = as_row(
                logs[part * GROUP * tokens : (part + 1) * GROUP * tokens]
            )
    for h in range(HEADS):
        for part in range(2):
            row = (part * GROUP + h % GROUP) * tokens
            natural[
                part * tokens : (part + 1) * tokens, h * HEAD_SIZE : (h + 1) * HEAD_SIZE
            ] = attention[h // GROUP, row : row + tokens, :].astype(low)
    middle = hidden_ref[...].astype(full) + dot(natural[...], output_w[...])
    middle_ref[...] = middle
    unit, _ = unit_rows(middle)
    mixed_norm = dot((unit * gain_ref[...]).astype(low), mixing)
    normed[...] = mixed_norm.astype(low)
    normed_t[...] = jnp.transpose(mixed_norm).astype(low)
    attended[...] = dot(natural[...], mixing).astype(low)


def feedforward_kernel(
    step,
    steps,
    source_ref,
    feature_ref,
    attention,
    attended,
    middle_ref,
    normed,
    normed_t,
    output_w,
    gain_ref,
    grad_ref,
    own_ref,
    come_low_ref,
    come_high_ref,
    down_own_ref,
    down_come_ref,
    out_ref,
    grad_middle_ref,
    head_grad_ref,
    delta_ref,
    keep_ref,
    send_ref,
    down_keep_ref,
    down_send_ref,
    gain_part_ref,
    come_ref,
    down_w,
    down_grad,
    total,
    grad_normed,
    extra_grad,
    output_folds,
    late_folds,
):
    rows, width = middle_ref.shape
    half = own_ref.shape[0]
    main = 2 * half
    rest = width - main
    fold = main // rest
    places = main // TILE
    ff = down_w.shape[0]
    chunk = 2 * ff // fold
    down_at = 2 * ff + chunk
    device_ff = ff // places
    groups = device_ff // TILE
    out_at = down_at
    mixing = mixing_of(feature_ref)
    tokens = rows // 2
    part = width // fold
    folded = slice(out_at + width, out_at + width + part)
    come_ref[: half // 2, :] = come_low_ref[...]
    come_ref[half // 2 :, :] = come_high_ref[...]
    middle = middle_ref[...]
    gain = gain_ref[...]
    unit, inverse = unit_rows(middle)
    for place in range(places):
        held = down_own_ref if place < places // 2 else down_come_ref
        row = (place % (places // 2)) * TILE
        for a in range(groups):
            at = pl.multiple_of(source_ref[place] * device_ff + a * TILE, TILE)
            lane = a * width
            down_w[pl.ds(at, TILE), :] = held[row : row + TILE, lane : lane + width]
    total[...] = jnp.zeros_like(total)
    grad_normed[...] = jnp.zeros_like(grad_normed)
    out_grad = grad_ref[...]
    fold_write(
        late_folds,
        jnp.concatenate([own_ref[:, 2 * ff : down_at], come_ref[:, 2 * ff : down_at]], axis=0),
    )

    def advance(c, carry):
        gate_at = pl.ds(pl.multiple_of(c * chunk, 128), chunk)
        up_at = pl.ds(pl.multiple_of(ff + c * chunk, 128), chunk)

        def columns(lanes, at):
            tail = fold_get(late_folds, at, fold, chunk)
            value = (
                dot(normed[:, :half], own_ref[:, lanes])
                + dot(normed[:, half:main], come_ref[:, lanes])
                + dot(normed[:, main:], tail)
            )
            return value, tail

        gate, gate_tail = columns(gate_at, c)
        up, up_tail = columns(up_at, c + fold // 2)
        down_at_c = pl.ds(pl.multiple_of(c * chunk, 128), chunk)
        down = down_w[down_at_c, :]
        sigma = 1.0 / (1.0 + jnp.exp(-gate))
        silu = gate * sigma
        inner = (silu * up).astype(low)
        total[...] += dot(inner, down)
        grad_inner = dot_right(out_grad, down)
        grad_gate = (grad_inner * up * sigma * (1.0 + gate * (1.0 - sigma))).astype(low)
        grad_up = (grad_inner * silu).astype(low)
        down_grad[down_at_c, :] = dot_left(inner, out_grad).astype(low)
        for grad, lanes, tail, at in (
            (grad_gate, gate_at, gate_tail, c),
            (grad_up, up_at, up_tail, c + fold // 2),
        ):
            grad_normed[:, :half] += dot_right(grad, own_ref[:, lanes])
            grad_normed[:, half:main] += dot_right(grad, come_ref[:, lanes])
            grad_normed[:, main:] += dot_right(grad, tail)
            keep_ref[:, lanes] = dot(normed_t[:half], grad).astype(low)
            send_ref[:, lanes] = dot(normed_t[half:main], grad).astype(low)
            fold_put(extra_grad, at, fold, dot(normed_t[main:], grad))
        return carry

    lax.fori_loop(0, ff // chunk, advance, 0)
    out_ref[...] = (middle + total[...]).astype(low)
    extra = fold_read(extra_grad, chunk)
    keep_ref[:, 2 * ff : down_at] = extra[:half]
    send_ref[:, 2 * ff : down_at] = extra[half:]
    for place in range(places):
        held = down_keep_ref if place < places // 2 else down_send_ref
        row = (place % (places // 2)) * TILE
        for a in range(groups):
            at = pl.multiple_of(source_ref[place] * device_ff + a * TILE, TILE)
            lane = a * width
            held[row : row + TILE, lane : lane + width] = down_grad[pl.ds(at, TILE), :]
    unused = jnp.zeros((half, down_keep_ref.shape[1] - groups * width), low)
    down_keep_ref[:, groups * width :] = unused
    down_send_ref[:, groups * width :] = unused

    high = grad_normed[...].astype(low)
    tail = (grad_normed[...] - high.astype(full)).astype(low)
    back = dot_right(high, mixing) + dot_right(tail, mixing)
    gain_part_ref[...] = jnp.sum(back * unit, axis=0, keepdims=True)
    grad_middle = out_grad.astype(full) + norm_back(unit, inverse, gain, back)
    grad_middle_ref[...] = grad_middle
    grad_branch = grad_middle.astype(low)
    output_grad = dot_left(attended[...], grad_branch)
    keep_ref[:, out_at : out_at + width] = output_grad[:half].astype(low)
    send_ref[:, out_at : out_at + width] = output_grad[half:main].astype(low)
    for at in range(fold):
        fold_put(output_folds, at, fold, output_grad[main:, at * part : (at + 1) * part])
    extra = fold_read(output_folds, part)
    unused = jnp.zeros((half, keep_ref.shape[1] - folded.stop), low)
    for held, rows_of_half in ((keep_ref, extra[:half]), (send_ref, extra[half:])):
        held[:, folded] = rows_of_half
        held[:, folded.stop :] = unused
    grad_low = dot_right(grad_branch, output_w[...]).astype(low)
    for head in range(KV_HEADS):
        for part in range(2):
            grads = jnp.concatenate(
                [
                    grad_low[
                        part * tokens : (part + 1) * tokens, h * HEAD_SIZE : (h + 1) * HEAD_SIZE
                    ]
                    for h in range(head * GROUP, (head + 1) * GROUP)
                ],
                axis=0,
            )
            at = slice(part * GROUP * tokens, (part + 1) * GROUP * tokens)
            head_grad_ref[head, at] = grads
            delta_ref[2 * head + part] = as_row(
                jnp.sum(grads.astype(full) * attention[head, at], axis=1, keepdims=True)
            )


def backward_kernel(
    is_first,
    key_half,
    low_blocks,
    joined,
    step,
    steps,
    own,
    key_ref,
    query_ref,
    grad_ref,
    lse_ref,
    delta_ref,
    kv_ref,
    tokens_ref,
    cos_ref,
    sin_ref,
    times,
    *rest,
):
    if not is_first:
        held, rest = rest[:2], rest[2:]
    if joined:
        high_ref, rest = rest[0], rest[1:]
        rest[2][:, high_ref.shape[1] :] = high_ref[...]
    grad_query, grad_weight, out_ref, grad_kv = rest
    rows = query_ref.shape[1] // 2
    groups = kv_ref.shape[1] // (2 * KV_WIDTH)
    key_rows = kv_ref.shape[0]
    width = tokens_ref.shape[1] // groups
    members = range(key_half * groups // 2, (key_half + 1) * groups // 2)

    def first():
        if is_first:
            grad_query[...] = jnp.zeros_like(grad_query)
            grad_weight[...] = jnp.zeros_like(grad_weight)
        else:
            grad_query[...] = held[0][...]
            grad_weight[...] = held[1][...]

    once(step, steps, 0, first)
    key_index = key_row(key_ref, key_half, members)
    key_index = jnp.transpose(jnp.broadcast_to(key_index, (128, key_index.shape[1])))[:, 0:1]

    def attend(query_half, add):
        at = slice(query_half * rows, (query_half + 1) * rows)
        first_key, last_key = query_range(own, query_half, rows, 1)
        allowed = (key_index >= first_key) & (key_index <= last_key)
        for head in range(KV_HEADS):
            keys = key_part(kv_ref, members, head)
            scores = dot_right(keys, query_ref[head, at])
            probs = jnp.where(allowed, jnp.exp(scores - lse_ref[2 * head + query_half]), 0.0)
            d_probs = dot_right(key_part(kv_ref, members, KV_HEADS + head), grad_ref[head, at])
            d_scores = (probs * (d_probs - delta_ref[2 * head + query_half])).astype(low)
            grad_query[2 * head + query_half] += dot_left(keys, d_scores)
            parts = (
                (head, dot(d_scores, query_ref[head, at])),
                (KV_HEADS + head, dot(probs.astype(low), grad_ref[head, at])),
            )
            for column, value in parts:
                lanes = slice(column * HEAD_SIZE, (column + 1) * HEAD_SIZE)
                if add:
                    grad_kv[:, lanes] += value
                else:
                    grad_kv[:, lanes] = value

    if key_half == 0:
        attend(0, False)
        pl.when(reaches_low(own, low_blocks))(lambda: attend(1, True))
    else:
        attend(1, False)
    for i, a in enumerate(members):
        at = slice(i * key_rows, (i + 1) * key_rows)
        rope = rope_of(cos_ref, sin_ref, times, key_half, i)
        turned = jnp.concatenate(
            [
                turn(grad_kv[at, head * HEAD_SIZE : (head + 1) * HEAD_SIZE], rope, -1.0)
                for head in range(KV_HEADS)
            ]
            + [grad_kv[at, KV_WIDTH:]],
            axis=1,
        ).astype(low)
        lane = i * 2 * KV_WIDTH
        out_ref[:, lane : lane + 2 * KV_WIDTH] = turned
        grad_weight[...] += dot_left(turned, tokens_ref[:, a * width : (a + 1) * width])


def qkv_grad_kernel(
    step,
    steps,
    feature_ref,
    grad_query,
    grad_weight,
    normed_ref,
    weight_ref,
    cos_ref,
    sin_ref,
    times,
    gain_ref,
    gain_two_ref,
    query_grad_ref,
    gains_ref,
    keep_ref,
    send_ref,
    natural,
    folds,
):
    tokens, width = normed_ref.shape
    half = tokens // 2
    rope = rope_own_of(cos_ref, sin_ref, times)
    for head in range(KV_HEADS):
        rotated = [
            jnp.transpose(grad_query[2 * head + part]) * HEAD_SIZE**-0.5 for part in range(2)
        ]
        for g in range(GROUP):
            h = head * GROUP + g
            value = jnp.concatenate([part[g * half : (g + 1) * half] for part in rotated], axis=0)
            query_grad_ref[:, h * HEAD_SIZE : (h + 1) * HEAD_SIZE] = turn(value, rope, -1.0).astype(
                low
            )
    natural[:, :width] = dot_left(normed_ref[...], query_grad_ref[...])
    natural[:, width:] = jnp.transpose(grad_weight[...])
    products = natural[...] * weight_ref[...].astype(full)
    gain_part = as_row(jnp.sum(products, axis=1, keepdims=True)) / gain_ref[...]
    gains = fold_gains([gain_part, gain_two_ref[...]])
    gains_ref[...] = gains
    mixed = dot_left(mixing_of(feature_ref), natural[...].astype(low)).astype(low)
    columns = mixed.shape[1]
    rows = keep_ref.shape[0]
    main = 2 * rows
    fold = main // (width - main)
    part = columns // fold
    for at in range(fold):
        fold_put(folds, at, fold, mixed[main:, at * part : (at + 1) * part].astype(full))
    extra = fold_read(folds, part)
    unused = jnp.zeros((rows, keep_ref.shape[1] - columns - part), low)
    for held, at in ((keep_ref, 0), (send_ref, rows)):
        held[:rows, :columns] = mixed[at : at + rows]
        held[:rows, columns : columns + part] = extra[at : at + rows]
        held[:rows, columns + part :] = unused
    send_ref[:TILE, columns + part : columns + part + gains.shape[1]] = gains.astype(low)


def merge_kernel(gain_at, step, steps, *refs):
    keep_low, keep_high, kv_come, w_keep, w_come, gains_ref, keep_out, send_out, gains_out = refs
    half = w_keep.shape[0] // 2
    part = keep_low.shape[1]
    base = 2 * part
    lane = 0
    for keep, come, first in (
        (keep_low, kv_come, 0),
        (keep_high, kv_come, part),
        (w_keep, w_come, 0),
    ):
        columns = keep.shape[1]
        for out, at in ((keep_out, 0), (send_out, half)):
            value = keep[at : at + half, :].astype(full) + come[
                at : at + half, first : first + columns
            ].astype(full)
            out[:, lane : lane + columns] = value.astype(low)
        lane += columns
    lanes = slice(gain_at, gain_at + gains_ref.shape[1])
    gains = sum_gains(gains_ref[...], w_come[:TILE, lanes])
    gains_out[...] = gains
    send_out[:TILE, base + lanes.start : base + lanes.stop] = gains.astype(low)


def add_kernel(gain_at, step, steps, keep_ref, come_ref, *rest):
    rows = keep_ref.shape[0]
    if gain_at is not None:
        gains_ref, keep_out, send_out, gains_out = rest
        lanes = slice(gain_at, gain_at + gains_ref.shape[1])
        gains = sum_gains(gains_ref[...], come_ref[:TILE, lanes])
        gains_out[...] = gains
        rest = rest[1:-1]

    def tile(at):
        at = pl.ds(at, TILE)
        return keep_ref[at, :].astype(full) + come_ref[at, :].astype(full)

    if rows == TILE:
        rest[0][...] = tile(0)
        return
    keep_out, send_out = rest
    half = rows // 2

    def advance(i, carry):
        at = pl.multiple_of(i * TILE, TILE)
        keep_out[pl.ds(at, TILE), :] = tile(at).astype(low)
        send_out[pl.ds(at, TILE), :] = tile(pl.multiple_of(half + at, TILE)).astype(low)
        return carry

    lax.fori_loop(0, half // TILE, advance, 0)
    if gain_at is not None:
        send_out[:TILE, lanes] = gains.astype(low)


def scatter_halves(
    keep, leaving, steps, name, gains=None, gain_at=None, after=None, between=None
):
    for at, partner in enumerate(reversed(steps)):
        come = send(leaving, partner)
        rows, columns = keep.shape
        ins = [("whole", keep), ("whole", come)]
        if rows == TILE:
            if gains is not None:
                return keep, come, gains
            outs = [("whole", shape_of((rows, columns), full))]
        else:
            outs = [("whole", shape_of((rows // 2, columns), low))] * 2
        if gains is not None:
            ins.append(("whole", gains))
            outs.append(("whole", shape_of(gains.shape, full)))
        result = one_call(
            functools.partial(add_kernel, gain_at),
            name,
            ins,
            outs,
            [],
            1,
            (after or {}).get(at, ()),
        )
        if between:
            between(at, result[-1])
        if gains is not None:
            gains = result[-2]
        if rows == TILE:
            return result[0]
        keep, leaving = result[0], result[1]


def final_kernel(
    base,
    step,
    steps,
    keep_ref,
    come_ref,
    query_grad_ref,
    weight_ref,
    hidden_ref,
    gain_ref,
    grad_middle_ref,
    *rest,
):
    grads = rest[-1]
    tokens, width = hidden_ref.shape
    grads[:, :width] = query_grad_ref[...]
    for a in range(tokens // TILE):
        rows = slice(a * TILE, (a + 1) * TILE)
        lanes = slice(a * 2 * KV_WIDTH, (a + 1) * 2 * KV_WIDTH)
        value = keep_ref[:, lanes].astype(full) + come_ref[:, lanes].astype(full)
        grads[rows, width:] = value.astype(low)
    back = dot_right(grads[...], weight_ref[...])
    unit, inverse = unit_rows(hidden_ref[...].astype(full))
    out_ref = rest[-6] if base else rest[-2]
    input_grad = grad_middle_ref[...] + norm_back(unit, inverse, gain_ref[...], back)
    out_ref[...] = jnp.transpose(input_grad).astype(low)
    if not base:
        return
    gains_ref, _, query_out, key_out, value_out, gains_out, _ = rest
    columns = weight_ref.shape[1]
    total = keep_ref[:, base:].astype(full) + come_ref[:, base:].astype(full)
    fold = gains_ref.shape[0] // 2
    part = columns // fold
    for row in range(TILE + TILE // fold):
        if row < TILE:
            value = total[row : row + 1, :columns]
        else:
            at = (row - TILE) * fold
            value = jnp.concatenate(
                [total[at + i : at + i + 1, columns : columns + part] for i in range(fold)], axis=1
            )
        query_out[:, row * width : (row + 1) * width] = value[:, :width]
        for out, first in ((key_out, width), (value_out, width + KV_WIDTH)):
            out[:, row * KV_WIDTH : (row + 1) * KV_WIDTH] = value[:, first : first + KV_WIDTH]
    at = columns + part
    lanes = slice(at, at + gains_ref.shape[1])
    gains = sum_gains(gains_ref[...], come_ref[:TILE, base + lanes.start : base + lanes.stop])
    for k in range(2):
        gains_out[k : k + 1, :] = jnp.concatenate(
            [gains[k * fold + i : k * fold + i + 1] for i in range(fold)], axis=1
        )


def body(
    hidden_in,
    attention_gain,
    query_weight,
    key_weight,
    value_weight,
    output_weight,
    feedforward_gain,
    gate_weight,
    up_weight,
    down_weight,
    doc_of_block,
    pair_table,
    out_grad,
):
    tokens, width = hidden_in.shape
    half_rows = tokens // 2
    count = lax.axis_size("ctx")
    device = lax.axis_index("ctx")
    ff = gate_weight.shape[1] * count // width
    low_bits = low_bits_of(query_weight.shape[1], width)
    merged = low_bits == 0
    row_steps = exchange_steps(count, low_bits)
    token_steps = exchange_steps(count, 0)
    down_steps = row_steps[2:4] + row_steps[:2] + row_steps[4:] if merged else row_steps
    group_count = count >> low_bits
    group_rows = width // group_count
    groups = tokens // TILE
    steps = max(1, TILE * count // 512)
    places = count // (2 * steps)
    gain_one = attention_gain.reshape(1, width)
    gain_two = feedforward_gain.reshape(1, width)
    columns = width + 2 * KV_WIDTH
    main = TILE * group_count
    fold = main // (width - main)
    w_lanes = whole_lanes(columns + columns // fold + 2 * width // TILE)
    projection_lanes = whole_lanes((columns + width) + (columns + width) // fold)
    ff_folded = 2 * ff // fold
    out_at = 2 * ff + ff_folded
    device_groups = ff // group_count // TILE
    late_lanes = whole_lanes(out_at + width + width // fold)
    gate_lanes = whole_lanes(out_at)
    down_lanes = whole_lanes(device_groups * width)
    call = Call(steps)
    one = Call(1)

    def rows_of(piece, piece_columns):
        if low_bits:
            piece = whole_rows(piece, device, low_bits, piece_columns)
        return ("whole", piece)

    projections = [
        rows_of(query_weight, width),
        rows_of(key_weight, KV_WIDTH),
        rows_of(value_weight, KV_WIDTH),
        rows_of(output_weight, width),
    ]
    token_parts = (groups * width, projection_lanes) if merged else (groups * width,)
    packed, normed, hidden_rows, pack_mark = one(
        pack_kernel,
        "norm_and_pack",
        [("whole", hidden_in.T), ("whole", gain_one)] + (projections if merged else []),
        [
            ("whole", shape_of((TILE, sum(token_parts)), low)),
            ("whole", shape_of((tokens, width), low)),
            ("whole", shape_of((tokens, width), low)),
        ],
        [],
        1,
    )

    def table_row(table):
        return lax.dynamic_index_in_dim(jnp.asarray(table), device, 0, keepdims=False)

    sources = table_row(source_table(count, 0, token_steps))
    down_sources = table_row(source_table(count, low_bits, down_steps))
    group_table = source_table(count, low_bits, row_steps)
    inside = np.arange(group_rows)[None, None, :]
    features = group_table[:, :, None] * group_rows + inside
    features = np.concatenate(
        [
            features[:, :, :TILE].reshape(count, -1),
            features[:, :, TILE:].reshape(count, -1),
        ],
        axis=1,
    ).astype(np.int32)
    feature_row = table_row(features).reshape(1, width)

    device_iota = jnp.arange(count, dtype=jnp.int32)
    pairs = jnp.sum(
        jnp.where(sources[:, None] == device_iota[None, :], pair_table[None, :], 0), axis=1
    )
    blocks = jnp.stack([pairs, 2 * count - 1 - pairs], axis=1).reshape(-1)
    block_iota = jnp.arange(2 * count, dtype=jnp.int32)
    block_docs = jnp.sum(
        jnp.where(blocks[:, None] == block_iota[None, :], doc_of_block[None, :], 0), axis=1
    )
    doc_start = jnp.min(
        jnp.where(block_docs[:, None] == doc_of_block[None, :], block_iota[None, :], 2 * count),
        axis=1,
    )
    own = jnp.concatenate([blocks[:2], doc_start[:2]])

    def by_step(values):
        return values.reshape(2, steps, places, 2).transpose(0, 1, 3, 2)

    inner = jnp.arange(TILE, dtype=jnp.int32)
    key_index = by_step(blocks)[..., None] * half_rows + inner
    key_index = key_index.astype(full).reshape(2, 2 * steps, 1, -1)
    frequency = rope_base ** (-jnp.arange(HEAD_SIZE // 2, dtype=full) * (2.0 / HEAD_SIZE))
    block_angle = (by_step(blocks - doc_start) * half_rows).astype(full)[..., None] * frequency
    offset = jnp.arange(half_rows, dtype=full).reshape(groups // 2, TILE)
    offset_angle = offset[..., None] * frequency
    cos_in, sin_in = jnp.cos(offset_angle), jnp.sin(offset_angle)
    times_cos = jnp.concatenate([cos_in] * 4 + [-sin_in, sin_in] * 2, axis=-1)
    times_sin = jnp.concatenate([sin_in] * 4 + [cos_in, -cos_in] * 2, axis=-1)
    times = jnp.stack([times_cos, times_sin])
    block_cos = jnp.tile(jnp.cos(block_angle), 8).reshape(2, 2 * steps, places, 1, 4 * HEAD_SIZE)
    block_sin = jnp.tile(jnp.sin(block_angle), 8).reshape(2, 2 * steps, places, 1, 4 * HEAD_SIZE)
    own_cos, own_sin = block_cos[0, :2, :1], block_sin[0, :2, :1]
    rope_own = [("whole", own_cos), ("whole", own_sin), ("whole", times)]
    key_index, block_cos, block_sin = (
        [values[0], values[1]] for values in (key_index, block_cos, block_sin)
    )
    tables = key_index + block_cos + block_sin + [own, own_cos, own_sin, times, feature_row]
    late_at = 2
    down, down_mark = one(
        functools.partial(fold_down_kernel, width),
        "fold_down",
        [rows_of(down_weight, width)],
        [("whole", shape_of((TILE, down_lanes), low))],
        [],
        1,
        [pack_mark],
    )
    late, late_mark = one(
        functools.partial(fold_gates_kernel, ff),
        "fold_gates",
        [rows_of(gate_weight, ff), rows_of(up_weight, ff)],
        [("whole", shape_of((TILE, gate_lanes), low))],
        [],
        1,
        [pack_mark],
    )

    def release(values, name, after):
        return one(
            copy_kernel,
            "release_" + name,
            [("whole", values)],
            [("whole", shape_of(values.shape, low))],
            [],
            1,
            after,
        )[0]

    mark = None
    for at, partner in enumerate(token_steps[:-1]):
        after = []
        if at == 0:
            after = [down_mark]
        elif at == 1:
            down = release(down, "down", [mark])
            down, down_mark = join(down, send(down, down_steps[0]), "down", [])
            after = [down_mark, late_mark] + tables
        elif at == late_at:
            late = release(late, "gates", [mark])
            late, late_mark = join(late, send(late, row_steps[0]), "gates", [])
            down, down_mark = join(down, send(down, down_steps[1]), "down", [])
            after = [late_mark, down_mark]
        elif at == late_at + 1:
            late, late_mark = join(late, send(late, row_steps[1]), "gates", [])
            down = release(down, "down", [late_mark])
            down, down_mark = join(down, send(down, down_steps[2]), "down", [])
            after = [down_mark]
        last = at == len(token_steps) - 2
        *held, mark = join(
            packed,
            send(packed, partner),
            "tokens",
            after,
            token_parts if last else (),
        )
        packed = held[0]
    token_own = packed
    if merged:
        w_own, w_come = held[1], send(held[1], token_steps[-1])
    else:
        qkv_piece, _ = one(
            functools.partial(fold_projections_kernel, width),
            "fold_projections",
            projections,
            [("whole", shape_of((TILE, projection_lanes), low))],
            [],
            1,
        )
        w_own, w_come = gather_halves(qkv_piece, row_steps, "qkv")
    token_come = send(token_own, token_steps[-1])

    halves = [
        (
            held,
            key_index[place],
            [("rows", block_cos[place]), ("rows", block_sin[place]), ("whole", times)],
        )
        for place, held in enumerate((token_own, token_come))
    ]

    rows = GROUP * tokens
    half = TILE * count // 2
    kv_shape = shape_of((half, groups * 2 * KV_WIDTH), low)
    head_shape = (KV_HEADS, rows, HEAD_SIZE)
    weight, kv_weight, output_w, _ = one(
        weights_kernel,
        "qkv_weights",
        [("whole", feature_row), ("whole", w_own), ("whole", w_come)],
        [
            ("whole", shape_of((width, columns), low)),
            ("whole", shape_of((width, 3 * KV_WIDTH), low)),
            ("whole", shape_of((width, width), low)),
        ],
        [
            pltpu.VMEM((width, columns + width), low),
            fold_scratch(main, columns // fold),
            fold_scratch(main, width // fold),
        ],
        3,
    )
    queries, _ = one(
        queries_kernel,
        "queries",
        [("whole", normed), ("whole", weight)] + rope_own,
        [("whole", shape_of(head_shape, low))],
        [],
        2,
    )

    def project(place, after):
        token_rows, _, turns = halves[place]
        return call(
            project_kernel,
            "project",
            [("rows", token_rows), ("whole", kv_weight)] + turns,
            [("rows", kv_shape)],
            [],
            5,
            after,
        )

    state_shapes = [("whole", shape_of((KV_HEADS, rows, 2 * HEAD_SIZE), full))]

    def attend(place, kv, state, after):
        return call(
            functools.partial(forward_kernel, not state, count),
            "attention_forward",
            [
                ("smem", own),
                ("rows", halves[place][1]),
                ("whole", queries),
                ("rows", kv),
            ]
            + [("whole", held) for held in state],
            state_shapes,
            [],
            6,
            after,
        )

    kv_own, mark = project(0, [])
    late, late_mark = join(late, send(late, row_steps[2]), "gates", [mark])
    down, down_mark = join(down, send(down, down_steps[3]), "down", [mark])
    come_low = send(late, row_steps[4])
    down_come = send(down, down_steps[4])
    *state, mark = attend(0, kv_own, [], [late_mark, down_mark])
    kv_come, mark = project(1, [mark])
    *state, mark = attend(1, kv_come, state, [])
    late_high = release(send(late, row_steps[3]), "high", [mark])
    come_high = send(late_high, row_steps[4])
    late_own, mark = join(late, late_high, "gates", [])

    row_shape = ("whole", shape_of((2 * KV_HEADS, 1, rows // 2), full))
    token_low = ("whole", shape_of((tokens, width), low))
    token_full = ("whole", shape_of((tokens, width), full))
    *inner_values, lse, _ = one(
        middle_kernel,
        "middle",
        [
            ("whole", feature_row),
            ("whole", state[0]),
            ("whole", hidden_rows),
            ("whole", output_w),
            ("whole", gain_two),
        ],
        [
            ("whole", shape_of(head_shape, full)),
            token_low,
            token_full,
            token_low,
            ("whole", shape_of((width, tokens), low)),
            row_shape,
        ],
        [pltpu.VMEM((tokens, width), low)],
        3,
        [mark],
    )
    late_shape = shape_of((late_own.shape[0], late_lanes), low)
    down_shape = shape_of(down.shape, low)
    (
        block_out,
        grad_middle,
        head_grads,
        delta,
        late_keep,
        late_send,
        down_keep,
        down_send,
        gain_two_part,
        _,
    ) = one(
        feedforward_kernel,
        "feedforward",
        [
            ("smem", down_sources),
            ("whole", feature_row),
        ]
        + [("whole", held) for held in inner_values]
        + [
            ("whole", output_w),
            ("whole", gain_two),
            ("whole", out_grad),
            ("whole", late_own),
            ("whole", come_low),
            ("whole", come_high),
            ("whole", down),
            ("whole", down_come),
        ],
        [
            token_low,
            token_full,
            ("whole", shape_of(head_shape, low)),
            row_shape,
            ("whole", late_shape),
            ("whole", late_shape),
            ("whole", down_shape),
            ("whole", down_shape),
            ("whole", shape_of((1, width), full)),
        ],
        [
            pltpu.VMEM(late_own.shape, low),
            pltpu.VMEM((ff, width), low),
            pltpu.VMEM((ff, width), low),
            pltpu.VMEM((tokens, width), full),
            pltpu.VMEM((tokens, width), full),
            fold_scratch(main, ff_folded),
            fold_scratch(main, width // fold),
            fold_scratch(main, ff_folded),
        ],
        11,
        vmem=16,
    )

    def attend_back(place, key_half, kv, carried, after, joined=()):
        token_rows, keys, turns = halves[place]
        return call(
            functools.partial(backward_kernel, not carried, key_half, count, bool(joined)),
            "attention_backward",
            [
                ("smem", own),
                ("rows", keys),
                ("whole", queries),
                ("whole", head_grads),
                ("whole", lse),
                ("whole", delta),
                ("rows", kv),
                ("rows", token_rows),
            ]
            + turns
            + [("whole", held) for held in carried]
            + [("rows", part) for part in joined],
            [
                ("whole", shape_of((2 * KV_HEADS, HEAD_SIZE, rows // 2), full)),
                ("whole", shape_of((2 * KV_WIDTH, width), full)),
                ("rows", shape_of((half, groups * KV_WIDTH * (1 + len(joined))), low)),
            ],
            [pltpu.VMEM((groups // 2 * places * TILE, 2 * KV_WIDTH), full)],
            6,
            after,
        )

    class Adding:
        def __init__(self, keep, leaving, steps, name):
            self.keep, self.leaving, self.steps, self.name = keep, leaving, steps[::-1], name

        def step(self, after):
            come = send(self.leaving, self.steps[0])
            self.steps = self.steps[1:]
            rows, columns = self.keep.shape
            outs = [shape_of((rows // 2, columns), low)] * 2
            if rows == TILE:
                outs = [shape_of((rows, columns), full)]
            *result, token = one(
                functools.partial(add_kernel, None),
                self.name,
                [("whole", self.keep), ("whole", come)],
                [("whole", out) for out in outs],
                [],
                1,
                after,
            )
            self.keep, self.leaving = result[0], result[-1]
            return token

    late_chain = Adding(late_keep, late_send, row_steps, "add_late")
    down_chain = Adding(down_keep, down_send, down_steps, "add_down")
    *carried, send_high, mark = attend_back(1, 1, kv_come, [], [])
    marks = [late_chain.step([mark]), down_chain.step([mark])]
    *carried, kv_send, mark = attend_back(1, 0, kv_come, carried, marks, [send_high])
    *carried, keep_high, mark = attend_back(0, 1, kv_own, carried, [])
    marks = [late_chain.step([mark]), down_chain.step([mark])]
    *carried, keep_low, mark = attend_back(0, 0, kv_own, carried, marks)
    query_grad, gains, w_keep, w_send, mark = one(
        qkv_grad_kernel,
        "qkv_gradients",
        [
            ("whole", feature_row),
            ("whole", carried[0]),
            ("whole", carried[1]),
            ("whole", normed),
            ("whole", weight),
        ]
        + rope_own
        + [
            ("whole", gain_one),
            ("whole", gain_two_part),
        ],
        [
            ("whole", shape_of((tokens, width), low)),
            ("whole", shape_of((TILE, 2 * width // TILE), full)),
            ("whole", shape_of((main // 2, w_lanes), low)),
            ("whole", shape_of((main // 2, w_lanes), low)),
        ],
        [pltpu.VMEM((width, columns), full), fold_scratch(main, columns // fold)],
        3,
    )
    late_mark = late_chain.step([mark])
    ends = [
        ("whole", query_grad),
        ("whole", weight),
        ("whole", hidden_rows),
        ("whole", gain_one),
        ("whole", grad_middle),
    ]
    end_scratch = [pltpu.VMEM((tokens, columns), low)]
    input_shape = ("whole", shape_of((width, tokens), low))
    if merged:
        gain_at = columns + columns // fold
        base = kv_send.shape[1]
        lanes = base + w_lanes
        keep, leaving, gains, mark = one(
            functools.partial(merge_kernel, gain_at),
            "add_first",
            [
                ("whole", keep_low),
                ("whole", keep_high),
                ("whole", send(kv_send, token_steps[-1])),
                ("whole", w_keep),
                ("whole", send(w_send, token_steps[-1])),
                ("whole", gains),
            ],
            [
                ("whole", shape_of((half // 2, lanes), low)),
                ("whole", shape_of((half // 2, lanes), low)),
                ("whole", shape_of(gains.shape, full)),
            ],
            [],
            2,
            [late_mark],
        )
        others = {0: [down_chain.step([mark])]}

        def between(at, token):
            if at < 2:
                others[at + 1] = [late_chain.step([token]), down_chain.step([token])]

        keep, come, gains = scatter_halves(
            keep, leaving, token_steps[:-1], "add_chain", gains, base + gain_at, others, between
        )
        input_grad, query_w_grad, key_w_grad, value_w_grad, gains, _ = one(
            functools.partial(final_kernel, base),
            "last_gradients",
            [("whole", keep), ("whole", come)] + ends + [("whole", gains)],
            [
                input_shape,
                ("whole", shape_of((1, query_weight.shape[1]), full)),
                ("whole", shape_of((1, key_weight.shape[1]), full)),
                ("whole", shape_of((1, value_weight.shape[1]), full)),
                ("whole", shape_of((2, width), full)),
            ],
            end_scratch,
            1,
        )
        gain_sums = (gains[0], gains[1])
    else:
        for _ in range(2):
            late_chain.step([])
        for _ in range(3):
            down_chain.step([])
        kv_keep = jnp.concatenate([keep_low, keep_high], axis=1)
        kv_sum = scatter_halves(kv_keep, kv_send, token_steps, "add_kv")
        qkv_sum = scatter_halves(w_keep, w_send, row_steps, "add_qkv")
        gains = lax.psum(gains, "ctx").reshape(2, width)
        gain_sums = (gains[0], gains[1])
        input_grad, _ = one(
            functools.partial(final_kernel, 0),
            "input_gradient",
            [("whole", kv_sum), ("whole", jnp.zeros_like(kv_sum))] + ends,
            [input_shape],
            end_scratch,
            1,
        )
        qkv_rows = unfold_rows(qkv_sum, columns, columns // fold)
        query_w_grad, key_w_grad, value_w_grad = (
            own_piece(qkv_rows[:, first:last], device, low_bits)
            for first, last in (
                (0, width),
                (width, width + KV_WIDTH),
                (width + KV_WIDTH, columns),
            )
        )

    def piece_of(piece_rows):
        return own_piece(piece_rows, device, low_bits)

    late_sum, down_sum = late_chain.keep, down_chain.keep
    ff_rows = unfold_rows(late_sum, 2 * ff, ff_folded)
    down_rows = jnp.concatenate(
        [down_sum[:, a * width : (a + 1) * width] for a in range(device_groups)], axis=0
    )
    output_rows = unfold_rows(late_sum[:, out_at:], width, width // fold)
    return (
        block_out,
        input_grad.T,
        gain_sums[0],
        query_w_grad,
        key_w_grad,
        value_w_grad,
        piece_of(output_rows),
        gain_sums[1],
        piece_of(ff_rows[:, :ff]),
        piece_of(ff_rows[:, ff:]),
        piece_of(down_rows),
    )


def solution(mesh):
    row = P("ctx", None)
    in_specs = (row, P(), row, row, row, row, P(), row, row, row, P(), P(), row)
    out_specs = (row, row, P(), row, row, row, row, P(), row, row, row)
    return jax.shard_map(body, mesh=mesh, in_specs=in_specs, out_specs=out_specs, check_vma=False)
```
